32 devices in a mesh: dp: 2 (over x), blk: 4 (over y, core), tensor: 4 (over z).
Axes of the slice: x: 2, y: 2, z: 4, core: 2. Of those that a mesh axis runs over, the one named last changes fastest.
Arguments:
- tokens: bfloat16 [8, 512, 768], P('dp', 'blk'), may hold values from -6 to 6
- bucket_ids: int32 [8], P('dp'), may hold values from 0 to 2, as said below
- seq_lengths: int32 [8, 4], P('dp'), may hold values from 0 to 512, as said below
- w_query: bfloat16 [768, 768], P(None, 'tensor'), may hold values from -0.21875 to 0.21875
- b_query: float32 [768], P('tensor'), may hold values from -3 to 3
- w_key: bfloat16 [768, 768], P(None, 'tensor'), may hold values from -0.21875 to 0.21875
- w_value: bfloat16 [768, 768], P(None, 'tensor'), may hold values from -0.21875 to 0.21875
- b_value: float32 [768], P('tensor'), may hold values from -3 to 3
- w_out: bfloat16 [768, 768], P('tensor'), may hold values from -1.25 to 1.25
- b_out: float32 [768], replicated, may hold values from -3 to 3
- norm1_gain: float32 [768], replicated, may hold values from 0.25 to 1.75
- norm1_bias: float32 [768], replicated, may hold values from -3 to 3
- w_inner: bfloat16 [768, 3072], P(None, 'tensor'), may hold values from -0.21875 to 0.21875
- b_inner: float32 [3072], P('tensor'), may hold values from -3 to 3
- w_outer: bfloat16 [3072, 768], P('tensor'), may hold values from -0.109375 to 0.109375
- b_outer: float32 [768], replicated, may hold values from -3 to 3
- norm2_gain: float32 [768], replicated, may hold values from 0.25 to 1.75
- norm2_bias: float32 [768], replicated, may hold values from -3 to 3
- cotangent: bfloat16 [8, 512, 768], P('dp', 'blk'), may hold values from -6 to 6
Outputs:
- output: bfloat16 [8, 512, 768], P('dp', 'blk')
- d_tokens: bfloat16 [8, 512, 768], P('dp', 'blk')
- g_w_query: float32 [768, 768], P(None, 'tensor')
- g_b_query: float32 [768], P('tensor')
- g_w_key: float32 [768, 768], P(None, 'tensor')
- g_w_value: float32 [768, 768], P(None, 'tensor')
- g_b_value: float32 [768], P('tensor')
- g_w_out: float32 [768, 768], P('tensor')
- g_b_out: float32 [768], replicated
- g_norm1_gain: float32 [768], replicated
- g_norm1_bias: float32 [768], replicated
- g_w_inner: float32 [768, 3072], P(None, 'tensor')
- g_b_inner: float32 [3072], P('tensor')
- g_w_outer: float32 [3072, 768], P('tensor')
- g_b_outer: float32 [768], replicated
- g_norm2_gain: float32 [768], replicated
- g_norm2_bias: float32 [768], replicated
The draws below stay inside these ranges and needn't reach their ends.
Inputs may be any that keep to these rules, and one draw needn't show every extreme that they name: `bucket_ids`: A row's slots hold 128 * 2**id positions each. Among the 4 rows of each index of dp at least one, drawn from the seed, has id 2. `seq_lengths`: entry s is the length of the sequence in slot s of the row, from a quarter of the slot's positions to all of them; entries for slots past the row's end are 0. The row of id 2 named above has length 512 in slot 0.
All inputs are finite; a program needn't handle non-finite values.
Results may differ from the reference program's by a relative error of at most 0.03.
Values may be sent and summed in bfloat16 or wider, within the bound.
No kernel may reach another device: no remote copies, remote signals or barrier semaphores. Data moves between devices by JAX's collectives and lax.ppermute only.
A program may use at most 128 MiB of HBM per device.

```python
import jax
import jax.numpy as jnp
from jax import lax

D = 768
HEADS = 12
FF = 3072
HEAD_DIM = 64
BLOCK = 128
ROWS_DEV = 4
ROWS = 8
ROW_LEN = 512
N_DP = 2
N_BLK = 4


def row_plan(key):
    pick_key, bucket_key, length_key = jax.random.split(key, 3)
    bucket = jax.random.randint(bucket_key, (ROWS,), 0, 3).astype(jnp.int32)
    chosen = jax.random.randint(pick_key, (ROWS // ROWS_DEV,), 0, ROWS_DEV)
    forced = jnp.arange(ROWS) % ROWS_DEV == jnp.repeat(chosen, ROWS_DEV)
    bucket = jnp.where(forced, 2, bucket).astype(jnp.int32)
    factor = jnp.where(bucket == 0, 1, jnp.where(bucket == 1, 2, 4))
    slot_size = BLOCK * factor
    slot_count = 4 // factor
    lowest = jnp.maximum(slot_size // 4, 1)[:, None]
    lengths = jax.random.randint(length_key, (ROWS, 4), lowest, slot_size[:, None] + 1)
    slot_ids = jnp.arange(4)[None, :]
    lengths = jnp.where(forced[:, None] & (slot_ids == 0), slot_size[:, None], lengths)
    lengths = jnp.where(slot_ids < slot_count[:, None], lengths, 0)
    return (bucket, lengths.astype(jnp.int32))


def draw_bucket_ids(key, part):
    return row_plan(key)[0]


def draw_seq_lengths(key, part):
    return row_plan(key)[1]


def shard_levels(own_key, shape, cuts, least, largest):
    def one(dim, parts):
        heights = jax.random.uniform(jax.random.fold_in(jax.random.fold_in(own_key, 6), dim), (parts,), jnp.float32, least / len(cuts), largest / len(cuts))
        return jnp.repeat(jnp.exp(heights), shape[dim] // parts).reshape((-1,) + (1,) * (len(shape) - dim - 1))

    level = one(*cuts[0])
    for cut in cuts[1:]:
        level = level * one(*cut)
    return level


def bell_draw(rng, extent, scale, most, shards=(), kind=jnp.bfloat16):
    entries = scale * jax.random.normal(rng, extent, jnp.float32)
    if shards:
        entries = entries * shard_levels(rng, extent, shards, -0.22, 0.18)
    return jnp.clip(entries, -most, most).astype(kind)


def setup_inputs(seed: int = 0) -> dict:
    splits = jax.random.split(jax.random.key(seed), 20)
    return {
        "tokens": bell_draw(splits[0], (ROWS, ROW_LEN, D), 1.0, 6.0, ((0, 2), (1, 4))),
        "bucket_ids": draw_bucket_ids(jax.random.fold_in(splits[19], 71), 0),
        "seq_lengths": draw_seq_lengths(jax.random.fold_in(splits[19], 71), 0),
        "w_query": bell_draw(splits[3], (D, D), D ** -0.5, 0.21875, ((1, 4),)),
        "b_query": bell_draw(splits[4], (D,), 0.5, 3.0, ((0, 4),), jnp.float32),
        "w_key": bell_draw(splits[5], (D, D), D ** -0.5, 0.21875, ((1, 4),)),
        "w_value": bell_draw(splits[6], (D, D), D ** -0.5, 0.21875, ((1, 4),)),
        "b_value": bell_draw(splits[7], (D,), 0.5, 3.0, ((0, 4),), jnp.float32),
        "w_out": bell_draw(splits[8], (D, D), (D // 32) ** -0.5, 1.25, ((0, 4),)),
        "b_out": bell_draw(splits[9], (D,), 0.5, 3.0, (), jnp.float32),
        "norm1_gain": jnp.clip(1.0 + 0.15 * jax.random.normal(splits[10], (D,), jnp.float32), 0.25, 1.75),
        "norm1_bias": bell_draw(splits[11], (D,), 0.5, 3.0, (), jnp.float32),
        "w_inner": bell_draw(splits[12], (D, FF), D ** -0.5, 0.21875, ((1, 4),)),
        "b_inner": bell_draw(splits[13], (FF,), 0.5, 3.0, ((0, 4),), jnp.float32),
        "w_outer": bell_draw(splits[14], (FF, D), FF ** -0.5, 0.109375, ((0, 4),)),
        "b_outer": bell_draw(splits[15], (D,), 0.5, 3.0, (), jnp.float32),
        "norm2_gain": jnp.clip(1.0 + 0.15 * jax.random.normal(splits[16], (D,), jnp.float32), 0.25, 1.75),
        "norm2_bias": bell_draw(splits[17], (D,), 0.5, 3.0, (), jnp.float32),
        "cotangent": bell_draw(splits[18], (ROWS, ROW_LEN, D), 1.0, 6.0, ((0, 2), (1, 4))),
    }


@jax.custom_vjp
def low(v):
    return lax.optimization_barrier(v.astype(jnp.bfloat16)).astype(jnp.float32)

@jax.custom_vjp
def low_back(v):
    return v

def low_keep(v):
    return (low(v), None)

def low_pass(kept, grad):
    return (grad,)

def back_keep(v):
    return (v, None)

def back_low(kept, grad):
    return (low(grad),)
low.defvjp(low_keep, low_pass)
low_back.defvjp(back_keep, back_low)
norm_eps = 1e-12
highest = lax.Precision.HIGHEST

def matmul(left, right):
    return jnp.dot(left, right, precision=highest, preferred_element_type=jnp.float32)

def layer_norm(resid, gain, shift):
    center = resid - lax.optimization_barrier(jnp.mean(resid, axis=-1, keepdims=True))
    spread = lax.optimization_barrier(jnp.mean(center * center, axis=-1, keepdims=True))
    return center * lax.rsqrt(spread + norm_eps) * gain + shift

def slot_groups(bucket, lengths, start, count, block_len):
    positions = start + jnp.arange(count, dtype=jnp.int32)
    factor = jnp.where(bucket == 0, 1, jnp.where(bucket == 1, 2, 4)).astype(jnp.int32)
    slot_size = (block_len * factor)[:, None]
    slot_index = positions[None, :] // slot_size
    within = positions[None, :] - slot_index * slot_size
    slot_ids = jnp.arange(lengths.shape[1], dtype=jnp.int32)
    chosen = lax.optimization_barrier(jnp.sum(jnp.where(slot_index[:, :, None] == slot_ids, lengths[:, None, :], 0), axis=-1))
    return slot_index * 2 + jnp.where(within < chosen, 0, 1)

def attend_row(pieces):
    query, key_rows, value_rows, groups = pieces
    seq_len = query.shape[0]
    query_heads = query.reshape(seq_len, HEADS, HEAD_DIM)
    key_heads = key_rows.reshape(seq_len, HEADS, HEAD_DIM)
    value_heads = value_rows.reshape(seq_len, HEADS, HEAD_DIM)
    scores = low_back(jnp.einsum('qhd,khd->hqk', query_heads, key_heads, precision=highest) * HEAD_DIM ** (-0.5))
    allowed = (groups[:, None] == groups[None, :])[None]
    masked = jnp.where(allowed, scores, -1e+30)
    row_top = lax.optimization_barrier(jnp.max(masked, axis=-1, keepdims=True))
    weights = jnp.where(allowed, jnp.exp(masked - row_top), 0.0)
    probs = low(weights / lax.optimization_barrier(jnp.sum(weights, axis=-1, keepdims=True)))
    mixed = jnp.einsum('hqk,khd->qhd', probs, value_heads, precision=highest)
    return mixed.reshape(seq_len, HEADS * HEAD_DIM)

def layer(tokens_f32, w_query, b_query, w_key, w_value, b_value, w_out, b_out, norm1_gain, norm1_bias, w_inner, b_inner, w_outer, b_outer, norm2_gain, norm2_bias, groups):
    row_count, seq_len, model_width = tokens_f32.shape
    flat = tokens_f32.reshape(row_count * seq_len, model_width)
    query = low_back(low(matmul(flat, w_query) + b_query))
    key_rows = low_back(low(matmul(flat, w_key)))
    value_rows = low_back(low(matmul(flat, w_value) + b_value))
    shaped = (query.reshape(row_count, seq_len, model_width), key_rows.reshape(row_count, seq_len, model_width), value_rows.reshape(row_count, seq_len, model_width), groups)
    mixed = lax.map(jax.checkpoint(attend_row), shaped)
    heads_out = low_back(low(mixed.reshape(row_count * seq_len, model_width)))
    attn_out = low_back(matmul(heads_out, w_out) + b_out)
    hidden = layer_norm(flat + attn_out, norm1_gain, norm1_bias)
    inner = low_back(matmul(low(hidden), w_inner) + b_inner)
    act = low(jax.nn.gelu(inner, approximate=False))
    ffn_out = low_back(matmul(act, w_outer) + b_outer)
    result = layer_norm(hidden + ffn_out, norm2_gain, norm2_bias)
    return result.reshape(row_count, seq_len, model_width)

def reference(tokens, bucket_ids, seq_lengths, w_query, b_query, w_key, w_value, b_value, w_out, b_out, norm1_gain, norm1_bias, w_inner, b_inner, w_outer, b_outer, norm2_gain, norm2_bias, cotangent):
    weights_f32 = tuple((item.astype(jnp.float32) for item in (w_query, b_query, w_key, w_value, b_value, w_out, b_out, norm1_gain, norm1_bias, w_inner, b_inner, w_outer, b_outer, norm2_gain, norm2_bias)))

    def one_group(totals, inputs_now):
        group_tokens, group_buckets, group_lengths, group_cot = inputs_now
        groups = slot_groups(group_buckets, group_lengths, 0, ROW_LEN, BLOCK)

        def run_layer(tokens_f32, *weight_list):
            return layer(tokens_f32, *weight_list, groups)
        result, pull = jax.vjp(run_layer, group_tokens.astype(jnp.float32), *weights_f32)
        gradients = pull(group_cot.astype(jnp.float32))
        totals = tuple((total + grad for total, grad in zip(totals, gradients[1:])))
        return (totals, (result.astype(jnp.bfloat16), gradients[0].astype(jnp.bfloat16)))
    zeros = tuple((jnp.zeros_like(item) for item in weights_f32))
    stacked = (tokens.reshape(N_DP, ROWS_DEV, ROW_LEN, D), bucket_ids.reshape(N_DP, ROWS_DEV), seq_lengths.reshape(N_DP, ROWS_DEV, N_BLK), cotangent.reshape(N_DP, ROWS_DEV, ROW_LEN, D))
    totals, (results, d_inputs) = lax.scan(one_group, zeros, stacked)
    return (results.reshape(ROWS, ROW_LEN, D), d_inputs.reshape(ROWS, ROW_LEN, D), totals[0], totals[1], totals[2], totals[3], totals[4], totals[5], totals[6], totals[7], totals[8], totals[9], totals[10], totals[11], totals[12], totals[13], totals[14])
```

```python
import functools

import jax
import jax.numpy as jnp
from jax import lax
from jax.experimental import pallas as pl
from jax.experimental.pallas import tpu as pltpu
from jax.sharding import PartitionSpec as P

HEAD_DIM = 64
BLOCK = 128
LANES = 128
SCALE = HEAD_DIM**-0.5
EPS = 1e-12
f32 = jnp.float32
bf16 = jnp.bfloat16
i32 = jnp.int32
MIB = 1 << 20


def nn(a, b):
    return lax.dot_general(a, b, (((1,), (0,)), ((), ())), preferred_element_type=f32)


def nt(a, b):
    return lax.dot_general(a, b, (((1,), (1,)), ((), ())), preferred_element_type=f32)


def tn(a, b):
    return lax.dot_general(a, b, (((0,), (0,)), ((), ())), preferred_element_type=f32)


def mean(v):
    return jnp.mean(v, axis=-1, keepdims=True)


def col_sum(v):
    return jnp.sum(v, axis=0, keepdims=True)


def rows8(*rows):
    width = rows[0].shape[1]
    pad = jnp.zeros((8 - len(rows), width), f32)
    return jnp.concatenate(rows + (pad,), axis=0)


def shape(dims, dtype):
    return jax.ShapeDtypeStruct(dims, dtype)


SMEM = pl.BlockSpec(memory_space=pltpu.SMEM)
VMEM = pl.BlockSpec(memory_space=pltpu.VMEM)


def cost(flops, nbytes, trans=0):
    return pl.CostEstimate(flops=int(flops), bytes_accessed=int(nbytes), transcendentals=int(trans))


def plain(kernel, outs, specs, name, vmem=32, scratch=(), estimate=None):
    return pl.pallas_call(
        kernel,
        out_shape=outs,
        in_specs=specs,
        out_specs=jax.tree.map(lambda _: VMEM, outs),
        scratch_shapes=list(scratch),
        compiler_params=pltpu.CompilerParams(vmem_limit_bytes=vmem * MIB),
        cost_estimate=estimate,
        name=name,
    )


def chunked(kernel, outs, specs, name, vmem=32, scratch=(), estimate=None):
    def whole(s):
        nd = len(s.shape)
        return pl.BlockSpec(s.shape, lambda i, at: (0,) * nd)

    return pl.pallas_call(
        kernel,
        out_shape=outs,
        grid_spec=pltpu.PrefetchScalarGridSpec(
            num_scalar_prefetch=1,
            grid=(1,),
            in_specs=specs,
            out_specs=jax.tree.map(whole, outs),
            scratch_shapes=list(scratch),
        ),
        compiler_params=pltpu.CompilerParams(vmem_limit_bytes=vmem * MIB),
        cost_estimate=estimate,
        name=name,
    )


def whole_of(a):
    nd = a.ndim
    return pl.BlockSpec(a.shape, lambda i, at: (0,) * nd)


def block_of(rows, width):
    return pl.BlockSpec((rows, width), lambda i, at: (at[0], 0))


def kv_kernel(tok, wk, wv, bv, kv, wkv):
    heads = wk.shape[1] // HEAD_DIM
    cols, bias = [], []
    for h in range(heads):
        part = slice(h * HEAD_DIM, (h + 1) * HEAD_DIM)
        cols += [wk[:, part], wv[:, part]]
        bias += [jnp.zeros((1, HEAD_DIM), f32), bv[:, part]]
    both = jnp.concatenate(cols, axis=1)
    wkv[...] = both
    kv[...] = (nn(tok[...], both) + jnp.concatenate(bias, axis=1)).astype(bf16)


def q_kernel(tok, wq, bq, q):
    heads = wq.shape[1] // HEAD_DIM
    full = (nn(tok[...], wq[...]) + bq[...]).astype(bf16) * jnp.asarray(SCALE, bf16)
    zero = jnp.zeros((full.shape[0], HEAD_DIM), bf16)
    cols = []
    for h in range(heads):
        cols += [full[:, h * HEAD_DIM : (h + 1) * HEAD_DIM], zero]
    q[...] = jnp.concatenate(cols, axis=1)


def wout_kernel(n, z, *refs):
    out = refs[n]
    for k in range(n):
        j = lax.rem(z[0] - k + n, n)
        out[pl.ds(pl.multiple_of(j * LANES, LANES), LANES), :] = refs[k][:LANES, :]
        at = n * LANES + j * HEAD_DIM
        out[pl.ds(pl.multiple_of(at, HEAD_DIM), HEAD_DIM), :] = refs[k][LANES:, :]


def attend_kernel(n_blk, bucket, lens, blk, q, *refs):
    kvs, hp, probs = refs[:n_blk], refs[n_blk], refs[n_blk + 1]
    rows = bucket.shape[0]
    heads = q.shape[1] // LANES
    b = blk[0]
    q_at = lax.broadcasted_iota(i32, (BLOCK, 1), 0)
    k_at = lax.broadcasted_iota(i32, (1, BLOCK), 1)
    for r in range(rows):
        bk = bucket[r]
        size = BLOCK << bk
        slot = b >> bk
        limit = lens[r, slot]
        q_in = jnp.where(q_at + (b * BLOCK - slot * size) < limit, 1, 0)
        k_in = []
        for j in range(n_blk):
            kb = b ^ j
            k_slot = kb >> bk
            inside = jnp.where(k_at + (kb * BLOCK - k_slot * size) < limit, 1, 0)
            k_in.append(jnp.where(k_slot == slot, inside, 2))
        allowed = q_in == jnp.concatenate(k_in, axis=1)
        at = slice(r * BLOCK, (r + 1) * BLOCK)
        outs = []
        for h in range(heads):
            lanes = slice(h * LANES, (h + 1) * LANES)
            kvh = jnp.concatenate([kv[at, lanes] for kv in kvs], axis=0)
            scores = jnp.where(allowed, nt(q[at, lanes], kvh), -1e30)
            weights = jnp.exp(scores - jnp.max(scores, axis=-1, keepdims=True))
            total = jnp.sum(weights, axis=-1, keepdims=True)
            p = (weights / total).astype(bf16)
            probs[(r * heads + h) * BLOCK : (r * heads + h + 1) * BLOCK, :] = p
            outs.append(nn(p, kvh)[:, HEAD_DIM:].astype(bf16))
        base = r * (BLOCK + HEAD_DIM)
        hp[base : base + BLOCK, :] = jnp.concatenate(outs[:2], axis=1)
        hp[base + BLOCK : base + BLOCK + HEAD_DIM, :] = jnp.concatenate(
            [outs[2][:HEAD_DIM], outs[2][HEAD_DIM:]], axis=1
        )


def ffn_kernel(n, at, tok, wfull, b_out, g1, b1, w_in, b_in, w_outer, *refs):
    hps = refs[:n]
    part, n1_out, s1_out, low_out, act_out, slope_out, held = refs[n:]
    z = at[1]
    for k in range(n):
        held[lax.rem(z - k + n, n)] = hps[k][...]
    pair = [held[j, :BLOCK, :] for j in range(n)]
    last = [
        jnp.concatenate([held[j, BLOCK:, :HEAD_DIM], held[j, BLOCK:, HEAD_DIM:]], axis=0)
        for j in range(n)
    ]
    attn = nn(jnp.concatenate(pair + last, axis=1), wfull[...])
    resid = tok[...].astype(f32) + (attn + b_out[...])
    center = resid - mean(resid)
    s1 = lax.rsqrt(mean(center * center) + EPS)
    n1 = center * s1
    low = (n1 * g1[...] + b1[...]).astype(bf16)
    inner = nn(low, w_in[...]) + b_in[...]
    cdf = 0.5 * (1.0 + lax.erf(inner * (0.5**0.5)))
    act = (inner * cdf).astype(bf16)
    slope = cdf + inner * (0.3989422804014327 * jnp.exp(-0.5 * inner * inner))
    part[...] = nn(act, w_outer[...]).astype(bf16)
    n1_out[...] = n1
    s1_out[...] = jnp.broadcast_to(s1, s1_out.shape)
    low_out[...] = low
    act_out[...] = act
    slope_out[...] = slope.astype(bf16)


def ffn_back_kernel(
    at, cot, n1, slope, ffn, g1, b1, b_outer, g2, b2, w_in, w_outer,
    out, dres2_out, dffn_out, dinner_out, part, sums,
):
    hidden = n1[...] * g1[...] + b1[...]
    resid = hidden + (ffn[...].astype(f32) + b_outer[...])
    center = resid - mean(resid)
    s2 = lax.rsqrt(mean(center * center) + EPS)
    n2 = center * s2
    out[...] = (n2 * g2[...] + b2[...]).astype(bf16)
    ct = cot[...].astype(f32)
    dn = ct * g2[...]
    dres2 = s2 * (dn - mean(dn) - n2 * mean(dn * n2))
    dffn = dres2.astype(bf16)
    dinner = (nt(dffn, w_outer[...]) * slope[...].astype(f32)).astype(bf16)
    part[...] = nt(dinner, w_in[...]).astype(bf16)
    dres2_out[...] = dres2
    dffn_out[...] = dffn
    dinner_out[...] = dinner
    sums[...] = rows8(
        col_sum(ct * n2), col_sum(ct), col_sum(dffn.astype(f32)), col_sum(dinner.astype(f32))
    )


def attend_back_kernel(n_blk, at, dh, dres2, n1, s1, g1, w_out, q, probs, *refs):
    kvs = refs[:n_blk]
    dres1_out, dattn_out, sums, dq_out, send, keep = refs[n_blk:]
    heads = q.shape[1] // LANES
    dhidden = dh[...].astype(f32) + dres2[...]
    norm = n1[...]
    dn = dhidden * g1[...]
    dres1 = s1[:, :1] * (dn - mean(dn) - norm * mean(dn * norm))
    dattn = dres1.astype(bf16)
    dres1_out[...] = dres1
    dattn_out[...] = dattn
    sums[...] = rows8(col_sum(dhidden * norm), col_sum(dhidden), col_sum(dattn.astype(f32)))
    zero = jnp.zeros((HEAD_DIM, w_out.shape[1]), bf16)
    spread = []
    for h in range(heads):
        spread += [zero, w_out[h * HEAD_DIM : (h + 1) * HEAD_DIM, :]]
    dheads = nt(dattn, jnp.concatenate(spread, axis=0)).astype(bf16)
    dqs = []
    for h in range(heads):
        lanes = slice(h * LANES, (h + 1) * LANES)
        kvh = jnp.concatenate([kv[:, lanes] for kv in kvs], axis=0)
        p = probs[h * BLOCK : (h + 1) * BLOCK, :]
        pf = p.astype(f32)
        dp = nt(dheads[:, lanes], kvh)
        delta = jnp.sum(pf * dp, axis=-1, keepdims=True)
        ds = (pf * (dp - delta)).astype(bf16)
        dqs.append((nn(ds, kvh) * SCALE)[:, :HEAD_DIM].astype(bf16))
        left = jnp.concatenate([q[:, lanes], dheads[:, lanes]], axis=0)
        dkv = tn(left, jnp.concatenate([ds, p], axis=0)).astype(bf16)
        for j in range(n_blk):
            target = keep if j % 2 == 0 else send
            target[j // 2, lanes, :] = dkv[:, j * BLOCK : (j + 1) * BLOCK]
    dq_out[...] = jnp.concatenate(dqs, axis=1)


def input_kernel(dq, keep, recv, far, wq, wkv, part, dkv_t, sums):
    total = keep[0].astype(f32) + recv[0].astype(f32) + far[...].astype(f32)
    low_t = total.astype(bf16)
    low = low_t.T
    part[...] = (nt(dq[...], wq[...]) + nt(low, wkv[...])).astype(bf16)
    dkv_t[...] = low_t
    width = sums.shape[1]
    first = col_sum(dq[...].astype(f32))
    second = col_sum(low.astype(f32))
    sums[...] = rows8(
        jnp.concatenate([first, jnp.zeros((1, width - first.shape[1]), f32)], axis=1),
        jnp.concatenate([second, jnp.zeros((1, width - second.shape[1]), f32)], axis=1),
    )


def ordered_sum(n, z, refs, held):
    for k in range(n):
        held[lax.rem(z - k + n, n)] = refs[k][...]
    total = held[0]
    for j in range(1, n):
        total = total + held[j]
    return total


def pick(first, one, other):
    return jnp.where(first, one, other)


def ffn_grad_kernel(n, at, *refs):
    low, dinner, act, dffn, sums = (refs[i * n : (i + 1) * n] for i in range(5))
    keep, send, held = refs[5 * n :]
    first = at[2] == 0
    tail = ordered_sum(n, at[1], sums, held).astype(bf16)
    a = jnp.concatenate([pick(first, x[...], y[...]) for x, y in zip(low, act)], axis=0)
    b = jnp.concatenate([pick(first, x[...], y[...]) for x, y in zip(dinner, dffn)], axis=0)
    c = jnp.concatenate([pick(first, y[...], x[...]) for x, y in zip(low, act)], axis=0)
    d = jnp.concatenate([pick(first, y[...], x[...]) for x, y in zip(dinner, dffn)], axis=0)
    rows = a.shape[1]
    rest = keep.shape[0] - rows
    tail = jnp.concatenate([tail, jnp.zeros((rest - 8, tail.shape[1]), bf16)], axis=0)
    send[:rows, :] = tn(c, d).astype(bf16)
    send[rows:, :] = tail
    keep[:rows, :] = tn(a, b).astype(bf16)
    keep[rows:, :] = tail


def attend_grad_kernel(n, at, tok, hp, *refs):
    dattn, dq, dkv_t, sums1, sums2 = (refs[i * n : (i + 1) * n] for i in range(5))
    keep, send, held1, held2 = refs[5 * n :]
    z = at[1]
    first = at[2] == 0
    total1 = ordered_sum(n, z, sums1, held1)
    total2 = ordered_sum(n, z, sums2, held2)
    tail = jnp.concatenate([total1, total2], axis=0).astype(bf16)
    toks, heads = [], []
    for k in range(n):
        c = lax.rem(z - k + n, n)
        toks.append(tok[pl.ds(pl.multiple_of(c * BLOCK, BLOCK), BLOCK), :])
        step = BLOCK + HEAD_DIM
        h = hp[pl.ds(pl.multiple_of(c * step, HEAD_DIM), step), :]
        odd = jnp.concatenate([h[BLOCK:, :HEAD_DIM], h[BLOCK:, HEAD_DIM:]], axis=0)
        heads.append(jnp.concatenate([h[:BLOCK, :], odd], axis=1))
    toks = jnp.concatenate(toks, axis=0)
    g_out = tn(jnp.concatenate(heads, axis=0), jnp.concatenate([x[...] for x in dattn], axis=0))
    g_q = tn(jnp.concatenate([x[...] for x in dq], axis=0), toks)
    g_kv = nn(jnp.concatenate([x[...] for x in dkv_t], axis=1), toks)
    one = jnp.concatenate([g_out, g_q], axis=0).astype(bf16)
    two = g_kv.astype(bf16)
    rows = two.shape[0]
    rest = keep.shape[0] - rows
    tail = jnp.concatenate([tail, jnp.zeros((rest - 16, tail.shape[1]), bf16)], axis=0)
    send[:rows, :] = pick(first, two, one)
    send[rows:, :] = tail
    keep[:rows, :] = pick(first, one, two)
    keep[rows:, :] = tail


def gather_kernel(m, i, *refs):
    out = refs[m]
    for s in range(m):
        out[i[0] ^ s] = refs[s][...]


def ffn_final_kernel(at, mine, other, g_in, g_outer, tail):
    first = at[2] == 0
    rows = g_in.shape[0]
    a = mine[...]
    b = other[...]
    g_in[...] = pick(first, a[:rows], b[:rows]).astype(f32)
    g_outer[...] = pick(first, b[:rows], a[:rows]).astype(f32)
    tail[...] = pick(first, a[rows : rows + 16], b[rows : rows + 16]).astype(f32)


def attend_final_kernel(at, mine, other, g_out, g_q, g_k, g_v, tail):
    first = at[2] == 0
    width = g_out.shape[0]
    a = mine[...]
    b = other[...]
    one = pick(first, a, b).astype(f32)
    two = pick(first, b, a).astype(f32)
    g_out[...] = one[:width]
    g_q[...] = one[width : 2 * width].T
    ks, vs = [], []
    for h in range(width // HEAD_DIM):
        ks.append(two[h * LANES : h * LANES + HEAD_DIM])
        vs.append(two[h * LANES + HEAD_DIM : (h + 1) * LANES])
    g_k[...] = jnp.concatenate(ks, axis=0).T
    g_v[...] = jnp.concatenate(vs, axis=0).T
    tail[...] = one[2 * width : 2 * width + 16]


def output_kernel(n, at, *refs):
    out = refs[n]
    for k in range(n):
        out[lax.rem(at[1] - k + n, n)] = refs[k][...]


def solution(mesh):
    n_dp = mesh.shape["dp"]
    n_blk = mesh.shape["blk"]
    n = mesh.shape["tensor"]
    half_blk = n_blk // 2
    m = n_dp * half_blk

    def shift(v, k):
        return lax.ppermute(v, "tensor", [(i, (i + k) % n) for i in range(n)])

    def flip(v, bit):
        return lax.ppermute(v, "blk", [(i, i ^ bit) for i in range(n_blk)])

    def flip_member(v, s):
        perm = []
        for dp in range(n_dp):
            for blk in range(n_blk):
                i = (dp * half_blk + blk // 2) ^ s
                to = (i // half_blk) * n_blk + (i % half_blk) * 2 + blk % 2
                perm.append((dp * n_blk + blk, to))
        return lax.ppermute(v, ("dp", "blk"), perm)

    def sum_grads(keep, send, member, name):
        recv = flip(send, 1)
        rows = keep.shape[0] // m
        width = keep.shape[1]
        keep3 = keep.reshape(m, rows, width)
        recv3 = recv.reshape(m, rows, width)

        def piece(s):
            mine = lax.dynamic_index_in_dim(keep3, member ^ s, 0, keepdims=False)
            theirs = lax.dynamic_index_in_dim(recv3, member ^ s, 0, keepdims=False)
            return mine.astype(f32) + theirs.astype(f32)

        got = [flip_member(piece(s).astype(bf16), s) for s in range(1, m)]
        total = piece(0)
        for part in got:
            total = total + part.astype(f32)
        total = total.astype(bf16)
        every = [total] + [flip_member(total, s) for s in range(1, m)]
        mine = plain(
            functools.partial(gather_kernel, m),
            shape((m, rows, width), bf16),
            [SMEM] + [VMEM] * m,
            name,
        )(member.reshape(1), *every)
        mine = mine.reshape(m * rows, width)
        return mine, flip(mine, 1)

    def body(
        tokens, bucket_ids, seq_lengths, w_query, b_query, w_key, w_value, b_value, w_out, b_out,
        norm1_gain, norm1_bias, w_inner, b_inner, w_outer, b_outer, norm2_gain, norm2_bias,
        cotangent,
    ):
        row_count, block, width = tokens.shape
        count = row_count * block
        local = w_query.shape[1]
        heads = local // HEAD_DIM
        hidden_units = w_inner.shape[1]
        blk = lax.axis_index("blk").astype(i32)
        z = lax.axis_index("tensor").astype(i32)
        member = (lax.axis_index("dp") * half_blk + blk // 2).astype(i32)
        tok = tokens.reshape(count, width)
        cot = cotangent.reshape(count, width)
        row = lambda v: v.reshape(1, -1)
        ats = [jnp.stack([lax.rem(z - k + n, n), z, blk % 2]).astype(i32) for k in range(n)]

        kv, wkv = plain(
            kv_kernel,
            (shape((count, heads * LANES), bf16), shape((width, heads * LANES), bf16)),
            [VMEM] * 4,
            "kv_rows",
            estimate=cost(4 * count * width * local, 3 * MIB),
        )(tok, w_key, w_value, row(b_value))
        kv_far = flip(kv, 2)
        kv_core = flip(kv, 1)
        wouts = [w_out] + [shift(w_out, k) for k in range(1, n)]
        q = plain(
            q_kernel,
            shape((count, heads * LANES), bf16),
            [VMEM] * 3,
            "query_rows",
            estimate=cost(2 * count * width * local, 2 * MIB),
        )(tok, w_query, row(b_query))
        kv_both = flip(kv_far, 1)
        kvs = [kv, kv_core, kv_far, kv_both]
        hp, probs = plain(
            functools.partial(attend_kernel, n_blk),
            (
                shape((row_count * (BLOCK + HEAD_DIM), LANES), bf16),
                shape((row_count * heads * BLOCK, n_blk * BLOCK), bf16),
            ),
            [SMEM] * 3 + [VMEM] * (1 + n_blk),
            "attend",
            estimate=cost(2e9, 4 * MIB),
        )(bucket_ids, seq_lengths, blk.reshape(1), q, *kvs)
        hps = [hp] + [shift(hp, k) for k in range(1, n)]
        wfull = plain(
            functools.partial(wout_kernel, n),
            shape((n * local, width), bf16),
            [SMEM] + [VMEM] * n,
            "all_w_out",
            estimate=cost(0, 3 * MIB),
        )(z.reshape(1), *wouts)

        chunk = lambda w, dt: shape((BLOCK, w), dt)
        order = [k for k in range(1, n)] + [0]

        def ffn(k):
            weights = (wfull, row(b_out), row(norm1_gain), row(norm1_bias), w_inner, row(b_inner), w_outer)
            return chunked(
                functools.partial(ffn_kernel, n),
                (
                    chunk(width, bf16), chunk(width, f32), chunk(LANES, f32), chunk(width, bf16),
                    chunk(hidden_units, bf16), chunk(hidden_units, bf16),
                ),
                [block_of(BLOCK, width)]
                + [whole_of(w) for w in weights]
                + [block_of(BLOCK + HEAD_DIM, LANES)] * n,
                "ffn",
                scratch=[pltpu.VMEM((n, BLOCK + HEAD_DIM, LANES), bf16)],
                estimate=cost(6 * BLOCK * width * width, 5 * MIB),
            )(ats[k], tok, *weights, *hps)

        def scatter_gather(parts, extra=None):
            total = parts[0].astype(f32)
            for k in range(1, n):
                total = total + shift(parts[k], -k).astype(f32)
            if extra is not None:
                total = total + extra
            total = total.astype(bf16)
            return [total] + [shift(total, k) for k in range(1, n)]

        first = {k: ffn(k) for k in order}
        ffns = scatter_gather([first[k][0] for k in range(n)])

        def ffn_back(k):
            _, n1, _, _, _, slope = first[k]
            args = (n1, slope, ffns[k], row(norm1_gain), row(norm1_bias), row(b_outer),
                    row(norm2_gain), row(norm2_bias), w_inner, w_outer)
            return chunked(
                ffn_back_kernel,
                (
                    chunk(width, bf16), chunk(width, f32), chunk(width, bf16),
                    chunk(hidden_units, bf16), chunk(width, bf16), shape((8, width), f32),
                ),
                [block_of(BLOCK, width)] + [whole_of(a) for a in args],
                "ffn_back",
                estimate=cost(4 * BLOCK * width * width, 5 * MIB),
            )(ats[k], cot, *args)

        second = {k: ffn_back(k) for k in [0] + order[:-1]}
        dhs = scatter_gather([second[k][4] for k in range(n)])

        half = width + 16 * m
        half += -half % (16 * m)
        keep1, send1 = chunked(
            functools.partial(ffn_grad_kernel, n),
            (shape((half, width), bf16), shape((half, width), bf16)),
            [pl.BlockSpec((BLOCK, width), lambda i, at: (0, 0))] * (4 * n)
            + [pl.BlockSpec((8, width), lambda i, at: (0, 0))] * n,
            "ffn_grads",
            vmem=48,
            scratch=[pltpu.VMEM((n, 8, width), f32)],
            estimate=cost(4 * count * width * width, 6 * MIB),
        )(
            ats[0],
            *[first[k][3] for k in range(n)],
            *[second[k][3] for k in range(n)],
            *[first[k][4] for k in range(n)],
            *[second[k][2] for k in range(n)],
            *[second[k][5] for k in range(n)],
        )
        mine1, other1 = sum_grads(keep1, send1, member, "gather_ffn_grads")

        def attend_back(k):
            _, n1, s1, _, _, _ = first[k]
            args = (dhs[k], second[k][1], n1, s1, row(norm1_gain), w_out)
            return chunked(
                functools.partial(attend_back_kernel, n_blk),
                (
                    chunk(width, f32), chunk(width, bf16), shape((8, width), f32), chunk(local, bf16),
                    shape((half_blk, heads * LANES, BLOCK), bf16),
                    shape((half_blk, heads * LANES, BLOCK), bf16),
                ),
                [whole_of(a) for a in args]
                + [block_of(BLOCK, heads * LANES), block_of(heads * BLOCK, n_blk * BLOCK)]
                + [block_of(BLOCK, heads * LANES)] * n_blk,
                "attend_back",
                estimate=cost(1e9, 4 * MIB),
            )(ats[k], *args, q, probs, *kvs)

        third = {k: attend_back(k) for k in [0] + order[:-1]}

        def input_part(k):
            _, _, _, dq, send, keep = third[k]
            recv = flip(send, 1)
            out = (keep[1].astype(f32) + recv[1].astype(f32)).astype(bf16)
            far = flip(out, 2)
            return plain(
                input_kernel,
                (chunk(width, bf16), shape((heads * LANES, BLOCK), bf16), shape((8, width), f32)),
                [VMEM] * 6,
                "input_part",
                estimate=cost(6 * BLOCK * width * local, 2 * MIB),
            )(dq, keep, recv, far, w_query, wkv)

        fourth = {k: input_part(k) for k in order}
        d_tok = scatter_gather([fourth[k][0] for k in range(n)], third[0][0])

        rows2 = 2 * local + 16
        rows2 += -rows2 % (16 * m)
        keep2, send2 = plain(
            functools.partial(attend_grad_kernel, n),
            (shape((rows2, width), bf16), shape((rows2, width), bf16)),
            [SMEM] + [VMEM] * (2 + 5 * n),
            "attend_grads",
            vmem=48,
            scratch=[pltpu.VMEM((n, 8, width), f32)] * 2,
            estimate=cost(2 * count * width * 4 * local, 5 * MIB),
        )(
            ats[0], tok, hp,
            *[third[k][1] for k in range(n)],
            *[third[k][3] for k in range(n)],
            *[fourth[k][1] for k in range(n)],
            *[third[k][2] for k in range(n)],
            *[fourth[k][2] for k in range(n)],
        )
        mine2, other2 = sum_grads(keep2, send2, member, "gather_attend_grads")

        assemble = lambda parts, name: plain(
            functools.partial(output_kernel, n),
            shape((row_count, block, width), bf16),
            [SMEM] + [VMEM] * n,
            name,
            estimate=cost(0, 2 * MIB),
        )(ats[0], *parts)
        output = assemble([second[k][0] for k in range(n)], "output_rows")
        d_tokens = assemble(d_tok, "input_grad_rows")

        g_w_inner, g_w_outer, tail1 = plain(
            ffn_final_kernel,
            (shape((width, hidden_units), f32), shape((hidden_units, width), f32), shape((16, width), f32)),
            [SMEM] + [VMEM] * 2,
            "ffn_grads_out",
            estimate=cost(0, 8 * MIB),
        )(ats[0], mine1, other1)
        g_w_out, g_w_query, g_w_key, g_w_value, tail2 = plain(
            attend_final_kernel,
            (shape((local, width), f32),) + (shape((width, local), f32),) * 3 + (shape((16, width), f32),),
            [SMEM] + [VMEM] * 2,
            "attend_grads_out",
            estimate=cost(0, 5 * MIB),
        )(ats[0], mine2, other2)
        g_b_query = tail2[8, :local]
        g_b_value = tail2[9, : heads * LANES].reshape(heads, 2, HEAD_DIM)[:, 1].reshape(local)
        return (
            output, d_tokens, g_w_query, g_b_query, g_w_key, g_w_value, g_b_value, g_w_out,
            tail2[2], tail2[0], tail2[1], g_w_inner, tail1[3], g_w_outer, tail1[2], tail1[0], tail1[1],
        )

    spread, cols, vec, rows_ = P("dp", "blk", None), P(None, "tensor"), P("tensor"), P("tensor", None)
    return jax.shard_map(
        body,
        mesh=mesh,
        in_specs=(
            spread, P("dp"), P("dp", None), cols, vec, cols, cols, vec, rows_, P(), P(), P(),
            cols, vec, rows_, P(), P(), P(), spread,
        ),
        out_specs=(
            spread, spread, cols, vec, cols, cols, vec, rows_, P(), P(), P(), cols, vec, rows_,
            P(), P(), P(),
        ),
        check_vma=False,
    )
```

```python
import functools

import jax
import jax.numpy as jnp
from jax import lax
from jax.experimental import pallas as pl
from jax.experimental.pallas import tpu as pltpu
from jax.sharding import PartitionSpec as P

HEAD_DIM = 64
BLOCK = 128
LANES = 128
SCALE = HEAD_DIM**-0.5
EPS = 1e-12
f32 = jnp.float32
bf16 = jnp.bfloat16
i32 = jnp.int32
MIB = 1 << 20


def nn(a, b):
    return lax.dot_general(a, b, (((1,), (0,)), ((), ())), preferred_element_type=f32)


def nt(a, b):
    return lax.dot_general(a, b, (((1,), (1,)), ((), ())), preferred_element_type=f32)


def tn(a, b):
    return lax.dot_general(a, b, (((0,), (0,)), ((), ())), preferred_element_type=f32)


def mean(v):
    return jnp.mean(v, axis=-1, keepdims=True)


def col_sum(v):
    return jnp.sum(v, axis=0, keepdims=True)


def rows8(*rows):
    width = rows[0].shape[1]
    pad = jnp.zeros((8 - len(rows), width), f32)
    return jnp.concatenate(rows + (pad,), axis=0)


def shape(dims, dtype):
    return jax.ShapeDtypeStruct(dims, dtype)


def near(dims, dtype):
    return pltpu.VMEM(dims, dtype)


SMEM = pl.BlockSpec(memory_space=pltpu.SMEM)
VMEM = pl.BlockSpec(memory_space=pltpu.VMEM)


def cost(flops, nbytes, trans=0):
    return pl.CostEstimate(flops=int(flops), bytes_accessed=int(nbytes), transcendentals=int(trans))


def call(kernel, outs, name, args, scalars=0, vmem=16, scratch=(), estimate=None):
    return pl.pallas_call(
        kernel,
        out_shape=outs,
        in_specs=[SMEM] * scalars + [VMEM] * (len(args) - scalars),
        out_specs=jax.tree.map(lambda _: VMEM, outs),
        scratch_shapes=list(scratch),
        compiler_params=pltpu.CompilerParams(vmem_limit_bytes=vmem * MIB),
        cost_estimate=estimate,
        name=name,
    )(*args)


def chunk_of(ref, c, rows):
    return ref[pl.ds(pl.multiple_of(c * rows, rows), rows), :]


def kv_kernel(tok, wk_t, wv_t, bv, kv, wkv_t):
    heads = wk_t.shape[0] // HEAD_DIM
    rows, bias = [], []
    for h in range(heads):
        part = slice(h * HEAD_DIM, (h + 1) * HEAD_DIM)
        rows += [wk_t[part, :], wv_t[part, :]]
        bias += [jnp.zeros((1, HEAD_DIM), f32), bv[:, part]]
    both = jnp.concatenate(rows, axis=0)
    wkv_t[...] = both
    kv[...] = (nt(tok[...], both) + jnp.concatenate(bias, axis=1)).astype(bf16)


def q_kernel(tok, wq_t, bq, q):
    heads = wq_t.shape[0] // HEAD_DIM
    full = (nt(tok[...], wq_t[...]) + bq[...]).astype(bf16) * jnp.asarray(SCALE, bf16)
    zero = jnp.zeros((full.shape[0], HEAD_DIM), bf16)
    cols = []
    for h in range(heads):
        cols += [full[:, h * HEAD_DIM : (h + 1) * HEAD_DIM], zero]
    q[...] = jnp.concatenate(cols, axis=1)


def attend_kernel(n_blk, at, bucket, lens, q, *refs):
    kvs, hp, probs = refs[:n_blk], refs[n_blk], refs[n_blk + 1]
    rows = bucket.shape[0]
    heads = q.shape[1] // LANES
    b = at[2]
    q_at = lax.broadcasted_iota(i32, (BLOCK, 1), 0)
    k_at = lax.broadcasted_iota(i32, (1, BLOCK), 1)
    for r in range(rows):
        bk = bucket[r]
        size = BLOCK << bk
        slot = b >> bk
        limit = lens[r, slot]
        q_in = jnp.where(q_at + (b * BLOCK - slot * size) < limit, 1, 0)
        k_in = []
        for j in range(n_blk):
            kb = b ^ j
            k_slot = kb >> bk
            inside = jnp.where(k_at + (kb * BLOCK - k_slot * size) < limit, 1, 0)
            k_in.append(jnp.where(k_slot == slot, inside, 2))
        allowed = q_in == jnp.concatenate(k_in, axis=1)
        here = slice(r * BLOCK, (r + 1) * BLOCK)
        outs = []
        for h in range(heads):
            lanes = slice(h * LANES, (h + 1) * LANES)
            kvh = jnp.concatenate([kv[here, lanes] for kv in kvs], axis=0)
            scores = jnp.where(allowed, nt(q[here, lanes], kvh), -1e30)
            weights = jnp.exp(scores - jnp.max(scores, axis=-1, keepdims=True))
            total = jnp.sum(weights, axis=-1, keepdims=True)
            p = (weights / total).astype(bf16)
            probs[(r * heads + h) * BLOCK : (r * heads + h + 1) * BLOCK, :] = p
            outs.append(nn(p, kvh)[:, HEAD_DIM:].astype(bf16))
        base = r * (BLOCK + HEAD_DIM)
        hp[base : base + BLOCK, :] = jnp.concatenate(outs[:2], axis=1)
        hp[base + BLOCK : base + BLOCK + HEAD_DIM, :] = jnp.concatenate(
            [outs[2][:HEAD_DIM], outs[2][HEAD_DIM:]], axis=1
        )


def unpack(h):
    odd = jnp.concatenate([h[BLOCK:, :HEAD_DIM], h[BLOCK:, HEAD_DIM:]], axis=0)
    return jnp.concatenate([h[:BLOCK, :], odd], axis=1)


def ffn_kernel(n, k, at, tok, b_out, g1, b1, w_in, b_in, w_outer, *refs):
    hps, wouts = refs[:n], refs[n : 2 * n]
    part, n1_out, s1_out, low_out, act_out, slope_out, held = refs[2 * n :]
    z = at[0]
    c = lax.rem(z - k + n, n)
    for i in range(n):
        held[lax.rem(z - i + n, n)] = nn(unpack(chunk_of(hps[i], c, BLOCK + HEAD_DIM)), wouts[i][...])
    attn = held[0]
    for j in range(1, n):
        attn = attn + held[j]
    resid = chunk_of(tok, c, BLOCK).astype(f32) + (attn + b_out[...])
    center = resid - mean(resid)
    s1 = lax.rsqrt(mean(center * center) + EPS)
    n1 = center * s1
    low = (n1 * g1[...] + b1[...]).astype(bf16)
    inner = nn(low, w_in[...]) + b_in[...]
    cdf = 0.5 * (1.0 + lax.erf(inner * (0.5**0.5)))
    act = (inner * cdf).astype(bf16)
    slope = cdf + inner * (0.3989422804014327 * jnp.exp(-0.5 * inner * inner))
    part[...] = nn(act, w_outer[...]).astype(bf16)
    n1_out[...] = n1
    s1_out[...] = jnp.broadcast_to(s1, s1_out.shape)
    low_out[...] = low
    act_out[...] = act
    slope_out[...] = slope.astype(bf16)


def ffn_back_kernel(
    n, k, at, cot, n1, slope, ffn, g1, b1, b_outer, g2, b2, w_in, w_outer,
    out, dres2_out, dffn_out, dinner_out, part, sums,
):
    hidden = n1[...] * g1[...] + b1[...]
    resid = hidden + (ffn[...].astype(f32) + b_outer[...])
    center = resid - mean(resid)
    s2 = lax.rsqrt(mean(center * center) + EPS)
    n2 = center * s2
    out[...] = (n2 * g2[...] + b2[...]).astype(bf16)
    ct = chunk_of(cot, lax.rem(at[0] - k + n, n), BLOCK).astype(f32)
    dn = ct * g2[...]
    dres2 = s2 * (dn - mean(dn) - n2 * mean(dn * n2))
    dffn = dres2.astype(bf16)
    dinner = (nt(dffn, w_outer[...]) * slope[...].astype(f32)).astype(bf16)
    part[...] = nt(dinner, w_in[...]).astype(bf16)
    dres2_out[...] = dres2
    dffn_out[...] = dffn
    dinner_out[...] = dinner
    sums[...] = rows8(
        col_sum(ct * n2), col_sum(ct), col_sum(dffn.astype(f32)), col_sum(dinner.astype(f32))
    )


def attend_back_kernel(n_blk, n, k, at, dh, dres2, n1, s1, g1, w_out, q, probs, *refs):
    kvs = refs[:n_blk]
    dres1_out, dattn_out, sums, dq_out, send, keep = refs[n_blk:]
    heads = q.shape[1] // LANES
    c = lax.rem(at[0] - k + n, n)
    here = pl.ds(pl.multiple_of(c * BLOCK, BLOCK), BLOCK)
    dhidden = dh[...].astype(f32) + dres2[...]
    norm = n1[...]
    dn = dhidden * g1[...]
    dres1 = s1[:, :1] * (dn - mean(dn) - norm * mean(dn * norm))
    dattn = dres1.astype(bf16)
    dres1_out[...] = dres1
    dattn_out[...] = dattn
    sums[...] = rows8(col_sum(dhidden * norm), col_sum(dhidden), col_sum(dattn.astype(f32)))
    zero = jnp.zeros((HEAD_DIM, w_out.shape[1]), bf16)
    spread = []
    for h in range(heads):
        spread += [zero, w_out[h * HEAD_DIM : (h + 1) * HEAD_DIM, :]]
    dheads = nt(dattn, jnp.concatenate(spread, axis=0)).astype(bf16)
    dqs = []
    for h in range(heads):
        lanes = slice(h * LANES, (h + 1) * LANES)
        kvh = jnp.concatenate([kv[here, lanes] for kv in kvs], axis=0)
        p = chunk_of(probs, c * heads + h, BLOCK)
        pf = p.astype(f32)
        dp = nt(dheads[:, lanes], kvh)
        delta = jnp.sum(pf * dp, axis=-1, keepdims=True)
        ds = (pf * (dp - delta)).astype(bf16)
        dqs.append((nn(ds, kvh) * SCALE)[:, :HEAD_DIM].astype(bf16))
        left = jnp.concatenate([q[here, lanes], dheads[:, lanes]], axis=0)
        dkv = tn(left, jnp.concatenate([ds, p], axis=0)).astype(bf16)
        for j in range(n_blk):
            target = keep if j % 2 == 0 else send
            target[j // 2, lanes, :] = dkv[:, j * BLOCK : (j + 1) * BLOCK]
    dq_out[...] = jnp.concatenate(dqs, axis=1)


def input_kernel(dq, keep, recv, far, wq_t, wkv_t, part, dkv_t, sums):
    total = keep[0].astype(f32) + recv[0].astype(f32) + far[...].astype(f32)
    low_t = total.astype(bf16)
    low = low_t.T
    part[...] = (nn(dq[...], wq_t[...]) + nn(low, wkv_t[...])).astype(bf16)
    dkv_t[...] = low_t
    width = sums.shape[1]
    first = col_sum(dq[...].astype(f32))
    second = col_sum(low.astype(f32))
    sums[...] = rows8(
        jnp.concatenate([first, jnp.zeros((1, width - first.shape[1]), f32)], axis=1),
        jnp.concatenate([second, jnp.zeros((1, width - second.shape[1]), f32)], axis=1),
    )


def ordered_sum(n, z, refs, held):
    for k in range(n):
        held[lax.rem(z - k + n, n)] = refs[k][...]
    total = held[0]
    for j in range(1, n):
        total = total + held[j]
    return total


def pick(first, one, other):
    return jnp.where(first, one, other)


def ffn_grad_kernel(n, at, *refs):
    low, dinner, act, dffn, sums = (refs[i * n : (i + 1) * n] for i in range(5))
    keep, send, held = refs[5 * n :]
    first = at[1] == 0
    tail = ordered_sum(n, at[0], sums, held).astype(bf16)
    a = jnp.concatenate([pick(first, x[...], y[...]) for x, y in zip(low, act)], axis=0)
    b = jnp.concatenate([pick(first, x[...], y[...]) for x, y in zip(dinner, dffn)], axis=0)
    c = jnp.concatenate([pick(first, y[...], x[...]) for x, y in zip(low, act)], axis=0)
    d = jnp.concatenate([pick(first, y[...], x[...]) for x, y in zip(dinner, dffn)], axis=0)
    rows = a.shape[1]
    rest = keep.shape[0] - rows
    tail = jnp.concatenate([tail, jnp.zeros((rest - 8, tail.shape[1]), bf16)], axis=0)
    send[:rows, :] = tn(c, d).astype(bf16)
    send[rows:, :] = tail
    keep[:rows, :] = tn(a, b).astype(bf16)
    keep[rows:, :] = tail


def attend_grad_kernel(n, at, tok, hp, *refs):
    dattn, dq, dkv_t, sums1, sums2 = (refs[i * n : (i + 1) * n] for i in range(5))
    keep, send, held1, held2 = refs[5 * n :]
    z = at[0]
    first = at[1] == 0
    total1 = ordered_sum(n, z, sums1, held1)
    total2 = ordered_sum(n, z, sums2, held2)
    tail = jnp.concatenate([total1, total2], axis=0).astype(bf16)
    toks, heads = [], []
    for k in range(n):
        c = lax.rem(z - k + n, n)
        toks.append(chunk_of(tok, c, BLOCK))
        heads.append(unpack(chunk_of(hp, c, BLOCK + HEAD_DIM)))
    toks = jnp.concatenate(toks, axis=0)
    g_out = tn(jnp.concatenate(heads, axis=0), jnp.concatenate([x[...] for x in dattn], axis=0))
    g_q = tn(jnp.concatenate([x[...] for x in dq], axis=0), toks)
    g_kv = nn(jnp.concatenate([x[...] for x in dkv_t], axis=1), toks)
    one = jnp.concatenate([g_out, g_q], axis=0).astype(bf16)
    two = g_kv.astype(bf16)
    rows = two.shape[0]
    rest = keep.shape[0] - rows
    tail = jnp.concatenate([tail, jnp.zeros((rest - 16, tail.shape[1]), bf16)], axis=0)
    send[:rows, :] = pick(first, two, one)
    send[rows:, :] = tail
    keep[:rows, :] = pick(first, one, two)
    keep[rows:, :] = tail


def gather_kernel(m, at, *refs):
    out = refs[m]
    for s in range(m):
        out[at[3] ^ s] = refs[s][...]


def ffn_final_kernel(at, mine, other, g_in, g_outer, gain, bias, b_outer, b_in):
    first = at[1] == 0
    rows = g_in.shape[0]
    a = mine[...]
    b = other[...]
    g_in[...] = pick(first, a[:rows], b[:rows]).astype(f32)
    g_outer[...] = pick(first, b[:rows], a[:rows]).astype(f32)
    tail = pick(first, a[rows : rows + 16], b[rows : rows + 16]).astype(f32)
    for i, ref in enumerate((gain, bias, b_outer, b_in)):
        ref[...] = tail[i : i + 1]


def attend_final_kernel(at, mine, other, g_out, g_q, g_k, g_v, gain, bias, b_out, b_q, b_v):
    first = at[1] == 0
    width = g_out.shape[0]
    a = mine[...]
    b = other[...]
    one = pick(first, a, b).astype(f32)
    two = pick(first, b, a).astype(f32)
    g_out[...] = one[:width]
    g_q[...] = one[width : 2 * width]
    tail = one[2 * width : 2 * width + 16]
    values = []
    for h in range(width // HEAD_DIM):
        part = slice(h * HEAD_DIM, (h + 1) * HEAD_DIM)
        g_k[part, :] = two[h * LANES : h * LANES + HEAD_DIM]
        g_v[part, :] = two[h * LANES + HEAD_DIM : (h + 1) * LANES]
        values.append(tail[9:10, h * LANES + HEAD_DIM : (h + 1) * LANES])
    for i, ref in enumerate((gain, bias, b_out)):
        ref[...] = tail[i : i + 1]
    b_q[...] = tail[8:9, :width]
    b_v[...] = jnp.concatenate(values, axis=1)


def output_kernel(n, at, *refs):
    out = refs[n]
    for k in range(n):
        out[lax.rem(at[0] - k + n, n)] = refs[k][...]


def solution(mesh):
    n_dp = mesh.shape["dp"]
    n_blk = mesh.shape["blk"]
    n = mesh.shape["tensor"]
    half_blk = n_blk // 2
    m = n_dp * half_blk

    def shift(v, k):
        return lax.ppermute(v, "tensor", [(i, (i + k) % n) for i in range(n)])

    def flip(v, bit):
        return lax.ppermute(v, "blk", [(i, i ^ bit) for i in range(n_blk)])

    def flip_member(v, s):
        perm = []
        for dp in range(n_dp):
            for blk in range(n_blk):
                i = (dp * half_blk + blk // 2) ^ s
                to = (i // half_blk) * n_blk + (i % half_blk) * 2 + blk % 2
                perm.append((dp * n_blk + blk, to))
        return lax.ppermute(v, ("dp", "blk"), perm)

    def scatter_grads(keep, send, member):
        recv = flip(send, 1)
        rows = keep.shape[0] // m
        width = keep.shape[1]
        keep3 = keep.reshape(m, rows, width)
        recv3 = recv.reshape(m, rows, width)

        def piece(s):
            mine = lax.dynamic_index_in_dim(keep3, member ^ s, 0, keepdims=False)
            theirs = lax.dynamic_index_in_dim(recv3, member ^ s, 0, keepdims=False)
            return mine.astype(f32) + theirs.astype(f32)

        got = [flip_member(piece(s).astype(bf16), s) for s in range(1, m)]
        total = piece(0)
        for part in got:
            total = total + part.astype(f32)
        return total.astype(bf16)

    def gather_grads(total, at, name):
        rows, width = total.shape
        every = [total] + [flip_member(total, s) for s in range(1, m)]
        mine = call(
            functools.partial(gather_kernel, m),
            shape((m, rows, width), bf16),
            name,
            (at, *every),
            scalars=1,
        )
        return mine.reshape(m * rows, width)

    def body(
        tokens, bucket_ids, seq_lengths, w_query, b_query, w_key, w_value, b_value, w_out, b_out,
        norm1_gain, norm1_bias, w_inner, b_inner, w_outer, b_outer, norm2_gain, norm2_bias,
        cotangent,
    ):
        row_count, block, width = tokens.shape
        count = row_count * block
        local = w_query.shape[1]
        heads = local // HEAD_DIM
        lanes = heads * LANES
        hidden_units = w_inner.shape[1]
        blk = lax.axis_index("blk").astype(i32)
        z = lax.axis_index("tensor").astype(i32)
        member = (lax.axis_index("dp") * half_blk + blk // 2).astype(i32)
        at = jnp.stack([z, blk % 2, blk, member])
        tok = tokens.reshape(count, width)
        cot = cotangent.reshape(count, width)
        row = lambda v: v.reshape(1, -1)
        wq_t, wk_t, wv_t = w_query.T, w_key.T, w_value.T

        wouts = [w_out] + [shift(w_out, k) for k in range(1, n)]
        kv, wkv_t = call(
            kv_kernel,
            (near((count, lanes), bf16), near((lanes, width), bf16)),
            "kv_rows",
            (tok, wk_t, wv_t, row(b_value)),
            estimate=cost(4 * count * width * local, 3 * MIB),
        )
        kv_far = flip(kv, 2)
        kv_core = flip(kv, 1)
        q = call(
            q_kernel,
            near((count, lanes), bf16),
            "query_rows",
            (tok, wq_t, row(b_query)),
            estimate=cost(2 * count * width * local, 2 * MIB),
        )
        kv_both = flip(kv_far, 1)
        kvs = [kv, kv_core, kv_far, kv_both]
        q, *wouts = lax.optimization_barrier((q, *wouts))
        hp, probs = call(
            functools.partial(attend_kernel, n_blk),
            (
                near((row_count * (BLOCK + HEAD_DIM), LANES), bf16),
                near((row_count * heads * BLOCK, n_blk * BLOCK), bf16),
            ),
            "attend",
            (at, bucket_ids, seq_lengths, q, *kvs),
            scalars=3,
            estimate=cost(2e9, 4 * MIB),
        )
        hps = [hp] + [shift(hp, k) for k in range(1, n)]

        chunk = lambda w, dt: near((BLOCK, w), dt)
        order = [k for k in range(1, n)] + [0]

        def ffn(k):
            return call(
                functools.partial(ffn_kernel, n, k),
                (
                    chunk(width, bf16), chunk(width, f32), chunk(LANES, f32), chunk(width, bf16),
                    chunk(hidden_units, bf16), chunk(hidden_units, bf16),
                ),
                "ffn",
                (
                    at, tok, row(b_out), row(norm1_gain), row(norm1_bias), w_inner, row(b_inner),
                    w_outer, *hps, *wouts,
                ),
                scalars=1,
                scratch=[pltpu.VMEM((n, BLOCK, width), f32)],
                estimate=cost(6 * BLOCK * width * width, 5 * MIB),
            )

        def scatter(parts, extra=None):
            total = parts[0].astype(f32)
            for k in range(1, n):
                total = total + shift(parts[k], -k).astype(f32)
            if extra is not None:
                total = total + extra
            return total.astype(bf16)

        def gather(total):
            return [total] + [shift(total, k) for k in range(1, n)]

        first = {k: ffn(k) for k in order}
        ffns = gather(scatter([first[k][0] for k in range(n)]))

        def ffn_back(k):
            _, n1, _, _, _, slope = first[k]
            return call(
                functools.partial(ffn_back_kernel, n, k),
                (
                    chunk(width, bf16), chunk(width, f32), chunk(width, bf16),
                    chunk(hidden_units, bf16), chunk(width, bf16), near((8, width), f32),
                ),
                "ffn_back",
                (
                    at, cot, n1, slope, ffns[k], row(norm1_gain), row(norm1_bias), row(b_outer),
                    row(norm2_gain), row(norm2_bias), w_inner, w_outer,
                ),
                scalars=1,
                estimate=cost(4 * BLOCK * width * width, 5 * MIB),
            )

        second = {k: ffn_back(k) for k in range(n)}
        dhs = gather(scatter([second[k][4] for k in range(n)]))

        half = width + 16 * m
        half += -half % (16 * m)
        keep1, send1 = call(
            functools.partial(ffn_grad_kernel, n),
            (near((half, width), bf16), near((half, width), bf16)),
            "ffn_grads",
            (
                at,
                *[first[k][3] for k in range(n)],
                *[second[k][3] for k in range(n)],
                *[first[k][4] for k in range(n)],
                *[second[k][2] for k in range(n)],
                *[second[k][5] for k in range(n)],
            ),
            scalars=1,
            scratch=[pltpu.VMEM((n, 8, width), f32)],
            estimate=cost(4 * count * width * width, 6 * MIB),
        )
        total1 = scatter_grads(keep1, send1, member)

        def attend_back(k, dh):
            _, n1, s1, _, _, _ = first[k]
            return call(
                functools.partial(attend_back_kernel, n_blk, n, k),
                (
                    chunk(width, f32), chunk(width, bf16), near((8, width), f32), chunk(local, bf16),
                    near((half_blk, lanes, BLOCK), bf16), near((half_blk, lanes, BLOCK), bf16),
                ),
                "attend_back",
                (at, dh, second[k][1], n1, s1, row(norm1_gain), w_out, q, probs, *kvs),
                scalars=1,
                estimate=cost(1e9, 4 * MIB),
            )

        third = {}
        for k in range(n):
            dh = dhs[k]
            if k == n - 1:
                dh, total1 = lax.optimization_barrier((dh, total1))
            third[k] = attend_back(k, dh)
        mine1 = gather_grads(total1, at, "gather_ffn_grads")

        def input_part(k):
            _, _, _, dq, send, keep = third[k]
            recv = flip(send, 1)
            out = (keep[1].astype(f32) + recv[1].astype(f32)).astype(bf16)
            far = flip(out, 2)
            return call(
                input_kernel,
                (chunk(width, bf16), near((lanes, BLOCK), bf16), near((8, width), f32)),
                "input_part",
                (dq, keep, recv, far, wq_t, wkv_t),
                estimate=cost(6 * BLOCK * width * local, 2 * MIB),
            )

        fourth = {k: input_part(k) for k in order}
        d_tok = scatter([fourth[k][0] for k in range(n)], third[0][0])

        rows2 = 2 * local + 16
        rows2 += -rows2 % (16 * m)
        hp, mine1 = lax.optimization_barrier((hp, mine1))
        keep2, send2 = call(
            functools.partial(attend_grad_kernel, n),
            (near((rows2, width), bf16), near((rows2, width), bf16)),
            "attend_grads",
            (
                at, tok, hp,
                *[third[k][1] for k in range(n)],
                *[third[k][3] for k in range(n)],
                *[fourth[k][1] for k in range(n)],
                *[third[k][2] for k in range(n)],
                *[fourth[k][2] for k in range(n)],
            ),
            scalars=1,
            scratch=[pltpu.VMEM((n, 8, width), f32)] * 2,
            estimate=cost(2 * count * width * 4 * local, 5 * MIB),
        )
        other1 = flip(mine1, 1)
        vector = shape((1, width), f32)
        short = shape((1, local), f32)
        g_w_inner, g_w_outer, g_gain2, g_bias2, g_b_outer, g_b_inner = call(
            ffn_final_kernel,
            (shape((width, hidden_units), f32), shape((hidden_units, width), f32)) + (vector,) * 4,
            "ffn_grads_out",
            (at, mine1, other1),
            scalars=1,
            estimate=cost(0, 8 * MIB),
        )
        total2 = scatter_grads(keep2, send2, member)
        total2, d_tok, g_b_outer = lax.optimization_barrier((total2, d_tok, g_b_outer))
        mine2 = gather_grads(total2, at, "gather_attend_grads")
        other2 = flip(mine2, 1)

        assemble = lambda parts, name: call(
            functools.partial(output_kernel, n),
            shape((row_count, block, width), bf16),
            name,
            (at, *parts),
            scalars=1,
            estimate=cost(0, 2 * MIB),
        )
        output = assemble([second[k][0] for k in range(n)], "output_rows")
        d_tokens = assemble(gather(d_tok), "input_grad_rows")
        wide = shape((local, width), f32)
        g_w_out, g_q, g_k, g_v, g_gain1, g_bias1, g_b_out, g_b_query, g_b_value = call(
            attend_final_kernel,
            (wide,) * 4 + (vector,) * 3 + (short,) * 2,
            "attend_grads_out",
            (at, mine2, other2),
            scalars=1,
            estimate=cost(0, 5 * MIB),
        )
        flat = lambda v: v.reshape(-1)
        return (
            output, d_tokens, g_q.T, flat(g_b_query), g_k.T, g_v.T, flat(g_b_value), g_w_out,
            flat(g_b_out), flat(g_gain1), flat(g_bias1), g_w_inner, flat(g_b_inner), g_w_outer,
            flat(g_b_outer), flat(g_gain2), flat(g_bias2),
        )

    spread, cols, vec, rows_ = P("dp", "blk", None), P(None, "tensor"), P("tensor"), P("tensor", None)
    return jax.shard_map(
        body,
        mesh=mesh,
        in_specs=(
            spread, P("dp"), P("dp", None), cols, vec, cols, cols, vec, rows_, P(), P(), P(),
            cols, vec, rows_, P(), P(), P(), spread,
        ),
        out_specs=(
            spread, spread, cols, vec, cols, cols, vec, rows_, P(), P(), P(), cols, vec, rows_,
            P(), P(), P(),
        ),
        check_vma=False,
    )
```

```python
import functools

import jax
import jax.numpy as jnp
from jax import lax
from jax.experimental import pallas as pl
from jax.experimental.pallas import tpu as pltpu
from jax.sharding import PartitionSpec as P

HEAD_DIM = 64
BLOCK = 128
LANES = 128
SCALE = HEAD_DIM**-0.5
EPS = 1e-12
f32 = jnp.float32
bf16 = jnp.bfloat16
i32 = jnp.int32
MIB = 1 << 20
PACKED = BLOCK + HEAD_DIM


def nn(a, b):
    return lax.dot_general(a, b, (((1,), (0,)), ((), ())), preferred_element_type=f32)


def nt(a, b):
    return lax.dot_general(a, b, (((1,), (1,)), ((), ())), preferred_element_type=f32)


def tn(a, b):
    return lax.dot_general(a, b, (((0,), (0,)), ((), ())), preferred_element_type=f32)


def mean(v):
    return jnp.mean(v, axis=-1, keepdims=True)


def col_sum(v):
    return jnp.sum(v, axis=0, keepdims=True)


def row_at(at, i):
    half = at[0] % 2
    return 2 * half + i if i < 2 else 2 * (1 - half) + (i - 2)


def rows8(*rows):
    width = rows[0].shape[1]
    pad = jnp.zeros((8 - len(rows), width), f32)
    return jnp.concatenate(rows + (pad,), axis=0)


def shape(dims, dtype):
    return jax.ShapeDtypeStruct(dims, dtype)


def near(dims, dtype):
    return pltpu.VMEM(dims, dtype)


SMEM = pl.BlockSpec(memory_space=pltpu.SMEM)
VMEM = pl.BlockSpec(memory_space=pltpu.VMEM)


def call(kernel, outs, name, args, scalars=0, vmem=16, scratch=()):
    return pl.pallas_call(
        kernel,
        out_shape=outs,
        in_specs=[SMEM] * scalars + [VMEM] * (len(args) - scalars),
        out_specs=jax.tree.map(lambda _: VMEM, outs),
        scratch_shapes=list(scratch),
        compiler_params=pltpu.CompilerParams(vmem_limit_bytes=vmem * MIB),
        cost_estimate=pl.CostEstimate(flops=1, bytes_accessed=1, transcendentals=0),
        name=name,
    )(*args)


def chunk_of(ref, c, rows):
    return ref[pl.ds(pl.multiple_of(c * rows, rows), rows), :]


def kv_kernel(tok, wk_t, wv_t, bv, kv, wkv_t):
    heads = wk_t.shape[0] // HEAD_DIM
    rows, bias = [], []
    for h in range(heads):
        part = slice(h * HEAD_DIM, (h + 1) * HEAD_DIM)
        rows += [wk_t[part, :], wv_t[part, :]]
        bias += [jnp.zeros((1, HEAD_DIM), f32), bv[:, part]]
    both = jnp.concatenate(rows, axis=0)
    wkv_t[...] = both
    kv[...] = (nt(tok[...], both) + jnp.concatenate(bias, axis=1)).astype(bf16)


def q_kernel(tok, wq_t, bq, q):
    heads = wq_t.shape[0] // HEAD_DIM
    full = (nt(tok[...], wq_t[...]) + bq[...]).astype(bf16) * jnp.asarray(SCALE, bf16)
    zero = jnp.zeros((full.shape[0], HEAD_DIM), bf16)
    cols = []
    for h in range(heads):
        cols += [full[:, h * HEAD_DIM : (h + 1) * HEAD_DIM], zero]
    q[...] = jnp.concatenate(cols, axis=1)


def weights_kernel(n, at, w_out, first_z, first_core, second_z, second_core, *refs):
    outs_z, outs_core = refs[: n - 2], refs[n - 2 : 2 * (n - 2)]
    w_out_all, w_in_far, w_outer_far = refs[2 * (n - 2) :]
    z = at[0]
    local = w_out.shape[0]
    part = local // 2
    half = second_z.shape[0]

    def put(ref, base, rows, value):
        ref[pl.ds(pl.multiple_of(base, rows), rows), :] = value

    w_out_all[pl.ds(pl.multiple_of(z * local, local), local), :] = w_out[...]
    for b, first, second, outs in (
        (at[1], first_z, second_z, outs_z),
        (1 - at[1], first_core, second_core, outs_core),
    ):
        put(w_in_far, b * half, half, first[:half, :])
        put(w_outer_far, b * half, half, second[...])
        put(w_out_all, ((z ^ 1) * 2 + b) * part, part, first[half:, :])
        for i, ref in enumerate(outs):
            put(w_out_all, ((z ^ (i + 2)) * 2 + b) * part, part, ref[...])


def attend_kernel(n_blk, ids, at, bucket, lens, q, *refs):
    kvs, hp, probs = refs[:n_blk], refs[n_blk], refs[n_blk + 1]
    heads = q.shape[1] // LANES
    b = at[2]
    q_at = lax.broadcasted_iota(i32, (BLOCK, 1), 0)
    k_at = lax.broadcasted_iota(i32, (1, BLOCK), 1)
    for i, row in enumerate(ids):
        r = row_at(at, row)
        bk = bucket[r]
        size = BLOCK << bk
        slot = b >> bk
        limit = lens[r, slot]
        q_in = jnp.where(q_at + (b * BLOCK - slot * size) < limit, 1, 0)
        k_in = []
        for j in range(n_blk):
            kb = b ^ j
            k_slot = kb >> bk
            inside = jnp.where(k_at + (kb * BLOCK - k_slot * size) < limit, 1, 0)
            k_in.append(jnp.where(k_slot == slot, inside, 2))
        allowed = q_in == jnp.concatenate(k_in, axis=1)
        here = pl.ds(pl.multiple_of(r * BLOCK, BLOCK), BLOCK)
        outs = []
        for h in range(heads):
            lanes = slice(h * LANES, (h + 1) * LANES)
            kvh = jnp.concatenate([kv[here, lanes] for kv in kvs], axis=0)
            scores = jnp.where(allowed, nt(q[here, lanes], kvh), -1e30)
            weights = jnp.exp(scores - jnp.max(scores, axis=-1, keepdims=True))
            total = jnp.sum(weights, axis=-1, keepdims=True)
            p = (weights / total).astype(bf16)
            probs[(i * heads + h) * BLOCK : (i * heads + h + 1) * BLOCK, :] = p
            outs.append(nn(p, kvh)[:, HEAD_DIM:].astype(bf16))
        base = i * PACKED
        hp[base : base + BLOCK, :] = jnp.concatenate(outs[:2], axis=1)
        hp[base + BLOCK : base + PACKED, :] = jnp.concatenate(
            [outs[2][:HEAD_DIM], outs[2][HEAD_DIM:]], axis=1
        )


def unpack(h):
    odd = jnp.concatenate([h[BLOCK:, :HEAD_DIM], h[BLOCK:, HEAD_DIM:]], axis=0)
    return jnp.concatenate([h[:BLOCK, :], odd], axis=1)


def pack(v):
    odd = jnp.concatenate([v[:HEAD_DIM, LANES:], v[HEAD_DIM:, LANES:]], axis=1)
    return jnp.concatenate([v[:, :LANES], odd], axis=0)


def gelu_and_slope(inner):
    cdf = 0.5 * (1.0 + lax.erf(inner * (0.5**0.5)))
    slope = cdf + inner * (0.3989422804014327 * jnp.exp(-0.5 * inner * inner))
    return (inner * cdf).astype(bf16), slope.astype(bf16)


def ffn_kernel(
    n, i, at, tok, w_out, b_out, g1, b1, w_in, w_in_far, b_in, b_in_far, w_outer, w_outer_far, *refs
):
    hps = refs[:n]
    part, n1_out, s1_out, share, act_out, slopes, held = refs[n:]
    z = at[0]
    local = w_out.shape[0] // n
    for s in range(n):
        j = z ^ s
        held[j] = nn(unpack(hps[s][i * PACKED : (i + 1) * PACKED, :]), chunk_of(w_out, j, local))
    attn = held[0]
    for j in range(1, n):
        attn = attn + held[j]
    resid = chunk_of(tok, row_at(at, i), BLOCK).astype(f32) + (attn + b_out[...])
    center = resid - mean(resid)
    s1 = lax.rsqrt(mean(center * center) + EPS)
    n1 = center * s1
    low = (n1 * g1[...] + b1[...]).astype(bf16)
    act, slope = gelu_and_slope(nn(low, w_in[...]) + b_in[...])
    act_far, slope_far = gelu_and_slope(nn(low, w_in_far[...]) + b_in_far[...])
    part[...] = (nn(act, w_outer[...]) + nn(act_far, w_outer_far[...])).astype(bf16)
    n1_out[...] = n1
    s1_out[...] = jnp.broadcast_to(s1, s1_out.shape)
    share[:BLOCK, :] = low
    share[BLOCK:, :] = act_far
    act_out[...] = act
    slopes[:BLOCK, :] = slope
    slopes[BLOCK:, :] = slope_far


def ffn_back_kernel(
    i, at, cot, n1, slopes, mine, theirs, g1, b1, b_outer, g2, b2, w_in, w_in_far, w_outer,
    w_outer_far, share, dinner_out, part, dres2_out
):
    hidden = n1[...] * g1[...] + b1[...]
    ffn = mine[...].astype(f32) + theirs[...].astype(f32)
    resid = hidden + (ffn + b_outer[...])
    center = resid - mean(resid)
    s2 = lax.rsqrt(mean(center * center) + EPS)
    n2 = center * s2
    ct = chunk_of(cot, row_at(at, i), BLOCK).astype(f32)
    dn = ct * g2[...]
    dres2 = s2 * (dn - mean(dn) - n2 * mean(dn * n2))
    dffn = dres2.astype(bf16)
    dinner = (nt(dffn, w_outer[...]) * slopes[:BLOCK, :].astype(f32)).astype(bf16)
    dinner_far = (nt(dffn, w_outer_far[...]) * slopes[BLOCK:, :].astype(f32)).astype(bf16)
    part[...] = (nt(dinner, w_in[...]) + nt(dinner_far, w_in_far[...])).astype(bf16)
    dres2_out[...] = dres2
    dinner_out[...] = dinner
    share[:BLOCK, :] = dffn
    share[BLOCK : 2 * BLOCK, :] = dinner_far
    share[2 * BLOCK : 3 * BLOCK, :] = (n2 * g2[...] + b2[...]).astype(bf16)
    sums = rows8(col_sum(ct * n2), col_sum(ct), col_sum(dffn.astype(f32)))
    share[3 * BLOCK :, :] = jnp.concatenate([sums, jnp.zeros_like(sums)], axis=0).astype(bf16)


def norm_back_kernel(n, at, mine, theirs, dres2, n1, s1, g1, w_out, dres1_out, dattn_out, dh, dh_far):
    dhidden = (mine[...].astype(f32) + theirs[...].astype(f32)) + dres2[...]
    norm = n1[...]
    dn = dhidden * g1[...]
    dres1 = s1[:, :1] * (dn - mean(dn) - norm * mean(dn * norm))
    dattn = dres1.astype(bf16)
    dres1_out[...] = dres1
    dattn_out[:BLOCK, :] = dattn
    sums = rows8(col_sum(dhidden * norm), col_sum(dhidden), col_sum(dattn.astype(f32)))
    dattn_out[BLOCK:, :] = jnp.concatenate([sums, jnp.zeros_like(sums)], axis=0).astype(bf16)
    local = w_out.shape[0] // n
    dh[...] = pack(nt(dattn, chunk_of(w_out, at[0], local)).astype(bf16))
    dh_far[...] = pack(nt(dattn, chunk_of(w_out, at[0] ^ 1, local)).astype(bf16))


def attend_back_kernel(n_blk, i, at, packed, q, probs, *refs):
    kvs = refs[:n_blk]
    dq_out, send, keep = refs[n_blk:]
    heads = q.shape[1] // LANES
    c = row_at(at, i)
    here = pl.ds(pl.multiple_of(c * BLOCK, BLOCK), BLOCK)
    flat = unpack(packed[...])
    zero = jnp.zeros((BLOCK, HEAD_DIM), bf16)
    dqs = []
    for h in range(heads):
        lanes = slice(h * LANES, (h + 1) * LANES)
        dhead = jnp.concatenate([zero, flat[:, h * HEAD_DIM : (h + 1) * HEAD_DIM]], axis=1)
        kvh = jnp.concatenate([kv[here, lanes] for kv in kvs], axis=0)
        at_p = (i % 2) * heads + h
        p = probs[at_p * BLOCK : (at_p + 1) * BLOCK, :]
        pf = p.astype(f32)
        dp = nt(dhead, kvh)
        delta = jnp.sum(pf * dp, axis=-1, keepdims=True)
        ds = (pf * (dp - delta)).astype(bf16)
        dqs.append((nn(ds, kvh) * SCALE)[:, :HEAD_DIM].astype(bf16))
        left = jnp.concatenate([q[here, lanes], dhead], axis=0)
        dkv = tn(left, jnp.concatenate([ds, p], axis=0)).astype(bf16)
        for j in range(n_blk):
            target = keep if j % 2 == 0 else send
            target[j // 2, lanes, :] = dkv[:, j * BLOCK : (j + 1) * BLOCK]
    dq_out[...] = jnp.concatenate(dqs, axis=1)


def input_kernel(dq, keep, recv, far, wq_t, wkv_t, *refs):
    theirs, (part, dkv_t, sums) = refs[:-3], refs[-3:]
    total = keep[0].astype(f32) + recv[0].astype(f32) + far[...].astype(f32)
    low_t = total.astype(bf16)
    low = low_t.T
    grad = nn(dq[...], wq_t[...]) + nn(low, wkv_t[...])
    if theirs:
        grad = grad + theirs[0][...].astype(f32)
    part[...] = grad.astype(bf16)
    dkv_t[...] = low_t
    width = sums.shape[1]
    first = col_sum(dq[...].astype(f32))
    second = col_sum(low.astype(f32))
    sums[...] = rows8(
        jnp.concatenate([first, jnp.zeros((1, width - first.shape[1]), f32)], axis=1),
        jnp.concatenate([second, jnp.zeros((1, width - second.shape[1]), f32)], axis=1),
    )


def pick(first, one, other):
    return jnp.where(first, one, other)


def join(values, axis=0):
    return jnp.concatenate(list(values), axis=axis)


def ordered_sum(at, parts, held):
    for i, part in enumerate(parts):
        held[row_at(at, i)] = part.astype(f32)
    total = held[0]
    for r in range(1, len(parts)):
        total = total + held[r]
    return total


def ffn_grad_kernel(at, *refs):
    share1, share2, act, dinner = refs[:4], refs[4:8], refs[8:10], refs[10:12]
    keep, send, held = refs[12:]
    first = at[1] == 0
    low = join(x[:BLOCK, :] for x in share1)
    acts = join([x[...] for x in act] + [x[BLOCK:, :] for x in share1[2:]])
    dffn = join(x[:BLOCK, :] for x in share2)
    dinners = join([x[...] for x in dinner] + [x[BLOCK : 2 * BLOCK, :] for x in share2[2:]])
    tail = ordered_sum(at, [x[3 * BLOCK : 3 * BLOCK + 8, :] for x in share2], held)
    bias = rows8(tail[0:1], tail[1:2], tail[2:3], col_sum(dinners.astype(f32)))
    rows = low.shape[1]
    rest = keep.shape[0] - rows
    bias = join([bias, jnp.zeros((rest - 8, bias.shape[1]), f32)]).astype(bf16)
    send[:rows, :] = tn(pick(first, acts, low), pick(first, dffn, dinners)).astype(bf16)
    send[rows:, :] = bias
    keep[:rows, :] = tn(pick(first, low, acts), pick(first, dinners, dffn)).astype(bf16)
    keep[rows:, :] = bias


def attend_grad_kernel(at, tok, hp_mine, hp_other, *refs):
    dattn, dq, dkv_t, sums2 = (refs[4 * i : 4 * i + 4] for i in range(4))
    keep, send, held = refs[16:]
    first = at[1] == 0
    total1 = ordered_sum(at, [x[BLOCK : BLOCK + 8, :] for x in dattn], held)
    total2 = sums2[0][...] + sums2[1][...] + sums2[2][...] + sums2[3][...]
    toks = join(chunk_of(tok, row_at(at, i), BLOCK) for i in range(4))
    heads = join(unpack(hp[i * PACKED : (i + 1) * PACKED, :]) for hp in (hp_mine, hp_other) for i in range(2))
    g_out = tn(heads, join(x[:BLOCK, :] for x in dattn))
    g_q = tn(join(x[...] for x in dq), toks)
    g_kv = nn(join((x[...] for x in dkv_t), axis=1), toks)
    one = join([g_out, g_q]).astype(bf16)
    two = g_kv.astype(bf16)
    rows = two.shape[0]
    rest = keep.shape[0] - rows
    tail = join([total1, total2, jnp.zeros((rest - 16, total1.shape[1]), f32)]).astype(bf16)
    send[:rows, :] = pick(first, two, one)
    send[rows:, :] = tail
    keep[:rows, :] = pick(first, one, two)
    keep[rows:, :] = tail


def gather_kernel(m, at, *refs):
    out = refs[m]
    for s in range(m):
        out[at[3] ^ s] = refs[s][...]


def ffn_final_kernel(at, mine, other, g_in, g_outer, gain, bias, b_outer, b_in):
    first = at[1] == 0
    rows = g_in.shape[0]
    a = mine[...]
    b = other[...]
    g_in[...] = pick(first, a[:rows], b[:rows]).astype(f32)
    g_outer[...] = pick(first, b[:rows], a[:rows]).astype(f32)
    tail = pick(first, a[rows : rows + 16], b[rows : rows + 16]).astype(f32)
    for i, ref in enumerate((gain, bias, b_outer, b_in)):
        ref[...] = tail[i]


def attend_final_kernel(at, mine, other, g_out, g_q, g_k, g_v, gain, bias, b_out, b_q, b_v):
    first = at[1] == 0
    width = g_out.shape[0]
    a = mine[...]
    b = other[...]
    one = pick(first, a, b).astype(f32)
    two = pick(first, b, a).astype(f32)
    g_out[...] = one[:width]
    g_q[...] = one[width : 2 * width]
    tail = one[2 * width : 2 * width + 16]
    values = []
    for h in range(width // HEAD_DIM):
        part = slice(h * HEAD_DIM, (h + 1) * HEAD_DIM)
        g_k[part, :] = two[h * LANES : h * LANES + HEAD_DIM]
        g_v[part, :] = two[h * LANES + HEAD_DIM : (h + 1) * LANES]
        values.append(tail[9:10, h * LANES + HEAD_DIM : (h + 1) * LANES])
    for i, ref in enumerate((gain, bias, b_out)):
        ref[...] = tail[i]
    b_q[...] = tail[8, :width]
    b_v[...] = jnp.concatenate(values, axis=1)[0]


def output_kernel(at, *refs):
    out = refs[4]
    for i in range(4):
        out[row_at(at, i)] = refs[i][2 * BLOCK : 3 * BLOCK, :]


def rows_kernel(at, *refs):
    out = refs[4]
    for i in range(4):
        out[row_at(at, i)] = refs[i][...]


def solution(mesh):
    n_dp = mesh.shape["dp"]
    n_blk = mesh.shape["blk"]
    n = mesh.shape["tensor"]
    half_blk = n_blk // 2
    m = n_dp * half_blk

    def swap(v, bit):
        return lax.ppermute(v, "tensor", [(i, i ^ bit) for i in range(n)])

    def flip(v, bit):
        return lax.ppermute(v, "blk", [(i, i ^ bit) for i in range(n_blk)])

    def flip_member(v, s):
        perm = []
        for dp in range(n_dp):
            for blk in range(n_blk):
                i = (dp * half_blk + blk // 2) ^ s
                to = (i // half_blk) * n_blk + (i % half_blk) * 2 + blk % 2
                perm.append((dp * n_blk + blk, to))
        return lax.ppermute(v, ("dp", "blk"), perm)

    def scatter_grads(keep, send, member):
        recv = flip(send, 1)
        rows = keep.shape[0] // m
        width = keep.shape[1]
        keep3 = keep.reshape(m, rows, width)
        recv3 = recv.reshape(m, rows, width)

        def piece(s):
            mine = lax.dynamic_index_in_dim(keep3, member ^ s, 0, keepdims=False)
            theirs = lax.dynamic_index_in_dim(recv3, member ^ s, 0, keepdims=False)
            return mine.astype(f32) + theirs.astype(f32)

        got = [flip_member(piece(s).astype(bf16), s) for s in range(1, m)]
        total = piece(0)
        for part in got:
            total = total + part.astype(f32)
        return total.astype(bf16)

    def gather_grads(total, at, name):
        rows, width = total.shape
        every = [total] + [flip_member(total, s) for s in range(1, m)]
        mine = call(
            functools.partial(gather_kernel, m),
            shape((m, rows, width), bf16),
            name,
            (at, *every),
            scalars=1,
        )
        return mine.reshape(m * rows, width)

    def body(
        tokens, bucket_ids, seq_lengths, w_query, b_query, w_key, w_value, b_value, w_out, b_out,
        norm1_gain, norm1_bias, w_inner, b_inner, w_outer, b_outer, norm2_gain, norm2_bias,
        cotangent,
    ):
        row_count, block, width = tokens.shape
        count = row_count * block
        local = w_query.shape[1]
        heads = local // HEAD_DIM
        lanes = heads * LANES
        units = w_inner.shape[1]
        blk = lax.axis_index("blk").astype(i32)
        z = lax.axis_index("tensor").astype(i32)
        core = blk % 2
        member = (lax.axis_index("dp") * half_blk + blk // 2).astype(i32)
        at = jnp.stack([z, core, blk, member])
        tok = tokens.reshape(count, width)
        cot = cotangent.reshape(count, width)
        row = lambda v: v.reshape(1, -1)
        wq_t, wk_t, wv_t = w_query.T, w_key.T, w_value.T
        fence = lax.optimization_barrier

        half_of = lambda w: lax.dynamic_slice_in_dim(w, core * (w.shape[0] // 2), w.shape[0] // 2, 0)
        out_half = half_of(w_out)
        first_half = jnp.concatenate([half_of(w_inner), out_half], axis=0)
        first_z = swap(first_half, 1)
        second_z = swap(half_of(w_outer), 1)
        outs_z = [swap(out_half, s) for s in range(2, n)]
        b_inner_far = swap(b_inner, 1)

        kv, wkv_t = call(
            kv_kernel,
            (near((count, lanes), bf16), near((lanes, width), bf16)),
            "kv_rows",
            (tok, wk_t, wv_t, row(b_value)),
        )
        kv_far = flip(kv, 2)
        kv_core = flip(kv, 1)
        q = call(q_kernel, near((count, lanes), bf16), "query_rows", (tok, wq_t, row(b_query)))
        kv_far, first_z = fence((kv_far, first_z))
        kv_both = flip(kv_far, 1)
        kvs = [kv, kv_core, kv_far, kv_both]
        first_core = flip(first_z, 1)

        def attend(ids, q):
            return call(
                functools.partial(attend_kernel, n_blk, ids),
                (near((2 * PACKED, LANES), bf16), near((2 * heads * BLOCK, n_blk * BLOCK), bf16)),
                "attend",
                (at, bucket_ids, seq_lengths, q, *kvs),
                scalars=3,
            )

        q, second_z = fence((q, second_z))
        hp_other, probs_other = attend((2, 3), q)
        hps = {1: swap(hp_other, 1), 3: swap(hp_other, 3)}
        q, *outs_z = fence((q, *outs_z))
        hp_mine, probs_mine = attend((0, 1), q)
        hps[0] = hp_mine
        hps[2] = swap(hp_mine, 2)
        second_core = flip(second_z, 1)
        outs_core = [flip(v, 1) for v in outs_z]
        w_out_all, w_inner_far, w_outer_far = call(
            functools.partial(weights_kernel, n),
            (near((n * local, width), bf16), near(w_inner.shape, bf16), near(w_outer.shape, bf16)),
            "far_weights",
            (at, w_out, first_z, first_core, second_z, second_core, *outs_z, *outs_core),
            scalars=1,
        )

        chunk = lambda rows, dt: near((rows, width), dt)
        gains1 = (row(norm1_gain), row(norm1_bias))

        def ffn(i):
            return call(
                functools.partial(ffn_kernel, n, i),
                (
                    chunk(BLOCK, bf16), chunk(BLOCK, f32), near((BLOCK, LANES), f32),
                    chunk(2 * BLOCK, bf16), near((BLOCK, units), bf16), near((2 * BLOCK, units), bf16),
                ),
                "ffn",
                (
                    at, tok, w_out_all, row(b_out), *gains1, w_inner, w_inner_far, row(b_inner),
                    row(b_inner_far), w_outer, w_outer_far, *[hps[s] for s in range(n)],
                ),
                scalars=1,
                scratch=[pltpu.VMEM((n, BLOCK, width), f32)],
            )

        parts, n1s, s1s, share1, acts, slopes = map(list, zip(*[ffn(i) for i in range(2)]))
        theirs = [swap(v, 2) for v in parts]

        def ffn_back(i):
            return call(
                functools.partial(ffn_back_kernel, i),
                (
                    chunk(3 * BLOCK + 16, bf16), near((BLOCK, units), bf16), chunk(BLOCK, bf16),
                    chunk(BLOCK, f32),
                ),
                "ffn_back",
                (
                    at, cot, n1s[i], slopes[i], parts[i], theirs[i], *gains1, row(b_outer),
                    row(norm2_gain), row(norm2_bias), w_inner, w_inner_far, w_outer, w_outer_far,
                ),
                scalars=1,
            )

        share2, dinners, parts2, dres2 = map(list, zip(*[ffn_back(i) for i in range(2)]))
        theirs2 = [swap(v, 2) for v in parts2]
        *share1, theirs[1] = fence((*share1, theirs[1]))
        share1 += [swap(v, 1) for v in share1]

        def norm_back(i):
            return call(
                functools.partial(norm_back_kernel, n),
                (
                    chunk(BLOCK, f32), chunk(BLOCK + 16, bf16), near((PACKED, LANES), bf16),
                    near((PACKED, LANES), bf16),
                ),
                "norm_back",
                (at, parts2[i], theirs2[i], dres2[i], n1s[i], s1s[i], gains1[0], w_out_all),
                scalars=1,
            )

        dres1, dattn, dheads, dheads_far = map(list, zip(*[norm_back(i) for i in range(2)]))
        dheads += [swap(v, 1) for v in dheads_far]
        share2 += [swap(v, 1) for v in share2]
        dattn += [swap(v, 1) for v in dattn]

        def attend_back(i):
            return call(
                functools.partial(attend_back_kernel, n_blk, i),
                (
                    near((BLOCK, local), bf16), near((half_blk, lanes, BLOCK), bf16),
                    near((half_blk, lanes, BLOCK), bf16),
                ),
                "attend_back",
                (at, dheads[i], q, probs_mine if i < 2 else probs_other, *kvs),
                scalars=1,
            )

        thirds = [attend_back(i) for i in range(4)]

        grad_rows = width + 16 * m
        grad_rows += -grad_rows % (16 * m)
        keep1, send1 = call(
            ffn_grad_kernel,
            (chunk(grad_rows, bf16), chunk(grad_rows, bf16)),
            "ffn_grads",
            (at, *share1, *share2, *acts, *dinners),
            scalars=1,
            scratch=[pltpu.VMEM((n, 8, width), f32)],
        )
        total1 = scatter_grads(keep1, send1, member)
        mine1 = gather_grads(total1, at, "gather_ffn_grads")
        output = call(
            output_kernel,
            shape((row_count, block, width), bf16),
            "output_rows",
            (at, *share2),
            scalars=1,
        )

        recvs = [flip(t[1], 1) for t in thirds]
        fars = [
            flip((t[2][1].astype(f32) + recv[1].astype(f32)).astype(bf16), 2)
            for t, recv in zip(thirds, recvs)
        ]

        def input_part(i, *theirs):
            dq, _, keep = thirds[i]
            return call(
                input_kernel,
                (chunk(BLOCK, bf16), near((lanes, BLOCK), bf16), chunk(8, f32)),
                "input_part",
                (dq, keep, recvs[i], fars[i], wq_t, wkv_t, *theirs),
            )

        fourth = {i: input_part(i) for i in (2, 3)}
        fourth |= {i: input_part(i, swap(fourth[i + 2][0], 1)) for i in (0, 1)}
        d_toks = []
        for i in range(2):
            pair = fourth[i][0]
            total = (pair.astype(f32) + swap(pair, 2).astype(f32)) + dres1[i]
            d_toks.append(total.astype(bf16))
        d_toks += [swap(v, 1) for v in d_toks]

        rows2 = 2 * local + 16
        rows2 += -rows2 % (16 * m)
        keep2, send2 = call(
            attend_grad_kernel,
            (chunk(rows2, bf16), chunk(rows2, bf16)),
            "attend_grads",
            (
                at, tok, hp_mine, hp_other, *dattn,
                *[thirds[i][0] for i in range(4)],
                *[fourth[i][1] for i in range(4)],
                *[fourth[i][2] for i in range(4)],
            ),
            scalars=1,
            scratch=[pltpu.VMEM((n, 8, width), f32)],
        )
        vector = shape((width,), f32)
        short = shape((local,), f32)
        total2 = scatter_grads(keep2, send2, member)
        mine2 = gather_grads(total2, at, "gather_attend_grads")
        other1 = flip(mine1, 1)
        other2 = flip(mine2, 1)
        g_w_inner, g_w_outer, g_gain2, g_bias2, g_b_outer, g_b_inner = call(
            ffn_final_kernel,
            (shape((width, units), f32), shape((units, width), f32)) + (vector,) * 4,
            "ffn_grads_out",
            (at, mine1, other1),
            scalars=1,
        )
        d_tokens = call(
            rows_kernel,
            shape((row_count, block, width), bf16),
            "input_grad_rows",
            (at, *d_toks),
            scalars=1,
        )
        wide = shape((local, width), f32)
        g_w_out, g_q, g_k, g_v, g_gain1, g_bias1, g_b_out, g_b_query, g_b_value = call(
            attend_final_kernel,
            (wide,) * 4 + (vector,) * 3 + (short,) * 2,
            "attend_grads_out",
            (at, mine2, other2),
            scalars=1,
        )
        return (
            output, d_tokens, g_q.T, g_b_query, g_k.T, g_v.T, g_b_value, g_w_out, g_b_out, g_gain1,
            g_bias1, g_w_inner, g_b_inner, g_w_outer, g_b_outer, g_gain2, g_bias2,
        )

    spread, cols, vec, rows_ = P("dp", "blk", None), P(None, "tensor"), P("tensor"), P("tensor", None)
    return jax.shard_map(
        body,
        mesh=mesh,
        in_specs=(
            spread, P("dp"), P("dp", None), cols, vec, cols, cols, vec, rows_, P(), P(), P(),
            cols, vec, rows_, P(), P(), P(), spread,
        ),
        out_specs=(
            spread, spread, cols, vec, cols, cols, vec, rows_, P(), P(), P(), cols, vec, rows_,
            P(), P(), P(),
        ),
        check_vma=False,
    )
```

```python
import functools

import jax
import jax.numpy as jnp
from jax import lax
from jax.experimental import pallas as pl
from jax.experimental.pallas import tpu as pltpu
from jax.sharding import PartitionSpec as P

HEAD_DIM = 64
BLOCK = 128
LANES = 128
SCALE = HEAD_DIM**-0.5
EPS = 1e-12
f32 = jnp.float32
bf16 = jnp.bfloat16
i32 = jnp.int32
MIB = 1 << 20
FLOPS_US = 1e9
ATTEND_US = 50.0
BACK_US = 50.0
PACKED = BLOCK + HEAD_DIM


def nn(a, b):
    return lax.dot_general(a, b, (((1,), (0,)), ((), ())), preferred_element_type=f32)


def nt(a, b):
    return lax.dot_general(a, b, (((1,), (1,)), ((), ())), preferred_element_type=f32)


def tn(a, b):
    return lax.dot_general(a, b, (((0,), (0,)), ((), ())), preferred_element_type=f32)


def mean(v):
    return jnp.mean(v, axis=-1, keepdims=True)


def col_sum(v):
    return jnp.sum(v, axis=0, keepdims=True)


def row_at(at, i):
    half = at[0] % 2
    return 2 * half + i if i < 2 else 2 * (1 - half) + (i - 2)


def rows8(*rows):
    width = rows[0].shape[1]
    pad = jnp.zeros((8 - len(rows), width), f32)
    return jnp.concatenate(rows + (pad,), axis=0)


def shape(dims, dtype):
    return jax.ShapeDtypeStruct(dims, dtype)


def near(dims, dtype):
    return pltpu.VMEM(dims, dtype)


SMEM = pl.BlockSpec(memory_space=pltpu.SMEM)
VMEM = pl.BlockSpec(memory_space=pltpu.VMEM)


def call(kernel, outs, name, args, scalars=0, us=1.0, vmem=16, scratch=()):
    return pl.pallas_call(
        kernel,
        out_shape=outs,
        in_specs=[SMEM] * scalars + [VMEM] * (len(args) - scalars),
        out_specs=jax.tree.map(lambda _: VMEM, outs),
        scratch_shapes=list(scratch),
        compiler_params=pltpu.CompilerParams(vmem_limit_bytes=vmem * MIB),
        cost_estimate=pl.CostEstimate(flops=int(us * FLOPS_US), bytes_accessed=1, transcendentals=0),
        name=name,
    )(*args)


def chunk_of(ref, c, rows):
    return ref[pl.ds(pl.multiple_of(c * rows, rows), rows), :]


def kv_kernel(tok, wk_t, wv_t, bv, kv, wkv_t):
    heads = wk_t.shape[0] // HEAD_DIM
    rows, bias = [], []
    for h in range(heads):
        part = slice(h * HEAD_DIM, (h + 1) * HEAD_DIM)
        rows += [wk_t[part, :], wv_t[part, :]]
        bias += [jnp.zeros((1, HEAD_DIM), f32), bv[:, part]]
    both = jnp.concatenate(rows, axis=0)
    wkv_t[...] = both
    kv[...] = (nt(tok[...], both) + jnp.concatenate(bias, axis=1)).astype(bf16)


def q_kernel(tok, wq_t, bq, q):
    heads = wq_t.shape[0] // HEAD_DIM
    full = (nt(tok[...], wq_t[...]) + bq[...]).astype(bf16) * jnp.asarray(SCALE, bf16)
    zero = jnp.zeros((full.shape[0], HEAD_DIM), bf16)
    cols = []
    for h in range(heads):
        cols += [full[:, h * HEAD_DIM : (h + 1) * HEAD_DIM], zero]
    q[...] = jnp.concatenate(cols, axis=1)


def piece_kernel(at, w_in, w_outer, w_out, piece, out_piece, sems):
    tail = out_piece.shape[0]
    half = (piece.shape[0] - tail) // 2

    def part(ref, index, size):
        return ref.at[pl.ds(pl.multiple_of(index * size, 16), size), :]

    copies = [
        pltpu.make_async_copy(part(w_in, at[4], half), piece.at[pl.ds(0, half), :], sems.at[0]),
        pltpu.make_async_copy(part(w_outer, at[4], half), piece.at[pl.ds(half, half), :], sems.at[1]),
        pltpu.make_async_copy(part(w_out, at[2], tail), out_piece, sems.at[2]),
    ]
    for copy in copies:
        copy.start()
    for copy in copies:
        copy.wait()
    piece[2 * half :, :] = out_piece[...]


def weights_kernel(n, at, w_out, *refs):
    pieces, (w_out_all, w_in_far, w_outer_far) = refs[:8], refs[8:]
    z = at[0]
    local = w_out.shape[0]
    part = local // 4
    rows = w_in_far.shape[0] // 8

    def put(ref, base, value):
        size = value.shape[0]
        ref[pl.ds(pl.multiple_of(base, 16), size), :] = value

    put(w_out_all, z * local, w_out[...])
    for j, piece in enumerate(pieces):
        put(w_in_far, (at[4] ^ j) * rows, piece[:rows, :])
        put(w_outer_far, (at[4] ^ j) * rows, piece[rows : 2 * rows, :])
        for s in range(1, n if j < 4 else 0):
            base = 2 * rows + (s - 1) * part
            put(w_out_all, (z ^ s) * local + (at[2] ^ j) * part, piece[base : base + part, :])


def attend_kernel(n_blk, ids, at, bucket, lens, q, *refs):
    kvs, outs_to = refs[:n_blk], refs[n_blk:]
    heads = q.shape[1] // LANES
    b = at[2]
    q_at = lax.broadcasted_iota(i32, (BLOCK, 1), 0)
    k_at = lax.broadcasted_iota(i32, (1, BLOCK), 1)
    for order, row in enumerate(ids):
        hp, probs = outs_to[2 * (order // 2)], outs_to[2 * (order // 2) + 1]
        i = order % 2
        r = row_at(at, row)
        bk = bucket[r]
        size = BLOCK << bk
        slot = b >> bk
        limit = lens[r, slot]
        q_in = jnp.where(q_at + (b * BLOCK - slot * size) < limit, 1, 0)
        k_in = []
        for j in range(n_blk):
            kb = b ^ j
            k_slot = kb >> bk
            inside = jnp.where(k_at + (kb * BLOCK - k_slot * size) < limit, 1, 0)
            k_in.append(jnp.where(k_slot == slot, inside, 2))
        allowed = q_in == jnp.concatenate(k_in, axis=1)
        here = pl.ds(pl.multiple_of(r * BLOCK, BLOCK), BLOCK)
        outs = []
        for h in range(heads):
            lanes = slice(h * LANES, (h + 1) * LANES)
            kvh = jnp.concatenate([kv[here, lanes] for kv in kvs], axis=0)
            scores = jnp.where(allowed, nt(q[here, lanes], kvh), -1e30)
            weights = jnp.exp(scores - jnp.max(scores, axis=-1, keepdims=True))
            total = jnp.sum(weights, axis=-1, keepdims=True)
            p = (weights / total).astype(bf16)
            probs[(i * heads + h) * BLOCK : (i * heads + h + 1) * BLOCK, :] = p
            outs.append(nn(p, kvh)[:, HEAD_DIM:].astype(bf16))
        base = i * PACKED
        hp[base : base + BLOCK, :] = jnp.concatenate(outs[:2], axis=1)
        hp[base + BLOCK : base + PACKED, :] = jnp.concatenate(
            [outs[2][:HEAD_DIM], outs[2][HEAD_DIM:]], axis=1
        )


def unpack(h):
    odd = jnp.concatenate([h[BLOCK:, :HEAD_DIM], h[BLOCK:, HEAD_DIM:]], axis=0)
    return jnp.concatenate([h[:BLOCK, :], odd], axis=1)


def pack(v):
    odd = jnp.concatenate([v[:HEAD_DIM, LANES:], v[HEAD_DIM:, LANES:]], axis=1)
    return jnp.concatenate([v[:, :LANES], odd], axis=0)


def gelu_and_slope(inner):
    cdf = 0.5 * (1.0 + lax.erf(inner * (0.5**0.5)))
    slope = cdf + inner * (0.3989422804014327 * jnp.exp(-0.5 * inner * inner))
    return (inner * cdf).astype(bf16), slope.astype(bf16)


def ffn_kernel(
    n, i, at, tok, w_out, b_out, g1, b1, w_in, w_in_far, b_in, b_in_far, w_outer, w_outer_far, *refs
):
    hps = refs[:n]
    part, n1_out, s1_out, low_out, act_out, act_far_out, slopes, held = refs[n:]
    z = at[0]
    local = w_out.shape[0] // n
    for s in range(n):
        j = z ^ s
        held[j] = nn(unpack(hps[s][i * PACKED : (i + 1) * PACKED, :]), chunk_of(w_out, j, local))
    attn = held[0]
    for j in range(1, n):
        attn = attn + held[j]
    resid = chunk_of(tok, row_at(at, i), BLOCK).astype(f32) + (attn + b_out[...])
    center = resid - mean(resid)
    s1 = lax.rsqrt(mean(center * center) + EPS)
    n1 = center * s1
    low = (n1 * g1[...] + b1[...]).astype(bf16)
    act, slope = gelu_and_slope(nn(low, w_in[...]) + b_in[...])
    act_far, slope_far = gelu_and_slope(nn(low, w_in_far[...]) + b_in_far[...])
    part[...] = (nn(act, w_outer[...]) + nn(act_far, w_outer_far[...])).astype(bf16)
    n1_out[...] = n1
    s1_out[...] = jnp.broadcast_to(s1, s1_out.shape)
    low_out[...] = low
    act_out[...] = act
    act_far_out[...] = act_far
    slopes[:BLOCK, :] = slope
    slopes[BLOCK:, :] = slope_far


def ffn_back_kernel(
    i, at, cot, n1, slopes, mine, theirs, g1, b1, b_outer, g2, b2, w_in, w_in_far, w_outer,
    w_outer_far, out, dffn_out, dinner_out, dinner_far_out, part, dres2_out, sums
):
    hidden = n1[...] * g1[...] + b1[...]
    ffn = mine[...].astype(f32) + theirs[...].astype(f32)
    resid = hidden + (ffn + b_outer[...])
    center = resid - mean(resid)
    s2 = lax.rsqrt(mean(center * center) + EPS)
    n2 = center * s2
    ct = chunk_of(cot, row_at(at, i), BLOCK).astype(f32)
    dn = ct * g2[...]
    dres2 = s2 * (dn - mean(dn) - n2 * mean(dn * n2))
    dffn = dres2.astype(bf16)
    dinner = (nt(dffn, w_outer[...]) * slopes[:BLOCK, :].astype(f32)).astype(bf16)
    dinner_far = (nt(dffn, w_outer_far[...]) * slopes[BLOCK:, :].astype(f32)).astype(bf16)
    part[...] = (nt(dinner, w_in[...]) + nt(dinner_far, w_in_far[...])).astype(bf16)
    dres2_out[...] = dres2
    dinner_out[...] = dinner
    out[...] = (n2 * g2[...] + b2[...]).astype(bf16)
    dffn_out[...] = dffn
    dinner_far_out[...] = dinner_far
    sums[...] = rows8(
        col_sum(ct * n2), col_sum(ct), col_sum(dffn.astype(f32)),
        col_sum(dinner.astype(f32)), col_sum(dinner_far.astype(f32)),
    )


def norm_back_kernel(n, at, mine, theirs, dres2, n1, s1, g1, w_out, dres1_out, dattn_out, sums, dh, dh_far):
    dhidden = (mine[...].astype(f32) + theirs[...].astype(f32)) + dres2[...]
    norm = n1[...]
    dn = dhidden * g1[...]
    dres1 = s1[:, :1] * (dn - mean(dn) - norm * mean(dn * norm))
    dattn = dres1.astype(bf16)
    dres1_out[...] = dres1
    dattn_out[...] = dattn
    sums[...] = rows8(col_sum(dhidden * norm), col_sum(dhidden), col_sum(dattn.astype(f32)))
    local = w_out.shape[0] // n
    dh[...] = pack(nt(dattn, chunk_of(w_out, at[0], local)).astype(bf16))
    dh_far[...] = pack(nt(dattn, chunk_of(w_out, at[0] ^ 1, local)).astype(bf16))


def attend_back_kernel(n_blk, ids, at, first, second, q, probs, *refs):
    kvs = refs[:n_blk]
    dq_out, send, keep = refs[n_blk:]
    heads = q.shape[1] // LANES
    zero = jnp.zeros((BLOCK, HEAD_DIM), bf16)
    for i, packed in enumerate((first, second)):
        c = row_at(at, ids[i])
        here = pl.ds(pl.multiple_of(c * BLOCK, BLOCK), BLOCK)
        flat = unpack(packed[...])
        dqs = []
        for h in range(heads):
            lanes = slice(h * LANES, (h + 1) * LANES)
            dhead = jnp.concatenate([zero, flat[:, h * HEAD_DIM : (h + 1) * HEAD_DIM]], axis=1)
            kvh = jnp.concatenate([kv[here, lanes] for kv in kvs], axis=0)
            at_p = (i * heads + h) * BLOCK
            p = probs[at_p : at_p + BLOCK, :]
            pf = p.astype(f32)
            dp = nt(dhead, kvh)
            delta = jnp.sum(pf * dp, axis=-1, keepdims=True)
            ds = (pf * (dp - delta)).astype(bf16)
            dqs.append((nn(ds, kvh) * SCALE)[:, :HEAD_DIM].astype(bf16))
            left = jnp.concatenate([q[here, lanes], dhead], axis=0)
            dkv = tn(left, jnp.concatenate([ds, p], axis=0)).astype(bf16)
            for j in range(n_blk):
                target = keep if j % 2 == 0 else send
                target[j // 2, i, lanes, :] = dkv[:, j * BLOCK : (j + 1) * BLOCK]
        dq_out[i * BLOCK : (i + 1) * BLOCK, :] = jnp.concatenate(dqs, axis=1)


def input_kernel(dq, keep, recv, far, wq_t, wkv_t, *refs):
    theirs, (part, dkv_t, sums) = refs[:-3], refs[-3:]
    total = keep[0].astype(f32) + recv[0].astype(f32) + far[...].astype(f32)
    lows = [total[i].astype(bf16) for i in range(2)]
    low = jnp.concatenate([v.T for v in lows], axis=0)
    grad = nn(dq[...], wq_t[...]) + nn(low, wkv_t[...])
    if theirs:
        grad = grad + theirs[0][...].astype(f32)
    part[...] = grad.astype(bf16)
    dkv_t[...] = jnp.concatenate(lows, axis=1)
    width = sums.shape[1]
    one = col_sum(dq[...].astype(f32))
    two = col_sum(low.astype(f32))
    sums[...] = rows8(
        jnp.concatenate([one, jnp.zeros((1, width - one.shape[1]), f32)], axis=1),
        jnp.concatenate([two, jnp.zeros((1, width - two.shape[1]), f32)], axis=1),
    )


def pick(first, one, other):
    return jnp.where(first, one, other)


def join(values, axis=0):
    return jnp.concatenate(list(values), axis=axis)


def ffn_grad_kernel(m, at, hp_mine, hp_near, *refs):
    low, act, act_far, dffn, dinner, dinner_far, dattn, sums2, sums1 = (
        refs[2 * i : 2 * i + 2] for i in range(9)
    )
    keep, send = refs[18:]
    first = at[1] == 0
    both = lambda pair: join(x[...] for x in pair)
    lows, dffns, dattns = both(low), both(dffn), both(dattn)
    tail2 = sums2[0][...] + sums2[1][...]
    tail1 = sums1[0][...] + sums1[1][...]
    rows = lows.shape[1] // m
    out_rows = keep.shape[2] - rows - 16
    for q, (acts, dinners, hp) in enumerate(
        ((both(act), both(dinner), hp_mine), (both(act_far), both(dinner_far), hp_near))
    ):
        heads = join(unpack(hp[i * PACKED : (i + 1) * PACKED, :]) for i in range(2))
        g_out = tn(heads, dattns).astype(bf16)
        cut = g_out.shape[0] // 2
        tail = join([tail2[:3], tail2[3 + q : 4 + q], tail1[:3], jnp.zeros((9, tail1.shape[1]), f32)])
        tail = tail.astype(bf16)
        for target, one in ((keep, first), (send, jnp.logical_not(first))):
            main = tn(pick(one, lows, acts), pick(one, dinners, dffns)).astype(bf16)
            outs = pick(one, g_out[:cut], g_out[cut:])
            for i in range(m):
                target[i, q, :rows, :] = main[i * rows : (i + 1) * rows]
                if i * out_rows < cut:
                    block = outs[i * out_rows : (i + 1) * out_rows]
                else:
                    block = jnp.zeros((out_rows, outs.shape[1]), bf16)
                target[i, q, rows : rows + out_rows, :] = block
                target[i, q, rows + out_rows :, :] = tail


def attend_grad_kernel(m, at, tok, *refs):
    dq, dkv_t, sums = (refs[2 * i : 2 * i + 2] for i in range(3))
    keep, send = refs[6:]
    first = at[1] == 0
    toks = join(chunk_of(tok, row_at(at, i), BLOCK) for i in range(4))
    g_q = tn(join(x[...] for x in dq), toks)
    g_kv = nn(join((x[...] for x in dkv_t), axis=1), toks)
    half = (g_q.shape[0] + g_kv.shape[0]) // 2
    cut = half - g_q.shape[0]
    one = join([g_q, g_kv[:cut]]).astype(bf16)
    two = g_kv[cut:].astype(bf16)
    total = sums[0][...] + sums[1][...]
    rest = keep.shape[0] - half
    tail = join([total, jnp.zeros((rest - 8, total.shape[1]), f32)]).astype(bf16)
    keep[:half, :] = pick(first, one, two)
    keep[half:, :] = tail
    send[:half, :] = pick(first, two, one)
    send[half:, :] = tail


def gather_kernel(m, at, *refs):
    out = refs[m]
    for s in range(m):
        out[at[3] ^ s] = refs[s][...]


def ffn_final_kernel(m, at, mine, other, g_in, g_outer, g_out, *vectors):
    first = at[1] == 0
    rows = g_in.shape[0] // m
    out_rows = mine.shape[1] - rows - 16
    cut = g_out.shape[0] // 2
    for i in range(m):
        a, b = mine[i], other[i]
        one = pick(first, a, b).astype(f32)
        two = pick(first, b, a).astype(f32)
        g_in[i * rows : (i + 1) * rows, :] = one[:rows]
        g_outer[i * rows : (i + 1) * rows, :] = two[:rows]
        if i * out_rows < cut:
            at_row = i * out_rows
            g_out[at_row : at_row + out_rows, :] = one[rows : rows + out_rows]
            g_out[cut + at_row : cut + at_row + out_rows, :] = two[rows : rows + out_rows]
        if i == 0:
            for k, ref in enumerate(vectors):
                ref[...] = one[rows + out_rows + k]


def attend_final_kernel(at, mine, other, g_q, g_k, g_v, b_q, b_v):
    first = at[1] == 0
    width = g_q.shape[0]
    half = 3 * width // 2
    a = mine[...]
    b = other[...]
    one = pick(first, a, b).astype(f32)
    two = pick(first, b, a).astype(f32)
    g_q[...] = one[:width]
    g_kv = join([one[width:half], two[:half]])
    tail = one[half : half + 8]
    values = []
    for h in range(width // HEAD_DIM):
        part = slice(h * HEAD_DIM, (h + 1) * HEAD_DIM)
        g_k[part, :] = g_kv[h * LANES : h * LANES + HEAD_DIM]
        g_v[part, :] = g_kv[h * LANES + HEAD_DIM : (h + 1) * LANES]
        values.append(tail[1:2, h * LANES + HEAD_DIM : (h + 1) * LANES])
    b_q[...] = tail[0, :width]
    b_v[...] = jnp.concatenate(values, axis=1)[0]


def rows_kernel(at, *refs):
    out = refs[-1]
    rows = [v[i * BLOCK : (i + 1) * BLOCK, :] for v in refs[:-1] for i in range(v.shape[0] // BLOCK)]
    for i, value in enumerate(rows):
        out[row_at(at, i)] = value


def solution(mesh):
    n_dp = mesh.shape["dp"]
    n_blk = mesh.shape["blk"]
    n = mesh.shape["tensor"]
    half_blk = n_blk // 2
    m = n_dp * half_blk

    def swap(v, bit):
        return lax.ppermute(v, "tensor", [(i, i ^ bit) for i in range(n)])

    def flip(v, bit):
        return lax.ppermute(v, "blk", [(i, i ^ bit) for i in range(n_blk)])

    def flip_member(v, s):
        perm = []
        for dp in range(n_dp):
            for blk in range(n_blk):
                i = (dp * half_blk + blk // 2) ^ s
                to = (i // half_blk) * n_blk + (i % half_blk) * 2 + blk % 2
                perm.append((dp * n_blk + blk, to))
        return lax.ppermute(v, ("dp", "blk"), perm)

    def share_pieces(keep, recv, member):
        def piece(s):
            mine = lax.dynamic_index_in_dim(keep, member ^ s, 0, keepdims=False)
            theirs = lax.dynamic_index_in_dim(recv, member ^ s, 0, keepdims=False)
            return (mine.astype(f32) + theirs.astype(f32)).astype(bf16)

        return [piece(s) for s in range(m)]

    def add(own, got):
        total = own.astype(f32)
        for part in got:
            total = total + part.astype(f32)
        return total.astype(bf16)

    def gather_grads(total, at, name):
        rows, width = total.shape
        every = [total] + [flip_member(total, s) for s in range(1, m)]
        mine = call(
            functools.partial(gather_kernel, m),
            near((m, rows, width), bf16),
            name,
            (at, *every),
            scalars=1,
        )
        return mine

    def body(
        tokens, bucket_ids, seq_lengths, w_query, b_query, w_key, w_value, b_value, w_out, b_out,
        norm1_gain, norm1_bias, w_inner, b_inner, w_outer, b_outer, norm2_gain, norm2_bias,
        cotangent,
    ):
        row_count, block, width = tokens.shape
        count = row_count * block
        local = w_query.shape[1]
        heads = local // HEAD_DIM
        lanes = heads * LANES
        units = w_inner.shape[1]
        blk = lax.axis_index("blk").astype(i32)
        z = lax.axis_index("tensor").astype(i32)
        core = blk % 2
        member = (lax.axis_index("dp") * half_blk + blk // 2).astype(i32)
        cut_at = (lax.axis_index("dp") % 2) * n_blk + blk
        at = jnp.stack([z, core, blk, member, cut_at]).astype(i32)
        tok = tokens.reshape(count, width)
        cot = cotangent.reshape(count, width)
        row = lambda v: v.reshape(1, -1)
        wq_t, wk_t, wv_t = w_query.T, w_key.T, w_value.T
        fence = lax.optimization_barrier

        part = local // 4
        piece_rows = (width + units) // 8
        piece, out_piece = pl.pallas_call(
            piece_kernel,
            out_shape=(near((piece_rows + part, width), bf16), near((part, width), bf16)),
            in_specs=[SMEM] + [pl.BlockSpec(memory_space=pl.ANY)] * 3,
            out_specs=(VMEM, VMEM),
            scratch_shapes=[pltpu.SemaphoreType.DMA((3,))],
            compiler_params=pltpu.CompilerParams(vmem_limit_bytes=8 * MIB),
            name="weight_piece",
        )(at, w_inner, w_outer, w_out)
        kv, wkv_t = call(
            kv_kernel,
            (near((count, lanes), bf16), near((lanes, width), bf16)),
            "kv_rows",
            (tok, wk_t, wv_t, row(b_value)),
        )
        kv, piece, out_piece, b_far = fence((kv, piece, out_piece, b_inner))
        kv_far = flip(kv, 2)
        kv_core = flip(kv, 1)
        pieces = [swap(piece, 1)] + [swap(out_piece, s) for s in range(2, n)]
        b_inner_far = swap(b_far, 1)
        kv_far, *pieces = fence((kv_far, *pieces))
        own_piece = jnp.concatenate(pieces, axis=0)
        ffn_piece = pieces[0][:piece_rows]

        def across(v, dp_bit, blk_bit):
            there = lambda i: ((i // n_blk) ^ dp_bit) * n_blk + ((i % n_blk) ^ blk_bit)
            return lax.ppermute(v, ("dp", "blk"), [(i, there(i)) for i in range(n_dp * n_blk)])

        arrived = {0: own_piece, 2: across(own_piece, 0, 2)}
        arrived |= {4: across(ffn_piece, 1, 0), 6: across(ffn_piece, 1, 2)}

        q = call(q_kernel, near((count, lanes), bf16), "query_rows", (tok, wq_t, row(b_query)), us=0.5)
        kv_both = flip(kv_far, 1)
        kvs = [kv, kv_core, kv_far, kv_both]

        pair = (near((2 * PACKED, LANES), bf16), near((2 * heads * BLOCK, n_blk * BLOCK), bf16))
        hp_other, probs_other, hp_mine, probs_mine = call(
            functools.partial(attend_kernel, n_blk, (2, 3, 0, 1)),
            pair + pair,
            "attend",
            (at, bucket_ids, seq_lengths, q, *kvs),
            us=ATTEND_US,
            scalars=3,
        )
        hps = {0: hp_mine, 1: swap(hp_other, 1), 2: swap(hp_mine, 2), 3: swap(hp_other, 3)}
        held = [arrived[2], arrived[4], arrived[6], b_inner_far]
        hps[1], *held = fence((hps[1], *held))
        arrived[2], arrived[4], arrived[6], b_inner_far = held
        arrived |= {j + 1: flip(v, 1) for j, v in arrived.items()}
        w_out_all, w_inner_far, w_outer_far = call(
            functools.partial(weights_kernel, n),
            (near((n * local, width), bf16), near(w_inner.shape, bf16), near(w_outer.shape, bf16)),
            "far_weights",
            (at, w_out, *[arrived[j] for j in range(8)]),
            us=2.2,
            scalars=1,
        )

        chunk = lambda rows, dt: near((rows, width), dt)
        gains1 = (row(norm1_gain), row(norm1_bias))

        def ffn(i):
            return call(
                functools.partial(ffn_kernel, n, i),
                (
                    chunk(BLOCK, bf16), chunk(BLOCK, f32), near((BLOCK, LANES), f32),
                    chunk(BLOCK, bf16), near((BLOCK, units), bf16), near((BLOCK, units), bf16),
                    near((2 * BLOCK, units), bf16),
                ),
                "ffn",
                (
                    at, tok, w_out_all, row(b_out), *gains1, w_inner, w_inner_far, row(b_inner),
                    row(b_inner_far), w_outer, w_outer_far, *[hps[s] for s in range(n)],
                ),
                us=2.4,
                scalars=1,
                scratch=[pltpu.VMEM((n, BLOCK, width), f32)],
            )

        parts, n1s, s1s, lows, acts, acts_far, slopes = map(list, zip(*[ffn(i) for i in range(2)]))
        theirs = [swap(v, 2) for v in parts]

        def ffn_back(i):
            return call(
                functools.partial(ffn_back_kernel, i),
                (
                    chunk(BLOCK, bf16), chunk(BLOCK, bf16), near((BLOCK, units), bf16),
                    near((BLOCK, units), bf16), chunk(BLOCK, bf16), chunk(BLOCK, f32), chunk(8, f32),
                ),
                "ffn_back",
                (
                    at, cot, n1s[i], slopes[i], parts[i], theirs[i], *gains1, row(b_outer),
                    row(norm2_gain), row(norm2_bias), w_inner, w_inner_far, w_outer, w_outer_far,
                ),
                us=2.7,
                scalars=1,
            )

        outs, dffns, dinners, dinners_far, parts2, dres2, sums2 = map(list, zip(*[ffn_back(i) for i in range(2)]))
        theirs2 = [swap(v, 2) for v in parts2]
        def norm_back(i):
            return call(
                functools.partial(norm_back_kernel, n),
                (
                    chunk(BLOCK, f32), chunk(BLOCK, bf16), chunk(8, f32), near((PACKED, LANES), bf16),
                    near((PACKED, LANES), bf16),
                ),
                "norm_back",
                (at, parts2[i], theirs2[i], dres2[i], n1s[i], s1s[i], gains1[0], w_out_all),
                us=1.2,
                scalars=1,
            )

        dres1, dattn, sums1, dheads, dheads_far = map(list, zip(*[norm_back(i) for i in range(2)]))
        dheads += [swap(v, 1) for v in dheads_far]
        outs += [swap(v, 1) for v in outs]

        def attend_back(ids, probs, *packed):
            return call(
                functools.partial(attend_back_kernel, n_blk, ids),
                (
                    near((2 * BLOCK, local), bf16), near((half_blk, 2, lanes, BLOCK), bf16),
                    near((half_blk, 2, lanes, BLOCK), bf16),
                ),
                "attend_back",
                (at, *packed, q, probs, *kvs),
                scalars=1,
                us=BACK_US,
            )

        own = attend_back((0, 1), probs_mine, dheads[0], dheads[1])
        after, dheads[2], dheads[3] = fence((own[1], dheads[2], dheads[3]))
        own = (own[0], after, own[2])
        other = attend_back((2, 3), probs_other, dheads[2], dheads[3])

        out_rows = local // 2 // m
        out_rows += -out_rows % 16
        grad_rows = width // m + out_rows + 16
        after, dattn[0] = fence((other[1], dattn[0]))
        other = (other[0], after, other[2])
        keep1, send1 = call(
            functools.partial(ffn_grad_kernel, m),
            (near((m, 2, grad_rows, width), bf16), near((m, 2, grad_rows, width), bf16)),
            "ffn_grads",
            (
                at, hp_mine, hps[1], *lows, *acts, *acts_far, *dffns, *dinners, *dinners_far, *dattn,
                *sums2, *sums1,
            ),
            us=4.0,
            vmem=24,
            scalars=1,
        )
        def exchange(third):
            _, send, keep = third
            recv = flip(send, 1)
            return recv, (keep[1].astype(f32) + recv[1].astype(f32)).astype(bf16)

        def input_part(third, recv, far, *theirs):
            dq, _, keep = third
            return call(
                input_kernel,
                (chunk(2 * BLOCK, bf16), near((lanes, 2 * BLOCK), bf16), chunk(8, f32)),
                "input_part",
                (dq, keep, recv, far, wq_t, wkv_t, *theirs),
                us=1.0,
            )

        recv_own, sum_own = exchange(own)
        recv_other, sum_other = exchange(other)
        send1, sum_own, sum_other = fence((send1, sum_own, sum_other))
        recv1 = flip(send1, 1)
        far_own, far_other = flip(sum_own, 2), flip(sum_other, 2)
        pieces1 = share_pieces(keep1, recv1, member)
        far_own, far_other, pieces1, *ends = fence((far_own, far_other, pieces1, *outs[2:]))
        outs[2:] = ends
        part, *late = input_part(other, recv_other, far_other)
        got1 = [flip_member(v, s) for s, v in enumerate(pieces1[1:], 1)]
        pair, dkv_own, sums_own = input_part(own, recv_own, far_own, swap(part, 1))
        d_tok = pair.astype(f32) + swap(pair, 2).astype(f32) + jnp.concatenate(dres1, axis=0)
        d_tok = d_tok.astype(bf16)

        rows2 = 3 * local // 2 + 16
        rows2 += -rows2 % (16 * m)
        keep2, send2 = call(
            functools.partial(attend_grad_kernel, m),
            (chunk(rows2, bf16), chunk(rows2, bf16)),
            "attend_grads",
            (at, tok, own[0], other[0], dkv_own, late[0], sums_own, late[1]),
            us=1.5,
            scalars=1,
        )
        by_member = lambda v: v.reshape(m, rows2 // m, width)
        pieces2 = share_pieces(by_member(keep2), by_member(flip(send2, 1)), member)
        pieces2, got1 = fence((pieces2, got1))
        got2 = [flip_member(v, s) for s, v in enumerate(pieces2[1:], 1)]
        total1 = fence(add(pieces1[0], got1))
        near1 = swap(total1[1], 1)
        d_tok, near1 = fence((d_tok, near1))
        d_toks = [d_tok, swap(d_tok, 1)]
        share1 = total1[0].astype(f32) + near1.astype(f32)
        share1, got2 = fence((share1.astype(bf16), got2))
        mine1 = gather_grads(share1, at, "gather_ffn_grads")
        other1 = flip(mine1, 1)
        total2 = add(pieces2[0], got2)
        total2, *d_toks = fence((total2, *d_toks))
        mine2 = gather_grads(total2, at, "gather_attend_grads").reshape(rows2, width)
        other2 = flip(mine2, 1)

        vector = shape((width,), f32)
        short = shape((local,), f32)
        square = shape((width, units), f32)
        wide = shape((local, width), f32)
        g_w_inner, g_w_outer, g_w_out, g_gain2, g_bias2, g_b_outer, g_b_inner, g_gain1, g_bias1, g_b_out = call(
            functools.partial(ffn_final_kernel, m),
            (square, square, wide) + (vector,) * 7,
            "ffn_grads_out",
            (at, mine1, other1),
            us=3.0,
            scalars=1,
        )
        assemble = lambda parts, name: call(
            rows_kernel,
            shape((row_count, block, width), bf16),
            name,
            (at, *parts),
            us=1.5,
            scalars=1,
        )
        output = assemble(outs, "output_rows")
        d_tokens = assemble(d_toks, "input_grad_rows")
        other2, g_b_out = fence((other2, g_b_out))
        g_q, g_k, g_v, g_b_query, g_b_value = call(
            attend_final_kernel,
            (wide,) * 3 + (short,) * 2,
            "attend_grads_out",
            (at, mine2, other2),
            us=2.0,
            scalars=1,
        )
        return (
            output, d_tokens, g_q.T, g_b_query, g_k.T, g_v.T, g_b_value, g_w_out, g_b_out, g_gain1,
            g_bias1, g_w_inner, g_b_inner, g_w_outer, g_b_outer, g_gain2, g_bias2,
        )

    spread, cols, vec, rows_ = P("dp", "blk", None), P(None, "tensor"), P("tensor"), P("tensor", None)
    return jax.shard_map(
        body,
        mesh=mesh,
        in_specs=(
            spread, P("dp"), P("dp", None), cols, vec, cols, cols, vec, rows_, P(), P(), P(),
            cols, vec, rows_, P(), P(), P(), spread,
        ),
        out_specs=(
            spread, spread, cols, vec, cols, cols, vec, rows_, P(), P(), P(), cols, vec, rows_,
            P(), P(), P(),
        ),
        check_vma=False,
    )
```

```python
import functools

import jax
import jax.numpy as jnp
from jax import lax
from jax.experimental import pallas as pl
from jax.experimental.pallas import tpu as pltpu
from jax.sharding import PartitionSpec as P

HEAD_DIM = 64
BLOCK = 128
LANES = 128
SCALE = HEAD_DIM**-0.5
EPS = 1e-12
f32 = jnp.float32
bf16 = jnp.bfloat16
i32 = jnp.int32
MIB = 1 << 20
FLOPS_US = 1e9
ATTEND_US = 50.0
BACK_US = 50.0
FILL_US = 50.0
INPUT_US = 50.0
GRADS_US = 1.0
PACKED = BLOCK + HEAD_DIM


def nn(a, b):
    return lax.dot_general(a, b, (((1,), (0,)), ((), ())), preferred_element_type=f32)


def nt(a, b):
    return lax.dot_general(a, b, (((1,), (1,)), ((), ())), preferred_element_type=f32)


def tn(a, b):
    return lax.dot_general(a, b, (((0,), (0,)), ((), ())), preferred_element_type=f32)


def mean(v):
    return jnp.mean(v, axis=-1, keepdims=True)


def col_sum(v):
    return jnp.sum(v, axis=0, keepdims=True)


def row_at(at, i):
    half = at[0] % 2
    return 2 * half + i if i < 2 else 2 * (1 - half) + (i - 2)


def rows8(*rows):
    width = rows[0].shape[1]
    pad = jnp.zeros((8 - len(rows), width), f32)
    return jnp.concatenate(rows + (pad,), axis=0)


def shape(dims, dtype):
    return jax.ShapeDtypeStruct(dims, dtype)


def near(dims, dtype):
    return pltpu.VMEM(dims, dtype)


SMEM = pl.BlockSpec(memory_space=pltpu.SMEM)
VMEM = pl.BlockSpec(memory_space=pltpu.VMEM)


def call(kernel, outs, name, args, scalars=0, us=1.0, vmem=16, scratch=()):
    return pl.pallas_call(
        kernel,
        out_shape=outs,
        in_specs=[SMEM] * scalars + [VMEM] * (len(args) - scalars),
        out_specs=jax.tree.map(lambda _: VMEM, outs),
        scratch_shapes=list(scratch),
        compiler_params=pltpu.CompilerParams(vmem_limit_bytes=vmem * MIB),
        cost_estimate=pl.CostEstimate(flops=int(us * FLOPS_US), bytes_accessed=1, transcendentals=0),
        name=name,
    )(*args)


def chunk_of(ref, c, rows):
    return ref[pl.ds(pl.multiple_of(c * rows, rows), rows), :]


def kv_kernel(tok, wk_t, wv_t, bv, kv, wkv_t):
    heads = wk_t.shape[0] // HEAD_DIM
    rows, bias = [], []
    for h in range(heads):
        part = slice(h * HEAD_DIM, (h + 1) * HEAD_DIM)
        rows += [wk_t[part, :], wv_t[part, :]]
        bias += [jnp.zeros((1, HEAD_DIM), f32), bv[:, part]]
    both = jnp.concatenate(rows, axis=0)
    wkv_t[...] = both
    kv[...] = (nt(tok[...], both) + jnp.concatenate(bias, axis=1)).astype(bf16)


def q_kernel(tok, wq_t, bq, q):
    heads = wq_t.shape[0] // HEAD_DIM
    full = (nt(tok[...], wq_t[...]) + bq[...]).astype(bf16) * jnp.asarray(SCALE, bf16)
    zero = jnp.zeros((full.shape[0], HEAD_DIM), bf16)
    cols = []
    for h in range(heads):
        cols += [full[:, h * HEAD_DIM : (h + 1) * HEAD_DIM], zero]
    q[...] = jnp.concatenate(cols, axis=1)


def piece_kernel(at, w_in, w_outer, w_out, piece, out_piece, sems):
    tail = out_piece.shape[0]
    half = (piece.shape[0] - tail) // 2

    def part(ref, index, size):
        return ref.at[pl.ds(pl.multiple_of(index * size, 16), size), :]

    copies = [
        pltpu.make_async_copy(part(w_in, at[4], half), piece.at[pl.ds(0, half), :], sems.at[0]),
        pltpu.make_async_copy(part(w_outer, at[4], half), piece.at[pl.ds(half, half), :], sems.at[1]),
        pltpu.make_async_copy(part(w_out, at[2], tail), out_piece, sems.at[2]),
    ]
    for copy in copies:
        copy.start()
    for copy in copies:
        copy.wait()
    piece[2 * half :, :] = out_piece[...]


def weights_kernel(n, at, w_out, *refs):
    pieces, (w_out_all, w_in_far, w_outer_far) = refs[:8], refs[8:]
    z = at[0]
    local = w_out.shape[0]
    part = local // 4
    rows = w_in_far.shape[0] // 8

    def put(ref, base, value):
        size = value.shape[0]
        ref[pl.ds(pl.multiple_of(base, 16), size), :] = value

    put(w_out_all, z * local, w_out[...])
    for j, piece in enumerate(pieces):
        put(w_in_far, (at[4] ^ j) * rows, piece[:rows, :])
        put(w_outer_far, (at[4] ^ j) * rows, piece[rows : 2 * rows, :])
        for s in range(1, n if j < 4 else 0):
            base = 2 * rows + (s - 1) * part
            put(w_out_all, (z ^ s) * local + (at[2] ^ j) * part, piece[base : base + part, :])


def attend_kernel(n_blk, ids, at, bucket, lens, q, *refs):
    kvs, outs_to = refs[:n_blk], refs[n_blk:]
    heads = q.shape[1] // LANES
    b = at[2]
    q_at = lax.broadcasted_iota(i32, (BLOCK, 1), 0)
    k_at = lax.broadcasted_iota(i32, (1, BLOCK), 1)
    for order, row in enumerate(ids):
        hp, probs = outs_to[2 * (order // 2)], outs_to[2 * (order // 2) + 1]
        i = order % 2
        r = row_at(at, row)
        bk = bucket[r]
        size = BLOCK << bk
        slot = b >> bk
        limit = lens[r, slot]
        q_in = jnp.where(q_at + (b * BLOCK - slot * size) < limit, 1, 0)
        k_in = []
        for j in range(n_blk):
            kb = b ^ j
            k_slot = kb >> bk
            inside = jnp.where(k_at + (kb * BLOCK - k_slot * size) < limit, 1, 0)
            k_in.append(jnp.where(k_slot == slot, inside, 2))
        allowed = q_in == jnp.concatenate(k_in, axis=1)
        here = pl.ds(pl.multiple_of(r * BLOCK, BLOCK), BLOCK)
        outs = []
        for h in range(heads):
            lanes = slice(h * LANES, (h + 1) * LANES)
            kvh = jnp.concatenate([kv[here, lanes] for kv in kvs], axis=0)
            scores = jnp.where(allowed, nt(q[here, lanes], kvh), -1e30)
            weights = jnp.exp(scores - jnp.max(scores, axis=-1, keepdims=True))
            total = jnp.sum(weights, axis=-1, keepdims=True)
            p = (weights / total).astype(bf16)
            probs[(i * heads + h) * BLOCK : (i * heads + h + 1) * BLOCK, :] = p
            outs.append(nn(p, kvh)[:, HEAD_DIM:].astype(bf16))
        base = i * PACKED
        hp[base : base + BLOCK, :] = jnp.concatenate(outs[:2], axis=1)
        hp[base + BLOCK : base + PACKED, :] = jnp.concatenate(
            [outs[2][:HEAD_DIM], outs[2][HEAD_DIM:]], axis=1
        )


def unpack(h):
    odd = jnp.concatenate([h[BLOCK:, :HEAD_DIM], h[BLOCK:, HEAD_DIM:]], axis=0)
    return jnp.concatenate([h[:BLOCK, :], odd], axis=1)


def pack(v):
    odd = jnp.concatenate([v[:HEAD_DIM, LANES:], v[HEAD_DIM:, LANES:]], axis=1)
    return jnp.concatenate([v[:, :LANES], odd], axis=0)


def gelu_and_slope(inner):
    cdf = 0.5 * (1.0 + lax.erf(inner * (0.5**0.5)))
    slope = cdf + inner * (0.3989422804014327 * jnp.exp(-0.5 * inner * inner))
    return (inner * cdf).astype(bf16), slope.astype(bf16)


def ffn_kernel(
    n, i, at, tok, w_out, b_out, g1, b1, w_in, w_in_far, b_in, b_in_far, w_outer, w_outer_far, *refs
):
    hps = refs[:n]
    part, n1_out, s1_out, low_out, act_out, act_far_out, slopes, held = refs[n:]
    z = at[0]
    local = w_out.shape[0] // n
    for s in range(n):
        j = z ^ s
        held[j] = nn(unpack(hps[s][i * PACKED : (i + 1) * PACKED, :]), chunk_of(w_out, j, local))
    attn = held[0]
    for j in range(1, n):
        attn = attn + held[j]
    resid = chunk_of(tok, row_at(at, i), BLOCK).astype(f32) + (attn + b_out[...])
    center = resid - mean(resid)
    s1 = lax.rsqrt(mean(center * center) + EPS)
    n1 = center * s1
    low = (n1 * g1[...] + b1[...]).astype(bf16)
    act, slope = gelu_and_slope(nn(low, w_in[...]) + b_in[...])
    act_far, slope_far = gelu_and_slope(nn(low, w_in_far[...]) + b_in_far[...])
    part[...] = (nn(act, w_outer[...]) + nn(act_far, w_outer_far[...])).astype(bf16)
    n1_out[...] = n1
    s1_out[...] = jnp.broadcast_to(s1, s1_out.shape)
    low_out[...] = low
    act_out[...] = act
    act_far_out[...] = act_far
    slopes[:BLOCK, :] = slope
    slopes[BLOCK:, :] = slope_far


def ffn_back_kernel(
    i, at, cot, n1, slopes, mine, theirs, g1, b1, b_outer, g2, b2, w_in, w_in_far, w_outer,
    w_outer_far, out, dffn_out, dinner_out, dinner_far_out, part, dres2_out, sums
):
    hidden = n1[...] * g1[...] + b1[...]
    ffn = mine[...].astype(f32) + theirs[...].astype(f32)
    resid = hidden + (ffn + b_outer[...])
    center = resid - mean(resid)
    s2 = lax.rsqrt(mean(center * center) + EPS)
    n2 = center * s2
    ct = chunk_of(cot, row_at(at, i), BLOCK).astype(f32)
    dn = ct * g2[...]
    dres2 = s2 * (dn - mean(dn) - n2 * mean(dn * n2))
    dffn = dres2.astype(bf16)
    dinner = (nt(dffn, w_outer[...]) * slopes[:BLOCK, :].astype(f32)).astype(bf16)
    dinner_far = (nt(dffn, w_outer_far[...]) * slopes[BLOCK:, :].astype(f32)).astype(bf16)
    part[...] = (nt(dinner, w_in[...]) + nt(dinner_far, w_in_far[...])).astype(bf16)
    dres2_out[...] = dres2
    dinner_out[...] = dinner
    out[...] = (n2 * g2[...] + b2[...]).astype(bf16)
    dffn_out[...] = dffn
    dinner_far_out[...] = dinner_far
    sums[...] = rows8(
        col_sum(ct * n2), col_sum(ct), col_sum(dffn.astype(f32)),
        col_sum(dinner.astype(f32)), col_sum(dinner_far.astype(f32)),
    )


def norm_back_kernel(n, at, mine, theirs, dres2, n1, s1, g1, w_out, dres1_out, share, dh, dh_far):
    dhidden = (mine[...].astype(f32) + theirs[...].astype(f32)) + dres2[...]
    norm = n1[...]
    dn = dhidden * g1[...]
    dres1 = s1[:, :1] * (dn - mean(dn) - norm * mean(dn * norm))
    dattn = dres1.astype(bf16)
    dres1_out[...] = dres1
    share[:BLOCK, :] = dattn
    sums = rows8(col_sum(dhidden * norm), col_sum(dhidden), col_sum(dattn.astype(f32)))
    share[BLOCK:, :] = jnp.concatenate([sums, jnp.zeros_like(sums)], axis=0).astype(bf16)
    local = w_out.shape[0] // n
    dh[...] = pack(nt(dattn, chunk_of(w_out, at[0], local)).astype(bf16))
    dh_far[...] = pack(nt(dattn, chunk_of(w_out, at[0] ^ 1, local)).astype(bf16))


def attend_back_kernel(n_blk, ids, at, first, second, q, probs, *refs):
    kvs = refs[:n_blk]
    dq_out, send, keep = refs[n_blk:]
    heads = q.shape[1] // LANES
    zero = jnp.zeros((BLOCK, HEAD_DIM), bf16)
    for i, packed in enumerate((first, second)):
        c = row_at(at, ids[i])
        here = pl.ds(pl.multiple_of(c * BLOCK, BLOCK), BLOCK)
        flat = unpack(packed[...])
        dqs = []
        for h in range(heads):
            lanes = slice(h * LANES, (h + 1) * LANES)
            dhead = jnp.concatenate([zero, flat[:, h * HEAD_DIM : (h + 1) * HEAD_DIM]], axis=1)
            kvh = jnp.concatenate([kv[here, lanes] for kv in kvs], axis=0)
            at_p = (i * heads + h) * BLOCK
            p = probs[at_p : at_p + BLOCK, :]
            pf = p.astype(f32)
            dp = nt(dhead, kvh)
            delta = jnp.sum(pf * dp, axis=-1, keepdims=True)
            ds = (pf * (dp - delta)).astype(bf16)
            dqs.append((nn(ds, kvh) * SCALE)[:, :HEAD_DIM].astype(bf16))
            left = jnp.concatenate([q[here, lanes], dhead], axis=0)
            dkv = tn(left, jnp.concatenate([ds, p], axis=0)).astype(bf16)
            for j in range(n_blk):
                target = keep if j % 2 == 0 else send
                target[j // 2, i, lanes, :] = dkv[:, j * BLOCK : (j + 1) * BLOCK]
        dq_out[i * BLOCK : (i + 1) * BLOCK, :] = jnp.concatenate(dqs, axis=1)


def input_kernel(dq, keep, recv, far, wq_t, wkv_t, part, dkv_t, sums):
    total = keep[0].astype(f32) + recv[0].astype(f32) + far[...].astype(f32)
    lows = [total[i].astype(bf16) for i in range(2)]
    low = jnp.concatenate([v.T for v in lows], axis=0)
    grad = nn(dq[...], wq_t[...]) + nn(low, wkv_t[...])
    part[...] = grad.astype(bf16)
    dkv_t[...] = jnp.concatenate(lows, axis=1)
    width = sums.shape[1]
    one = col_sum(dq[...].astype(f32))
    two = col_sum(low.astype(f32))
    sums[...] = rows8(
        jnp.concatenate([one, jnp.zeros((1, width - one.shape[1]), f32)], axis=1),
        jnp.concatenate([two, jnp.zeros((1, width - two.shape[1]), f32)], axis=1),
    )


def pick(first, one, other):
    return jnp.where(first, one, other)


def join(values, axis=0):
    return jnp.concatenate(list(values), axis=axis)


def ordered_sum(at, parts, held):
    for i, part in enumerate(parts):
        held[row_at(at, i)] = part.astype(f32)
    total = held[0]
    for r in range(1, len(parts)):
        total = total + held[r]
    return total


def ffn_grad_kernel(m, at, *refs):
    low, act, act_far, dffn, dinner, dinner_far, sums2 = (refs[2 * i : 2 * i + 2] for i in range(7))
    keep, send = refs[14:]
    first = at[1] == 0
    both = lambda pair: join(x[...] for x in pair)
    lows, dffns = both(low), both(dffn)
    tail2 = sums2[0][...] + sums2[1][...]
    rows = lows.shape[1] // m
    for q, (acts, dinners) in enumerate(((both(act), both(dinner)), (both(act_far), both(dinner_far)))):
        tail = join([tail2[:3], tail2[3 + q : 4 + q], jnp.zeros((12, tail2.shape[1]), f32)])
        tail = tail.astype(bf16)
        for target, one in ((keep, first), (send, jnp.logical_not(first))):
            main = tn(pick(one, lows, acts), pick(one, dinners, dffns)).astype(bf16)
            for i in range(m):
                target[i, q, :rows, :] = main[i * rows : (i + 1) * rows]
                target[i, q, rows:, :] = tail


def attend_grad_kernel(m, at, tok, hp_mine, hp_other, *refs):
    shares, (dq, dkv_t, sums) = refs[:4], (refs[4 + 2 * i : 6 + 2 * i] for i in range(3))
    keep, send, held = refs[10:]
    first = at[1] == 0
    toks = join(chunk_of(tok, row_at(at, i), BLOCK) for i in range(4))
    heads = join(unpack(hp[i * PACKED : (i + 1) * PACKED, :]) for hp in (hp_mine, hp_other) for i in range(2))
    g_out = tn(heads, join(x[:BLOCK, :] for x in shares))
    g_q = tn(join(x[...] for x in dq), toks)
    g_kv = nn(join((x[...] for x in dkv_t), axis=1), toks)
    one = join([g_out, g_q]).astype(bf16)
    two = g_kv.astype(bf16)
    half = two.shape[0]
    norm = ordered_sum(at, [x[BLOCK : BLOCK + 8, :] for x in shares], held)
    total = sums[0][...] + sums[1][...]
    rest = keep.shape[0] - half
    tail = join([norm, total, jnp.zeros((rest - 16, total.shape[1]), f32)]).astype(bf16)
    keep[:half, :] = pick(first, one, two)
    keep[half:, :] = tail
    send[:half, :] = pick(first, two, one)
    send[half:, :] = tail


def gather_kernel(m, at, *refs):
    out = refs[m]
    for s in range(m):
        out[at[3] ^ s] = refs[s][...]


def ffn_final_kernel(m, at, mine, other, g_in, g_outer, *vectors):
    first = at[1] == 0
    rows = g_in.shape[0] // m
    for i in range(m):
        a, b = mine[i], other[i]
        g_in[i * rows : (i + 1) * rows, :] = pick(first, a[:rows], b[:rows]).astype(f32)
        g_outer[i * rows : (i + 1) * rows, :] = pick(first, b[:rows], a[:rows]).astype(f32)
    tail = mine[0, rows:, :].astype(f32)
    for k, ref in enumerate(vectors):
        ref[...] = tail[k]


def attend_final_kernel(at, mine, other, g_out, g_q, g_k, g_v, gain, bias, b_out, b_q, b_v):
    first = at[1] == 0
    width = g_q.shape[0]
    a = mine[...]
    b = other[...]
    one = pick(first, a, b).astype(f32)
    two = pick(first, b, a).astype(f32)
    g_out[...] = one[:width]
    g_q[...] = one[width : 2 * width]
    tail = one[2 * width : 2 * width + 16]
    values = []
    for h in range(width // HEAD_DIM):
        part = slice(h * HEAD_DIM, (h + 1) * HEAD_DIM)
        g_k[part, :] = two[h * LANES : h * LANES + HEAD_DIM]
        g_v[part, :] = two[h * LANES + HEAD_DIM : (h + 1) * LANES]
        values.append(tail[9:10, h * LANES + HEAD_DIM : (h + 1) * LANES])
    for i, ref in enumerate((gain, bias, b_out)):
        ref[...] = tail[i]
    b_q[...] = tail[8, :width]
    b_v[...] = jnp.concatenate(values, axis=1)[0]


def rows_kernel(at, *refs):
    out = refs[-1]
    rows = [v[i * BLOCK : (i + 1) * BLOCK, :] for v in refs[:-1] for i in range(v.shape[0] // BLOCK)]
    for i, value in enumerate(rows):
        out[row_at(at, i)] = value


def solution(mesh):
    n_dp = mesh.shape["dp"]
    n_blk = mesh.shape["blk"]
    n = mesh.shape["tensor"]
    half_blk = n_blk // 2
    m = n_dp * half_blk

    def swap(v, bit):
        return lax.ppermute(v, "tensor", [(i, i ^ bit) for i in range(n)])

    def flip(v, bit):
        return lax.ppermute(v, "blk", [(i, i ^ bit) for i in range(n_blk)])

    def flip_member(v, s):
        perm = []
        for dp in range(n_dp):
            for blk in range(n_blk):
                i = (dp * half_blk + blk // 2) ^ s
                to = (i // half_blk) * n_blk + (i % half_blk) * 2 + blk % 2
                perm.append((dp * n_blk + blk, to))
        return lax.ppermute(v, ("dp", "blk"), perm)

    def share_pieces(keep, recv, member):
        def piece(s):
            mine = lax.dynamic_index_in_dim(keep, member ^ s, 0, keepdims=False)
            theirs = lax.dynamic_index_in_dim(recv, member ^ s, 0, keepdims=False)
            return (mine.astype(f32) + theirs.astype(f32)).astype(bf16)

        return [piece(s) for s in range(m)]

    def add(own, got):
        total = own.astype(f32)
        for part in got:
            total = total + part.astype(f32)
        return total.astype(bf16)

    def gather_grads(total, at, name, *extra):
        rows, width = total.shape
        got = [flip_member(total, s) for s in range(1, m)]
        got, extra = lax.optimization_barrier((got, extra))
        every = [total] + got
        mine = call(
            functools.partial(gather_kernel, m),
            near((m, rows, width), bf16),
            name,
            (at, *every),
            scalars=1,
        )
        return mine, *extra

    def body(
        tokens, bucket_ids, seq_lengths, w_query, b_query, w_key, w_value, b_value, w_out, b_out,
        norm1_gain, norm1_bias, w_inner, b_inner, w_outer, b_outer, norm2_gain, norm2_bias,
        cotangent,
    ):
        row_count, block, width = tokens.shape
        count = row_count * block
        local = w_query.shape[1]
        heads = local // HEAD_DIM
        lanes = heads * LANES
        units = w_inner.shape[1]
        blk = lax.axis_index("blk").astype(i32)
        z = lax.axis_index("tensor").astype(i32)
        core = blk % 2
        member = (lax.axis_index("dp") * half_blk + blk // 2).astype(i32)
        cut_at = (lax.axis_index("dp") % 2) * n_blk + blk
        at = jnp.stack([z, core, blk, member, cut_at]).astype(i32)
        tok = tokens.reshape(count, width)
        cot = cotangent.reshape(count, width)
        row = lambda v: v.reshape(1, -1)
        wq_t, wk_t, wv_t = w_query.T, w_key.T, w_value.T
        fence = lax.optimization_barrier

        part = local // 4
        piece_rows = (width + units) // 8
        piece, out_piece = pl.pallas_call(
            piece_kernel,
            out_shape=(near((piece_rows + part, width), bf16), near((part, width), bf16)),
            in_specs=[SMEM] + [pl.BlockSpec(memory_space=pl.ANY)] * 3,
            out_specs=(VMEM, VMEM),
            scratch_shapes=[pltpu.SemaphoreType.DMA((3,))],
            compiler_params=pltpu.CompilerParams(vmem_limit_bytes=8 * MIB),
            name="weight_piece",
        )(at, w_inner, w_outer, w_out)
        kv, wkv_t = call(
            kv_kernel,
            (near((count, lanes), bf16), near((lanes, width), bf16)),
            "kv_rows",
            (tok, wk_t, wv_t, row(b_value)),
        )
        kv, piece, out_piece, b_far = fence((kv, piece, out_piece, b_inner))
        kv_far = flip(kv, 2)
        kv_core = flip(kv, 1)
        pieces = [swap(piece, 1)] + [swap(out_piece, s) for s in range(2, n)]
        b_inner_far = swap(b_far, 1)
        kv_far, b_inner_far, *pieces = fence((kv_far, b_inner_far, *pieces))
        kv_both = flip(kv_far, 1)
        own_piece = jnp.concatenate(pieces, axis=0)
        ffn_piece = pieces[0][:piece_rows]

        def across(v, dp_bit, blk_bit):
            there = lambda i: ((i // n_blk) ^ dp_bit) * n_blk + ((i % n_blk) ^ blk_bit)
            return lax.ppermute(v, ("dp", "blk"), [(i, there(i)) for i in range(n_dp * n_blk)])

        arrived = {0: own_piece, 2: across(own_piece, 0, 2)}
        arrived |= {4: across(ffn_piece, 1, 0), 6: across(ffn_piece, 1, 2)}

        q = call(q_kernel, near((count, lanes), bf16), "query_rows", (tok, wq_t, row(b_query)), us=0.5)
        kvs = [kv, kv_core, kv_far, kv_both]

        pair = (near((2 * PACKED, LANES), bf16), near((2 * heads * BLOCK, n_blk * BLOCK), bf16))
        hp_other, probs_other, hp_mine, probs_mine = call(
            functools.partial(attend_kernel, n_blk, (2, 3, 0, 1)),
            pair + pair,
            "attend",
            (at, bucket_ids, seq_lengths, q, *kvs),
            us=ATTEND_US,
            scalars=3,
        )
        hps = {0: hp_mine, 1: swap(hp_other, 1), 2: swap(hp_mine, 2), 3: swap(hp_other, 3)}
        held = [arrived[2], arrived[4], arrived[6]]
        hps[1], hps[2], hps[3], *held = fence((hps[1], hps[2], hps[3], *held))
        arrived[2], arrived[4], arrived[6] = held
        arrived |= {j + 1: flip(v, 1) for j, v in arrived.items()}
        w_out_all, w_inner_far, w_outer_far = call(
            functools.partial(weights_kernel, n),
            (near((n * local, width), bf16), near(w_inner.shape, bf16), near(w_outer.shape, bf16)),
            "far_weights",
            (at, w_out, *[arrived[j] for j in range(8)]),
            us=2.2,
            scalars=1,
        )

        chunk = lambda rows, dt: near((rows, width), dt)
        gains1 = (row(norm1_gain), row(norm1_bias))

        def ffn(i):
            return call(
                functools.partial(ffn_kernel, n, i),
                (
                    chunk(BLOCK, bf16), chunk(BLOCK, f32), near((BLOCK, LANES), f32),
                    chunk(BLOCK, bf16), near((BLOCK, units), bf16), near((BLOCK, units), bf16),
                    near((2 * BLOCK, units), bf16),
                ),
                "ffn",
                (
                    at, tok, w_out_all, row(b_out), *gains1, w_inner, w_inner_far, row(b_inner),
                    row(b_inner_far), w_outer, w_outer_far, *[hps[s] for s in range(n)],
                ),
                us=2.4,
                scalars=1,
                scratch=[pltpu.VMEM((n, BLOCK, width), f32)],
            )

        parts, n1s, s1s, lows, acts, acts_far, slopes = map(list, zip(*[ffn(i) for i in range(2)]))
        theirs = [swap(v, 2) for v in parts]

        def ffn_back(i):
            return call(
                functools.partial(ffn_back_kernel, i),
                (
                    chunk(BLOCK, bf16), chunk(BLOCK, bf16), near((BLOCK, units), bf16),
                    near((BLOCK, units), bf16), chunk(BLOCK, bf16), chunk(BLOCK, f32), chunk(8, f32),
                ),
                "ffn_back",
                (
                    at, cot, n1s[i], slopes[i], parts[i], theirs[i], *gains1, row(b_outer),
                    row(norm2_gain), row(norm2_bias), w_inner, w_inner_far, w_outer, w_outer_far,
                ),
                us=2.7,
                scalars=1,
            )

        outs, dffns, dinners, dinners_far, parts2, dres2, sums2 = map(list, zip(*[ffn_back(i) for i in range(2)]))
        theirs2 = [swap(v, 2) for v in parts2]
        keep1, send1 = call(
            functools.partial(ffn_grad_kernel, m),
            (near((m, 2, width // m + 16, width), bf16),) * 2,
            "ffn_grads",
            (at, *lows, *acts, *acts_far, *dffns, *dinners, *dinners_far, *sums2),
            us=FILL_US,
            vmem=24,
            scalars=1,
        )
        recv1 = flip(send1, 1)
        pieces1 = share_pieces(keep1, recv1, member)

        def norm_back(i):
            return call(
                functools.partial(norm_back_kernel, n),
                (
                    chunk(BLOCK, f32), chunk(BLOCK + 16, bf16), near((PACKED, LANES), bf16),
                    near((PACKED, LANES), bf16),
                ),
                "norm_back",
                (at, parts2[i], theirs2[i], dres2[i], n1s[i], s1s[i], gains1[0], w_out_all),
                us=1.2,
                scalars=1,
            )

        dres1, shares, dheads, dheads_far = map(list, zip(*[norm_back(i) for i in range(2)]))
        dheads += [swap(v, 1) for v in dheads_far]
        shares += [swap(v, 1) for v in shares]
        outs += [swap(v, 1) for v in outs]

        def attend_back(ids, probs, *packed):
            return call(
                functools.partial(attend_back_kernel, n_blk, ids),
                (
                    near((2 * BLOCK, local), bf16), near((half_blk, 2, lanes, BLOCK), bf16),
                    near((half_blk, 2, lanes, BLOCK), bf16),
                ),
                "attend_back",
                (at, *packed, q, probs, *kvs),
                scalars=1,
                us=BACK_US,
            )

        own = attend_back((0, 1), probs_mine, dheads[0], dheads[1])
        after, dheads[2], dheads[3], pieces1 = fence((own[1], dheads[2], dheads[3], pieces1))
        own = (own[0], after, own[2])
        other = attend_back((2, 3), probs_other, dheads[2], dheads[3])

        def exchange(third):
            _, send, keep = third
            recv = flip(send, 1)
            return recv, (keep[1].astype(f32) + recv[1].astype(f32)).astype(bf16)

        def input_part(third, recv, far, us):
            dq, _, keep = third
            return call(
                input_kernel,
                (chunk(2 * BLOCK, bf16), near((lanes, 2 * BLOCK), bf16), chunk(8, f32)),
                "input_part",
                (dq, keep, recv, far, wq_t, wkv_t),
                us=us,
            )

        recv_own, sum_own = exchange(own)
        recv_other, sum_other = exchange(other)
        far_own, far_other = flip(sum_own, 2), flip(sum_other, 2)
        far_own, far_other, pieces1 = fence((far_own, far_other, pieces1))
        part, *late = input_part(other, recv_other, far_other, 1.0)
        part, pieces1, *ends = fence((part, pieces1, *shares[2:]))
        shares[2:] = ends
        from_near = swap(part, 1)
        got1 = [flip_member(v, s) for s, v in enumerate(pieces1[1:], 1)]
        part_own, dkv_own, sums_own = input_part(own, recv_own, far_own, INPUT_US)
        pair = (part_own.astype(f32) + from_near.astype(f32)).astype(bf16)

        rows2 = 2 * local + 16
        rows2 += -rows2 % (16 * m)
        keep2, send2 = call(
            functools.partial(attend_grad_kernel, m),
            (chunk(rows2, bf16), chunk(rows2, bf16)),
            "attend_grads",
            (
                at, tok, hp_mine, hp_other, *shares, own[0], other[0], dkv_own, late[0], sums_own,
                late[1],
            ),
            us=GRADS_US,
            scalars=1,
            scratch=[pltpu.VMEM((n, 8, width), f32)],
        )
        by_member = lambda v: v.reshape(m, rows2 // m, width)
        pieces2 = share_pieces(by_member(keep2), by_member(flip(send2, 1)), member)
        got2 = [flip_member(v, s) for s, v in enumerate(pieces2[1:], 1)]
        crossed, got1 = fence((swap(pair, 2), got1))
        d_tok = pair.astype(f32) + crossed.astype(f32) + jnp.concatenate(dres1, axis=0)
        d_tok = d_tok.astype(bf16)
        total1 = fence(add(pieces1[0], got1))
        near1, d_far, got2 = fence((swap(total1[1], 1), swap(d_tok, 1), got2))
        d_toks = [d_tok, d_far]
        share1 = (total1[0].astype(f32) + near1.astype(f32)).astype(bf16)
        total2 = add(pieces2[0], got2)
        mine1, *ends = gather_grads(share1, at, "gather_ffn_grads", *outs[2:])
        outs[2:] = ends
        other1 = flip(mine1, 1)
        (mine2,) = gather_grads(total2, at, "gather_attend_grads")
        mine2 = mine2.reshape(rows2, width)
        other2 = flip(mine2, 1)

        vector = shape((width,), f32)
        short = shape((local,), f32)
        square = shape((width, units), f32)
        wide = shape((local, width), f32)
        g_w_inner, g_w_outer, g_gain2, g_bias2, g_b_outer, g_b_inner = call(
            functools.partial(ffn_final_kernel, m),
            (square, square) + (vector,) * 4,
            "ffn_grads_out",
            (at, mine1, other1),
            us=3.0,
            scalars=1,
        )
        assemble = lambda parts, name: call(
            rows_kernel,
            shape((row_count, block, width), bf16),
            name,
            (at, *parts),
            us=1.5,
            scalars=1,
        )
        output = assemble(outs, "output_rows")
        d_tokens = assemble(d_toks, "input_grad_rows")
        other2, g_b_outer = fence((other2, g_b_outer))
        g_w_out, g_q, g_k, g_v, g_gain1, g_bias1, g_b_out, g_b_query, g_b_value = call(
            attend_final_kernel,
            (wide,) * 4 + (vector,) * 3 + (short,) * 2,
            "attend_grads_out",
            (at, mine2, other2),
            us=2.0,
            scalars=1,
        )
        return (
            output, d_tokens, g_q.T, g_b_query, g_k.T, g_v.T, g_b_value, g_w_out, g_b_out, g_gain1,
            g_bias1, g_w_inner, g_b_inner, g_w_outer, g_b_outer, g_gain2, g_bias2,
        )

    spread, cols, vec, rows_ = P("dp", "blk", None), P(None, "tensor"), P("tensor"), P("tensor", None)
    return jax.shard_map(
        body,
        mesh=mesh,
        in_specs=(
            spread, P("dp"), P("dp", None), cols, vec, cols, cols, vec, rows_, P(), P(), P(),
            cols, vec, rows_, P(), P(), P(), spread,
        ),
        out_specs=(
            spread, spread, cols, vec, cols, cols, vec, rows_, P(), P(), P(), cols, vec, rows_,
            P(), P(), P(),
        ),
        check_vma=False,
    )
```

```python
import functools

import jax
import jax.numpy as jnp
from jax import lax
from jax.experimental import pallas as pl
from jax.experimental.pallas import tpu as pltpu
from jax.sharding import PartitionSpec as P

HEAD_DIM = 64
BLOCK = 128
LANES = 128
SCALE = HEAD_DIM**-0.5
EPS = 1e-12
f32 = jnp.float32
bf16 = jnp.bfloat16
i32 = jnp.int32
MIB = 1 << 20
FLOPS_US = 1e9
ATTEND_US = 50.0
BACK_US = 50.0
FILL_US = 50.0
INPUT_US = 50.0
GRADS_US = 1.0
PACKED = BLOCK + HEAD_DIM


def nn(a, b):
    return lax.dot_general(a, b, (((1,), (0,)), ((), ())), preferred_element_type=f32)


def nt(a, b):
    return lax.dot_general(a, b, (((1,), (1,)), ((), ())), preferred_element_type=f32)


def tn(a, b):
    return lax.dot_general(a, b, (((0,), (0,)), ((), ())), preferred_element_type=f32)


def mean(v):
    return jnp.mean(v, axis=-1, keepdims=True)


def col_sum(v):
    return jnp.sum(v, axis=0, keepdims=True)


def row_at(at, i):
    half = at[0] % 2
    return 2 * half + i if i < 2 else 2 * (1 - half) + (i - 2)


def rows8(*rows):
    width = rows[0].shape[1]
    pad = jnp.zeros((8 - len(rows), width), f32)
    return jnp.concatenate(rows + (pad,), axis=0)


def shape(dims, dtype):
    return jax.ShapeDtypeStruct(dims, dtype)


def near(dims, dtype):
    return pltpu.VMEM(dims, dtype)


SMEM = pl.BlockSpec(memory_space=pltpu.SMEM)
VMEM = pl.BlockSpec(memory_space=pltpu.VMEM)
HBM = pl.BlockSpec(memory_space=pltpu.HBM)


def call(kernel, outs, name, args, scalars=0, us=1.0, vmem=16, scratch=()):
    return pl.pallas_call(
        kernel,
        out_shape=outs,
        in_specs=[SMEM] * scalars + [VMEM] * (len(args) - scalars),
        out_specs=jax.tree.map(lambda _: VMEM, outs),
        scratch_shapes=list(scratch),
        compiler_params=pltpu.CompilerParams(vmem_limit_bytes=vmem * MIB),
        cost_estimate=pl.CostEstimate(flops=int(us * FLOPS_US), bytes_accessed=1, transcendentals=0),
        name=name,
    )(*args)


def chunk_of(ref, c, rows):
    return ref[pl.ds(pl.multiple_of(c * rows, rows), rows), :]


def both_rows(wk_t, wv_t):
    rows = []
    for h in range(wk_t.shape[0] // HEAD_DIM):
        part = slice(h * HEAD_DIM, (h + 1) * HEAD_DIM)
        rows += [wk_t[part, :], wv_t[part, :]]
    return jnp.concatenate(rows, axis=0)


def front_kernel(at, tok, wk_t, wv_t, w_in, w_outer, w_out, bv, kv, piece, out_piece, tok_v, wk_v, wv_v, sems):
    tail = out_piece.shape[0]
    half = (piece.shape[0] - tail) // 2

    def part(ref, index, size):
        return ref.at[pl.ds(pl.multiple_of(index * size, 16), size), :]

    moves = [
        (tok, tok_v),
        (wk_t, wk_v),
        (wv_t, wv_v),
        (part(w_in, at[4], half), piece.at[pl.ds(0, half), :]),
        (part(w_outer, at[4], half), piece.at[pl.ds(half, half), :]),
        (part(w_out, at[2], tail), out_piece),
    ]
    copies = [pltpu.make_async_copy(a, b, sems.at[i]) for i, (a, b) in enumerate(moves)]
    for copy in copies:
        copy.start()
    for copy in copies[:3]:
        copy.wait()
    bias = []
    for h in range(wk_v.shape[0] // HEAD_DIM):
        bias += [jnp.zeros((1, HEAD_DIM), f32), bv[:, h * HEAD_DIM : (h + 1) * HEAD_DIM]]
    kv[...] = (nt(tok_v[...], both_rows(wk_v, wv_v)) + jnp.concatenate(bias, axis=1)).astype(bf16)
    for copy in copies[3:]:
        copy.wait()
    piece[2 * half :, :] = out_piece[...]


def q_kernel(tok, wq_t, bq, q):
    heads = wq_t.shape[0] // HEAD_DIM
    full = (nt(tok[...], wq_t[...]) + bq[...]).astype(bf16) * jnp.asarray(SCALE, bf16)
    zero = jnp.zeros((full.shape[0], HEAD_DIM), bf16)
    cols = []
    for h in range(heads):
        cols += [full[:, h * HEAD_DIM : (h + 1) * HEAD_DIM], zero]
    q[...] = jnp.concatenate(cols, axis=1)


def weights_kernel(n, at, w_out, *refs):
    pieces, (w_out_all, w_in_far, w_outer_far) = refs[:8], refs[8:]
    z = at[0]
    local = w_out.shape[0]
    part = local // 4
    rows = w_in_far.shape[0] // 8

    def put(ref, base, value):
        size = value.shape[0]
        ref[pl.ds(pl.multiple_of(base, 16), size), :] = value

    put(w_out_all, z * local, w_out[...])
    for j, piece in enumerate(pieces):
        put(w_in_far, (at[4] ^ j) * rows, piece[:rows, :])
        put(w_outer_far, (at[4] ^ j) * rows, piece[rows : 2 * rows, :])
        for s in range(1, n if j < 4 else 0):
            base = 2 * rows + (s - 1) * part
            put(w_out_all, (z ^ s) * local + (at[2] ^ j) * part, piece[base : base + part, :])


def attend_kernel(n_blk, ids, at, bucket, lens, q, *refs):
    kvs = refs[:n_blk]
    hp_first, hp_second, probs_first, probs_second, hp_late, held, sems = refs[n_blk:]
    copies = []
    heads = q.shape[1] // LANES
    b = at[2]
    q_at = lax.broadcasted_iota(i32, (BLOCK, 1), 0)
    k_at = lax.broadcasted_iota(i32, (1, BLOCK), 1)
    for order, row in enumerate(ids):
        hp, probs = ((hp_first, probs_first), (hp_second, probs_second))[order // 2]
        i = order % 2
        r = row_at(at, row)
        bk = bucket[r]
        size = BLOCK << bk
        slot = b >> bk
        limit = lens[r, slot]
        q_in = jnp.where(q_at + (b * BLOCK - slot * size) < limit, 1, 0)
        k_in = []
        for j in range(n_blk):
            kb = b ^ j
            k_slot = kb >> bk
            inside = jnp.where(k_at + (kb * BLOCK - k_slot * size) < limit, 1, 0)
            k_in.append(jnp.where(k_slot == slot, inside, 2))
        allowed = q_in == jnp.concatenate(k_in, axis=1)
        here = pl.ds(pl.multiple_of(r * BLOCK, BLOCK), BLOCK)
        outs = []
        for h in range(heads):
            lanes = slice(h * LANES, (h + 1) * LANES)
            kvh = jnp.concatenate([kv[here, lanes] for kv in kvs], axis=0)
            scores = jnp.where(allowed, nt(q[here, lanes], kvh), -1e30)
            weights = jnp.exp(scores - jnp.max(scores, axis=-1, keepdims=True))
            total = jnp.sum(weights, axis=-1, keepdims=True)
            p = (weights / total).astype(bf16)
            held[(order * heads + h) * BLOCK : (order * heads + h + 1) * BLOCK, :] = p
            outs.append(nn(p, kvh)[:, HEAD_DIM:].astype(bf16))
        base = i * PACKED
        hp[base : base + BLOCK, :] = jnp.concatenate(outs[:2], axis=1)
        hp[base + BLOCK : base + PACKED, :] = jnp.concatenate(
            [outs[2][:HEAD_DIM], outs[2][HEAD_DIM:]], axis=1
        )
        size = heads * BLOCK
        copies.append(
            pltpu.make_async_copy(
                held.at[pl.ds(order * size, size), :], probs.at[pl.ds(i * size, size), :], sems.at[order]
            )
        )
        copies[-1].start()
    for i, hp in enumerate((hp_first, hp_second)):
        rows = hp.shape[0]
        copies.append(pltpu.make_async_copy(hp, hp_late.at[pl.ds(i * rows, rows), :], sems.at[4 + i]))
        copies[-1].start()
    for copy in copies:
        copy.wait()


def unpack(h):
    odd = jnp.concatenate([h[BLOCK:, :HEAD_DIM], h[BLOCK:, HEAD_DIM:]], axis=0)
    return jnp.concatenate([h[:BLOCK, :], odd], axis=1)


def pack(v):
    odd = jnp.concatenate([v[:HEAD_DIM, LANES:], v[HEAD_DIM:, LANES:]], axis=1)
    return jnp.concatenate([v[:, :LANES], odd], axis=0)


def gelu_and_slope(inner):
    cdf = 0.5 * (1.0 + lax.erf(inner * (0.5**0.5)))
    slope = cdf + inner * (0.3989422804014327 * jnp.exp(-0.5 * inner * inner))
    return (inner * cdf).astype(bf16), slope.astype(bf16)


def ffn_kernel(
    n, i, at, tok, w_out, b_out, g1, b1, w_in, w_in_far, b_in, b_in_far, w_outer, w_outer_far, *refs
):
    hps = refs[:n] if len(refs) > n + 7 + 1 else [refs[0].at[pl.ds(s * PACKED, PACKED), :] for s in range(n)]
    refs = refs if len(refs) > n + 7 + 1 else refs[:1] * n + refs[1:]
    part, n1_out, s1_out, low_out, act_out, act_far_out, slopes, *rest, held = refs[n:]
    z = at[0]
    local = w_out.shape[0] // n
    for s in range(n):
        j = z ^ s
        held[j] = nn(unpack(hps[s][:PACKED, :]), chunk_of(w_out, j, local))
        if rest:
            rest[0][s * PACKED : (s + 1) * PACKED, :] = hps[s][PACKED:, :]
    attn = held[0]
    for j in range(1, n):
        attn = attn + held[j]
    resid = chunk_of(tok, row_at(at, i), BLOCK).astype(f32) + (attn + b_out[...])
    center = resid - mean(resid)
    s1 = lax.rsqrt(mean(center * center) + EPS)
    n1 = center * s1
    low = (n1 * g1[...] + b1[...]).astype(bf16)
    act, slope = gelu_and_slope(nn(low, w_in[...]) + b_in[...])
    act_far, slope_far = gelu_and_slope(nn(low, w_in_far[...]) + b_in_far[...])
    part[...] = (nn(act, w_outer[...]) + nn(act_far, w_outer_far[...])).astype(bf16)
    n1_out[...] = n1
    s1_out[...] = jnp.broadcast_to(s1, s1_out.shape)
    low_out[...] = low
    act_out[...] = act
    act_far_out[...] = act_far
    slopes[:BLOCK, :] = slope
    slopes[BLOCK:, :] = slope_far


def ffn_back_kernel(
    i, at, cot, n1, slopes, mine, theirs, g1, b1, b_outer, g2, b2, w_in, w_in_far, w_outer,
    w_outer_far, out, dffn_out, dinner_out, dinner_far_out, part, dres2_out, sums
):
    hidden = n1[...] * g1[...] + b1[...]
    ffn = mine[...].astype(f32) + theirs[...].astype(f32)
    resid = hidden + (ffn + b_outer[...])
    center = resid - mean(resid)
    s2 = lax.rsqrt(mean(center * center) + EPS)
    n2 = center * s2
    ct = chunk_of(cot, row_at(at, i), BLOCK).astype(f32)
    dn = ct * g2[...]
    dres2 = s2 * (dn - mean(dn) - n2 * mean(dn * n2))
    dffn = dres2.astype(bf16)
    dinner = (nt(dffn, w_outer[...]) * slopes[:BLOCK, :].astype(f32)).astype(bf16)
    dinner_far = (nt(dffn, w_outer_far[...]) * slopes[BLOCK:, :].astype(f32)).astype(bf16)
    part[...] = (nt(dinner, w_in[...]) + nt(dinner_far, w_in_far[...])).astype(bf16)
    dres2_out[...] = dres2
    dinner_out[...] = dinner
    out[...] = (n2 * g2[...] + b2[...]).astype(bf16)
    dffn_out[...] = dffn
    dinner_far_out[...] = dinner_far
    sums[...] = rows8(
        col_sum(ct * n2), col_sum(ct), col_sum(dffn.astype(f32)),
        col_sum(dinner.astype(f32)), col_sum(dinner_far.astype(f32)),
    )


def norm_back_kernel(n, at, mine, theirs, dres2, n1, s1, g1, w_out, dres1_out, share, dh, dh_far):
    dhidden = (mine[...].astype(f32) + theirs[...].astype(f32)) + dres2[...]
    norm = n1[...]
    dn = dhidden * g1[...]
    dres1 = s1[:, :1] * (dn - mean(dn) - norm * mean(dn * norm))
    dattn = dres1.astype(bf16)
    dres1_out[...] = dres1
    share[:BLOCK, :] = dattn
    sums = rows8(col_sum(dhidden * norm), col_sum(dhidden), col_sum(dattn.astype(f32)))
    share[BLOCK:, :] = jnp.concatenate([sums, jnp.zeros_like(sums)], axis=0).astype(bf16)
    local = w_out.shape[0] // n
    dh[...] = pack(nt(dattn, chunk_of(w_out, at[0], local)).astype(bf16))
    dh_far[...] = pack(nt(dattn, chunk_of(w_out, at[0] ^ 1, local)).astype(bf16))


def attend_back_kernel(n_blk, ids, at, first, second, q, probs, *refs):
    kvs = refs[:n_blk]
    dq_out, send, keep = refs[n_blk:]
    heads = q.shape[1] // LANES
    zero = jnp.zeros((BLOCK, HEAD_DIM), bf16)
    for i, packed in enumerate((first, second)):
        c = row_at(at, ids[i])
        here = pl.ds(pl.multiple_of(c * BLOCK, BLOCK), BLOCK)
        flat = unpack(packed[...])
        dqs = []
        for h in range(heads):
            lanes = slice(h * LANES, (h + 1) * LANES)
            dhead = jnp.concatenate([zero, flat[:, h * HEAD_DIM : (h + 1) * HEAD_DIM]], axis=1)
            kvh = jnp.concatenate([kv[here, lanes] for kv in kvs], axis=0)
            at_p = (i * heads + h) * BLOCK
            p = probs[at_p : at_p + BLOCK, :]
            pf = p.astype(f32)
            dp = nt(dhead, kvh)
            delta = jnp.sum(pf * dp, axis=-1, keepdims=True)
            ds = (pf * (dp - delta)).astype(bf16)
            dqs.append((nn(ds, kvh) * SCALE)[:, :HEAD_DIM].astype(bf16))
            left = jnp.concatenate([q[here, lanes], dhead], axis=0)
            dkv = tn(left, jnp.concatenate([ds, p], axis=0)).astype(bf16)
            for j in range(n_blk):
                target = keep if j % 2 == 0 else send
                target[j // 2, i, lanes, :] = dkv[:, j * BLOCK : (j + 1) * BLOCK]
        dq_out[i * BLOCK : (i + 1) * BLOCK, :] = jnp.concatenate(dqs, axis=1)


def input_kernel(dq, keep, recv, far, wq_t, wk_t, wv_t, part, dkv_t, sums):
    total = keep[0].astype(f32) + recv[0].astype(f32) + far[...].astype(f32)
    lows = [total[i].astype(bf16) for i in range(2)]
    low = jnp.concatenate([v.T for v in lows], axis=0)
    grad = nn(dq[...], wq_t[...]) + nn(low, both_rows(wk_t, wv_t))
    part[...] = grad.astype(bf16)
    dkv_t[...] = jnp.concatenate(lows, axis=1)
    width = sums.shape[1]
    one = col_sum(dq[...].astype(f32))
    two = col_sum(low.astype(f32))
    sums[...] = rows8(
        jnp.concatenate([one, jnp.zeros((1, width - one.shape[1]), f32)], axis=1),
        jnp.concatenate([two, jnp.zeros((1, width - two.shape[1]), f32)], axis=1),
    )


def pick(first, one, other):
    return jnp.where(first, one, other)


def join(values, axis=0):
    return jnp.concatenate(list(values), axis=axis)


def ordered_sum(at, parts, held):
    for i, part in enumerate(parts):
        held[row_at(at, i)] = part.astype(f32)
    total = held[0]
    for r in range(1, len(parts)):
        total = total + held[r]
    return total


def ffn_grad_kernel(m, at, *refs):
    low, act, act_far, dffn, dinner, dinner_far, sums2 = (refs[2 * i : 2 * i + 2] for i in range(7))
    keep, send = refs[14:]
    first = at[1] == 0
    both = lambda pair: join(x[...] for x in pair)
    lows, dffns = both(low), both(dffn)
    tail2 = sums2[0][...] + sums2[1][...]
    rows = lows.shape[1] // m
    for q, (acts, dinners) in enumerate(((both(act), both(dinner)), (both(act_far), both(dinner_far)))):
        tail = join([tail2[:3], tail2[3 + q : 4 + q], jnp.zeros((12, tail2.shape[1]), f32)])
        tail = tail.astype(bf16)
        for target, one in ((keep, first), (send, jnp.logical_not(first))):
            main = tn(pick(one, lows, acts), pick(one, dinners, dffns)).astype(bf16)
            for i in range(m):
                target[i, q, :rows, :] = main[i * rows : (i + 1) * rows]
                target[i, q, rows:, :] = tail


def attend_grad_kernel(m, at, tok, hp_late, *refs):
    shares, (dq, dkv_t, sums) = refs[:4], (refs[4 + 2 * i : 6 + 2 * i] for i in range(3))
    keep, send, held = refs[10:]
    first = at[1] == 0
    toks = join(chunk_of(tok, row_at(at, i), BLOCK) for i in range(4))
    heads = join(unpack(hp_late[i * PACKED : (i + 1) * PACKED, :]) for i in (2, 3, 0, 1))
    g_out = tn(heads, join(x[:BLOCK, :] for x in shares))
    g_q = tn(join(x[...] for x in dq), toks)
    g_kv = nn(join((x[...] for x in dkv_t), axis=1), toks)
    one = join([g_out, g_q]).astype(bf16)
    two = g_kv.astype(bf16)
    half = two.shape[0]
    norm = ordered_sum(at, [x[BLOCK : BLOCK + 8, :] for x in shares], held)
    total = sums[0][...] + sums[1][...]
    rest = keep.shape[0] - half
    tail = join([norm, total, jnp.zeros((rest - 16, total.shape[1]), f32)]).astype(bf16)
    keep[:half, :] = pick(first, one, two)
    keep[half:, :] = tail
    send[:half, :] = pick(first, two, one)
    send[half:, :] = tail


def gather_kernel(m, at, *refs):
    out = refs[m]
    for s in range(m):
        out[at[3] ^ s] = refs[s][...]


def ffn_final_kernel(m, at, mine, other, g_in, g_outer, *vectors):
    first = at[1] == 0
    rows = g_in.shape[0] // m
    for i in range(m):
        a, b = mine[i], other[i]
        g_in[i * rows : (i + 1) * rows, :] = pick(first, a[:rows], b[:rows]).astype(f32)
        g_outer[i * rows : (i + 1) * rows, :] = pick(first, b[:rows], a[:rows]).astype(f32)
    tail = mine[0, rows:, :].astype(f32)
    for k, ref in enumerate(vectors):
        ref[...] = tail[k]


def attend_final_kernel(at, mine, other, g_out, g_q, g_k, g_v, gain, bias, b_out, b_q, b_v):
    first = at[1] == 0
    width = g_q.shape[0]
    a = mine[...]
    b = other[...]
    one = pick(first, a, b).astype(f32)
    two = pick(first, b, a).astype(f32)
    g_out[...] = one[:width]
    g_q[...] = one[width : 2 * width]
    tail = one[2 * width : 2 * width + 16]
    values = []
    for h in range(width // HEAD_DIM):
        part = slice(h * HEAD_DIM, (h + 1) * HEAD_DIM)
        g_k[part, :] = two[h * LANES : h * LANES + HEAD_DIM]
        g_v[part, :] = two[h * LANES + HEAD_DIM : (h + 1) * LANES]
        values.append(tail[9:10, h * LANES + HEAD_DIM : (h + 1) * LANES])
    for i, ref in enumerate((gain, bias, b_out)):
        ref[...] = tail[i]
    b_q[...] = tail[8, :width]
    b_v[...] = jnp.concatenate(values, axis=1)[0]


def rows_kernel(at, *refs):
    out = refs[-1]
    rows = [v[i * BLOCK : (i + 1) * BLOCK, :] for v in refs[:-1] for i in range(v.shape[0] // BLOCK)]
    for i, value in enumerate(rows):
        out[row_at(at, i)] = value


def solution(mesh):
    n_dp = mesh.shape["dp"]
    n_blk = mesh.shape["blk"]
    n = mesh.shape["tensor"]
    half_blk = n_blk // 2
    m = n_dp * half_blk

    def swap(v, bit):
        return lax.ppermute(v, "tensor", [(i, i ^ bit) for i in range(n)])

    def flip(v, bit):
        return lax.ppermute(v, "blk", [(i, i ^ bit) for i in range(n_blk)])

    def flip_member(v, s):
        perm = []
        for dp in range(n_dp):
            for blk in range(n_blk):
                i = (dp * half_blk + blk // 2) ^ s
                to = (i // half_blk) * n_blk + (i % half_blk) * 2 + blk % 2
                perm.append((dp * n_blk + blk, to))
        return lax.ppermute(v, ("dp", "blk"), perm)

    def share_pieces(keep, recv, member):
        def piece(s):
            mine = lax.dynamic_index_in_dim(keep, member ^ s, 0, keepdims=False)
            theirs = lax.dynamic_index_in_dim(recv, member ^ s, 0, keepdims=False)
            return (mine.astype(f32) + theirs.astype(f32)).astype(bf16)

        return [piece(s) for s in range(m)]

    def add(own, got):
        total = own.astype(f32)
        for part in got:
            total = total + part.astype(f32)
        return total.astype(bf16)

    def gather_grads(every, at, name):
        rows, width = every[0].shape
        return call(
            functools.partial(gather_kernel, m),
            near((m, rows, width), bf16),
            name,
            (at, *every),
            scalars=1,
        )

    def body(
        tokens, bucket_ids, seq_lengths, w_query, b_query, w_key, w_value, b_value, w_out, b_out,
        norm1_gain, norm1_bias, w_inner, b_inner, w_outer, b_outer, norm2_gain, norm2_bias,
        cotangent,
    ):
        row_count, block, width = tokens.shape
        count = row_count * block
        local = w_query.shape[1]
        heads = local // HEAD_DIM
        lanes = heads * LANES
        units = w_inner.shape[1]
        blk = lax.axis_index("blk").astype(i32)
        z = lax.axis_index("tensor").astype(i32)
        core = blk % 2
        member = (lax.axis_index("dp") * half_blk + blk // 2).astype(i32)
        cut_at = (lax.axis_index("dp") % 2) * n_blk + blk
        at = jnp.stack([z, core, blk, member, cut_at]).astype(i32)
        tok = tokens.reshape(count, width)
        cot = cotangent.reshape(count, width)
        row = lambda v: v.reshape(1, -1)
        wq_t, wk_t, wv_t = w_query.T, w_key.T, w_value.T
        fence = lax.optimization_barrier

        part = local // 4
        piece_rows = (width + units) // 8
        kv, piece, out_piece = pl.pallas_call(
            front_kernel,
            out_shape=(
                near((count, lanes), bf16), near((piece_rows + part, width), bf16),
                near((part, width), bf16),
            ),
            in_specs=[SMEM] + [HBM] * 6 + [VMEM],
            out_specs=(VMEM,) * 3,
            scratch_shapes=[
                pltpu.VMEM((count, width), bf16), pltpu.VMEM((local, width), bf16),
                pltpu.VMEM((local, width), bf16), pltpu.SemaphoreType.DMA((6,)),
            ],
            compiler_params=pltpu.CompilerParams(vmem_limit_bytes=16 * MIB),
            name="front",
        )(at, *[pltpu.with_memory_space_constraint(v, pltpu.HBM) for v in (tok, wk_t, wv_t, w_inner, w_outer, w_out)], row(b_value))
        kv, piece, out_piece, b_far = fence((kv, piece, out_piece, b_inner))
        kv_far = flip(kv, 2)
        kv_core = flip(kv, 1)
        pieces = [swap(piece, 1)] + [swap(out_piece, s) for s in range(2, n)]
        b_inner_far = swap(b_far, 1)
        kv_far, b_inner_far, *pieces = fence((kv_far, b_inner_far, *pieces))
        kv_both = flip(kv_far, 1)
        own_piece = jnp.concatenate(pieces, axis=0)
        ffn_piece = pieces[0][:piece_rows]

        def across(v, dp_bit, blk_bit):
            there = lambda i: ((i // n_blk) ^ dp_bit) * n_blk + ((i % n_blk) ^ blk_bit)
            return lax.ppermute(v, ("dp", "blk"), [(i, there(i)) for i in range(n_dp * n_blk)])

        arrived = {0: own_piece, 2: across(own_piece, 0, 2)}
        arrived |= {4: across(ffn_piece, 1, 0), 6: across(ffn_piece, 1, 2)}

        q = call(q_kernel, near((count, lanes), bf16), "query_rows", (tok, wq_t, row(b_query)), us=0.5)
        kvs = [kv, kv_core, kv_far, kv_both]

        prob_rows = 2 * heads * BLOCK
        hp_other, hp_mine, probs_other, probs_mine, hp_late = pl.pallas_call(
            functools.partial(attend_kernel, n_blk, (2, 3, 0, 1)),
            out_shape=(near((2 * PACKED, LANES), bf16),) * 2
            + (pltpu.HBM((prob_rows, n_blk * BLOCK), bf16),) * 2
            + (pltpu.HBM((4 * PACKED, LANES), bf16),),
            in_specs=[SMEM] * 3 + [VMEM] * (1 + n_blk),
            out_specs=(VMEM,) * 2 + (HBM,) * 3,
            scratch_shapes=[
                pltpu.VMEM((2 * prob_rows, n_blk * BLOCK), bf16), pltpu.SemaphoreType.DMA((6,)),
            ],
            compiler_params=pltpu.CompilerParams(vmem_limit_bytes=16 * MIB),
            cost_estimate=pl.CostEstimate(
                flops=int(ATTEND_US * FLOPS_US), bytes_accessed=1, transcendentals=0
            ),
            name="attend",
        )(at, bucket_ids, seq_lengths, q, *kvs)
        hps = {0: hp_mine, 1: swap(hp_other, 1), 2: swap(hp_mine, 2), 3: swap(hp_other, 3)}
        held = [arrived[2], arrived[4], arrived[6]]
        hps[1], hps[2], hps[3], *held = fence((hps[1], hps[2], hps[3], *held))
        arrived[2], arrived[4], arrived[6] = held
        arrived |= {j + 1: flip(v, 1) for j, v in arrived.items()}
        w_out_all, w_inner_far, w_outer_far = call(
            functools.partial(weights_kernel, n),
            (near((n * local, width), bf16), near(w_inner.shape, bf16), near(w_outer.shape, bf16)),
            "far_weights",
            (at, w_out, *[arrived[j] for j in range(8)]),
            us=2.2,
            scalars=1,
        )

        chunk = lambda rows, dt: near((rows, width), dt)
        gains1 = (row(norm1_gain), row(norm1_bias))

        def ffn(i, heads_in):
            return call(
                functools.partial(ffn_kernel, n, i),
                (
                    chunk(BLOCK, bf16), chunk(BLOCK, f32), near((BLOCK, LANES), f32),
                    chunk(BLOCK, bf16), near((BLOCK, units), bf16), near((BLOCK, units), bf16),
                    near((2 * BLOCK, units), bf16),
                )
                + ((near((n * PACKED, LANES), bf16),) if i == 0 else ()),
                "ffn",
                (
                    at, tok, w_out_all, row(b_out), *gains1, w_inner, w_inner_far, row(b_inner),
                    row(b_inner_far), w_outer, w_outer_far, *heads_in,
                ),
                us=2.4,
                scalars=1,
                scratch=[pltpu.VMEM((n, BLOCK, width), f32)],
            )

        *row0, second_heads = ffn(0, [hps[s] for s in range(n)])
        parts, n1s, s1s, lows, acts, acts_far, slopes = map(list, zip(row0, ffn(1, [second_heads])))
        theirs = [swap(v, 2) for v in parts]

        def ffn_back(i):
            return call(
                functools.partial(ffn_back_kernel, i),
                (
                    chunk(BLOCK, bf16), chunk(BLOCK, bf16), near((BLOCK, units), bf16),
                    near((BLOCK, units), bf16), chunk(BLOCK, bf16), chunk(BLOCK, f32), chunk(8, f32),
                ),
                "ffn_back",
                (
                    at, cot, n1s[i], slopes[i], parts[i], theirs[i], *gains1, row(b_outer),
                    row(norm2_gain), row(norm2_bias), w_inner, w_inner_far, w_outer, w_outer_far,
                ),
                us=2.7,
                scalars=1,
            )

        outs, dffns, dinners, dinners_far, parts2, dres2, sums2 = map(list, zip(*[ffn_back(i) for i in range(2)]))
        theirs2 = [swap(v, 2) for v in parts2]
        keep1, send1 = call(
            functools.partial(ffn_grad_kernel, m),
            (near((m, 2, width // m + 16, width), bf16),) * 2,
            "ffn_grads",
            (at, *lows, *acts, *acts_far, *dffns, *dinners, *dinners_far, *sums2),
            us=FILL_US,
            vmem=24,
            scalars=1,
        )
        recv1 = flip(send1, 1)
        pieces1 = share_pieces(keep1, recv1, member)

        def norm_back(i):
            return call(
                functools.partial(norm_back_kernel, n),
                (
                    chunk(BLOCK, f32), chunk(BLOCK + 16, bf16), near((PACKED, LANES), bf16),
                    near((PACKED, LANES), bf16),
                ),
                "norm_back",
                (at, parts2[i], theirs2[i], dres2[i], n1s[i], s1s[i], gains1[0], w_out_all),
                us=1.2,
                scalars=1,
            )

        dres1, shares, dheads, dheads_far = map(list, zip(*[norm_back(i) for i in range(2)]))
        dheads += [swap(v, 1) for v in dheads_far]
        shares += [swap(v, 1) for v in shares]
        outs += [swap(v, 1) for v in outs]

        def attend_back(ids, probs, *packed):
            return call(
                functools.partial(attend_back_kernel, n_blk, ids),
                (
                    near((2 * BLOCK, local), bf16), near((half_blk, 2, lanes, BLOCK), bf16),
                    near((half_blk, 2, lanes, BLOCK), bf16),
                ),
                "attend_back",
                (at, *packed, q, probs, *kvs),
                scalars=1,
                us=BACK_US,
            )

        own = attend_back((0, 1), probs_mine, dheads[0], dheads[1])
        after, dheads[2], dheads[3], pieces1 = fence((own[1], dheads[2], dheads[3], pieces1))
        own = (own[0], after, own[2])
        other = attend_back((2, 3), probs_other, dheads[2], dheads[3])

        def exchange(third):
            _, send, keep = third
            recv = flip(send, 1)
            return recv, (keep[1].astype(f32) + recv[1].astype(f32)).astype(bf16)

        def input_part(third, recv, far, us):
            dq, _, keep = third
            return call(
                input_kernel,
                (chunk(2 * BLOCK, bf16), near((lanes, 2 * BLOCK), bf16), chunk(8, f32)),
                "input_part",
                (dq, keep, recv, far, wq_t, wk_t, wv_t),
                us=us,
            )

        recv_own, sum_own = exchange(own)
        recv_other, sum_other = exchange(other)
        far_own, far_other = flip(sum_own, 2), flip(sum_other, 2)
        far_own, far_other, pieces1 = fence((far_own, far_other, pieces1))
        part, *late = input_part(other, recv_other, far_other, 1.0)
        part, pieces1, *ends = fence((part, pieces1, *shares[2:]))
        shares[2:] = ends
        from_near = swap(part, 1)
        got1 = [flip_member(v, s) for s, v in enumerate(pieces1[1:], 1)]
        part_own, dkv_own, sums_own = input_part(own, recv_own, far_own, INPUT_US)
        pair = (part_own.astype(f32) + from_near.astype(f32)).astype(bf16)

        rows2 = 2 * local + 16
        rows2 += -rows2 % (16 * m)
        keep2, send2 = call(
            functools.partial(attend_grad_kernel, m),
            (chunk(rows2, bf16), chunk(rows2, bf16)),
            "attend_grads",
            (
                at, tok, hp_late, *shares, own[0], other[0], dkv_own, late[0], sums_own,
                late[1],
            ),
            us=GRADS_US,
            scalars=1,
            scratch=[pltpu.VMEM((n, 8, width), f32)],
        )
        by_member = lambda v: v.reshape(m, rows2 // m, width)
        pieces2 = share_pieces(by_member(keep2), by_member(flip(send2, 1)), member)
        got2 = [flip_member(v, s) for s, v in enumerate(pieces2[1:], 1)]
        got1, _, _ = fence((got1, keep2, pair))
        total1 = fence(add(pieces1[0], got1))
        near1 = swap(total1[1], 1)
        crossed, near1, got2, *ends = fence((swap(pair, 2), near1, got2, *outs[2:]))
        outs[2:] = ends
        d_tok = pair.astype(f32) + crossed.astype(f32) + jnp.concatenate(dres1, axis=0)
        d_tok = d_tok.astype(bf16)
        share1 = (total1[0].astype(f32) + near1.astype(f32)).astype(bf16)
        total2 = add(pieces2[0], got2)
        shares1 = [flip_member(share1, k) for k in range(1, m)]
        shares2 = [flip_member(total2, k) for k in range(1, m)]
        shares1, shares2, d_far = fence((shares1, shares2, swap(d_tok, 1)))
        d_toks = [d_tok, d_far]
        assemble = lambda parts, name: call(
            rows_kernel,
            shape((row_count, block, width), bf16),
            name,
            (at, *parts),
            us=1.5,
            scalars=1,
        )
        output = assemble(outs, "output_rows")
        d_tokens = assemble(d_toks, "input_grad_rows")
        shares1, shares2, _, _ = fence((shares1, shares2, output, d_tokens))
        mine1 = gather_grads([share1] + shares1, at, "gather_ffn_grads")
        other1 = flip(mine1, 1)
        mine2 = gather_grads([total2] + shares2, at, "gather_attend_grads").reshape(rows2, width)
        other2 = flip(mine2, 1)

        vector = shape((width,), f32)
        short = shape((local,), f32)
        square = shape((width, units), f32)
        wide = shape((local, width), f32)
        g_w_inner, g_w_outer, g_gain2, g_bias2, g_b_outer, g_b_inner = call(
            functools.partial(ffn_final_kernel, m),
            (square, square) + (vector,) * 4,
            "ffn_grads_out",
            (at, mine1, other1),
            us=3.0,
            scalars=1,
        )
        other2, g_b_outer = fence((other2, g_b_outer))
        g_w_out, g_q, g_k, g_v, g_gain1, g_bias1, g_b_out, g_b_query, g_b_value = call(
            attend_final_kernel,
            (wide,) * 4 + (vector,) * 3 + (short,) * 2,
            "attend_grads_out",
            (at, mine2, other2),
            us=2.0,
            scalars=1,
        )
        return (
            output, d_tokens, g_q.T, g_b_query, g_k.T, g_v.T, g_b_value, g_w_out, g_b_out, g_gain1,
            g_bias1, g_w_inner, g_b_inner, g_w_outer, g_b_outer, g_gain2, g_bias2,
        )

    spread, cols, vec, rows_ = P("dp", "blk", None), P(None, "tensor"), P("tensor"), P("tensor", None)
    return jax.shard_map(
        body,
        mesh=mesh,
        in_specs=(
            spread, P("dp"), P("dp", None), cols, vec, cols, cols, vec, rows_, P(), P(), P(),
            cols, vec, rows_, P(), P(), P(), spread,
        ),
        out_specs=(
            spread, spread, cols, vec, cols, cols, vec, rows_, P(), P(), P(), cols, vec, rows_,
            P(), P(), P(),
        ),
        check_vma=False,
    )
```

```python
import functools

import jax
import jax.numpy as jnp
from jax import lax
from jax.experimental import pallas as pl
from jax.experimental.pallas import tpu as pltpu
from jax.sharding import PartitionSpec as P

HEAD_DIM = 64
BLOCK = 128
LANES = 128
SCALE = HEAD_DIM**-0.5
EPS = 1e-12
f32 = jnp.float32
bf16 = jnp.bfloat16
i32 = jnp.int32
MIB = 1 << 20
FLOPS_US = 1e9
ATTEND_US = 50.0
BACK_US = 50.0
FILL_US = 50.0
INPUT_US = 50.0
GRADS_US = 1.0
PACKED = BLOCK + HEAD_DIM


def nn(a, b):
    return lax.dot_general(a, b, (((1,), (0,)), ((), ())), preferred_element_type=f32)


def nt(a, b):
    return lax.dot_general(a, b, (((1,), (1,)), ((), ())), preferred_element_type=f32)


def tn(a, b):
    return lax.dot_general(a, b, (((0,), (0,)), ((), ())), preferred_element_type=f32)


def mean(v):
    return jnp.mean(v, axis=-1, keepdims=True)


def col_sum(v):
    return jnp.sum(v, axis=0, keepdims=True)


def row_at(at, i):
    half = at[0] % 2
    return 2 * half + i if i < 2 else 2 * (1 - half) + (i - 2)


def rows8(*rows):
    width = rows[0].shape[1]
    pad = jnp.zeros((8 - len(rows), width), f32)
    return jnp.concatenate(rows + (pad,), axis=0)


def shape(dims, dtype):
    return jax.ShapeDtypeStruct(dims, dtype)


def near(dims, dtype):
    return pltpu.VMEM(dims, dtype)


SMEM = pl.BlockSpec(memory_space=pltpu.SMEM)
VMEM = pl.BlockSpec(memory_space=pltpu.VMEM)
HBM = pl.BlockSpec(memory_space=pltpu.HBM)


def call(kernel, outs, name, args, scalars=0, us=1.0, vmem=16, scratch=()):
    return pl.pallas_call(
        kernel,
        out_shape=outs,
        in_specs=[SMEM] * scalars + [VMEM] * (len(args) - scalars),
        out_specs=jax.tree.map(lambda _: VMEM, outs),
        scratch_shapes=list(scratch),
        compiler_params=pltpu.CompilerParams(vmem_limit_bytes=vmem * MIB),
        cost_estimate=pl.CostEstimate(flops=int(us * FLOPS_US), bytes_accessed=1, transcendentals=0),
        name=name,
    )(*args)


def chunk_of(ref, c, rows):
    return ref[pl.ds(pl.multiple_of(c * rows, rows), rows), :]


def both_rows(wk_t, wv_t):
    rows = []
    for h in range(wk_t.shape[0] // HEAD_DIM):
        part = slice(h * HEAD_DIM, (h + 1) * HEAD_DIM)
        rows += [wk_t[part, :], wv_t[part, :]]
    return jnp.concatenate(rows, axis=0)


def front_kernel(at, tok, wk_t, wv_t, w_in, w_outer, w_out, bv, kv, piece, out_piece, tok_v, wk_v, wv_v, sems):
    tail = out_piece.shape[0]
    half = (piece.shape[0] - tail) // 2

    def part(ref, index, size):
        return ref.at[pl.ds(pl.multiple_of(index * size, 16), size), :]

    moves = [
        (tok, tok_v),
        (wk_t, wk_v),
        (wv_t, wv_v),
        (part(w_in, at[4], half), piece.at[pl.ds(0, half), :]),
        (part(w_outer, at[4], half), piece.at[pl.ds(half, half), :]),
        (part(w_out, at[2], tail), out_piece),
    ]
    copies = [pltpu.make_async_copy(a, b, sems.at[i]) for i, (a, b) in enumerate(moves)]
    for copy in copies:
        copy.start()
    for copy in copies[:3]:
        copy.wait()
    bias = []
    for h in range(wk_v.shape[0] // HEAD_DIM):
        bias += [jnp.zeros((1, HEAD_DIM), f32), bv[:, h * HEAD_DIM : (h + 1) * HEAD_DIM]]
    kv[...] = (nt(tok_v[...], both_rows(wk_v, wv_v)) + jnp.concatenate(bias, axis=1)).astype(bf16)
    for copy in copies[3:]:
        copy.wait()
    piece[2 * half :, :] = out_piece[...]


def q_kernel(tok, wq_t, bq, q):
    heads = wq_t.shape[0] // HEAD_DIM
    full = (nt(tok[...], wq_t[...]) + bq[...]).astype(bf16) * jnp.asarray(SCALE, bf16)
    zero = jnp.zeros((full.shape[0], HEAD_DIM), bf16)
    cols = []
    for h in range(heads):
        cols += [full[:, h * HEAD_DIM : (h + 1) * HEAD_DIM], zero]
    q[...] = jnp.concatenate(cols, axis=1)


def weights_kernel(n, at, w_out, *refs):
    pieces, (w_out_all, w_in_far, w_outer_far) = refs[:8], refs[8:]
    z = at[0]
    local = w_out.shape[0]
    part = local // 4
    rows = w_in_far.shape[0] // 8

    def put(ref, base, value):
        size = value.shape[0]
        ref[pl.ds(pl.multiple_of(base, 16), size), :] = value

    put(w_out_all, z * local, w_out[...])
    for j, piece in enumerate(pieces):
        put(w_in_far, (at[4] ^ j) * rows, piece[:rows, :])
        put(w_outer_far, (at[4] ^ j) * rows, piece[rows : 2 * rows, :])
        for s in range(1, n if j < 4 else 0):
            base = 2 * rows + (s - 1) * part
            put(w_out_all, (z ^ s) * local + (at[2] ^ j) * part, piece[base : base + part, :])


def attend_kernel(n_blk, ids, at, bucket, lens, q, *refs):
    kvs = refs[:n_blk]
    hp_first, hp_second, probs_first, probs_second, hp_late, held, sems = refs[n_blk:]
    copies = []
    heads = q.shape[1] // LANES
    b = at[2]
    q_at = lax.broadcasted_iota(i32, (BLOCK, 1), 0)
    k_at = lax.broadcasted_iota(i32, (1, BLOCK), 1)
    for order, row in enumerate(ids):
        hp, probs = ((hp_first, probs_first), (hp_second, probs_second))[order // 2]
        i = order % 2
        r = row_at(at, row)
        bk = bucket[r]
        size = BLOCK << bk
        slot = b >> bk
        limit = lens[r, slot]
        q_in = jnp.where(q_at + (b * BLOCK - slot * size) < limit, 1, 0)
        k_in = []
        for j in range(n_blk):
            kb = b ^ j
            k_slot = kb >> bk
            inside = jnp.where(k_at + (kb * BLOCK - k_slot * size) < limit, 1, 0)
            k_in.append(jnp.where(k_slot == slot, inside, 2))
        allowed = q_in == jnp.concatenate(k_in, axis=1)
        here = pl.ds(pl.multiple_of(r * BLOCK, BLOCK), BLOCK)
        outs = []
        for h in range(heads):
            lanes = slice(h * LANES, (h + 1) * LANES)
            kvh = jnp.concatenate([kv[here, lanes] for kv in kvs], axis=0)
            scores = jnp.where(allowed, nt(q[here, lanes], kvh), -1e30)
            weights = jnp.exp(scores - jnp.max(scores, axis=-1, keepdims=True))
            total = jnp.sum(weights, axis=-1, keepdims=True)
            p = (weights / total).astype(bf16)
            held[(order * heads + h) * BLOCK : (order * heads + h + 1) * BLOCK, :] = p
            outs.append(nn(p, kvh)[:, HEAD_DIM:].astype(bf16))
        base = i * PACKED
        hp[base : base + BLOCK, :] = jnp.concatenate(outs[:2], axis=1)
        hp[base + BLOCK : base + PACKED, :] = jnp.concatenate(
            [outs[2][:HEAD_DIM], outs[2][HEAD_DIM:]], axis=1
        )
        size = heads * BLOCK
        copies.append(
            pltpu.make_async_copy(
                held.at[pl.ds(order * size, size), :], probs.at[pl.ds(i * size, size), :], sems.at[order]
            )
        )
        copies[-1].start()
    for i, hp in enumerate((hp_first, hp_second)):
        rows = hp.shape[0]
        copies.append(pltpu.make_async_copy(hp, hp_late.at[pl.ds(i * rows, rows), :], sems.at[4 + i]))
        copies[-1].start()
    for copy in copies:
        copy.wait()


def unpack(h):
    odd = jnp.concatenate([h[BLOCK:, :HEAD_DIM], h[BLOCK:, HEAD_DIM:]], axis=0)
    return jnp.concatenate([h[:BLOCK, :], odd], axis=1)


def pack(v):
    odd = jnp.concatenate([v[:HEAD_DIM, LANES:], v[HEAD_DIM:, LANES:]], axis=1)
    return jnp.concatenate([v[:, :LANES], odd], axis=0)


def gelu_and_slope(inner):
    cdf = 0.5 * (1.0 + lax.erf(inner * (0.5**0.5)))
    slope = cdf + inner * (0.3989422804014327 * jnp.exp(-0.5 * inner * inner))
    return (inner * cdf).astype(bf16), slope.astype(bf16)


def ffn_kernel(
    n, i, at, tok, w_out, b_out, g1, b1, w_in, w_in_far, b_in, b_in_far, w_outer, w_outer_far, *refs
):
    hps = refs[:n] if len(refs) > n + 7 + 1 else [refs[0].at[pl.ds(s * PACKED, PACKED), :] for s in range(n)]
    refs = refs if len(refs) > n + 7 + 1 else refs[:1] * n + refs[1:]
    part, n1_out, s1_out, low_out, act_out, act_far_out, slopes, *rest, held = refs[n:]
    z = at[0]
    local = w_out.shape[0] // n
    for s in range(n):
        j = z ^ s
        held[j] = nn(unpack(hps[s][:PACKED, :]), chunk_of(w_out, j, local))
        if rest:
            rest[0][s * PACKED : (s + 1) * PACKED, :] = hps[s][PACKED:, :]
    attn = held[0]
    for j in range(1, n):
        attn = attn + held[j]
    resid = chunk_of(tok, row_at(at, i), BLOCK).astype(f32) + (attn + b_out[...])
    center = resid - mean(resid)
    s1 = lax.rsqrt(mean(center * center) + EPS)
    n1 = center * s1
    low = (n1 * g1[...] + b1[...]).astype(bf16)
    act, slope = gelu_and_slope(nn(low, w_in[...]) + b_in[...])
    act_far, slope_far = gelu_and_slope(nn(low, w_in_far[...]) + b_in_far[...])
    part[...] = (nn(act, w_outer[...]) + nn(act_far, w_outer_far[...])).astype(bf16)
    n1_out[...] = n1
    s1_out[...] = jnp.broadcast_to(s1, s1_out.shape)
    low_out[...] = low
    act_out[...] = act
    act_far_out[...] = act_far
    slopes[:BLOCK, :] = slope
    slopes[BLOCK:, :] = slope_far


def ffn_back_kernel(
    i, at, cot, n1, slopes, mine, theirs, g1, b1, b_outer, g2, b2, w_in, w_in_far, w_outer,
    w_outer_far, out, dffn_out, dinner_out, dinner_far_out, part, dres2_out, sums
):
    hidden = n1[...] * g1[...] + b1[...]
    ffn = mine[...].astype(f32) + theirs[...].astype(f32)
    resid = hidden + (ffn + b_outer[...])
    center = resid - mean(resid)
    s2 = lax.rsqrt(mean(center * center) + EPS)
    n2 = center * s2
    ct = chunk_of(cot, row_at(at, i), BLOCK).astype(f32)
    dn = ct * g2[...]
    dres2 = s2 * (dn - mean(dn) - n2 * mean(dn * n2))
    dffn = dres2.astype(bf16)
    dinner = (nt(dffn, w_outer[...]) * slopes[:BLOCK, :].astype(f32)).astype(bf16)
    dinner_far = (nt(dffn, w_outer_far[...]) * slopes[BLOCK:, :].astype(f32)).astype(bf16)
    part[...] = (nt(dinner, w_in[...]) + nt(dinner_far, w_in_far[...])).astype(bf16)
    dres2_out[...] = dres2
    dinner_out[...] = dinner
    out[...] = (n2 * g2[...] + b2[...]).astype(bf16)
    dffn_out[...] = dffn
    dinner_far_out[...] = dinner_far
    sums[...] = rows8(
        col_sum(ct * n2), col_sum(ct), col_sum(dffn.astype(f32)),
        col_sum(dinner.astype(f32)), col_sum(dinner_far.astype(f32)),
    )


def norm_back_kernel(n, at, mine, theirs, dres2, n1, s1, g1, w_out, sums2, dres1_out, share, dh, dh_far):
    dhidden = (mine[...].astype(f32) + theirs[...].astype(f32)) + dres2[...]
    norm = n1[...]
    dn = dhidden * g1[...]
    dres1 = s1[:, :1] * (dn - mean(dn) - norm * mean(dn * norm))
    dattn = dres1.astype(bf16)
    dres1_out[...] = dres1
    share[:BLOCK, :] = dattn
    sums = jnp.concatenate(
        [col_sum(dhidden * norm), col_sum(dhidden), col_sum(dattn.astype(f32)), sums2[:5, :]], axis=0
    )
    share[BLOCK:, :] = jnp.concatenate([sums, jnp.zeros_like(sums)], axis=0).astype(bf16)
    local = w_out.shape[0] // n
    dh[...] = pack(nt(dattn, chunk_of(w_out, at[0], local)).astype(bf16))
    dh_far[...] = pack(nt(dattn, chunk_of(w_out, at[0] ^ 1, local)).astype(bf16))


def attend_back_kernel(n_blk, ids, at, first, second, q, probs, *refs):
    kvs = refs[:n_blk]
    dq_out, send, keep = refs[n_blk:]
    heads = q.shape[1] // LANES
    zero = jnp.zeros((BLOCK, HEAD_DIM), bf16)
    for i, packed in enumerate((first, second)):
        c = row_at(at, ids[i])
        here = pl.ds(pl.multiple_of(c * BLOCK, BLOCK), BLOCK)
        flat = unpack(packed[...])
        dqs = []
        for h in range(heads):
            lanes = slice(h * LANES, (h + 1) * LANES)
            dhead = jnp.concatenate([zero, flat[:, h * HEAD_DIM : (h + 1) * HEAD_DIM]], axis=1)
            kvh = jnp.concatenate([kv[here, lanes] for kv in kvs], axis=0)
            at_p = (i * heads + h) * BLOCK
            p = probs[at_p : at_p + BLOCK, :]
            pf = p.astype(f32)
            dp = nt(dhead, kvh)
            delta = jnp.sum(pf * dp, axis=-1, keepdims=True)
            ds = (pf * (dp - delta)).astype(bf16)
            dqs.append((nn(ds, kvh) * SCALE)[:, :HEAD_DIM].astype(bf16))
            left = jnp.concatenate([q[here, lanes], dhead], axis=0)
            dkv = tn(left, jnp.concatenate([ds, p], axis=0)).astype(bf16)
            for j in range(n_blk):
                target = keep if j % 2 == 0 else send
                target[j // 2, i, lanes, :] = dkv[:, j * BLOCK : (j + 1) * BLOCK]
        dq_out[i * BLOCK : (i + 1) * BLOCK, :] = jnp.concatenate(dqs, axis=1)


def input_kernel(dq, keep, recv, far, wq_t, wk_t, wv_t, part, dkv_t, sums):
    total = keep[0].astype(f32) + recv[0].astype(f32) + far[...].astype(f32)
    lows = [total[i].astype(bf16) for i in range(2)]
    low = jnp.concatenate([v.T for v in lows], axis=0)
    grad = nn(dq[...], wq_t[...]) + nn(low, both_rows(wk_t, wv_t))
    part[...] = grad.astype(bf16)
    dkv_t[...] = jnp.concatenate(lows, axis=1)
    width = sums.shape[1]
    one = col_sum(dq[...].astype(f32))
    two = col_sum(low.astype(f32))
    sums[...] = rows8(
        jnp.concatenate([one, jnp.zeros((1, width - one.shape[1]), f32)], axis=1),
        jnp.concatenate([two, jnp.zeros((1, width - two.shape[1]), f32)], axis=1),
    )


def pick(first, one, other):
    return jnp.where(first, one, other)


def join(values, axis=0):
    return jnp.concatenate(list(values), axis=axis)


def ordered_sum(at, parts, held):
    for i, part in enumerate(parts):
        held[row_at(at, i)] = part.astype(f32)
    total = held[0]
    for r in range(1, len(parts)):
        total = total + held[r]
    return total


def ffn_grad_kernel(m, at, *refs):
    low, act, act_far, dffn, dinner, dinner_far = (refs[2 * i : 2 * i + 2] for i in range(6))
    keep, send = refs[12:]
    first = at[1] == 0
    both = lambda pair: join(x[...] for x in pair)
    lows, dffns = both(low), both(dffn)
    rows = lows.shape[1] // m
    for q, (acts, dinners) in enumerate(((both(act), both(dinner)), (both(act_far), both(dinner_far)))):
        for target, one in ((keep, first), (send, jnp.logical_not(first))):
            main = tn(pick(one, lows, acts), pick(one, dinners, dffns)).astype(bf16)
            for i in range(m):
                target[i, q] = main[i * rows : (i + 1) * rows]


def attend_grad_kernel(m, at, tok, hp_late, *refs):
    shares, (dq, dkv_t, sums) = refs[:4], (refs[4 + 2 * i : 6 + 2 * i] for i in range(3))
    keep, send, held = refs[10:]
    first = at[1] == 0
    toks = join(chunk_of(tok, row_at(at, i), BLOCK) for i in range(4))
    heads = join(unpack(hp_late[i * PACKED : (i + 1) * PACKED, :]) for i in (2, 3, 0, 1))
    g_out = tn(heads, join(x[:BLOCK, :] for x in shares))
    g_q = tn(join(x[...] for x in dq), toks)
    g_kv = nn(join((x[...] for x in dkv_t), axis=1), toks)
    one = join([g_out, g_q]).astype(bf16)
    two = g_kv.astype(bf16)
    half = two.shape[0]
    norm = ordered_sum(at, [x[BLOCK : BLOCK + 8, :] for x in shares], held)
    total = sums[0][...] + sums[1][...]
    row = lambda x, k: x[BLOCK + k : BLOCK + k + 1, :].astype(f32)
    inner = row(shares[0], 6) + row(shares[1], 6) + row(shares[2], 7) + row(shares[3], 7)
    norm = join([norm[:6], inner, jnp.zeros_like(inner)])
    rest = keep.shape[0] - half
    tail = join([norm, total, jnp.zeros((rest - 16, total.shape[1]), f32)]).astype(bf16)
    keep[:half, :] = pick(first, one, two)
    keep[half:, :] = tail
    send[:half, :] = pick(first, two, one)
    send[half:, :] = tail


def gather_kernel(m, at, *refs):
    out = refs[m]
    for s in range(m):
        out[at[3] ^ s] = refs[s][...]


def share_kernel(total1, near1, *refs):
    parts, share = refs[:-1], refs[-1]
    rows = near1.shape[0]
    share[:rows, :] = (total1[0].astype(f32) + near1[...].astype(f32)).astype(bf16)
    total = parts[0][...].astype(f32)
    for part in parts[1:]:
        total = total + part[...].astype(f32)
    share[rows:, :] = total.astype(bf16)


def final_kernel(m, at, mine, other, g_in, g_outer, g_out, g_q, g_k, g_v, *vectors):
    first = at[1] == 0
    rows = g_in.shape[0] // m
    for i in range(m):
        a, b = mine[i, :rows, :], other[i, :rows, :]
        g_in[i * rows : (i + 1) * rows, :] = pick(first, a, b).astype(f32)
        g_outer[i * rows : (i + 1) * rows, :] = pick(first, b, a).astype(f32)
    width = g_q.shape[0]
    a = join(mine[i, rows:, :] for i in range(m))
    b = join(other[i, rows:, :] for i in range(m))
    one = pick(first, a, b).astype(f32)
    two = pick(first, b, a).astype(f32)
    g_out[...] = one[:width]
    g_q[...] = one[width : 2 * width]
    tail = one[2 * width : 2 * width + 16]
    values = []
    for h in range(width // HEAD_DIM):
        part = slice(h * HEAD_DIM, (h + 1) * HEAD_DIM)
        g_k[part, :] = two[h * LANES : h * LANES + HEAD_DIM]
        g_v[part, :] = two[h * LANES + HEAD_DIM : (h + 1) * LANES]
        values.append(tail[9:10, h * LANES + HEAD_DIM : (h + 1) * LANES])
    b_q, b_v = vectors[7:]
    for i, ref in enumerate(vectors[:7]):
        ref[...] = tail[i]
    b_q[...] = tail[8, :width]
    b_v[...] = jnp.concatenate(values, axis=1)[0]


def rows_kernel(at, *refs):
    out = refs[-1]
    rows = [v[i * BLOCK : (i + 1) * BLOCK, :] for v in refs[:-1] for i in range(v.shape[0] // BLOCK)]
    for i, value in enumerate(rows):
        out[row_at(at, i)] = value


def solution(mesh):
    n_dp = mesh.shape["dp"]
    n_blk = mesh.shape["blk"]
    n = mesh.shape["tensor"]
    half_blk = n_blk // 2
    m = n_dp * half_blk

    def swap(v, bit):
        return lax.ppermute(v, "tensor", [(i, i ^ bit) for i in range(n)])

    def flip(v, bit):
        return lax.ppermute(v, "blk", [(i, i ^ bit) for i in range(n_blk)])

    def flip_member(v, s):
        perm = []
        for dp in range(n_dp):
            for blk in range(n_blk):
                i = (dp * half_blk + blk // 2) ^ s
                to = (i // half_blk) * n_blk + (i % half_blk) * 2 + blk % 2
                perm.append((dp * n_blk + blk, to))
        return lax.ppermute(v, ("dp", "blk"), perm)

    def share_pieces(keep, recv, member):
        def piece(s):
            mine = lax.dynamic_index_in_dim(keep, member ^ s, 0, keepdims=False)
            theirs = lax.dynamic_index_in_dim(recv, member ^ s, 0, keepdims=False)
            return (mine.astype(f32) + theirs.astype(f32)).astype(bf16)

        return [piece(s) for s in range(m)]

    def add(own, got):
        total = own.astype(f32)
        for part in got:
            total = total + part.astype(f32)
        return total.astype(bf16)

    def gather_grads(every, at, name):
        rows, width = every[0].shape
        return call(
            functools.partial(gather_kernel, m),
            near((m, rows, width), bf16),
            name,
            (at, *every),
            scalars=1,
        )

    def body(
        tokens, bucket_ids, seq_lengths, w_query, b_query, w_key, w_value, b_value, w_out, b_out,
        norm1_gain, norm1_bias, w_inner, b_inner, w_outer, b_outer, norm2_gain, norm2_bias,
        cotangent,
    ):
        row_count, block, width = tokens.shape
        count = row_count * block
        local = w_query.shape[1]
        heads = local // HEAD_DIM
        lanes = heads * LANES
        units = w_inner.shape[1]
        blk = lax.axis_index("blk").astype(i32)
        z = lax.axis_index("tensor").astype(i32)
        core = blk % 2
        member = (lax.axis_index("dp") * half_blk + blk // 2).astype(i32)
        cut_at = (lax.axis_index("dp") % 2) * n_blk + blk
        at = jnp.stack([z, core, blk, member, cut_at]).astype(i32)
        tok = tokens.reshape(count, width)
        cot = cotangent.reshape(count, width)
        row = lambda v: v.reshape(1, -1)
        wq_t, wk_t, wv_t = w_query.T, w_key.T, w_value.T
        fence = lax.optimization_barrier

        part = local // 4
        piece_rows = (width + units) // 8
        kv, piece, out_piece = pl.pallas_call(
            front_kernel,
            out_shape=(
                near((count, lanes), bf16), near((piece_rows + part, width), bf16),
                near((part, width), bf16),
            ),
            in_specs=[SMEM] + [HBM] * 6 + [VMEM],
            out_specs=(VMEM,) * 3,
            scratch_shapes=[
                pltpu.VMEM((count, width), bf16), pltpu.VMEM((local, width), bf16),
                pltpu.VMEM((local, width), bf16), pltpu.SemaphoreType.DMA((6,)),
            ],
            compiler_params=pltpu.CompilerParams(vmem_limit_bytes=16 * MIB),
            name="front",
        )(at, *[pltpu.with_memory_space_constraint(v, pltpu.HBM) for v in (tok, wk_t, wv_t, w_inner, w_outer, w_out)], row(b_value))
        kv, piece, out_piece, b_far = fence((kv, piece, out_piece, b_inner))
        kv_far = flip(kv, 2)
        kv_core = flip(kv, 1)
        pieces = [swap(piece, 1)] + [swap(out_piece, s) for s in range(2, n)]
        b_inner_far = swap(b_far, 1)
        kv_far, b_inner_far, *pieces = fence((kv_far, b_inner_far, *pieces))
        kv_both = flip(kv_far, 1)
        own_piece = jnp.concatenate(pieces, axis=0)
        ffn_piece = pieces[0][:piece_rows]

        def across(v, dp_bit, blk_bit):
            there = lambda i: ((i // n_blk) ^ dp_bit) * n_blk + ((i % n_blk) ^ blk_bit)
            return lax.ppermute(v, ("dp", "blk"), [(i, there(i)) for i in range(n_dp * n_blk)])

        arrived = {0: own_piece, 2: across(own_piece, 0, 2)}
        arrived |= {4: across(ffn_piece, 1, 0), 6: across(ffn_piece, 1, 2)}

        q = call(q_kernel, near((count, lanes), bf16), "query_rows", (tok, wq_t, row(b_query)), us=0.5)
        kvs = [kv, kv_core, kv_far, kv_both]

        prob_rows = 2 * heads * BLOCK
        hp_other, hp_mine, probs_other, probs_mine, hp_late = pl.pallas_call(
            functools.partial(attend_kernel, n_blk, (2, 3, 0, 1)),
            out_shape=(near((2 * PACKED, LANES), bf16),) * 2
            + (pltpu.HBM((prob_rows, n_blk * BLOCK), bf16),) * 2
            + (pltpu.HBM((4 * PACKED, LANES), bf16),),
            in_specs=[SMEM] * 3 + [VMEM] * (1 + n_blk),
            out_specs=(VMEM,) * 2 + (HBM,) * 3,
            scratch_shapes=[
                pltpu.VMEM((2 * prob_rows, n_blk * BLOCK), bf16), pltpu.SemaphoreType.DMA((6,)),
            ],
            compiler_params=pltpu.CompilerParams(vmem_limit_bytes=16 * MIB),
            cost_estimate=pl.CostEstimate(
                flops=int(ATTEND_US * FLOPS_US), bytes_accessed=1, transcendentals=0
            ),
            name="attend",
        )(at, bucket_ids, seq_lengths, q, *kvs)
        hps = {0: hp_mine, 1: swap(hp_other, 1), 2: swap(hp_mine, 2), 3: swap(hp_other, 3)}
        held = [arrived[2], arrived[4], arrived[6]]
        hps[1], hps[2], hps[3], *held = fence((hps[1], hps[2], hps[3], *held))
        arrived[2], arrived[4], arrived[6] = held
        arrived |= {j + 1: flip(v, 1) for j, v in arrived.items()}
        w_out_all, w_inner_far, w_outer_far = call(
            functools.partial(weights_kernel, n),
            (near((n * local, width), bf16), near(w_inner.shape, bf16), near(w_outer.shape, bf16)),
            "far_weights",
            (at, w_out, *[arrived[j] for j in range(8)]),
            us=2.2,
            scalars=1,
        )

        chunk = lambda rows, dt: near((rows, width), dt)
        gains1 = (row(norm1_gain), row(norm1_bias))

        def ffn(i, heads_in):
            return call(
                functools.partial(ffn_kernel, n, i),
                (
                    chunk(BLOCK, bf16), chunk(BLOCK, f32), near((BLOCK, LANES), f32),
                    chunk(BLOCK, bf16), near((BLOCK, units), bf16), near((BLOCK, units), bf16),
                    near((2 * BLOCK, units), bf16),
                )
                + ((near((n * PACKED, LANES), bf16),) if i == 0 else ()),
                "ffn",
                (
                    at, tok, w_out_all, row(b_out), *gains1, w_inner, w_inner_far, row(b_inner),
                    row(b_inner_far), w_outer, w_outer_far, *heads_in,
                ),
                us=2.4,
                scalars=1,
                scratch=[pltpu.VMEM((n, BLOCK, width), f32)],
            )

        *row0, second_heads = ffn(0, [hps[s] for s in range(n)])
        parts, n1s, s1s, lows, acts, acts_far, slopes = map(list, zip(row0, ffn(1, [second_heads])))
        theirs = [swap(v, 2) for v in parts]

        def ffn_back(i):
            return call(
                functools.partial(ffn_back_kernel, i),
                (
                    chunk(BLOCK, bf16), chunk(BLOCK, bf16), near((BLOCK, units), bf16),
                    near((BLOCK, units), bf16), chunk(BLOCK, bf16), chunk(BLOCK, f32), chunk(8, f32),
                ),
                "ffn_back",
                (
                    at, cot, n1s[i], slopes[i], parts[i], theirs[i], *gains1, row(b_outer),
                    row(norm2_gain), row(norm2_bias), w_inner, w_inner_far, w_outer, w_outer_far,
                ),
                us=2.7,
                scalars=1,
            )

        outs, dffns, dinners, dinners_far, parts2, dres2, sums2 = map(list, zip(*[ffn_back(i) for i in range(2)]))
        theirs2 = [swap(v, 2) for v in parts2]
        keep1, send1 = call(
            functools.partial(ffn_grad_kernel, m),
            (near((m, 2, width // m, width), bf16),) * 2,
            "ffn_grads",
            (at, *lows, *acts, *acts_far, *dffns, *dinners, *dinners_far),
            us=FILL_US,
            vmem=24,
            scalars=1,
        )
        recv1 = flip(send1, 1)
        pieces1 = share_pieces(keep1, recv1, member)

        def norm_back(i):
            return call(
                functools.partial(norm_back_kernel, n),
                (
                    chunk(BLOCK, f32), chunk(BLOCK + 16, bf16), near((PACKED, LANES), bf16),
                    near((PACKED, LANES), bf16),
                ),
                "norm_back",
                (at, parts2[i], theirs2[i], dres2[i], n1s[i], s1s[i], gains1[0], w_out_all, sums2[i]),
                us=1.2,
                scalars=1,
            )

        dres1, shares, dheads, dheads_far = map(list, zip(*[norm_back(i) for i in range(2)]))
        dheads += [swap(v, 1) for v in dheads_far]
        shares += [swap(v, 1) for v in shares]
        outs += [swap(v, 1) for v in outs]

        def attend_back(ids, probs, *packed):
            return call(
                functools.partial(attend_back_kernel, n_blk, ids),
                (
                    near((2 * BLOCK, local), bf16), near((half_blk, 2, lanes, BLOCK), bf16),
                    near((half_blk, 2, lanes, BLOCK), bf16),
                ),
                "attend_back",
                (at, *packed, q, probs, *kvs),
                scalars=1,
                us=BACK_US,
            )

        own = attend_back((0, 1), probs_mine, dheads[0], dheads[1])
        after, dheads[2], dheads[3], pieces1 = fence((own[1], dheads[2], dheads[3], pieces1))
        own = (own[0], after, own[2])
        other = attend_back((2, 3), probs_other, dheads[2], dheads[3])

        def exchange(third):
            _, send, keep = third
            recv = flip(send, 1)
            return recv, (keep[1].astype(f32) + recv[1].astype(f32)).astype(bf16)

        def input_part(third, recv, far, us):
            dq, _, keep = third
            return call(
                input_kernel,
                (chunk(2 * BLOCK, bf16), near((lanes, 2 * BLOCK), bf16), chunk(8, f32)),
                "input_part",
                (dq, keep, recv, far, wq_t, wk_t, wv_t),
                us=us,
            )

        recv_own, sum_own = exchange(own)
        recv_other, sum_other = exchange(other)
        far_own, far_other = flip(sum_own, 2), flip(sum_other, 2)
        far_own, far_other, pieces1 = fence((far_own, far_other, pieces1))
        part, *late = input_part(other, recv_other, far_other, 1.0)
        part, pieces1 = fence((part, pieces1))
        from_near, *ends = fence((swap(part, 1), *shares[2:]))
        shares[2:] = ends
        got1 = [flip_member(v, s) for s, v in enumerate(pieces1[1:], 1)]
        part_own, dkv_own, sums_own = input_part(own, recv_own, far_own, INPUT_US)
        pair = (part_own.astype(f32) + from_near.astype(f32)).astype(bf16)

        rows2 = 2 * local + 16
        rows2 += -rows2 % (16 * m)
        keep2, send2 = call(
            functools.partial(attend_grad_kernel, m),
            (chunk(rows2, bf16), chunk(rows2, bf16)),
            "attend_grads",
            (
                at, tok, hp_late, *shares, own[0], other[0], dkv_own, late[0], sums_own,
                late[1],
            ),
            us=GRADS_US,
            scalars=1,
            scratch=[pltpu.VMEM((n, 8, width), f32)],
        )
        by_member = lambda v: v.reshape(m, rows2 // m, width)
        pieces2 = share_pieces(by_member(keep2), by_member(flip(send2, 1)), member)
        got2 = [flip_member(v, s) for s, v in enumerate(pieces2[1:], 1)]
        got1, _, _ = fence((got1, keep2, pair))
        total1 = fence(add(pieces1[0], got1))
        near1 = swap(total1[1], 1)
        crossed, near1, got2, *ends = fence((swap(pair, 2), near1, got2, *outs[2:]))
        outs[2:] = ends
        d_tok = pair.astype(f32) + crossed.astype(f32) + jnp.concatenate(dres1, axis=0)
        d_tok = d_tok.astype(bf16)
        share = call(
            share_kernel,
            chunk(width // m + rows2 // m, bf16),
            "grad_share",
            (total1, near1, pieces2[0], *got2),
            us=0.5,
        )
        shares_in = [flip_member(share, k) for k in range(1, m)]
        shares_in, d_far = fence((shares_in, swap(d_tok, 1)))
        d_toks = [d_tok, d_far]
        assemble = lambda parts, name: call(
            rows_kernel,
            shape((row_count, block, width), bf16),
            name,
            (at, *parts),
            us=1.5,
            scalars=1,
        )
        output = assemble(outs, "output_rows")
        d_tokens = assemble(d_toks, "input_grad_rows")
        mine = gather_grads([share] + shares_in, at, "gather_grads")
        other, _, _ = fence((flip(mine, 1), output, d_tokens))
        vector = shape((width,), f32)
        short = shape((local,), f32)
        square = shape((width, units), f32)
        wide = shape((local, width), f32)
        (
            g_w_inner, g_w_outer, g_w_out, g_q, g_k, g_v, g_gain1, g_bias1, g_b_out, g_gain2, g_bias2,
            g_b_outer, g_b_inner, g_b_query, g_b_value,
        ) = call(
            functools.partial(final_kernel, m),
            (square,) * 2 + (wide,) * 4 + (vector,) * 7 + (short,) * 2,
            "grads_out",
            (at, mine, other),
            us=4.0,
            vmem=24,
            scalars=1,
        )
        return (
            output, d_tokens, g_q.T, g_b_query, g_k.T, g_v.T, g_b_value, g_w_out, g_b_out, g_gain1,
            g_bias1, g_w_inner, g_b_inner, g_w_outer, g_b_outer, g_gain2, g_bias2,
        )

    spread, cols, vec, rows_ = P("dp", "blk", None), P(None, "tensor"), P("tensor"), P("tensor", None)
    return jax.shard_map(
        body,
        mesh=mesh,
        in_specs=(
            spread, P("dp"), P("dp", None), cols, vec, cols, cols, vec, rows_, P(), P(), P(),
            cols, vec, rows_, P(), P(), P(), spread,
        ),
        out_specs=(
            spread, spread, cols, vec, cols, cols, vec, rows_, P(), P(), P(), cols, vec, rows_,
            P(), P(), P(),
        ),
        check_vma=False,
    )
```

```python
import functools

import jax
import jax.numpy as jnp
from jax import lax
from jax.experimental import pallas as pl
from jax.experimental.pallas import tpu as pltpu
from jax.sharding import PartitionSpec as P

HEAD_DIM = 64
BLOCK = 128
LANES = 128
SCALE = HEAD_DIM**-0.5
EPS = 1e-12
f32 = jnp.float32
bf16 = jnp.bfloat16
i32 = jnp.int32
MIB = 1 << 20
FLOPS_US = 1e9
ATTEND_US = 50.0
BACK_US = 50.0
FILL_US = 50.0
INPUT_US = 50.0
GRADS_US = 1.0
PACKED = BLOCK + HEAD_DIM


def nn(a, b):
    return lax.dot_general(a, b, (((1,), (0,)), ((), ())), preferred_element_type=f32)


def nt(a, b):
    return lax.dot_general(a, b, (((1,), (1,)), ((), ())), preferred_element_type=f32)


def tn(a, b):
    return lax.dot_general(a, b, (((0,), (0,)), ((), ())), preferred_element_type=f32)


def mean(v):
    return jnp.mean(v, axis=-1, keepdims=True)


def col_sum(v):
    return jnp.sum(v, axis=0, keepdims=True)


def row_at(at, i):
    half = at[0] % 2
    return 2 * half + i if i < 2 else 2 * (1 - half) + (i - 2)


def rows8(*rows):
    width = rows[0].shape[1]
    pad = jnp.zeros((8 - len(rows), width), f32)
    return jnp.concatenate(rows + (pad,), axis=0)


def shape(dims, dtype):
    return jax.ShapeDtypeStruct(dims, dtype)


def near(dims, dtype):
    return pltpu.VMEM(dims, dtype)


SMEM = pl.BlockSpec(memory_space=pltpu.SMEM)
VMEM = pl.BlockSpec(memory_space=pltpu.VMEM)
HBM = pl.BlockSpec(memory_space=pltpu.HBM)


def call(kernel, outs, name, args, scalars=0, us=1.0, vmem=16, scratch=()):
    return pl.pallas_call(
        kernel,
        out_shape=outs,
        in_specs=[SMEM] * scalars + [VMEM] * (len(args) - scalars),
        out_specs=jax.tree.map(lambda _: VMEM, outs),
        scratch_shapes=list(scratch),
        compiler_params=pltpu.CompilerParams(vmem_limit_bytes=vmem * MIB),
        cost_estimate=pl.CostEstimate(flops=int(us * FLOPS_US), bytes_accessed=1, transcendentals=0),
        name=name,
    )(*args)


def chunk_of(ref, c, rows):
    return ref[pl.ds(pl.multiple_of(c * rows, rows), rows), :]


def both_rows(wk_t, wv_t):
    rows = []
    for h in range(wk_t.shape[0] // HEAD_DIM):
        part = slice(h * HEAD_DIM, (h + 1) * HEAD_DIM)
        rows += [wk_t[part, :], wv_t[part, :]]
    return jnp.concatenate(rows, axis=0)


def front_kernel(at, tok, wk_t, wv_t, w_in, w_outer, w_out, bv, kv, piece, out_piece, tok_v, wk_v, wv_v, sems):
    tail = out_piece.shape[0]
    half = (piece.shape[0] - tail) // 2

    def part(ref, index, size):
        return ref.at[pl.ds(pl.multiple_of(index * size, 16), size), :]

    moves = [
        (tok, tok_v),
        (wk_t, wk_v),
        (wv_t, wv_v),
        (part(w_in, at[4], half), piece.at[pl.ds(0, half), :]),
        (part(w_outer, at[4], half), piece.at[pl.ds(half, half), :]),
        (part(w_out, at[2], tail), out_piece),
    ]
    copies = [pltpu.make_async_copy(a, b, sems.at[i]) for i, (a, b) in enumerate(moves)]
    for copy in copies:
        copy.start()
    for copy in copies[:3]:
        copy.wait()
    bias = []
    for h in range(wk_v.shape[0] // HEAD_DIM):
        bias += [jnp.zeros((1, HEAD_DIM), f32), bv[:, h * HEAD_DIM : (h + 1) * HEAD_DIM]]
    kv[...] = (nt(tok_v[...], both_rows(wk_v, wv_v)) + jnp.concatenate(bias, axis=1)).astype(bf16)
    for copy in copies[3:]:
        copy.wait()
    piece[2 * half :, :] = out_piece[...]


def q_kernel(tok, wq_t, bq, q):
    heads = wq_t.shape[0] // HEAD_DIM
    full = (nt(tok[...], wq_t[...]) + bq[...]).astype(bf16) * jnp.asarray(SCALE, bf16)
    zero = jnp.zeros((full.shape[0], HEAD_DIM), bf16)
    cols = []
    for h in range(heads):
        cols += [full[:, h * HEAD_DIM : (h + 1) * HEAD_DIM], zero]
    q[...] = jnp.concatenate(cols, axis=1)


def weights_kernel(n, at, w_out, *refs):
    pieces, (w_out_all, w_in_far, w_outer_far) = refs[:8], refs[8:]
    z = at[0]
    local = w_out.shape[0]
    part = local // 4
    rows = w_in_far.shape[0] // 8

    def put(ref, base, value):
        size = value.shape[0]
        ref[pl.ds(pl.multiple_of(base, 16), size), :] = value

    put(w_out_all, z * local, w_out[...])
    for j, piece in enumerate(pieces):
        put(w_in_far, (at[4] ^ j) * rows, piece[:rows, :])
        put(w_outer_far, (at[4] ^ j) * rows, piece[rows : 2 * rows, :])
        for s in range(1, n if j < 4 else 0):
            base = 2 * rows + (s - 1) * part
            put(w_out_all, (z ^ s) * local + (at[2] ^ j) * part, piece[base : base + part, :])


def attend_kernel(n_blk, ids, at, bucket, lens, q, *refs):
    kvs = refs[:n_blk]
    hp_first, hp_second, probs_first, probs_second, hp_late, held, sems = refs[n_blk:]
    copies = []
    heads = q.shape[1] // LANES
    b = at[2]
    q_at = lax.broadcasted_iota(i32, (BLOCK, 1), 0)
    k_at = lax.broadcasted_iota(i32, (1, BLOCK), 1)
    for order, row in enumerate(ids):
        hp, probs = ((hp_first, probs_first), (hp_second, probs_second))[order // 2]
        i = order % 2
        r = row_at(at, row)
        bk = bucket[r]
        size = BLOCK << bk
        slot = b >> bk
        limit = lens[r, slot]
        q_in = jnp.where(q_at + (b * BLOCK - slot * size) < limit, 1, 0)
        k_in = []
        for j in range(n_blk):
            kb = b ^ j
            k_slot = kb >> bk
            inside = jnp.where(k_at + (kb * BLOCK - k_slot * size) < limit, 1, 0)
            k_in.append(jnp.where(k_slot == slot, inside, 2))
        allowed = q_in == jnp.concatenate(k_in, axis=1)
        here = pl.ds(pl.multiple_of(r * BLOCK, BLOCK), BLOCK)
        outs = []
        for h in range(heads):
            lanes = slice(h * LANES, (h + 1) * LANES)
            kvh = jnp.concatenate([kv[here, lanes] for kv in kvs], axis=0)
            scores = jnp.where(allowed, nt(q[here, lanes], kvh), -1e30)
            weights = jnp.exp(scores - jnp.max(scores, axis=-1, keepdims=True))
            total = jnp.sum(weights, axis=-1, keepdims=True)
            p = (weights / total).astype(bf16)
            held[(order * heads + h) * BLOCK : (order * heads + h + 1) * BLOCK, :] = p
            outs.append(nn(p, kvh)[:, HEAD_DIM:].astype(bf16))
        base = i * PACKED
        hp[base : base + BLOCK, :] = jnp.concatenate(outs[:2], axis=1)
        hp[base + BLOCK : base + PACKED, :] = jnp.concatenate(
            [outs[2][:HEAD_DIM], outs[2][HEAD_DIM:]], axis=1
        )
        size = heads * BLOCK
        copies.append(
            pltpu.make_async_copy(
                held.at[pl.ds(order * size, size), :], probs.at[pl.ds(i * size, size), :], sems.at[order]
            )
        )
        copies[-1].start()
    for i, hp in enumerate((hp_first, hp_second)):
        rows = hp.shape[0]
        copies.append(pltpu.make_async_copy(hp, hp_late.at[pl.ds(i * rows, rows), :], sems.at[4 + i]))
        copies[-1].start()
    for copy in copies:
        copy.wait()


def unpack(h):
    odd = jnp.concatenate([h[BLOCK:, :HEAD_DIM], h[BLOCK:, HEAD_DIM:]], axis=0)
    return jnp.concatenate([h[:BLOCK, :], odd], axis=1)


def pack(v):
    odd = jnp.concatenate([v[:HEAD_DIM, LANES:], v[HEAD_DIM:, LANES:]], axis=1)
    return jnp.concatenate([v[:, :LANES], odd], axis=0)


def gelu_and_slope(inner):
    cdf = 0.5 * (1.0 + lax.erf(inner * (0.5**0.5)))
    slope = cdf + inner * (0.3989422804014327 * jnp.exp(-0.5 * inner * inner))
    return (inner * cdf).astype(bf16), slope.astype(bf16)


def ffn_kernel(
    n, i, at, tok, w_out, b_out, g1, b1, w_in, w_in_far, b_in, b_in_far, w_outer, w_outer_far, *refs
):
    hps = refs[:n] if len(refs) > n + 7 + 1 else [refs[0].at[pl.ds(s * PACKED, PACKED), :] for s in range(n)]
    refs = refs if len(refs) > n + 7 + 1 else refs[:1] * n + refs[1:]
    part, n1_out, s1_out, low_out, act_out, act_far_out, slopes, *rest, held = refs[n:]
    z = at[0]
    local = w_out.shape[0] // n
    for s in range(n):
        j = z ^ s
        held[j] = nn(unpack(hps[s][:PACKED, :]), chunk_of(w_out, j, local))
        if rest:
            rest[0][s * PACKED : (s + 1) * PACKED, :] = hps[s][PACKED:, :]
    attn = held[0]
    for j in range(1, n):
        attn = attn + held[j]
    resid = chunk_of(tok, row_at(at, i), BLOCK).astype(f32) + (attn + b_out[...])
    center = resid - mean(resid)
    s1 = lax.rsqrt(mean(center * center) + EPS)
    n1 = center * s1
    low = (n1 * g1[...] + b1[...]).astype(bf16)
    act, slope = gelu_and_slope(nn(low, w_in[...]) + b_in[...])
    act_far, slope_far = gelu_and_slope(nn(low, w_in_far[...]) + b_in_far[...])
    part[...] = (nn(act, w_outer[...]) + nn(act_far, w_outer_far[...])).astype(bf16)
    n1_out[...] = n1
    s1_out[...] = jnp.broadcast_to(s1, s1_out.shape)
    low_out[...] = low
    act_out[...] = act
    act_far_out[...] = act_far
    slopes[:BLOCK, :] = slope
    slopes[BLOCK:, :] = slope_far


def ffn_back_kernel(
    i, at, cot, n1, slopes, mine, theirs, g1, b1, b_outer, g2, b2, w_in, w_in_far, w_outer,
    w_outer_far, out, dffn_out, dinner_out, dinner_far_out, part, dres2_out, sums
):
    hidden = n1[...] * g1[...] + b1[...]
    ffn = mine[...].astype(f32) + theirs[...].astype(f32)
    resid = hidden + (ffn + b_outer[...])
    center = resid - mean(resid)
    s2 = lax.rsqrt(mean(center * center) + EPS)
    n2 = center * s2
    ct = chunk_of(cot, row_at(at, i), BLOCK).astype(f32)
    dn = ct * g2[...]
    dres2 = s2 * (dn - mean(dn) - n2 * mean(dn * n2))
    dffn = dres2.astype(bf16)
    dinner = (nt(dffn, w_outer[...]) * slopes[:BLOCK, :].astype(f32)).astype(bf16)
    dinner_far = (nt(dffn, w_outer_far[...]) * slopes[BLOCK:, :].astype(f32)).astype(bf16)
    part[...] = (nt(dinner, w_in[...]) + nt(dinner_far, w_in_far[...])).astype(bf16)
    dres2_out[...] = dres2
    dinner_out[...] = dinner
    out[...] = (n2 * g2[...] + b2[...]).astype(bf16)
    dffn_out[...] = dffn
    dinner_far_out[...] = dinner_far
    sums[...] = rows8(
        col_sum(ct * n2), col_sum(ct), col_sum(dffn.astype(f32)),
        col_sum(dinner.astype(f32)), col_sum(dinner_far.astype(f32)),
    )


def norm_back_kernel(n, at, mine, theirs, dres2, n1, s1, g1, w_out, sums2, dres1_out, share, dh, dh_far):
    dhidden = (mine[...].astype(f32) + theirs[...].astype(f32)) + dres2[...]
    norm = n1[...]
    dn = dhidden * g1[...]
    dres1 = s1[:, :1] * (dn - mean(dn) - norm * mean(dn * norm))
    dattn = dres1.astype(bf16)
    dres1_out[...] = dres1
    share[:BLOCK, :] = dattn
    sums = jnp.concatenate(
        [col_sum(dhidden * norm), col_sum(dhidden), col_sum(dattn.astype(f32)), sums2[:5, :]], axis=0
    )
    share[BLOCK:, :] = jnp.concatenate([sums, jnp.zeros_like(sums)], axis=0).astype(bf16)
    local = w_out.shape[0] // n
    dh[...] = pack(nt(dattn, chunk_of(w_out, at[0], local)).astype(bf16))
    dh_far[...] = pack(nt(dattn, chunk_of(w_out, at[0] ^ 1, local)).astype(bf16))


def attend_back_kernel(n_blk, ids, at, first, second, q, probs, *refs):
    kvs = refs[:n_blk]
    dq_out, send, keep = refs[n_blk:]
    heads = q.shape[1] // LANES
    zero = jnp.zeros((BLOCK, HEAD_DIM), bf16)
    for i, packed in enumerate((first, second)):
        c = row_at(at, ids[i])
        here = pl.ds(pl.multiple_of(c * BLOCK, BLOCK), BLOCK)
        flat = unpack(packed[...])
        dqs = []
        for h in range(heads):
            lanes = slice(h * LANES, (h + 1) * LANES)
            dhead = jnp.concatenate([zero, flat[:, h * HEAD_DIM : (h + 1) * HEAD_DIM]], axis=1)
            kvh = jnp.concatenate([kv[here, lanes] for kv in kvs], axis=0)
            at_p = (i * heads + h) * BLOCK
            p = probs[at_p : at_p + BLOCK, :]
            pf = p.astype(f32)
            dp = nt(dhead, kvh)
            delta = jnp.sum(pf * dp, axis=-1, keepdims=True)
            ds = (pf * (dp - delta)).astype(bf16)
            dqs.append((nn(ds, kvh) * SCALE)[:, :HEAD_DIM].astype(bf16))
            left = jnp.concatenate([q[here, lanes], dhead], axis=0)
            dkv = tn(left, jnp.concatenate([ds, p], axis=0)).astype(bf16)
            for j in range(n_blk):
                target = keep if j % 2 == 0 else send
                target[j // 2, i, lanes, :] = dkv[:, j * BLOCK : (j + 1) * BLOCK]
        dq_out[i * BLOCK : (i + 1) * BLOCK, :] = jnp.concatenate(dqs, axis=1)


def input_kernel(dq, keep, recv, far, wq_t, wk_t, wv_t, part, dkv_t, sums):
    total = keep[0].astype(f32) + recv[0].astype(f32) + far[...].astype(f32)
    lows = [total[i].astype(bf16) for i in range(2)]
    low = jnp.concatenate([v.T for v in lows], axis=0)
    grad = nn(dq[...], wq_t[...]) + nn(low, both_rows(wk_t, wv_t))
    part[...] = grad.astype(bf16)
    dkv_t[...] = jnp.concatenate(lows, axis=1)
    width = sums.shape[1]
    one = col_sum(dq[...].astype(f32))
    two = col_sum(low.astype(f32))
    sums[...] = rows8(
        jnp.concatenate([one, jnp.zeros((1, width - one.shape[1]), f32)], axis=1),
        jnp.concatenate([two, jnp.zeros((1, width - two.shape[1]), f32)], axis=1),
    )


def pick(first, one, other):
    return jnp.where(first, one, other)


def join(values, axis=0):
    return jnp.concatenate(list(values), axis=axis)


def ordered_sum(at, parts, held):
    for i, part in enumerate(parts):
        held[row_at(at, i)] = part.astype(f32)
    total = held[0]
    for r in range(1, len(parts)):
        total = total + held[r]
    return total


def ffn_grad_kernel(m, at, *refs):
    low, act, act_far, dffn, dinner, dinner_far = (refs[2 * i : 2 * i + 2] for i in range(6))
    keep, send = refs[12:]
    first = at[1] == 0
    both = lambda pair: join(x[...] for x in pair)
    lows, dffns = both(low), both(dffn)
    rows = lows.shape[1] // m
    for q, (acts, dinners) in enumerate(((both(act), both(dinner)), (both(act_far), both(dinner_far)))):
        for target, one in ((keep, first), (send, jnp.logical_not(first))):
            main = tn(pick(one, lows, acts), pick(one, dinners, dffns)).astype(bf16)
            for i in range(m):
                target[i, q] = main[i * rows : (i + 1) * rows]


def attend_grad_kernel(m, at, tok, hp_late, *refs):
    shares, (dq, dkv_t, sums) = refs[:4], (refs[4 + 2 * i : 6 + 2 * i] for i in range(3))
    keep, send, held = refs[10:]
    first = at[1] == 0
    toks = join(chunk_of(tok, row_at(at, i), BLOCK) for i in range(4))
    heads = join(unpack(hp_late[i * PACKED : (i + 1) * PACKED, :]) for i in (2, 3, 0, 1))
    g_out = tn(heads, join(x[:BLOCK, :] for x in shares))
    g_q = tn(join(x[...] for x in dq), toks)
    g_kv = nn(join((x[...] for x in dkv_t), axis=1), toks)
    one = join([g_out, g_q]).astype(bf16)
    two = g_kv.astype(bf16)
    half = two.shape[0]
    norm = ordered_sum(at, [x[BLOCK : BLOCK + 8, :] for x in shares], held)
    total = sums[0][...] + sums[1][...]
    row = lambda x, k: x[BLOCK + k : BLOCK + k + 1, :].astype(f32)
    inner = row(shares[0], 6) + row(shares[1], 6) + row(shares[2], 7) + row(shares[3], 7)
    norm = join([norm[:6], inner, jnp.zeros_like(inner)])
    rest = keep.shape[0] - half
    tail = join([norm, total, jnp.zeros((rest - 16, total.shape[1]), f32)]).astype(bf16)
    keep[:half, :] = pick(first, one, two)
    keep[half:, :] = tail
    send[:half, :] = pick(first, two, one)
    send[half:, :] = tail


def share_kernel(total1, near1, *refs):
    parts, share = refs[:-1], refs[-1]
    rows = near1.shape[0]
    share[:rows, :] = (total1[0].astype(f32) + near1[...].astype(f32)).astype(bf16)
    total = parts[0][...].astype(f32)
    for part in parts[1:]:
        total = total + part[...].astype(f32)
    share[rows:, :] = total.astype(bf16)


def final_kernel(m, at, *refs):
    mine, other = refs[:m], refs[m : 2 * m]
    g_in, g_outer, g_out, g_q, g_k, g_v, *vectors, packed = refs[2 * m :]
    first = at[1] == 0
    rows = g_in.shape[0] // m
    for s in range(m):
        i = at[3] ^ s
        a, b = mine[s], other[s]
        here = pl.ds(pl.multiple_of(i * rows, rows), rows)
        g_in[here, :] = pick(first, a[:rows, :], b[:rows, :]).astype(f32)
        g_outer[here, :] = pick(first, b[:rows, :], a[:rows, :]).astype(f32)
        packed[0, i] = pick(first, a[rows:, :], b[rows:, :])
        packed[1, i] = pick(first, b[rows:, :], a[rows:, :])
    width = g_q.shape[0]
    one = join(packed[0, i] for i in range(m)).astype(f32)
    two = join(packed[1, i] for i in range(m)).astype(f32)
    g_out[...] = one[:width]
    g_q[...] = one[width : 2 * width]
    tail = one[2 * width : 2 * width + 16]
    values = []
    for h in range(width // HEAD_DIM):
        part = slice(h * HEAD_DIM, (h + 1) * HEAD_DIM)
        g_k[part, :] = two[h * LANES : h * LANES + HEAD_DIM]
        g_v[part, :] = two[h * LANES + HEAD_DIM : (h + 1) * LANES]
        values.append(tail[9:10, h * LANES + HEAD_DIM : (h + 1) * LANES])
    b_q, b_v = vectors[7:]
    for i, ref in enumerate(vectors[:7]):
        ref[...] = tail[i]
    b_q[...] = tail[8, :width]
    b_v[...] = jnp.concatenate(values, axis=1)[0]


def rows_kernel(at, *refs):
    out = refs[-1]
    rows = [v[i * BLOCK : (i + 1) * BLOCK, :] for v in refs[:-1] for i in range(v.shape[0] // BLOCK)]
    for i, value in enumerate(rows):
        out[row_at(at, i)] = value


def solution(mesh):
    n_dp = mesh.shape["dp"]
    n_blk = mesh.shape["blk"]
    n = mesh.shape["tensor"]
    half_blk = n_blk // 2
    m = n_dp * half_blk

    def swap(v, bit):
        return lax.ppermute(v, "tensor", [(i, i ^ bit) for i in range(n)])

    def flip(v, bit):
        return lax.ppermute(v, "blk", [(i, i ^ bit) for i in range(n_blk)])

    def flip_member(v, s):
        perm = []
        for dp in range(n_dp):
            for blk in range(n_blk):
                i = (dp * half_blk + blk // 2) ^ s
                to = (i // half_blk) * n_blk + (i % half_blk) * 2 + blk % 2
                perm.append((dp * n_blk + blk, to))
        return lax.ppermute(v, ("dp", "blk"), perm)

    def share_pieces(keep, recv, member):
        def piece(s):
            mine = lax.dynamic_index_in_dim(keep, member ^ s, 0, keepdims=False)
            theirs = lax.dynamic_index_in_dim(recv, member ^ s, 0, keepdims=False)
            return (mine.astype(f32) + theirs.astype(f32)).astype(bf16)

        return [piece(s) for s in range(m)]

    def add(own, got):
        total = own.astype(f32)
        for part in got:
            total = total + part.astype(f32)
        return total.astype(bf16)

    def body(
        tokens, bucket_ids, seq_lengths, w_query, b_query, w_key, w_value, b_value, w_out, b_out,
        norm1_gain, norm1_bias, w_inner, b_inner, w_outer, b_outer, norm2_gain, norm2_bias,
        cotangent,
    ):
        row_count, block, width = tokens.shape
        count = row_count * block
        local = w_query.shape[1]
        heads = local // HEAD_DIM
        lanes = heads * LANES
        units = w_inner.shape[1]
        blk = lax.axis_index("blk").astype(i32)
        z = lax.axis_index("tensor").astype(i32)
        core = blk % 2
        member = (lax.axis_index("dp") * half_blk + blk // 2).astype(i32)
        cut_at = (lax.axis_index("dp") % 2) * n_blk + blk
        at = jnp.stack([z, core, blk, member, cut_at]).astype(i32)
        tok = tokens.reshape(count, width)
        cot = cotangent.reshape(count, width)
        row = lambda v: v.reshape(1, -1)
        wq_t, wk_t, wv_t = w_query.T, w_key.T, w_value.T
        fence = lax.optimization_barrier

        part = local // 4
        piece_rows = (width + units) // 8
        kv, piece, out_piece = pl.pallas_call(
            front_kernel,
            out_shape=(
                near((count, lanes), bf16), near((piece_rows + part, width), bf16),
                near((part, width), bf16),
            ),
            in_specs=[SMEM] + [HBM] * 6 + [VMEM],
            out_specs=(VMEM,) * 3,
            scratch_shapes=[
                pltpu.VMEM((count, width), bf16), pltpu.VMEM((local, width), bf16),
                pltpu.VMEM((local, width), bf16), pltpu.SemaphoreType.DMA((6,)),
            ],
            compiler_params=pltpu.CompilerParams(vmem_limit_bytes=16 * MIB),
            name="front",
        )(at, *[pltpu.with_memory_space_constraint(v, pltpu.HBM) for v in (tok, wk_t, wv_t, w_inner, w_outer, w_out)], row(b_value))
        kv, piece, out_piece, b_far = fence((kv, piece, out_piece, b_inner))
        kv_far = flip(kv, 2)
        kv_core = flip(kv, 1)
        pieces = [swap(piece, 1)] + [swap(out_piece, s) for s in range(2, n)]
        b_inner_far = swap(b_far, 1)
        kv_far, b_inner_far, *pieces = fence((kv_far, b_inner_far, *pieces))
        kv_both = flip(kv_far, 1)
        own_piece = jnp.concatenate(pieces, axis=0)
        ffn_piece = pieces[0][:piece_rows]

        def across(v, dp_bit, blk_bit):
            there = lambda i: ((i // n_blk) ^ dp_bit) * n_blk + ((i % n_blk) ^ blk_bit)
            return lax.ppermute(v, ("dp", "blk"), [(i, there(i)) for i in range(n_dp * n_blk)])

        arrived = {0: own_piece, 2: across(own_piece, 0, 2)}
        arrived |= {4: across(ffn_piece, 1, 0), 6: across(ffn_piece, 1, 2)}

        q = call(q_kernel, near((count, lanes), bf16), "query_rows", (tok, wq_t, row(b_query)), us=0.5)
        kvs = [kv, kv_core, kv_far, kv_both]

        prob_rows = 2 * heads * BLOCK
        hp_other, hp_mine, probs_other, probs_mine, hp_late = pl.pallas_call(
            functools.partial(attend_kernel, n_blk, (2, 3, 0, 1)),
            out_shape=(near((2 * PACKED, LANES), bf16),) * 2
            + (pltpu.HBM((prob_rows, n_blk * BLOCK), bf16),) * 2
            + (pltpu.HBM((4 * PACKED, LANES), bf16),),
            in_specs=[SMEM] * 3 + [VMEM] * (1 + n_blk),
            out_specs=(VMEM,) * 2 + (HBM,) * 3,
            scratch_shapes=[
                pltpu.VMEM((2 * prob_rows, n_blk * BLOCK), bf16), pltpu.SemaphoreType.DMA((6,)),
            ],
            compiler_params=pltpu.CompilerParams(vmem_limit_bytes=16 * MIB),
            cost_estimate=pl.CostEstimate(
                flops=int(ATTEND_US * FLOPS_US), bytes_accessed=1, transcendentals=0
            ),
            name="attend",
        )(at, bucket_ids, seq_lengths, q, *kvs)
        hps = {0: hp_mine, 1: swap(hp_other, 1), 2: swap(hp_mine, 2), 3: swap(hp_other, 3)}
        held = [arrived[2], arrived[4], arrived[6]]
        hps[1], hps[2], hps[3], *held = fence((hps[1], hps[2], hps[3], *held))
        arrived[2], arrived[4], arrived[6] = held
        arrived |= {j + 1: flip(v, 1) for j, v in arrived.items()}
        w_out_all, w_inner_far, w_outer_far = call(
            functools.partial(weights_kernel, n),
            (near((n * local, width), bf16), near(w_inner.shape, bf16), near(w_outer.shape, bf16)),
            "far_weights",
            (at, w_out, *[arrived[j] for j in range(8)]),
            us=2.2,
            scalars=1,
        )

        chunk = lambda rows, dt: near((rows, width), dt)
        gains1 = (row(norm1_gain), row(norm1_bias))

        def ffn(i, heads_in):
            return call(
                functools.partial(ffn_kernel, n, i),
                (
                    chunk(BLOCK, bf16), chunk(BLOCK, f32), near((BLOCK, LANES), f32),
                    chunk(BLOCK, bf16), near((BLOCK, units), bf16), near((BLOCK, units), bf16),
                    near((2 * BLOCK, units), bf16),
                )
                + ((near((n * PACKED, LANES), bf16),) if i == 0 else ()),
                "ffn",
                (
                    at, tok, w_out_all, row(b_out), *gains1, w_inner, w_inner_far, row(b_inner),
                    row(b_inner_far), w_outer, w_outer_far, *heads_in,
                ),
                us=2.4,
                scalars=1,
                scratch=[pltpu.VMEM((n, BLOCK, width), f32)],
            )

        *row0, second_heads = ffn(0, [hps[s] for s in range(n)])
        parts, n1s, s1s, lows, acts, acts_far, slopes = map(list, zip(row0, ffn(1, [second_heads])))
        theirs = [swap(v, 2) for v in parts]

        def ffn_back(i):
            return call(
                functools.partial(ffn_back_kernel, i),
                (
                    chunk(BLOCK, bf16), chunk(BLOCK, bf16), near((BLOCK, units), bf16),
                    near((BLOCK, units), bf16), chunk(BLOCK, bf16), chunk(BLOCK, f32), chunk(8, f32),
                ),
                "ffn_back",
                (
                    at, cot, n1s[i], slopes[i], parts[i], theirs[i], *gains1, row(b_outer),
                    row(norm2_gain), row(norm2_bias), w_inner, w_inner_far, w_outer, w_outer_far,
                ),
                us=2.7,
                scalars=1,
            )

        outs, dffns, dinners, dinners_far, parts2, dres2, sums2 = map(list, zip(*[ffn_back(i) for i in range(2)]))
        theirs2 = [swap(v, 2) for v in parts2]
        keep1, send1 = call(
            functools.partial(ffn_grad_kernel, m),
            (near((m, 2, width // m, width), bf16),) * 2,
            "ffn_grads",
            (at, *lows, *acts, *acts_far, *dffns, *dinners, *dinners_far),
            us=FILL_US,
            vmem=24,
            scalars=1,
        )
        recv1 = flip(send1, 1)
        pieces1 = share_pieces(keep1, recv1, member)

        def norm_back(i):
            return call(
                functools.partial(norm_back_kernel, n),
                (
                    chunk(BLOCK, f32), chunk(BLOCK + 16, bf16), near((PACKED, LANES), bf16),
                    near((PACKED, LANES), bf16),
                ),
                "norm_back",
                (at, parts2[i], theirs2[i], dres2[i], n1s[i], s1s[i], gains1[0], w_out_all, sums2[i]),
                us=1.2,
                scalars=1,
            )

        dres1, shares, dheads, dheads_far = map(list, zip(*[norm_back(i) for i in range(2)]))
        dheads += [swap(v, 1) for v in dheads_far]
        shares += [swap(v, 1) for v in shares]
        outs += [swap(v, 1) for v in outs]

        def attend_back(ids, probs, *packed):
            return call(
                functools.partial(attend_back_kernel, n_blk, ids),
                (
                    near((2 * BLOCK, local), bf16), near((half_blk, 2, lanes, BLOCK), bf16),
                    near((half_blk, 2, lanes, BLOCK), bf16),
                ),
                "attend_back",
                (at, *packed, q, probs, *kvs),
                scalars=1,
                us=BACK_US,
            )

        own = attend_back((0, 1), probs_mine, dheads[0], dheads[1])
        after, dheads[2], dheads[3], pieces1 = fence((own[1], dheads[2], dheads[3], pieces1))
        own = (own[0], after, own[2])
        other = attend_back((2, 3), probs_other, dheads[2], dheads[3])

        def exchange(third):
            _, send, keep = third
            recv = flip(send, 1)
            return recv, (keep[1].astype(f32) + recv[1].astype(f32)).astype(bf16)

        def input_part(third, recv, far, us):
            dq, _, keep = third
            return call(
                input_kernel,
                (chunk(2 * BLOCK, bf16), near((lanes, 2 * BLOCK), bf16), chunk(8, f32)),
                "input_part",
                (dq, keep, recv, far, wq_t, wk_t, wv_t),
                us=us,
            )

        recv_own, sum_own = exchange(own)
        recv_other, sum_other = exchange(other)
        far_own, far_other = flip(sum_own, 2), flip(sum_other, 2)
        far_own, far_other, pieces1 = fence((far_own, far_other, pieces1))
        part, *late = input_part(other, recv_other, far_other, 1.0)
        part, pieces1 = fence((part, pieces1))
        from_near, *ends = fence((swap(part, 1), *shares[2:]))
        shares[2:] = ends
        got1 = [flip_member(v, s) for s, v in enumerate(pieces1[1:], 1)]
        part_own, dkv_own, sums_own = input_part(own, recv_own, far_own, INPUT_US)
        pair = (part_own.astype(f32) + from_near.astype(f32)).astype(bf16)

        rows2 = 2 * local + 16
        rows2 += -rows2 % (16 * m)
        hp_late, _ = fence((hp_late, pair))
        keep2, send2 = call(
            functools.partial(attend_grad_kernel, m),
            (chunk(rows2, bf16), chunk(rows2, bf16)),
            "attend_grads",
            (
                at, tok, hp_late, *shares, own[0], other[0], dkv_own, late[0], sums_own,
                late[1],
            ),
            us=GRADS_US,
            scalars=1,
            scratch=[pltpu.VMEM((n, 8, width), f32)],
        )
        by_member = lambda v: v.reshape(m, rows2 // m, width)
        pieces2 = share_pieces(by_member(keep2), by_member(flip(send2, 1)), member)
        got2 = [flip_member(v, s) for s, v in enumerate(pieces2[1:], 1)]
        got1, _, _ = fence((got1, keep2, pair))
        total1 = fence(add(pieces1[0], got1))
        near1 = swap(total1[1], 1)
        crossed, near1, got2, *ends = fence((swap(pair, 2), near1, got2, *outs[2:]))
        outs[2:] = ends
        d_tok = pair.astype(f32) + crossed.astype(f32) + jnp.concatenate(dres1, axis=0)
        d_tok = d_tok.astype(bf16)
        share = call(
            share_kernel,
            chunk(width // m + rows2 // m, bf16),
            "grad_share",
            (total1, near1, pieces2[0], *got2),
            us=0.5,
        )
        shares_in = [flip_member(share, k) for k in range(1, m)]
        shares_in[0], d_far = fence((shares_in[0], swap(d_tok, 1)))
        d_toks = [d_tok, d_far]
        assemble = lambda parts, name: call(
            rows_kernel,
            shape((row_count, block, width), bf16),
            name,
            (at, *parts),
            us=1.5,
            scalars=1,
        )
        output = assemble(outs, "output_rows")
        d_tokens = assemble(d_toks, "input_grad_rows")
        mine = [share] + shares_in
        held, _, _ = fence((shares_in[0], output, d_tokens))
        others = [flip(v, 1) for v in [share, held] + shares_in[1:]]
        vector = shape((width,), f32)
        short = shape((local,), f32)
        square = shape((width, units), f32)
        wide = shape((local, width), f32)
        (
            g_w_inner, g_w_outer, g_w_out, g_q, g_k, g_v, g_gain1, g_bias1, g_b_out, g_gain2, g_bias2,
            g_b_outer, g_b_inner, g_b_query, g_b_value,
        ) = call(
            functools.partial(final_kernel, m),
            (square,) * 2 + (wide,) * 4 + (vector,) * 7 + (short,) * 2,
            "grads_out",
            (at, *mine, *others),
            us=4.0,
            vmem=24,
            scalars=1,
            scratch=[pltpu.VMEM((2, m, rows2 // m, width), bf16)],
        )
        return (
            output, d_tokens, g_q.T, g_b_query, g_k.T, g_v.T, g_b_value, g_w_out, g_b_out, g_gain1,
            g_bias1, g_w_inner, g_b_inner, g_w_outer, g_b_outer, g_gain2, g_bias2,
        )

    spread, cols, vec, rows_ = P("dp", "blk", None), P(None, "tensor"), P("tensor"), P("tensor", None)
    return jax.shard_map(
        body,
        mesh=mesh,
        in_specs=(
            spread, P("dp"), P("dp", None), cols, vec, cols, cols, vec, rows_, P(), P(), P(),
            cols, vec, rows_, P(), P(), P(), spread,
        ),
        out_specs=(
            spread, spread, cols, vec, cols, cols, vec, rows_, P(), P(), P(), cols, vec, rows_,
            P(), P(), P(),
        ),
        check_vma=False,
    )
```

```python
import functools

import jax
import jax.numpy as jnp
from jax import lax
from jax.experimental import pallas as pl
from jax.experimental.pallas import tpu as pltpu
from jax.sharding import PartitionSpec as P

HEAD_DIM = 64
BLOCK = 128
LANES = 128
SCALE = HEAD_DIM**-0.5
EPS = 1e-12
f32 = jnp.float32
bf16 = jnp.bfloat16
i32 = jnp.int32
MIB = 1 << 20
FLOPS_US = 1e9
ATTEND_US = 50.0
BACK_US = 50.0
FILL_US = 50.0
INPUT_US = 50.0
GRADS_US = 1.0
PACKED = BLOCK + HEAD_DIM


def nn(a, b):
    return lax.dot_general(a, b, (((1,), (0,)), ((), ())), preferred_element_type=f32)


def nt(a, b):
    return lax.dot_general(a, b, (((1,), (1,)), ((), ())), preferred_element_type=f32)


def tn(a, b):
    return lax.dot_general(a, b, (((0,), (0,)), ((), ())), preferred_element_type=f32)


def mean(v):
    return jnp.mean(v, axis=-1, keepdims=True)


def col_sum(v):
    return jnp.sum(v, axis=0, keepdims=True)


def row_at(at, i):
    half = at[0] % 2
    return 2 * half + i if i < 2 else 2 * (1 - half) + (i - 2)


def rows8(*rows):
    width = rows[0].shape[1]
    pad = jnp.zeros((8 - len(rows), width), f32)
    return jnp.concatenate(rows + (pad,), axis=0)


def shape(dims, dtype):
    return jax.ShapeDtypeStruct(dims, dtype)


def near(dims, dtype):
    return pltpu.VMEM(dims, dtype)


SMEM = pl.BlockSpec(memory_space=pltpu.SMEM)
VMEM = pl.BlockSpec(memory_space=pltpu.VMEM)
HBM = pl.BlockSpec(memory_space=pltpu.HBM)


def call(kernel, outs, name, args, scalars=0, us=1.0, vmem=16, scratch=()):
    return pl.pallas_call(
        kernel,
        out_shape=outs,
        in_specs=[SMEM] * scalars + [VMEM] * (len(args) - scalars),
        out_specs=jax.tree.map(lambda _: VMEM, outs),
        scratch_shapes=list(scratch),
        compiler_params=pltpu.CompilerParams(vmem_limit_bytes=vmem * MIB),
        cost_estimate=pl.CostEstimate(flops=int(us * FLOPS_US), bytes_accessed=1, transcendentals=0),
        name=name,
    )(*args)


def chunk_of(ref, c, rows):
    return ref[pl.ds(pl.multiple_of(c * rows, rows), rows), :]


def both_rows(wk_t, wv_t):
    rows = []
    for h in range(wk_t.shape[0] // HEAD_DIM):
        part = slice(h * HEAD_DIM, (h + 1) * HEAD_DIM)
        rows += [wk_t[part, :], wv_t[part, :]]
    return jnp.concatenate(rows, axis=0)


def front_kernel(at, tok, wk_t, wv_t, w_in, w_outer, w_out, bv, kv, piece, out_piece, tok_v, wk_v, wv_v, sems):
    tail = out_piece.shape[0]
    half = (piece.shape[0] - tail) // 2

    def part(ref, index, size):
        return ref.at[pl.ds(pl.multiple_of(index * size, 16), size), :]

    moves = [
        (tok, tok_v),
        (wk_t, wk_v),
        (wv_t, wv_v),
        (part(w_in, at[4], half), piece.at[pl.ds(0, half), :]),
        (part(w_outer, at[4], half), piece.at[pl.ds(half, half), :]),
        (part(w_out, at[2], tail), out_piece),
    ]
    copies = [pltpu.make_async_copy(a, b, sems.at[i]) for i, (a, b) in enumerate(moves)]
    for copy in copies:
        copy.start()
    for copy in copies[:3]:
        copy.wait()
    bias = []
    for h in range(wk_v.shape[0] // HEAD_DIM):
        bias += [jnp.zeros((1, HEAD_DIM), f32), bv[:, h * HEAD_DIM : (h + 1) * HEAD_DIM]]
    kv[...] = (nt(tok_v[...], both_rows(wk_v, wv_v)) + jnp.concatenate(bias, axis=1)).astype(bf16)
    for copy in copies[3:]:
        copy.wait()
    piece[2 * half :, :] = out_piece[...]


def q_kernel(tok, wq_t, bq, q):
    heads = wq_t.shape[0] // HEAD_DIM
    full = (nt(tok[...], wq_t[...]) + bq[...]).astype(bf16) * jnp.asarray(SCALE, bf16)
    zero = jnp.zeros((full.shape[0], HEAD_DIM), bf16)
    cols = []
    for h in range(heads):
        cols += [full[:, h * HEAD_DIM : (h + 1) * HEAD_DIM], zero]
    q[...] = jnp.concatenate(cols, axis=1)


def weights_kernel(n, at, w_out, *refs):
    pieces, (w_out_all, w_in_far, w_outer_far) = refs[:8], refs[8:]
    z = at[0]
    local = w_out.shape[0]
    part = local // 4
    rows = w_in_far.shape[0] // 8

    def put(ref, base, value):
        size = value.shape[0]
        ref[pl.ds(pl.multiple_of(base, 16), size), :] = value

    put(w_out_all, z * local, w_out[...])
    for j, piece in enumerate(pieces):
        put(w_in_far, (at[4] ^ j) * rows, piece[:rows, :])
        put(w_outer_far, (at[4] ^ j) * rows, piece[rows : 2 * rows, :])
        for s in range(1, n if j < 4 else 0):
            base = 2 * rows + (s - 1) * part
            put(w_out_all, (z ^ s) * local + (at[2] ^ j) * part, piece[base : base + part, :])


def attend_kernel(n_blk, ids, at, bucket, lens, q, *refs):
    kvs = refs[:n_blk]
    hp_first, hp_second, probs_first, probs_second, hp_late, held, sems = refs[n_blk:]
    copies = []
    heads = q.shape[1] // LANES
    b = at[2]
    q_at = lax.broadcasted_iota(i32, (BLOCK, 1), 0)
    k_at = lax.broadcasted_iota(i32, (1, BLOCK), 1)
    for order, row in enumerate(ids):
        hp, probs = ((hp_first, probs_first), (hp_second, probs_second))[order // 2]
        i = order % 2
        r = row_at(at, row)
        bk = bucket[r]
        size = BLOCK << bk
        slot = b >> bk
        limit = lens[r, slot]
        q_in = jnp.where(q_at + (b * BLOCK - slot * size) < limit, 1, 0)
        k_in = []
        for j in range(n_blk):
            kb = b ^ j
            k_slot = kb >> bk
            inside = jnp.where(k_at + (kb * BLOCK - k_slot * size) < limit, 1, 0)
            k_in.append(jnp.where(k_slot == slot, inside, 2))
        allowed = q_in == jnp.concatenate(k_in, axis=1)
        here = pl.ds(pl.multiple_of(r * BLOCK, BLOCK), BLOCK)
        outs = []
        for h in range(heads):
            lanes = slice(h * LANES, (h + 1) * LANES)
            kvh = jnp.concatenate([kv[here, lanes] for kv in kvs], axis=0)
            scores = jnp.where(allowed, nt(q[here, lanes], kvh), -1e30)
            weights = jnp.exp(scores - jnp.max(scores, axis=-1, keepdims=True))
            total = jnp.sum(weights, axis=-1, keepdims=True)
            p = (weights / total).astype(bf16)
            held[(order * heads + h) * BLOCK : (order * heads + h + 1) * BLOCK, :] = p
            outs.append(nn(p, kvh)[:, HEAD_DIM:].astype(bf16))
        base = i * PACKED
        hp[base : base + BLOCK, :] = jnp.concatenate(outs[:2], axis=1)
        hp[base + BLOCK : base + PACKED, :] = jnp.concatenate(
            [outs[2][:HEAD_DIM], outs[2][HEAD_DIM:]], axis=1
        )
        size = heads * BLOCK
        copies.append(
            pltpu.make_async_copy(
                held.at[pl.ds(order * size, size), :], probs.at[pl.ds(i * size, size), :], sems.at[order]
            )
        )
        copies[-1].start()
    for i, hp in enumerate((hp_first, hp_second)):
        rows = hp.shape[0]
        copies.append(pltpu.make_async_copy(hp, hp_late.at[pl.ds(i * rows, rows), :], sems.at[4 + i]))
        copies[-1].start()
    for copy in copies:
        copy.wait()


def unpack(h):
    odd = jnp.concatenate([h[BLOCK:, :HEAD_DIM], h[BLOCK:, HEAD_DIM:]], axis=0)
    return jnp.concatenate([h[:BLOCK, :], odd], axis=1)


def pack(v):
    odd = jnp.concatenate([v[:HEAD_DIM, LANES:], v[HEAD_DIM:, LANES:]], axis=1)
    return jnp.concatenate([v[:, :LANES], odd], axis=0)


def gelu_and_slope(inner):
    cdf = 0.5 * (1.0 + lax.erf(inner * (0.5**0.5)))
    slope = cdf + inner * (0.3989422804014327 * jnp.exp(-0.5 * inner * inner))
    return (inner * cdf).astype(bf16), slope.astype(bf16)


def ffn_kernel(
    n, i, at, tok, w_out, b_out, g1, b1, w_in, w_in_far, b_in, b_in_far, w_outer, w_outer_far, *refs
):
    hps = refs[:n] if len(refs) > n + 7 + 1 else [refs[0].at[pl.ds(s * PACKED, PACKED), :] for s in range(n)]
    refs = refs if len(refs) > n + 7 + 1 else refs[:1] * n + refs[1:]
    part, n1_out, s1_out, low_out, act_out, act_far_out, slopes, *rest, held = refs[n:]
    z = at[0]
    local = w_out.shape[0] // n
    for s in range(n):
        j = z ^ s
        held[j] = nn(unpack(hps[s][:PACKED, :]), chunk_of(w_out, j, local))
        if rest:
            rest[0][s * PACKED : (s + 1) * PACKED, :] = hps[s][PACKED:, :]
    attn = held[0]
    for j in range(1, n):
        attn = attn + held[j]
    resid = chunk_of(tok, row_at(at, i), BLOCK).astype(f32) + (attn + b_out[...])
    center = resid - mean(resid)
    s1 = lax.rsqrt(mean(center * center) + EPS)
    n1 = center * s1
    low = (n1 * g1[...] + b1[...]).astype(bf16)
    act, slope = gelu_and_slope(nn(low, w_in[...]) + b_in[...])
    act_far, slope_far = gelu_and_slope(nn(low, w_in_far[...]) + b_in_far[...])
    part[...] = (nn(act, w_outer[...]) + nn(act_far, w_outer_far[...])).astype(bf16)
    n1_out[...] = n1
    s1_out[...] = jnp.broadcast_to(s1, s1_out.shape)
    low_out[...] = low
    act_out[...] = act
    act_far_out[...] = act_far
    slopes[:BLOCK, :] = slope
    slopes[BLOCK:, :] = slope_far


def ffn_back_kernel(
    i, at, cot, n1, slopes, mine, theirs, g1, b1, b_outer, g2, b2, w_in, w_in_far, w_outer,
    w_outer_far, out, dffn_out, dinner_out, dinner_far_out, part, dres2_out, sums
):
    hidden = n1[...] * g1[...] + b1[...]
    ffn = mine[...].astype(f32) + theirs[...].astype(f32)
    resid = hidden + (ffn + b_outer[...])
    center = resid - mean(resid)
    s2 = lax.rsqrt(mean(center * center) + EPS)
    n2 = center * s2
    ct = chunk_of(cot, row_at(at, i), BLOCK).astype(f32)
    dn = ct * g2[...]
    dres2 = s2 * (dn - mean(dn) - n2 * mean(dn * n2))
    dffn = dres2.astype(bf16)
    dinner = (nt(dffn, w_outer[...]) * slopes[:BLOCK, :].astype(f32)).astype(bf16)
    dinner_far = (nt(dffn, w_outer_far[...]) * slopes[BLOCK:, :].astype(f32)).astype(bf16)
    part[...] = (nt(dinner, w_in[...]) + nt(dinner_far, w_in_far[...])).astype(bf16)
    dres2_out[...] = dres2
    dinner_out[...] = dinner
    out[...] = (n2 * g2[...] + b2[...]).astype(bf16)
    dffn_out[...] = dffn
    dinner_far_out[...] = dinner_far
    sums[...] = rows8(
        col_sum(ct * n2), col_sum(ct), col_sum(dffn.astype(f32)),
        col_sum(dinner.astype(f32)), col_sum(dinner_far.astype(f32)),
    )


def norm_back_kernel(n, at, mine, theirs, dres2, n1, s1, g1, w_out, sums2, dres1_out, share, dh, dh_far):
    dhidden = (mine[...].astype(f32) + theirs[...].astype(f32)) + dres2[...]
    norm = n1[...]
    dn = dhidden * g1[...]
    dres1 = s1[:, :1] * (dn - mean(dn) - norm * mean(dn * norm))
    dattn = dres1.astype(bf16)
    dres1_out[...] = dres1
    share[:BLOCK, :] = dattn
    sums = jnp.concatenate(
        [col_sum(dhidden * norm), col_sum(dhidden), col_sum(dattn.astype(f32)), sums2[:5, :]], axis=0
    )
    share[BLOCK:, :] = jnp.concatenate([sums, jnp.zeros_like(sums)], axis=0).astype(bf16)
    local = w_out.shape[0] // n
    dh[...] = pack(nt(dattn, chunk_of(w_out, at[0], local)).astype(bf16))
    dh_far[...] = pack(nt(dattn, chunk_of(w_out, at[0] ^ 1, local)).astype(bf16))


def attend_back_kernel(n_blk, ids, at, first, second, q, probs, *refs):
    kvs = refs[:n_blk]
    dq_out, send, keep = refs[n_blk:]
    heads = q.shape[1] // LANES
    zero = jnp.zeros((BLOCK, HEAD_DIM), bf16)
    for i, packed in enumerate((first, second)):
        c = row_at(at, ids[i])
        here = pl.ds(pl.multiple_of(c * BLOCK, BLOCK), BLOCK)
        flat = unpack(packed[...])
        dqs = []
        for h in range(heads):
            lanes = slice(h * LANES, (h + 1) * LANES)
            dhead = jnp.concatenate([zero, flat[:, h * HEAD_DIM : (h + 1) * HEAD_DIM]], axis=1)
            kvh = jnp.concatenate([kv[here, lanes] for kv in kvs], axis=0)
            at_p = (i * heads + h) * BLOCK
            p = probs[at_p : at_p + BLOCK, :]
            pf = p.astype(f32)
            dp = nt(dhead, kvh)
            delta = jnp.sum(pf * dp, axis=-1, keepdims=True)
            ds = (pf * (dp - delta)).astype(bf16)
            dqs.append((nn(ds, kvh) * SCALE)[:, :HEAD_DIM].astype(bf16))
            left = jnp.concatenate([q[here, lanes], dhead], axis=0)
            dkv = tn(left, jnp.concatenate([ds, p], axis=0)).astype(bf16)
            for j in range(n_blk):
                target = keep if j % 2 == 0 else send
                target[j // 2, i, lanes, :] = dkv[:, j * BLOCK : (j + 1) * BLOCK]
        dq_out[i * BLOCK : (i + 1) * BLOCK, :] = jnp.concatenate(dqs, axis=1)


def input_kernel(dq, keep, recv, far, wq_t, wk_t, wv_t, part, dkv_t, sums):
    total = keep[0].astype(f32) + recv[0].astype(f32) + far[...].astype(f32)
    lows = [total[i].astype(bf16) for i in range(2)]
    low = jnp.concatenate([v.T for v in lows], axis=0)
    grad = nn(dq[...], wq_t[...]) + nn(low, both_rows(wk_t, wv_t))
    part[...] = grad.astype(bf16)
    dkv_t[...] = jnp.concatenate(lows, axis=1)
    width = sums.shape[1]
    one = col_sum(dq[...].astype(f32))
    two = col_sum(low.astype(f32))
    sums[...] = rows8(
        jnp.concatenate([one, jnp.zeros((1, width - one.shape[1]), f32)], axis=1),
        jnp.concatenate([two, jnp.zeros((1, width - two.shape[1]), f32)], axis=1),
    )


def pick(first, one, other):
    return jnp.where(first, one, other)


def join(values, axis=0):
    return jnp.concatenate(list(values), axis=axis)


def ordered_sum(at, parts, held):
    for i, part in enumerate(parts):
        held[row_at(at, i)] = part.astype(f32)
    total = held[0]
    for r in range(1, len(parts)):
        total = total + held[r]
    return total


def ffn_grad_kernel(m, at, *refs):
    low, act, act_far, dffn, dinner, dinner_far = (refs[2 * i : 2 * i + 2] for i in range(6))
    keep, send = refs[12:]
    first = at[1] == 0
    both = lambda pair: join(x[...] for x in pair)
    lows, dffns = both(low), both(dffn)
    rows = lows.shape[1] // m
    for q, (acts, dinners) in enumerate(((both(act), both(dinner)), (both(act_far), both(dinner_far)))):
        for target, one in ((keep, first), (send, jnp.logical_not(first))):
            main = tn(pick(one, lows, acts), pick(one, dinners, dffns)).astype(bf16)
            for i in range(m):
                target[i, q] = main[i * rows : (i + 1) * rows]


def attend_grad_kernel(m, at, tok, hp_late, *refs):
    shares, (dq, dkv_t, sums) = refs[:4], (refs[4 + 2 * i : 6 + 2 * i] for i in range(3))
    keep, send, held = refs[10:]
    first = at[1] == 0
    toks = join(chunk_of(tok, row_at(at, i), BLOCK) for i in range(4))
    heads = join(unpack(hp_late[i * PACKED : (i + 1) * PACKED, :]) for i in (2, 3, 0, 1))
    g_out = tn(heads, join(x[:BLOCK, :] for x in shares))
    g_q = tn(join(x[...] for x in dq), toks)
    g_kv = nn(join((x[...] for x in dkv_t), axis=1), toks)
    one = join([g_out, g_q]).astype(bf16)
    two = g_kv.astype(bf16)
    half = two.shape[0]
    tails = [x[BLOCK : BLOCK + 16, :].astype(f32) for x in shares]
    norm = ordered_sum(at, [x[:8] for x in tails], held)
    total = sums[0][...] + sums[1][...]
    inner = tails[0][6:7] + tails[1][6:7] + tails[2][7:8] + tails[3][7:8]
    norm = join([norm[:6], inner, jnp.zeros_like(inner)])
    rest = keep.shape[0] - half
    tail = join([norm, total, jnp.zeros((rest - 16, total.shape[1]), f32)]).astype(bf16)
    keep[:half, :] = pick(first, one, two)
    keep[half:, :] = tail
    send[:half, :] = pick(first, two, one)
    send[half:, :] = tail


def share_kernel(total1, near1, *refs):
    parts, share = refs[:-1], refs[-1]
    rows = near1.shape[0]
    share[:rows, :] = (total1[0].astype(f32) + near1[...].astype(f32)).astype(bf16)
    total = parts[0][...].astype(f32)
    for part in parts[1:]:
        total = total + part[...].astype(f32)
    share[rows:, :] = total.astype(bf16)


def final_kernel(m, at, *refs):
    mine, other = refs[:m], refs[m : 2 * m]
    g_in, g_outer, g_out, g_q, g_k, g_v, *vectors, packed = refs[2 * m :]
    first = at[1] == 0
    rows = g_in.shape[0] // m
    for s in range(m):
        i = at[3] ^ s
        a, b = mine[s], other[s]
        here = pl.ds(pl.multiple_of(i * rows, rows), rows)
        g_in[here, :] = pick(first, a[:rows, :], b[:rows, :]).astype(f32)
        g_outer[here, :] = pick(first, b[:rows, :], a[:rows, :]).astype(f32)
        packed[0, i] = pick(first, a[rows:, :], b[rows:, :])
        packed[1, i] = pick(first, b[rows:, :], a[rows:, :])
    width = g_q.shape[0]
    one = join(packed[0, i] for i in range(m)).astype(f32)
    two = join(packed[1, i] for i in range(m)).astype(f32)
    g_out[...] = one[:width]
    g_q[...] = one[width : 2 * width]
    tail = one[2 * width : 2 * width + 16]
    values = []
    for h in range(width // HEAD_DIM):
        part = slice(h * HEAD_DIM, (h + 1) * HEAD_DIM)
        g_k[part, :] = two[h * LANES : h * LANES + HEAD_DIM]
        g_v[part, :] = two[h * LANES + HEAD_DIM : (h + 1) * LANES]
        values.append(tail[9:10, h * LANES + HEAD_DIM : (h + 1) * LANES])
    b_q, b_v = vectors[7:]
    for i, ref in enumerate(vectors[:7]):
        ref[...] = tail[i]
    b_q[...] = tail[8, :width]
    b_v[...] = jnp.concatenate(values, axis=1)[0]


def rows_kernel(at, *refs):
    out = refs[-1]
    rows = [v[i * BLOCK : (i + 1) * BLOCK, :] for v in refs[:-1] for i in range(v.shape[0] // BLOCK)]
    for i, value in enumerate(rows):
        out[row_at(at, i)] = value


def solution(mesh):
    n_dp = mesh.shape["dp"]
    n_blk = mesh.shape["blk"]
    n = mesh.shape["tensor"]
    half_blk = n_blk // 2
    m = n_dp * half_blk

    def swap(v, bit):
        return lax.ppermute(v, "tensor", [(i, i ^ bit) for i in range(n)])

    def flip(v, bit):
        return lax.ppermute(v, "blk", [(i, i ^ bit) for i in range(n_blk)])

    def flip_member(v, s):
        perm = []
        for dp in range(n_dp):
            for blk in range(n_blk):
                i = (dp * half_blk + blk // 2) ^ s
                to = (i // half_blk) * n_blk + (i % half_blk) * 2 + blk % 2
                perm.append((dp * n_blk + blk, to))
        return lax.ppermute(v, ("dp", "blk"), perm)

    def share_pieces(keep, recv, member):
        def piece(s):
            mine = lax.dynamic_index_in_dim(keep, member ^ s, 0, keepdims=False)
            theirs = lax.dynamic_index_in_dim(recv, member ^ s, 0, keepdims=False)
            return (mine.astype(f32) + theirs.astype(f32)).astype(bf16)

        return [piece(s) for s in range(m)]

    def add(own, got):
        total = own.astype(f32)
        for part in got:
            total = total + part.astype(f32)
        return total.astype(bf16)

    def body(
        tokens, bucket_ids, seq_lengths, w_query, b_query, w_key, w_value, b_value, w_out, b_out,
        norm1_gain, norm1_bias, w_inner, b_inner, w_outer, b_outer, norm2_gain, norm2_bias,
        cotangent,
    ):
        row_count, block, width = tokens.shape
        count = row_count * block
        local = w_query.shape[1]
        heads = local // HEAD_DIM
        lanes = heads * LANES
        units = w_inner.shape[1]
        blk = lax.axis_index("blk").astype(i32)
        z = lax.axis_index("tensor").astype(i32)
        core = blk % 2
        member = (lax.axis_index("dp") * half_blk + blk // 2).astype(i32)
        cut_at = (lax.axis_index("dp") % 2) * n_blk + blk
        at = jnp.stack([z, core, blk, member, cut_at]).astype(i32)
        tok = tokens.reshape(count, width)
        cot = cotangent.reshape(count, width)
        row = lambda v: v.reshape(1, -1)
        wq_t, wk_t, wv_t = w_query.T, w_key.T, w_value.T
        fence = lax.optimization_barrier

        part = local // 4
        piece_rows = (width + units) // 8
        kv, piece, out_piece = pl.pallas_call(
            front_kernel,
            out_shape=(
                near((count, lanes), bf16), near((piece_rows + part, width), bf16),
                near((part, width), bf16),
            ),
            in_specs=[SMEM] + [HBM] * 6 + [VMEM],
            out_specs=(VMEM,) * 3,
            scratch_shapes=[
                pltpu.VMEM((count, width), bf16), pltpu.VMEM((local, width), bf16),
                pltpu.VMEM((local, width), bf16), pltpu.SemaphoreType.DMA((6,)),
            ],
            compiler_params=pltpu.CompilerParams(vmem_limit_bytes=16 * MIB),
            name="front",
        )(at, *[pltpu.with_memory_space_constraint(v, pltpu.HBM) for v in (tok, wk_t, wv_t, w_inner, w_outer, w_out)], row(b_value))
        kv, piece, out_piece, b_far = fence((kv, piece, out_piece, b_inner))
        kv_far = flip(kv, 2)
        kv_core = flip(kv, 1)
        pieces = [swap(piece, 1)] + [swap(out_piece, s) for s in range(2, n)]
        b_inner_far = swap(b_far, 1)
        kv_far, b_inner_far, *pieces = fence((kv_far, b_inner_far, *pieces))
        kv_both = flip(kv_far, 1)
        own_piece = jnp.concatenate(pieces, axis=0)
        ffn_piece = pieces[0][:piece_rows]

        def across(v, dp_bit, blk_bit):
            there = lambda i: ((i // n_blk) ^ dp_bit) * n_blk + ((i % n_blk) ^ blk_bit)
            return lax.ppermute(v, ("dp", "blk"), [(i, there(i)) for i in range(n_dp * n_blk)])

        arrived = {4: across(ffn_piece, 1, 0), 6: across(ffn_piece, 1, 2)}
        arrived |= {0: own_piece, 2: across(own_piece, 0, 2)}

        q = call(q_kernel, near((count, lanes), bf16), "query_rows", (tok, wq_t, row(b_query)), us=0.5)
        kvs = [kv, kv_core, kv_far, kv_both]

        prob_rows = 2 * heads * BLOCK
        hp_other, hp_mine, probs_other, probs_mine, hp_late = pl.pallas_call(
            functools.partial(attend_kernel, n_blk, (2, 3, 0, 1)),
            out_shape=(near((2 * PACKED, LANES), bf16),) * 2
            + (pltpu.HBM((prob_rows, n_blk * BLOCK), bf16),) * 2
            + (pltpu.HBM((4 * PACKED, LANES), bf16),),
            in_specs=[SMEM] * 3 + [VMEM] * (1 + n_blk),
            out_specs=(VMEM,) * 2 + (HBM,) * 3,
            scratch_shapes=[
                pltpu.VMEM((2 * prob_rows, n_blk * BLOCK), bf16), pltpu.SemaphoreType.DMA((6,)),
            ],
            compiler_params=pltpu.CompilerParams(vmem_limit_bytes=16 * MIB),
            cost_estimate=pl.CostEstimate(
                flops=int(ATTEND_US * FLOPS_US), bytes_accessed=1, transcendentals=0
            ),
            name="attend",
        )(at, bucket_ids, seq_lengths, q, *kvs)
        hps = {0: hp_mine, 1: swap(hp_other, 1), 2: swap(hp_mine, 2), 3: swap(hp_other, 3)}
        held = [arrived[2], arrived[4], arrived[6]]
        hps[1], hps[2], hps[3], *held = fence((hps[1], hps[2], hps[3], *held))
        arrived[2], arrived[4], arrived[6] = held
        arrived |= {j + 1: flip(v, 1) for j, v in arrived.items()}
        w_out_all, w_inner_far, w_outer_far = call(
            functools.partial(weights_kernel, n),
            (near((n * local, width), bf16), near(w_inner.shape, bf16), near(w_outer.shape, bf16)),
            "far_weights",
            (at, w_out, *[arrived[j] for j in range(8)]),
            us=2.2,
            scalars=1,
        )

        chunk = lambda rows, dt: near((rows, width), dt)
        gains1 = (row(norm1_gain), row(norm1_bias))

        def ffn(i, heads_in):
            return call(
                functools.partial(ffn_kernel, n, i),
                (
                    chunk(BLOCK, bf16), chunk(BLOCK, f32), near((BLOCK, LANES), f32),
                    chunk(BLOCK, bf16), near((BLOCK, units), bf16), near((BLOCK, units), bf16),
                    near((2 * BLOCK, units), bf16),
                )
                + ((near((n * PACKED, LANES), bf16),) if i == 0 else ()),
                "ffn",
                (
                    at, tok, w_out_all, row(b_out), *gains1, w_inner, w_inner_far, row(b_inner),
                    row(b_inner_far), w_outer, w_outer_far, *heads_in,
                ),
                us=2.4,
                scalars=1,
                scratch=[pltpu.VMEM((n, BLOCK, width), f32)],
            )

        *row0, second_heads = ffn(0, [hps[s] for s in range(n)])
        parts, n1s, s1s, lows, acts, acts_far, slopes = map(list, zip(row0, ffn(1, [second_heads])))
        theirs = [swap(v, 2) for v in parts]

        def ffn_back(i):
            return call(
                functools.partial(ffn_back_kernel, i),
                (
                    chunk(BLOCK, bf16), chunk(BLOCK, bf16), near((BLOCK, units), bf16),
                    near((BLOCK, units), bf16), chunk(BLOCK, bf16), chunk(BLOCK, f32), chunk(8, f32),
                ),
                "ffn_back",
                (
                    at, cot, n1s[i], slopes[i], parts[i], theirs[i], *gains1, row(b_outer),
                    row(norm2_gain), row(norm2_bias), w_inner, w_inner_far, w_outer, w_outer_far,
                ),
                us=2.7,
                scalars=1,
            )

        outs, dffns, dinners, dinners_far, parts2, dres2, sums2 = map(list, zip(*[ffn_back(i) for i in range(2)]))
        theirs2 = [swap(v, 2) for v in parts2]
        keep1, send1 = call(
            functools.partial(ffn_grad_kernel, m),
            (near((m, 2, width // m, width), bf16),) * 2,
            "ffn_grads",
            (at, *lows, *acts, *acts_far, *dffns, *dinners, *dinners_far),
            us=FILL_US,
            vmem=24,
            scalars=1,
        )
        recv1 = flip(send1, 1)
        pieces1 = share_pieces(keep1, recv1, member)

        def norm_back(i):
            return call(
                functools.partial(norm_back_kernel, n),
                (
                    chunk(BLOCK, f32), chunk(BLOCK + 16, bf16), near((PACKED, LANES), bf16),
                    near((PACKED, LANES), bf16),
                ),
                "norm_back",
                (at, parts2[i], theirs2[i], dres2[i], n1s[i], s1s[i], gains1[0], w_out_all, sums2[i]),
                us=1.2,
                scalars=1,
            )

        dres1, shares, dheads, dheads_far = map(list, zip(*[norm_back(i) for i in range(2)]))
        dheads += [swap(v, 1) for v in dheads_far]
        shares += [swap(v, 1) for v in shares]
        outs += [swap(v, 1) for v in outs]

        def attend_back(ids, probs, *packed):
            return call(
                functools.partial(attend_back_kernel, n_blk, ids),
                (
                    near((2 * BLOCK, local), bf16), near((half_blk, 2, lanes, BLOCK), bf16),
                    near((half_blk, 2, lanes, BLOCK), bf16),
                ),
                "attend_back",
                (at, *packed, q, probs, *kvs),
                scalars=1,
                us=BACK_US,
            )

        own = attend_back((0, 1), probs_mine, dheads[0], dheads[1])
        after, dheads[2], dheads[3], pieces1 = fence((own[1], dheads[2], dheads[3], pieces1))
        own = (own[0], after, own[2])
        other = attend_back((2, 3), probs_other, dheads[2], dheads[3])

        def exchange(third):
            _, send, keep = third
            recv = flip(send, 1)
            return recv, (keep[1].astype(f32) + recv[1].astype(f32)).astype(bf16)

        def input_part(third, recv, far, us):
            dq, _, keep = third
            return call(
                input_kernel,
                (chunk(2 * BLOCK, bf16), near((lanes, 2 * BLOCK), bf16), chunk(8, f32)),
                "input_part",
                (dq, keep, recv, far, wq_t, wk_t, wv_t),
                us=us,
            )

        recv_own, sum_own = exchange(own)
        recv_other, sum_other = exchange(other)
        far_own, far_other = flip(sum_own, 2), flip(sum_other, 2)
        far_own, far_other, pieces1 = fence((far_own, far_other, pieces1))
        part, *late = input_part(other, recv_other, far_other, 1.0)
        part, pieces1 = fence((part, pieces1))
        from_near, *ends = fence((swap(part, 1), *shares[2:]))
        shares[2:] = ends
        got1 = [flip_member(v, s) for s, v in enumerate(pieces1[1:], 1)]
        part_own, dkv_own, sums_own = input_part(own, recv_own, far_own, INPUT_US)
        pair = (part_own.astype(f32) + from_near.astype(f32)).astype(bf16)

        rows2 = 2 * local + 16
        rows2 += -rows2 % (16 * m)
        hp_late, _ = fence((hp_late, pair))
        keep2, send2 = call(
            functools.partial(attend_grad_kernel, m),
            (chunk(rows2, bf16), chunk(rows2, bf16)),
            "attend_grads",
            (
                at, tok, hp_late, *shares, own[0], other[0], dkv_own, late[0], sums_own,
                late[1],
            ),
            us=GRADS_US,
            scalars=1,
            scratch=[pltpu.VMEM((n, 8, width), f32)],
        )
        by_member = lambda v: v.reshape(m, rows2 // m, width)
        pieces2 = share_pieces(by_member(keep2), by_member(flip(send2, 1)), member)
        got2 = [flip_member(v, s) for s, v in enumerate(pieces2[1:], 1)]
        got1, _, _ = fence((got1, keep2, pair))
        total1 = fence(add(pieces1[0], got1))
        near1 = swap(total1[1], 1)
        crossed, near1, got2, *ends = fence((swap(pair, 2), near1, got2, *outs[2:]))
        outs[2:] = ends
        d_tok = pair.astype(f32) + crossed.astype(f32) + jnp.concatenate(dres1, axis=0)
        d_tok = d_tok.astype(bf16)
        share = call(
            share_kernel,
            chunk(width // m + rows2 // m, bf16),
            "grad_share",
            (total1, near1, pieces2[0], *got2),
            us=0.5,
        )
        shares_in = [flip_member(share, k) for k in range(1, m)]
        shares_in[0], d_far = fence((shares_in[0], swap(d_tok, 1)))
        d_toks = [d_tok, d_far]
        assemble = lambda parts, name: call(
            rows_kernel,
            shape((row_count, block, width), bf16),
            name,
            (at, *parts),
            us=1.5,
            scalars=1,
        )
        output = assemble(outs, "output_rows")
        d_tokens = assemble(d_toks, "input_grad_rows")
        mine = [share] + shares_in
        held, _, _ = fence((shares_in[0], output, d_tokens))
        others = [flip(v, 1) for v in [share, held] + shares_in[1:]]
        vector = shape((width,), f32)
        short = shape((local,), f32)
        square = shape((width, units), f32)
        wide = shape((local, width), f32)
        (
            g_w_inner, g_w_outer, g_w_out, g_q, g_k, g_v, g_gain1, g_bias1, g_b_out, g_gain2, g_bias2,
            g_b_outer, g_b_inner, g_b_query, g_b_value,
        ) = call(
            functools.partial(final_kernel, m),
            (square,) * 2 + (wide,) * 4 + (vector,) * 7 + (short,) * 2,
            "grads_out",
            (at, *mine, *others),
            us=4.0,
            vmem=24,
            scalars=1,
            scratch=[pltpu.VMEM((2, m, rows2 // m, width), bf16)],
        )
        return (
            output, d_tokens, g_q.T, g_b_query, g_k.T, g_v.T, g_b_value, g_w_out, g_b_out, g_gain1,
            g_bias1, g_w_inner, g_b_inner, g_w_outer, g_b_outer, g_gain2, g_bias2,
        )

    spread, cols, vec, rows_ = P("dp", "blk", None), P(None, "tensor"), P("tensor"), P("tensor", None)
    return jax.shard_map(
        body,
        mesh=mesh,
        in_specs=(
            spread, P("dp"), P("dp", None), cols, vec, cols, cols, vec, rows_, P(), P(), P(),
            cols, vec, rows_, P(), P(), P(), spread,
        ),
        out_specs=(
            spread, spread, cols, vec, cols, cols, vec, rows_, P(), P(), P(), cols, vec, rows_,
            P(), P(), P(),
        ),
        check_vma=False,
    )
```

```python
import functools

import jax
import jax.numpy as jnp
from jax import lax
from jax.experimental import pallas as pl
from jax.experimental.pallas import tpu as pltpu
from jax.sharding import PartitionSpec as P

HEAD_DIM = 64
BLOCK = 128
LANES = 128
SCALE = HEAD_DIM**-0.5
EPS = 1e-12
f32 = jnp.float32
bf16 = jnp.bfloat16
i32 = jnp.int32
MIB = 1 << 20
FLOPS_US = 1e9
ATTEND_US = 50.0
BACK_US = 50.0
FILL_US = 50.0
INPUT_US = 50.0
GRADS_US = 1.0
PACKED = BLOCK + HEAD_DIM


def nn(a, b):
    return lax.dot_general(a, b, (((1,), (0,)), ((), ())), preferred_element_type=f32)


def nt(a, b):
    return lax.dot_general(a, b, (((1,), (1,)), ((), ())), preferred_element_type=f32)


def tn(a, b):
    return lax.dot_general(a, b, (((0,), (0,)), ((), ())), preferred_element_type=f32)


def mean(v):
    return jnp.mean(v, axis=-1, keepdims=True)


def col_sum(v):
    return jnp.sum(v, axis=0, keepdims=True)


def row_at(at, i):
    half = at[0] % 2
    return 2 * half + i if i < 2 else 2 * (1 - half) + (i - 2)


def rows8(*rows):
    width = rows[0].shape[1]
    pad = jnp.zeros((8 - len(rows), width), f32)
    return jnp.concatenate(rows + (pad,), axis=0)


def shape(dims, dtype):
    return jax.ShapeDtypeStruct(dims, dtype)


def near(dims, dtype):
    return pltpu.VMEM(dims, dtype)


SMEM = pl.BlockSpec(memory_space=pltpu.SMEM)
VMEM = pl.BlockSpec(memory_space=pltpu.VMEM)
HBM = pl.BlockSpec(memory_space=pltpu.HBM)


def call(kernel, outs, name, args, scalars=0, us=1.0, vmem=16, scratch=()):
    return pl.pallas_call(
        kernel,
        out_shape=outs,
        in_specs=[SMEM] * scalars + [VMEM] * (len(args) - scalars),
        out_specs=jax.tree.map(lambda _: VMEM, outs),
        scratch_shapes=list(scratch),
        compiler_params=pltpu.CompilerParams(vmem_limit_bytes=vmem * MIB),
        cost_estimate=pl.CostEstimate(flops=int(us * FLOPS_US), bytes_accessed=1, transcendentals=0),
        name=name,
    )(*args)


def chunk_of(ref, c, rows):
    return ref[pl.ds(pl.multiple_of(c * rows, rows), rows), :]


def both_rows(wk_t, wv_t):
    rows = []
    for h in range(wk_t.shape[0] // HEAD_DIM):
        part = slice(h * HEAD_DIM, (h + 1) * HEAD_DIM)
        rows += [wk_t[part, :], wv_t[part, :]]
    return jnp.concatenate(rows, axis=0)


def front_kernel(at, tok, wk_t, wv_t, w_in, w_outer, w_out, bv, kv, piece, out_piece, tok_v, wk_v, wv_v, sems):
    tail = out_piece.shape[0]
    half = (piece.shape[0] - tail) // 2

    def part(ref, index, size):
        return ref.at[pl.ds(pl.multiple_of(index * size, 16), size), :]

    moves = [
        (tok, tok_v),
        (wk_t, wk_v),
        (wv_t, wv_v),
        (part(w_in, at[4], half), piece.at[pl.ds(0, half), :]),
        (part(w_outer, at[4], half), piece.at[pl.ds(half, half), :]),
        (part(w_out, at[2], tail), out_piece),
    ]
    copies = [pltpu.make_async_copy(a, b, sems.at[i]) for i, (a, b) in enumerate(moves)]
    for copy in copies:
        copy.start()
    for copy in copies[:3]:
        copy.wait()
    bias = []
    for h in range(wk_v.shape[0] // HEAD_DIM):
        bias += [jnp.zeros((1, HEAD_DIM), f32), bv[:, h * HEAD_DIM : (h + 1) * HEAD_DIM]]
    kv[...] = (nt(tok_v[...], both_rows(wk_v, wv_v)) + jnp.concatenate(bias, axis=1)).astype(bf16)
    for copy in copies[3:]:
        copy.wait()
    piece[2 * half :, :] = out_piece[...]


def q_kernel(tok, wq_t, bq, q):
    heads = wq_t.shape[0] // HEAD_DIM
    full = (nt(tok[...], wq_t[...]) + bq[...]).astype(bf16) * jnp.asarray(SCALE, bf16)
    zero = jnp.zeros((full.shape[0], HEAD_DIM), bf16)
    cols = []
    for h in range(heads):
        cols += [full[:, h * HEAD_DIM : (h + 1) * HEAD_DIM], zero]
    q[...] = jnp.concatenate(cols, axis=1)


def weights_kernel(n, at, w_out, *refs):
    pieces, (w_out_all, w_in_far, w_outer_far) = refs[:8], refs[8:]
    z = at[0]
    local = w_out.shape[0]
    part = local // 4
    rows = w_in_far.shape[0] // 8

    def put(ref, base, value):
        size = value.shape[0]
        ref[pl.ds(pl.multiple_of(base, 16), size), :] = value

    put(w_out_all, z * local, w_out[...])
    for j, piece in enumerate(pieces):
        put(w_in_far, (at[4] ^ j) * rows, piece[:rows, :])
        put(w_outer_far, (at[4] ^ j) * rows, piece[rows : 2 * rows, :])
        for s in range(1, n if j < 4 else 0):
            base = 2 * rows + (s - 1) * part
            put(w_out_all, (z ^ s) * local + (at[2] ^ j) * part, piece[base : base + part, :])


def attend_kernel(n_blk, ids, at, bucket, lens, q, *refs):
    kvs = refs[:n_blk]
    hp_first, hp_second, probs_first, probs_second, hp_late, held, sems = refs[n_blk:]
    copies = []
    heads = q.shape[1] // LANES
    b = at[2]
    q_at = lax.broadcasted_iota(i32, (BLOCK, 1), 0)
    k_at = lax.broadcasted_iota(i32, (1, BLOCK), 1)
    for order, row in enumerate(ids):
        hp, probs = ((hp_first, probs_first), (hp_second, probs_second))[order // 2]
        i = order % 2
        r = row_at(at, row)
        bk = bucket[r]
        size = BLOCK << bk
        slot = b >> bk
        limit = lens[r, slot]
        q_in = jnp.where(q_at + (b * BLOCK - slot * size) < limit, 1, 0)
        k_in = []
        for j in range(n_blk):
            kb = b ^ j
            k_slot = kb >> bk
            inside = jnp.where(k_at + (kb * BLOCK - k_slot * size) < limit, 1, 0)
            k_in.append(jnp.where(k_slot == slot, inside, 2))
        allowed = q_in == jnp.concatenate(k_in, axis=1)
        here = pl.ds(pl.multiple_of(r * BLOCK, BLOCK), BLOCK)
        outs = []
        for h in range(heads):
            lanes = slice(h * LANES, (h + 1) * LANES)
            kvh = jnp.concatenate([kv[here, lanes] for kv in kvs], axis=0)
            scores = jnp.where(allowed, nt(q[here, lanes], kvh), -1e30)
            weights = jnp.exp(scores - jnp.max(scores, axis=-1, keepdims=True))
            total = jnp.sum(weights, axis=-1, keepdims=True)
            p = (weights / total).astype(bf16)
            held[(order * heads + h) * BLOCK : (order * heads + h + 1) * BLOCK, :] = p
            outs.append(nn(p, kvh)[:, HEAD_DIM:].astype(bf16))
        base = i * PACKED
        hp[base : base + BLOCK, :] = jnp.concatenate(outs[:2], axis=1)
        hp[base + BLOCK : base + PACKED, :] = jnp.concatenate(
            [outs[2][:HEAD_DIM], outs[2][HEAD_DIM:]], axis=1
        )
        size = heads * BLOCK
        copies.append(
            pltpu.make_async_copy(
                held.at[pl.ds(order * size, size), :], probs.at[pl.ds(i * size, size), :], sems.at[order]
            )
        )
        copies[-1].start()
    for i, hp in enumerate((hp_first, hp_second)):
        rows = hp.shape[0]
        copies.append(pltpu.make_async_copy(hp, hp_late.at[pl.ds(i * rows, rows), :], sems.at[4 + i]))
        copies[-1].start()
    for copy in copies:
        copy.wait()


def unpack(h):
    odd = jnp.concatenate([h[BLOCK:, :HEAD_DIM], h[BLOCK:, HEAD_DIM:]], axis=0)
    return jnp.concatenate([h[:BLOCK, :], odd], axis=1)


def pack(v):
    odd = jnp.concatenate([v[:HEAD_DIM, LANES:], v[HEAD_DIM:, LANES:]], axis=1)
    return jnp.concatenate([v[:, :LANES], odd], axis=0)


def gelu_and_slope(inner):
    cdf = 0.5 * (1.0 + lax.erf(inner * (0.5**0.5)))
    slope = cdf + inner * (0.3989422804014327 * jnp.exp(-0.5 * inner * inner))
    return (inner * cdf).astype(bf16), slope.astype(bf16)


def ffn_kernel(
    n, i, at, tok, w_out, b_out, g1, b1, w_in, w_in_far, b_in, b_in_far, w_outer, w_outer_far, *refs
):
    hps = refs[:n] if len(refs) > n + 7 + 1 else [refs[0].at[pl.ds(s * PACKED, PACKED), :] for s in range(n)]
    refs = refs if len(refs) > n + 7 + 1 else refs[:1] * n + refs[1:]
    part, n1_out, s1_out, low_out, act_out, act_far_out, slopes, *rest, held = refs[n:]
    z = at[0]
    local = w_out.shape[0] // n
    for s in range(n):
        j = z ^ s
        held[j] = nn(unpack(hps[s][:PACKED, :]), chunk_of(w_out, j, local))
        if rest:
            rest[0][s * PACKED : (s + 1) * PACKED, :] = hps[s][PACKED:, :]
    attn = held[0]
    for j in range(1, n):
        attn = attn + held[j]
    resid = chunk_of(tok, row_at(at, i), BLOCK).astype(f32) + (attn + b_out[...])
    center = resid - mean(resid)
    s1 = lax.rsqrt(mean(center * center) + EPS)
    n1 = center * s1
    low = (n1 * g1[...] + b1[...]).astype(bf16)
    act, slope = gelu_and_slope(nn(low, w_in[...]) + b_in[...])
    act_far, slope_far = gelu_and_slope(nn(low, w_in_far[...]) + b_in_far[...])
    part[...] = (nn(act, w_outer[...]) + nn(act_far, w_outer_far[...])).astype(bf16)
    n1_out[...] = n1
    s1_out[...] = jnp.broadcast_to(s1, s1_out.shape)
    low_out[...] = low
    act_out[...] = act
    act_far_out[...] = act_far
    slopes[:BLOCK, :] = slope
    slopes[BLOCK:, :] = slope_far


def ffn_back_kernel(
    i, at, cot, n1, slopes, mine, theirs, g1, b1, b_outer, g2, b2, w_in, w_in_far, w_outer,
    w_outer_far, out, dffn_out, dinner_out, dinner_far_out, part, dres2_out, sums
):
    hidden = n1[...] * g1[...] + b1[...]
    ffn = mine[...].astype(f32) + theirs[...].astype(f32)
    resid = hidden + (ffn + b_outer[...])
    center = resid - mean(resid)
    s2 = lax.rsqrt(mean(center * center) + EPS)
    n2 = center * s2
    ct = chunk_of(cot, row_at(at, i), BLOCK).astype(f32)
    dn = ct * g2[...]
    dres2 = s2 * (dn - mean(dn) - n2 * mean(dn * n2))
    dffn = dres2.astype(bf16)
    dinner = (nt(dffn, w_outer[...]) * slopes[:BLOCK, :].astype(f32)).astype(bf16)
    dinner_far = (nt(dffn, w_outer_far[...]) * slopes[BLOCK:, :].astype(f32)).astype(bf16)
    part[...] = (nt(dinner, w_in[...]) + nt(dinner_far, w_in_far[...])).astype(bf16)
    dres2_out[...] = dres2
    dinner_out[...] = dinner
    out[...] = (n2 * g2[...] + b2[...]).astype(bf16)
    dffn_out[...] = dffn
    dinner_far_out[...] = dinner_far
    sums[...] = rows8(
        col_sum(ct * n2), col_sum(ct), col_sum(dffn.astype(f32)),
        col_sum(dinner.astype(f32)), col_sum(dinner_far.astype(f32)),
    )


def norm_back_kernel(n, at, mine, theirs, dres2, n1, s1, g1, w_out, sums2, dres1_out, share, dh, dh_far):
    dhidden = (mine[...].astype(f32) + theirs[...].astype(f32)) + dres2[...]
    norm = n1[...]
    dn = dhidden * g1[...]
    dres1 = s1[:, :1] * (dn - mean(dn) - norm * mean(dn * norm))
    dattn = dres1.astype(bf16)
    dres1_out[...] = dres1
    share[:BLOCK, :] = dattn
    sums = jnp.concatenate(
        [col_sum(dhidden * norm), col_sum(dhidden), col_sum(dattn.astype(f32)), sums2[:5, :]], axis=0
    )
    share[BLOCK:, :] = jnp.concatenate([sums, jnp.zeros_like(sums)], axis=0).astype(bf16)
    local = w_out.shape[0] // n
    dh[...] = pack(nt(dattn, chunk_of(w_out, at[0], local)).astype(bf16))
    dh_far[...] = pack(nt(dattn, chunk_of(w_out, at[0] ^ 1, local)).astype(bf16))


def attend_back_kernel(n_blk, ids, at, first, second, q, probs, *refs):
    kvs = refs[:n_blk]
    dq_out, send, keep = refs[n_blk:]
    heads = q.shape[1] // LANES
    zero = jnp.zeros((BLOCK, HEAD_DIM), bf16)
    for i, packed in enumerate((first, second)):
        c = row_at(at, ids[i])
        here = pl.ds(pl.multiple_of(c * BLOCK, BLOCK), BLOCK)
        flat = unpack(packed[...])
        dqs = []
        for h in range(heads):
            lanes = slice(h * LANES, (h + 1) * LANES)
            dhead = jnp.concatenate([zero, flat[:, h * HEAD_DIM : (h + 1) * HEAD_DIM]], axis=1)
            kvh = jnp.concatenate([kv[here, lanes] for kv in kvs], axis=0)
            at_p = (i * heads + h) * BLOCK
            p = probs[at_p : at_p + BLOCK, :]
            pf = p.astype(f32)
            dp = nt(dhead, kvh)
            delta = jnp.sum(pf * dp, axis=-1, keepdims=True)
            ds = (pf * (dp - delta)).astype(bf16)
            dqs.append((nn(ds, kvh) * SCALE)[:, :HEAD_DIM].astype(bf16))
            left = jnp.concatenate([q[here, lanes], dhead], axis=0)
            dkv = tn(left, jnp.concatenate([ds, p], axis=0)).astype(bf16)
            for j in range(n_blk):
                target = keep if j % 2 == 0 else send
                target[j // 2, i, lanes, :] = dkv[:, j * BLOCK : (j + 1) * BLOCK]
        dq_out[i * BLOCK : (i + 1) * BLOCK, :] = jnp.concatenate(dqs, axis=1)


def input_kernel(dq, keep, recv, far, wq_t, wk_t, wv_t, part, dkv_t, sums):
    total = keep[0].astype(f32) + recv[0].astype(f32) + far[...].astype(f32)
    lows = [total[i].astype(bf16) for i in range(2)]
    low = jnp.concatenate([v.T for v in lows], axis=0)
    grad = nn(dq[...], wq_t[...]) + nn(low, both_rows(wk_t, wv_t))
    part[...] = grad.astype(bf16)
    dkv_t[...] = jnp.concatenate(lows, axis=1)
    width = sums.shape[1]
    one = col_sum(dq[...].astype(f32))
    two = col_sum(low.astype(f32))
    sums[...] = rows8(
        jnp.concatenate([one, jnp.zeros((1, width - one.shape[1]), f32)], axis=1),
        jnp.concatenate([two, jnp.zeros((1, width - two.shape[1]), f32)], axis=1),
    )


def pick(first, one, other):
    return jnp.where(first, one, other)


def join(values, axis=0):
    return jnp.concatenate(list(values), axis=axis)


def ordered_sum(at, parts, held):
    for i, part in enumerate(parts):
        held[row_at(at, i)] = part.astype(f32)
    total = held[0]
    for r in range(1, len(parts)):
        total = total + held[r]
    return total


def ffn_grad_kernel(m, at, *refs):
    low, act, act_far, dffn, dinner, dinner_far = (refs[2 * i : 2 * i + 2] for i in range(6))
    keep, send = refs[12:]
    first = at[1] == 0
    both = lambda pair: join(x[...] for x in pair)
    lows, dffns = both(low), both(dffn)
    rows = lows.shape[1] // m
    for q, (acts, dinners) in enumerate(((both(act), both(dinner)), (both(act_far), both(dinner_far)))):
        for target, one in ((keep, first), (send, jnp.logical_not(first))):
            main = tn(pick(one, lows, acts), pick(one, dinners, dffns)).astype(bf16)
            for i in range(m):
                target[i, q] = main[i * rows : (i + 1) * rows]


def attend_grad_kernel(m, at, tok, hp_late, *refs):
    shares, (dq, dkv_t, sums) = refs[:4], (refs[4 + 2 * i : 6 + 2 * i] for i in range(3))
    keep, send, held = refs[10:]
    first = at[1] == 0
    toks = join(chunk_of(tok, row_at(at, i), BLOCK) for i in range(4))
    heads = join(unpack(hp_late[i * PACKED : (i + 1) * PACKED, :]) for i in (2, 3, 0, 1))
    g_out = tn(heads, join(x[:BLOCK, :] for x in shares))
    g_q = tn(join(x[...] for x in dq), toks)
    g_kv = nn(join((x[...] for x in dkv_t), axis=1), toks)
    one = join([g_out, g_q]).astype(bf16)
    two = g_kv.astype(bf16)
    half = two.shape[0]
    tails = [x[BLOCK : BLOCK + 16, :].astype(f32) for x in shares]
    norm = ordered_sum(at, [x[:8] for x in tails], held)
    total = sums[0][...] + sums[1][...]
    inner = tails[0][6:7] + tails[1][6:7] + tails[2][7:8] + tails[3][7:8]
    norm = join([norm[:6], inner, jnp.zeros_like(inner)])
    rest = keep.shape[0] - half
    tail = join([norm, total, jnp.zeros((rest - 16, total.shape[1]), f32)]).astype(bf16)
    keep[:half, :] = pick(first, one, two)
    keep[half:, :] = tail
    send[:half, :] = pick(first, two, one)
    send[half:, :] = tail


def share_kernel(total1, near1, *refs):
    parts, share = refs[:-1], refs[-1]
    rows = near1.shape[0]
    share[:rows, :] = (total1[0].astype(f32) + near1[...].astype(f32)).astype(bf16)
    total = parts[0][...].astype(f32)
    for part in parts[1:]:
        total = total + part[...].astype(f32)
    share[rows:, :] = total.astype(bf16)


def widen(at, members, mine, other, g_in, g_outer, wide, sems):
    first = at[1] == 0
    rows = wide.shape[2]
    copies = []
    for c, s in enumerate(members):
        here = pl.ds(pl.multiple_of((at[3] ^ s) * rows, rows), rows)
        a, b = mine[c][:rows, :], other[c][:rows, :]
        wide[0, c] = pick(first, a, b).astype(f32)
        wide[1, c] = pick(first, b, a).astype(f32)
        for k, ref in enumerate((g_in, g_outer)):
            copies.append(pltpu.make_async_copy(wide.at[k, c], ref.at[here, :], sems.at[2 * c + k]))
            copies[-1].start()
    return copies


def early_kernel(m, at, *refs):
    count = m - 1
    for copy in widen(at, range(count), refs[:count], refs[count : 2 * count], *refs[2 * count :]):
        copy.wait()


def final_kernel(m, at, *refs):
    mine, other = refs[:m], refs[m : 2 * m]
    g_in, g_outer, g_out, g_q, g_k, g_v, *vectors, packed, wide, sems = refs[2 * m + 2 :]
    first = at[1] == 0
    rows = wide.shape[2]
    copies = widen(at, [m - 1], mine[m - 1 :], other[m - 1 :], g_in, g_outer, wide, sems)
    for s in range(m):
        i = at[3] ^ s
        packed[0, i] = pick(first, mine[s][rows:, :], other[s][rows:, :])
        packed[1, i] = pick(first, other[s][rows:, :], mine[s][rows:, :])
    width = g_q.shape[0]
    one = join(packed[0, i] for i in range(m)).astype(f32)
    two = join(packed[1, i] for i in range(m)).astype(f32)
    g_out[...] = one[:width]
    g_q[...] = one[width : 2 * width]
    tail = one[2 * width : 2 * width + 16]
    values = []
    for h in range(width // HEAD_DIM):
        part = slice(h * HEAD_DIM, (h + 1) * HEAD_DIM)
        g_k[part, :] = two[h * LANES : h * LANES + HEAD_DIM]
        g_v[part, :] = two[h * LANES + HEAD_DIM : (h + 1) * LANES]
        values.append(tail[9:10, h * LANES + HEAD_DIM : (h + 1) * LANES])
    b_q, b_v = vectors[7:]
    for i, ref in enumerate(vectors[:7]):
        ref[...] = tail[i]
    b_q[...] = tail[8, :width]
    b_v[...] = jnp.concatenate(values, axis=1)[0]
    for copy in copies:
        copy.wait()


def rows_kernel(at, *refs):
    out = refs[-1]
    rows = [v[i * BLOCK : (i + 1) * BLOCK, :] for v in refs[:-1] for i in range(v.shape[0] // BLOCK)]
    for i, value in enumerate(rows):
        out[row_at(at, i)] = value


def solution(mesh):
    n_dp = mesh.shape["dp"]
    n_blk = mesh.shape["blk"]
    n = mesh.shape["tensor"]
    half_blk = n_blk // 2
    m = n_dp * half_blk

    def swap(v, bit):
        return lax.ppermute(v, "tensor", [(i, i ^ bit) for i in range(n)])

    def flip(v, bit):
        return lax.ppermute(v, "blk", [(i, i ^ bit) for i in range(n_blk)])

    def flip_member(v, s):
        perm = []
        for dp in range(n_dp):
            for blk in range(n_blk):
                i = (dp * half_blk + blk // 2) ^ s
                to = (i // half_blk) * n_blk + (i % half_blk) * 2 + blk % 2
                perm.append((dp * n_blk + blk, to))
        return lax.ppermute(v, ("dp", "blk"), perm)

    def share_pieces(keep, recv, member):
        def piece(s):
            mine = lax.dynamic_index_in_dim(keep, member ^ s, 0, keepdims=False)
            theirs = lax.dynamic_index_in_dim(recv, member ^ s, 0, keepdims=False)
            return (mine.astype(f32) + theirs.astype(f32)).astype(bf16)

        return [piece(s) for s in range(m)]

    def add(own, got):
        total = own.astype(f32)
        for part in got:
            total = total + part.astype(f32)
        return total.astype(bf16)

    def body(
        tokens, bucket_ids, seq_lengths, w_query, b_query, w_key, w_value, b_value, w_out, b_out,
        norm1_gain, norm1_bias, w_inner, b_inner, w_outer, b_outer, norm2_gain, norm2_bias,
        cotangent,
    ):
        row_count, block, width = tokens.shape
        count = row_count * block
        local = w_query.shape[1]
        heads = local // HEAD_DIM
        lanes = heads * LANES
        units = w_inner.shape[1]
        blk = lax.axis_index("blk").astype(i32)
        z = lax.axis_index("tensor").astype(i32)
        core = blk % 2
        member = (lax.axis_index("dp") * half_blk + blk // 2).astype(i32)
        cut_at = (lax.axis_index("dp") % 2) * n_blk + blk
        at = jnp.stack([z, core, blk, member, cut_at]).astype(i32)
        tok = tokens.reshape(count, width)
        cot = cotangent.reshape(count, width)
        row = lambda v: v.reshape(1, -1)
        wq_t, wk_t, wv_t = w_query.T, w_key.T, w_value.T
        fence = lax.optimization_barrier

        part = local // 4
        piece_rows = (width + units) // 8
        kv, piece, out_piece = pl.pallas_call(
            front_kernel,
            out_shape=(
                near((count, lanes), bf16), near((piece_rows + part, width), bf16),
                near((part, width), bf16),
            ),
            in_specs=[SMEM] + [HBM] * 6 + [VMEM],
            out_specs=(VMEM,) * 3,
            scratch_shapes=[
                pltpu.VMEM((count, width), bf16), pltpu.VMEM((local, width), bf16),
                pltpu.VMEM((local, width), bf16), pltpu.SemaphoreType.DMA((6,)),
            ],
            compiler_params=pltpu.CompilerParams(vmem_limit_bytes=16 * MIB),
            name="front",
        )(at, *[pltpu.with_memory_space_constraint(v, pltpu.HBM) for v in (tok, wk_t, wv_t, w_inner, w_outer, w_out)], row(b_value))
        kv, piece, out_piece, b_far = fence((kv, piece, out_piece, b_inner))
        kv_far = flip(kv, 2)
        kv_core = flip(kv, 1)
        pieces = [swap(piece, 1)] + [swap(out_piece, s) for s in range(2, n)]
        b_inner_far = swap(b_far, 1)
        kv_far, b_inner_far, *pieces = fence((kv_far, b_inner_far, *pieces))
        kv_both = flip(kv_far, 1)
        own_piece = jnp.concatenate(pieces, axis=0)
        ffn_piece = pieces[0][:piece_rows]

        def across(v, dp_bit, blk_bit):
            there = lambda i: ((i // n_blk) ^ dp_bit) * n_blk + ((i % n_blk) ^ blk_bit)
            return lax.ppermute(v, ("dp", "blk"), [(i, there(i)) for i in range(n_dp * n_blk)])

        arrived = {4: across(ffn_piece, 1, 0), 6: across(ffn_piece, 1, 2)}
        arrived |= {0: own_piece, 2: across(own_piece, 0, 2)}

        q = call(q_kernel, near((count, lanes), bf16), "query_rows", (tok, wq_t, row(b_query)), us=0.5)
        kvs = [kv, kv_core, kv_far, kv_both]

        prob_rows = 2 * heads * BLOCK
        hp_other, hp_mine, probs_other, probs_mine, hp_late = pl.pallas_call(
            functools.partial(attend_kernel, n_blk, (2, 3, 0, 1)),
            out_shape=(near((2 * PACKED, LANES), bf16),) * 2
            + (pltpu.HBM((prob_rows, n_blk * BLOCK), bf16),) * 2
            + (pltpu.HBM((4 * PACKED, LANES), bf16),),
            in_specs=[SMEM] * 3 + [VMEM] * (1 + n_blk),
            out_specs=(VMEM,) * 2 + (HBM,) * 3,
            scratch_shapes=[
                pltpu.VMEM((2 * prob_rows, n_blk * BLOCK), bf16), pltpu.SemaphoreType.DMA((6,)),
            ],
            compiler_params=pltpu.CompilerParams(vmem_limit_bytes=16 * MIB),
            cost_estimate=pl.CostEstimate(
                flops=int(ATTEND_US * FLOPS_US), bytes_accessed=1, transcendentals=0
            ),
            name="attend",
        )(at, bucket_ids, seq_lengths, q, *kvs)
        hps = {0: hp_mine, 1: swap(hp_other, 1), 2: swap(hp_mine, 2), 3: swap(hp_other, 3)}
        held = [arrived[2], arrived[4], arrived[6]]
        hps[1], hps[2], hps[3], *held = fence((hps[1], hps[2], hps[3], *held))
        arrived[2], arrived[4], arrived[6] = held
        arrived |= {j + 1: flip(v, 1) for j, v in arrived.items()}
        w_out_all, w_inner_far, w_outer_far = call(
            functools.partial(weights_kernel, n),
            (near((n * local, width), bf16), near(w_inner.shape, bf16), near(w_outer.shape, bf16)),
            "far_weights",
            (at, w_out, *[arrived[j] for j in range(8)]),
            us=2.2,
            scalars=1,
        )

        chunk = lambda rows, dt: near((rows, width), dt)
        gains1 = (row(norm1_gain), row(norm1_bias))

        def ffn(i, heads_in):
            return call(
                functools.partial(ffn_kernel, n, i),
                (
                    chunk(BLOCK, bf16), chunk(BLOCK, f32), near((BLOCK, LANES), f32),
                    chunk(BLOCK, bf16), near((BLOCK, units), bf16), near((BLOCK, units), bf16),
                    near((2 * BLOCK, units), bf16),
                )
                + ((near((n * PACKED, LANES), bf16),) if i == 0 else ()),
                "ffn",
                (
                    at, tok, w_out_all, row(b_out), *gains1, w_inner, w_inner_far, row(b_inner),
                    row(b_inner_far), w_outer, w_outer_far, *heads_in,
                ),
                us=2.4,
                scalars=1,
                scratch=[pltpu.VMEM((n, BLOCK, width), f32)],
            )

        *row0, second_heads = ffn(0, [hps[s] for s in range(n)])
        parts, n1s, s1s, lows, acts, acts_far, slopes = map(list, zip(row0, ffn(1, [second_heads])))
        theirs = [swap(v, 2) for v in parts]

        def ffn_back(i):
            return call(
                functools.partial(ffn_back_kernel, i),
                (
                    chunk(BLOCK, bf16), chunk(BLOCK, bf16), near((BLOCK, units), bf16),
                    near((BLOCK, units), bf16), chunk(BLOCK, bf16), chunk(BLOCK, f32), chunk(8, f32),
                ),
                "ffn_back",
                (
                    at, cot, n1s[i], slopes[i], parts[i], theirs[i], *gains1, row(b_outer),
                    row(norm2_gain), row(norm2_bias), w_inner, w_inner_far, w_outer, w_outer_far,
                ),
                us=2.7,
                scalars=1,
            )

        outs, dffns, dinners, dinners_far, parts2, dres2, sums2 = map(list, zip(*[ffn_back(i) for i in range(2)]))
        theirs2 = [swap(v, 2) for v in parts2]
        keep1, send1 = call(
            functools.partial(ffn_grad_kernel, m),
            (near((m, 2, width // m, width), bf16),) * 2,
            "ffn_grads",
            (at, *lows, *acts, *acts_far, *dffns, *dinners, *dinners_far),
            us=FILL_US,
            vmem=24,
            scalars=1,
        )
        recv1 = flip(send1, 1)
        pieces1 = share_pieces(keep1, recv1, member)

        def norm_back(i):
            return call(
                functools.partial(norm_back_kernel, n),
                (
                    chunk(BLOCK, f32), chunk(BLOCK + 16, bf16), near((PACKED, LANES), bf16),
                    near((PACKED, LANES), bf16),
                ),
                "norm_back",
                (at, parts2[i], theirs2[i], dres2[i], n1s[i], s1s[i], gains1[0], w_out_all, sums2[i]),
                us=1.2,
                scalars=1,
            )

        dres1, shares, dheads, dheads_far = map(list, zip(*[norm_back(i) for i in range(2)]))
        dheads += [swap(v, 1) for v in dheads_far]
        shares += [swap(v, 1) for v in shares]
        outs += [swap(v, 1) for v in outs]

        def attend_back(ids, probs, *packed):
            return call(
                functools.partial(attend_back_kernel, n_blk, ids),
                (
                    near((2 * BLOCK, local), bf16), near((half_blk, 2, lanes, BLOCK), bf16),
                    near((half_blk, 2, lanes, BLOCK), bf16),
                ),
                "attend_back",
                (at, *packed, q, probs, *kvs),
                scalars=1,
                us=BACK_US,
            )

        own = attend_back((0, 1), probs_mine, dheads[0], dheads[1])
        after, dheads[2], dheads[3], pieces1 = fence((own[1], dheads[2], dheads[3], pieces1))
        own = (own[0], after, own[2])
        other = attend_back((2, 3), probs_other, dheads[2], dheads[3])

        def exchange(third):
            _, send, keep = third
            recv = flip(send, 1)
            return recv, (keep[1].astype(f32) + recv[1].astype(f32)).astype(bf16)

        def input_part(third, recv, far, us):
            dq, _, keep = third
            return call(
                input_kernel,
                (chunk(2 * BLOCK, bf16), near((lanes, 2 * BLOCK), bf16), chunk(8, f32)),
                "input_part",
                (dq, keep, recv, far, wq_t, wk_t, wv_t),
                us=us,
            )

        recv_own, sum_own = exchange(own)
        recv_other, sum_other = exchange(other)
        far_own, far_other = flip(sum_own, 2), flip(sum_other, 2)
        far_own, far_other, pieces1 = fence((far_own, far_other, pieces1))
        part, *late = input_part(other, recv_other, far_other, 1.0)
        part, pieces1 = fence((part, pieces1))
        from_near, *ends = fence((swap(part, 1), *shares[2:]))
        shares[2:] = ends
        got1 = [flip_member(v, s) for s, v in enumerate(pieces1[1:], 1)]
        part_own, dkv_own, sums_own = input_part(own, recv_own, far_own, INPUT_US)
        pair = (part_own.astype(f32) + from_near.astype(f32)).astype(bf16)

        rows2 = 2 * local + 16
        rows2 += -rows2 % (16 * m)
        hp_late, _ = fence((hp_late, pair))
        keep2, send2 = call(
            functools.partial(attend_grad_kernel, m),
            (chunk(rows2, bf16), chunk(rows2, bf16)),
            "attend_grads",
            (
                at, tok, hp_late, *shares, own[0], other[0], dkv_own, late[0], sums_own,
                late[1],
            ),
            us=GRADS_US,
            scalars=1,
            scratch=[pltpu.VMEM((n, 8, width), f32)],
        )
        by_member = lambda v: v.reshape(m, rows2 // m, width)
        pieces2 = share_pieces(by_member(keep2), by_member(flip(send2, 1)), member)
        got2 = [flip_member(v, s) for s, v in enumerate(pieces2[1:], 1)]
        got1, _, _ = fence((got1, keep2, pair))
        total1 = fence(add(pieces1[0], got1))
        near1 = swap(total1[1], 1)
        crossed, near1, got2, *ends = fence((swap(pair, 2), near1, got2, *outs[2:]))
        outs[2:] = ends
        d_tok = pair.astype(f32) + crossed.astype(f32) + jnp.concatenate(dres1, axis=0)
        d_tok = d_tok.astype(bf16)
        share = call(
            share_kernel,
            chunk(width // m + rows2 // m, bf16),
            "grad_share",
            (total1, near1, pieces2[0], *got2),
            us=0.5,
        )
        shares_in = [flip_member(share, k) for k in range(1, m)]
        shares_in[0], d_far = fence((shares_in[0], swap(d_tok, 1)))
        d_toks = [d_tok, d_far]
        assemble = lambda parts, name: call(
            rows_kernel,
            shape((row_count, block, width), bf16),
            name,
            (at, *parts),
            us=1.5,
            scalars=1,
        )
        output = assemble(outs, "output_rows")
        d_tokens = assemble(d_toks, "input_grad_rows")
        mine = [share] + shares_in
        held, _, _ = fence((shares_in[0], output, d_tokens))
        others = [flip(v, 1) for v in [share, held] + shares_in[1:]]
        vector = shape((width,), f32)
        short = shape((local,), f32)
        wide = shape((local, width), f32)
        squares = (pltpu.HBM((width, units), f32), pltpu.HBM((units, width), f32))
        rows1 = width // m

        def grads_out(kernel, outs, arrays, before, members, scratch, us, name):
            return pl.pallas_call(
                kernel,
                out_shape=squares + outs,
                in_specs=[SMEM] + [VMEM] * len(arrays) + [HBM] * len(before),
                out_specs=(HBM,) * 2 + (VMEM,) * len(outs),
                scratch_shapes=scratch
                + [pltpu.VMEM((2, members, rows1, width), f32), pltpu.SemaphoreType.DMA((2 * members,))],
                input_output_aliases={1 + len(arrays) + k: k for k in range(len(before))},
                compiler_params=pltpu.CompilerParams(vmem_limit_bytes=24 * MIB),
                cost_estimate=pl.CostEstimate(
                    flops=int(us * FLOPS_US), bytes_accessed=1, transcendentals=0
                ),
                name=name,
            )(at, *arrays, *before)

        early = grads_out(
            functools.partial(early_kernel, m), (), (*mine[:-1], *others[:-1]), (), m - 1, [], 2.0,
            "early_grads",
        )
        (
            g_w_inner, g_w_outer, g_w_out, g_q, g_k, g_v, g_gain1, g_bias1, g_b_out, g_gain2, g_bias2,
            g_b_outer, g_b_inner, g_b_query, g_b_value,
        ) = grads_out(
            functools.partial(final_kernel, m), (wide,) * 4 + (vector,) * 7 + (short,) * 2,
            (*mine, *others), tuple(early), 1, [pltpu.VMEM((2, m, rows2 // m, width), bf16)], 2.0,
            "grads_out",
        )
        return (
            output, d_tokens, g_q.T, g_b_query, g_k.T, g_v.T, g_b_value, g_w_out, g_b_out, g_gain1,
            g_bias1, g_w_inner, g_b_inner, g_w_outer, g_b_outer, g_gain2, g_bias2,
        )

    spread, cols, vec, rows_ = P("dp", "blk", None), P(None, "tensor"), P("tensor"), P("tensor", None)
    return jax.shard_map(
        body,
        mesh=mesh,
        in_specs=(
            spread, P("dp"), P("dp", None), cols, vec, cols, cols, vec, rows_, P(), P(), P(),
            cols, vec, rows_, P(), P(), P(), spread,
        ),
        out_specs=(
            spread, spread, cols, vec, cols, cols, vec, rows_, P(), P(), P(), cols, vec, rows_,
            P(), P(), P(),
        ),
        check_vma=False,
    )
```

```python
import functools

import jax
import jax.numpy as jnp
from jax import lax
from jax.experimental import pallas as pl
from jax.experimental.pallas import tpu as pltpu
from jax.sharding import PartitionSpec as P

HEAD_DIM = 64
BLOCK = 128
LANES = 128
SCALE = HEAD_DIM**-0.5
EPS = 1e-12
f32 = jnp.float32
bf16 = jnp.bfloat16
i32 = jnp.int32
MIB = 1 << 20
FLOPS_US = 1e9
ATTEND_US = 50.0
BACK_US = 50.0
FILL_US = 50.0
INPUT_US = 50.0
GRADS_US = 1.0
PACKED = BLOCK + HEAD_DIM


def nn(a, b):
    return lax.dot_general(a, b, (((1,), (0,)), ((), ())), preferred_element_type=f32)


def nt(a, b):
    return lax.dot_general(a, b, (((1,), (1,)), ((), ())), preferred_element_type=f32)


def tn(a, b):
    return lax.dot_general(a, b, (((0,), (0,)), ((), ())), preferred_element_type=f32)


def mean(v):
    return jnp.mean(v, axis=-1, keepdims=True)


def col_sum(v):
    return jnp.sum(v, axis=0, keepdims=True)


def row_at(at, i):
    half = at[0] % 2
    return 2 * half + i if i < 2 else 2 * (1 - half) + (i - 2)


def rows8(*rows):
    width = rows[0].shape[1]
    pad = jnp.zeros((8 - len(rows), width), f32)
    return jnp.concatenate(rows + (pad,), axis=0)


def shape(dims, dtype):
    return jax.ShapeDtypeStruct(dims, dtype)


def near(dims, dtype):
    return pltpu.VMEM(dims, dtype)


SMEM = pl.BlockSpec(memory_space=pltpu.SMEM)
VMEM = pl.BlockSpec(memory_space=pltpu.VMEM)
HBM = pl.BlockSpec(memory_space=pltpu.HBM)


def call(kernel, outs, name, args, scalars=0, us=1.0, vmem=16, scratch=()):
    return pl.pallas_call(
        kernel,
        out_shape=outs,
        in_specs=[SMEM] * scalars + [VMEM] * (len(args) - scalars),
        out_specs=jax.tree.map(lambda _: VMEM, outs),
        scratch_shapes=list(scratch),
        compiler_params=pltpu.CompilerParams(vmem_limit_bytes=vmem * MIB),
        cost_estimate=pl.CostEstimate(flops=int(us * FLOPS_US), bytes_accessed=1, transcendentals=0),
        name=name,
    )(*args)


def chunk_of(ref, c, rows):
    return ref[pl.ds(pl.multiple_of(c * rows, rows), rows), :]


def both_rows(wk_t, wv_t):
    rows = []
    for h in range(wk_t.shape[0] // HEAD_DIM):
        part = slice(h * HEAD_DIM, (h + 1) * HEAD_DIM)
        rows += [wk_t[part, :], wv_t[part, :]]
    return jnp.concatenate(rows, axis=0)


def front_kernel(at, tok, wk_t, wv_t, w_in, w_outer, w_out, bv, kv, piece, out_piece, tok_v, wk_v, wv_v, sems):
    tail = out_piece.shape[0]
    half = (piece.shape[0] - tail) // 2

    def part(ref, index, size):
        return ref.at[pl.ds(pl.multiple_of(index * size, 16), size), :]

    moves = [
        (tok, tok_v),
        (wk_t, wk_v),
        (wv_t, wv_v),
        (part(w_in, at[4], half), piece.at[pl.ds(0, half), :]),
        (part(w_outer, at[4], half), piece.at[pl.ds(half, half), :]),
        (part(w_out, at[2], tail), out_piece),
    ]
    copies = [pltpu.make_async_copy(a, b, sems.at[i]) for i, (a, b) in enumerate(moves)]
    for copy in copies:
        copy.start()
    for copy in copies[:3]:
        copy.wait()
    bias = []
    for h in range(wk_v.shape[0] // HEAD_DIM):
        bias += [jnp.zeros((1, HEAD_DIM), f32), bv[:, h * HEAD_DIM : (h + 1) * HEAD_DIM]]
    kv[...] = (nt(tok_v[...], both_rows(wk_v, wv_v)) + jnp.concatenate(bias, axis=1)).astype(bf16)
    for copy in copies[3:]:
        copy.wait()
    piece[2 * half :, :] = out_piece[...]


def q_kernel(tok, wq_t, bq, q):
    heads = wq_t.shape[0] // HEAD_DIM
    full = (nt(tok[...], wq_t[...]) + bq[...]).astype(bf16) * jnp.asarray(SCALE, bf16)
    zero = jnp.zeros((full.shape[0], HEAD_DIM), bf16)
    cols = []
    for h in range(heads):
        cols += [full[:, h * HEAD_DIM : (h + 1) * HEAD_DIM], zero]
    q[...] = jnp.concatenate(cols, axis=1)


def weights_kernel(n, at, w_out, *refs):
    pieces, (w_out_all, w_in_far, w_outer_far) = refs[:8], refs[8:]
    z = at[0]
    local = w_out.shape[0]
    part = local // 4
    rows = w_in_far.shape[0] // 8

    def put(ref, base, value):
        size = value.shape[0]
        ref[pl.ds(pl.multiple_of(base, 16), size), :] = value

    put(w_out_all, z * local, w_out[...])
    for j, piece in enumerate(pieces):
        put(w_in_far, (at[4] ^ j) * rows, piece[:rows, :])
        put(w_outer_far, (at[4] ^ j) * rows, piece[rows : 2 * rows, :])
        for s in range(1, n if j < 4 else 0):
            base = 2 * rows + (s - 1) * part
            put(w_out_all, (z ^ s) * local + (at[2] ^ j) * part, piece[base : base + part, :])


def attend_kernel(n_blk, ids, at, bucket, lens, q, *refs):
    kvs = refs[:n_blk]
    hp_first, hp_second, probs_first, probs_second, hp_late, held, sems = refs[n_blk:]
    copies = []
    heads = q.shape[1] // LANES
    b = at[2]
    q_at = lax.broadcasted_iota(i32, (BLOCK, 1), 0)
    k_at = lax.broadcasted_iota(i32, (1, BLOCK), 1)
    for order, row in enumerate(ids):
        hp, probs = ((hp_first, probs_first), (hp_second, probs_second))[order // 2]
        i = order % 2
        r = row_at(at, row)
        bk = bucket[r]
        size = BLOCK << bk
        slot = b >> bk
        limit = lens[r, slot]
        q_in = jnp.where(q_at + (b * BLOCK - slot * size) < limit, 1, 0)
        k_in = []
        for j in range(n_blk):
            kb = b ^ j
            k_slot = kb >> bk
            inside = jnp.where(k_at + (kb * BLOCK - k_slot * size) < limit, 1, 0)
            k_in.append(jnp.where(k_slot == slot, inside, 2))
        allowed = q_in == jnp.concatenate(k_in, axis=1)
        here = pl.ds(pl.multiple_of(r * BLOCK, BLOCK), BLOCK)
        outs = []
        for h in range(heads):
            lanes = slice(h * LANES, (h + 1) * LANES)
            kvh = jnp.concatenate([kv[here, lanes] for kv in kvs], axis=0)
            scores = jnp.where(allowed, nt(q[here, lanes], kvh), -1e30)
            weights = jnp.exp(scores - jnp.max(scores, axis=-1, keepdims=True))
            total = jnp.sum(weights, axis=-1, keepdims=True)
            p = (weights / total).astype(bf16)
            held[(order * heads + h) * BLOCK : (order * heads + h + 1) * BLOCK, :] = p
            outs.append(nn(p, kvh)[:, HEAD_DIM:].astype(bf16))
        base = i * PACKED
        hp[base : base + BLOCK, :] = jnp.concatenate(outs[:2], axis=1)
        hp[base + BLOCK : base + PACKED, :] = jnp.concatenate(
            [outs[2][:HEAD_DIM], outs[2][HEAD_DIM:]], axis=1
        )
        size = heads * BLOCK
        copies.append(
            pltpu.make_async_copy(
                held.at[pl.ds(order * size, size), :], probs.at[pl.ds(i * size, size), :], sems.at[order]
            )
        )
        copies[-1].start()
    for i, hp in enumerate((hp_first, hp_second)):
        rows = hp.shape[0]
        copies.append(pltpu.make_async_copy(hp, hp_late.at[pl.ds(i * rows, rows), :], sems.at[4 + i]))
        copies[-1].start()
    for copy in copies:
        copy.wait()


def unpack(h):
    odd = jnp.concatenate([h[BLOCK:, :HEAD_DIM], h[BLOCK:, HEAD_DIM:]], axis=0)
    return jnp.concatenate([h[:BLOCK, :], odd], axis=1)


def pack(v):
    odd = jnp.concatenate([v[:HEAD_DIM, LANES:], v[HEAD_DIM:, LANES:]], axis=1)
    return jnp.concatenate([v[:, :LANES], odd], axis=0)


def gelu_and_slope(inner):
    cdf = 0.5 * (1.0 + lax.erf(inner * (0.5**0.5)))
    slope = cdf + inner * (0.3989422804014327 * jnp.exp(-0.5 * inner * inner))
    return (inner * cdf).astype(bf16), slope.astype(bf16)


def ffn_kernel(
    n, i, at, tok, w_out, b_out, g1, b1, w_in, w_in_far, b_in, b_in_far, w_outer, w_outer_far, *refs
):
    hps = refs[:n] if len(refs) > n + 7 + 1 else [refs[0].at[pl.ds(s * PACKED, PACKED), :] for s in range(n)]
    refs = refs if len(refs) > n + 7 + 1 else refs[:1] * n + refs[1:]
    part, n1_out, s1_out, low_out, act_out, act_far_out, slopes, *rest, held = refs[n:]
    z = at[0]
    local = w_out.shape[0] // n
    for s in range(n):
        j = z ^ s
        held[j] = nn(unpack(hps[s][:PACKED, :]), chunk_of(w_out, j, local))
        if rest:
            rest[0][s * PACKED : (s + 1) * PACKED, :] = hps[s][PACKED:, :]
    attn = held[0]
    for j in range(1, n):
        attn = attn + held[j]
    resid = chunk_of(tok, row_at(at, i), BLOCK).astype(f32) + (attn + b_out[...])
    center = resid - mean(resid)
    s1 = lax.rsqrt(mean(center * center) + EPS)
    n1 = center * s1
    low = (n1 * g1[...] + b1[...]).astype(bf16)
    act, slope = gelu_and_slope(nn(low, w_in[...]) + b_in[...])
    act_far, slope_far = gelu_and_slope(nn(low, w_in_far[...]) + b_in_far[...])
    part[...] = (nn(act, w_outer[...]) + nn(act_far, w_outer_far[...])).astype(bf16)
    n1_out[...] = n1
    s1_out[...] = jnp.broadcast_to(s1, s1_out.shape)
    low_out[...] = low
    act_out[...] = act
    act_far_out[...] = act_far
    slopes[:BLOCK, :] = slope
    slopes[BLOCK:, :] = slope_far


def ffn_back_kernel(
    i, at, cot, n1, slopes, mine, theirs, g1, b1, b_outer, g2, b2, w_in, w_in_far, w_outer,
    w_outer_far, out, dffn_out, dinner_out, dinner_far_out, part, dres2_out, sums
):
    hidden = n1[...] * g1[...] + b1[...]
    ffn = mine[...].astype(f32) + theirs[...].astype(f32)
    resid = hidden + (ffn + b_outer[...])
    center = resid - mean(resid)
    s2 = lax.rsqrt(mean(center * center) + EPS)
    n2 = center * s2
    ct = chunk_of(cot, row_at(at, i), BLOCK).astype(f32)
    dn = ct * g2[...]
    dres2 = s2 * (dn - mean(dn) - n2 * mean(dn * n2))
    dffn = dres2.astype(bf16)
    dinner = (nt(dffn, w_outer[...]) * slopes[:BLOCK, :].astype(f32)).astype(bf16)
    dinner_far = (nt(dffn, w_outer_far[...]) * slopes[BLOCK:, :].astype(f32)).astype(bf16)
    part[...] = (nt(dinner, w_in[...]) + nt(dinner_far, w_in_far[...])).astype(bf16)
    dres2_out[...] = dres2
    dinner_out[...] = dinner
    out[...] = (n2 * g2[...] + b2[...]).astype(bf16)
    dffn_out[...] = dffn
    dinner_far_out[...] = dinner_far
    sums[...] = rows8(
        col_sum(ct * n2), col_sum(ct), col_sum(dffn.astype(f32)),
        col_sum(dinner.astype(f32)), col_sum(dinner_far.astype(f32)),
    )


def norm_back_kernel(n, at, mine, theirs, dres2, n1, s1, g1, w_out, sums2, dres1_out, share, dh, dh_far):
    dhidden = (mine[...].astype(f32) + theirs[...].astype(f32)) + dres2[...]
    norm = n1[...]
    dn = dhidden * g1[...]
    dres1 = s1[:, :1] * (dn - mean(dn) - norm * mean(dn * norm))
    dattn = dres1.astype(bf16)
    dres1_out[...] = dres1
    share[:BLOCK, :] = dattn
    sums = jnp.concatenate(
        [col_sum(dhidden * norm), col_sum(dhidden), col_sum(dattn.astype(f32)), sums2[:5, :]], axis=0
    )
    share[BLOCK:, :] = jnp.concatenate([sums, jnp.zeros_like(sums)], axis=0).astype(bf16)
    local = w_out.shape[0] // n
    dh[...] = pack(nt(dattn, chunk_of(w_out, at[0], local)).astype(bf16))
    dh_far[...] = pack(nt(dattn, chunk_of(w_out, at[0] ^ 1, local)).astype(bf16))


def attend_back_kernel(n_blk, ids, at, first, second, q, probs, *refs):
    kvs = refs[:n_blk]
    dq_out, send, keep = refs[n_blk:]
    heads = q.shape[1] // LANES
    zero = jnp.zeros((BLOCK, HEAD_DIM), bf16)
    for i, packed in enumerate((first, second)):
        c = row_at(at, ids[i])
        here = pl.ds(pl.multiple_of(c * BLOCK, BLOCK), BLOCK)
        flat = unpack(packed[...])
        dqs = []
        for h in range(heads):
            lanes = slice(h * LANES, (h + 1) * LANES)
            dhead = jnp.concatenate([zero, flat[:, h * HEAD_DIM : (h + 1) * HEAD_DIM]], axis=1)
            kvh = jnp.concatenate([kv[here, lanes] for kv in kvs], axis=0)
            at_p = (i * heads + h) * BLOCK
            p = probs[at_p : at_p + BLOCK, :]
            pf = p.astype(f32)
            dp = nt(dhead, kvh)
            delta = jnp.sum(pf * dp, axis=-1, keepdims=True)
            ds = (pf * (dp - delta)).astype(bf16)
            dqs.append((nn(ds, kvh) * SCALE)[:, :HEAD_DIM].astype(bf16))
            left = jnp.concatenate([q[here, lanes], dhead], axis=0)
            dkv = tn(left, jnp.concatenate([ds, p], axis=0)).astype(bf16)
            for j in range(n_blk):
                target = keep if j % 2 == 0 else send
                target[j // 2, i, lanes, :] = dkv[:, j * BLOCK : (j + 1) * BLOCK]
        dq_out[i * BLOCK : (i + 1) * BLOCK, :] = jnp.concatenate(dqs, axis=1)


def input_kernel(dq, keep, recv, far, wq_t, wk_t, wv_t, part, dkv_t, sums):
    total = keep[0].astype(f32) + recv[0].astype(f32) + far[...].astype(f32)
    lows = [total[i].astype(bf16) for i in range(2)]
    low = jnp.concatenate([v.T for v in lows], axis=0)
    grad = nn(dq[...], wq_t[...]) + nn(low, both_rows(wk_t, wv_t))
    part[...] = grad.astype(bf16)
    dkv_t[...] = jnp.concatenate(lows, axis=1)
    width = sums.shape[1]
    one = col_sum(dq[...].astype(f32))
    two = col_sum(low.astype(f32))
    sums[...] = rows8(
        jnp.concatenate([one, jnp.zeros((1, width - one.shape[1]), f32)], axis=1),
        jnp.concatenate([two, jnp.zeros((1, width - two.shape[1]), f32)], axis=1),
    )


def pick(first, one, other):
    return jnp.where(first, one, other)


def join(values, axis=0):
    return jnp.concatenate(list(values), axis=axis)


def ordered_sum(at, parts, held):
    for i, part in enumerate(parts):
        held[row_at(at, i)] = part.astype(f32)
    total = held[0]
    for r in range(1, len(parts)):
        total = total + held[r]
    return total


def ffn_grad_kernel(m, at, *refs):
    low, act, act_far, dffn, dinner, dinner_far = (refs[2 * i : 2 * i + 2] for i in range(6))
    keep, send = refs[12:]
    first = at[1] == 0
    both = lambda pair: join(x[...] for x in pair)
    lows, dffns = both(low), both(dffn)
    rows = lows.shape[1] // m
    for q, (acts, dinners) in enumerate(((both(act), both(dinner)), (both(act_far), both(dinner_far)))):
        for target, one in ((keep, first), (send, jnp.logical_not(first))):
            main = tn(pick(one, lows, acts), pick(one, dinners, dffns)).astype(bf16)
            for i in range(m):
                target[i, q] = main[i * rows : (i + 1) * rows]


def attend_grad_kernel(m, at, tok, hp_late, *refs):
    shares, (dq, dkv_t, sums) = refs[:4], (refs[4 + 2 * i : 6 + 2 * i] for i in range(3))
    keep, send, held = refs[10:]
    first = at[1] == 0
    toks = join(chunk_of(tok, row_at(at, i), BLOCK) for i in range(4))
    heads = join(unpack(hp_late[i * PACKED : (i + 1) * PACKED, :]) for i in (2, 3, 0, 1))
    g_out = tn(heads, join(x[:BLOCK, :] for x in shares))
    g_q = tn(join(x[...] for x in dq), toks)
    g_kv = nn(join((x[...] for x in dkv_t), axis=1), toks)
    one = join([g_out, g_q]).astype(bf16)
    two = g_kv.astype(bf16)
    half = two.shape[0]
    tails = [x[BLOCK : BLOCK + 16, :].astype(f32) for x in shares]
    norm = ordered_sum(at, [x[:8] for x in tails], held)
    total = sums[0][...] + sums[1][...]
    inner = tails[0][6:7] + tails[1][6:7] + tails[2][7:8] + tails[3][7:8]
    norm = join([norm[:6], inner, jnp.zeros_like(inner)])
    rest = keep.shape[0] - half
    tail = join([norm, total, jnp.zeros((rest - 16, total.shape[1]), f32)]).astype(bf16)
    keep[:half, :] = pick(first, one, two)
    keep[half:, :] = tail
    send[:half, :] = pick(first, two, one)
    send[half:, :] = tail


def share_kernel(total1, near1, *refs):
    parts, share = refs[:-1], refs[-1]
    rows = near1.shape[0]
    share[:rows, :] = (total1[0].astype(f32) + near1[...].astype(f32)).astype(bf16)
    total = parts[0][...].astype(f32)
    for part in parts[1:]:
        total = total + part[...].astype(f32)
    share[rows:, :] = total.astype(bf16)


def widen(at, members, mine, other, g_in, g_outer, wide, sems):
    first = at[1] == 0
    rows = wide.shape[2]
    copies = []
    for c, s in enumerate(members):
        here = pl.ds(pl.multiple_of((at[3] ^ s) * rows, rows), rows)
        a, b = mine[c][:rows, :], other[c][:rows, :]
        wide[0, c] = pick(first, a, b).astype(f32)
        wide[1, c] = pick(first, b, a).astype(f32)
        for k, ref in enumerate((g_in, g_outer)):
            copies.append(pltpu.make_async_copy(wide.at[k, c], ref.at[here, :], sems.at[2 * c + k]))
            copies[-1].start()
    return copies


def early_kernel(m, at, *refs):
    count = m - 1
    for copy in widen(at, range(count), refs[:count], refs[count : 2 * count], *refs[2 * count :]):
        copy.wait()


def final_kernel(m, at, *refs):
    mine, other = refs[:m], refs[m : 2 * m]
    g_in, g_outer, g_out, g_q, g_k, g_v, *vectors, packed, wide, sems = refs[2 * m + 2 :]
    first = at[1] == 0
    rows = wide.shape[2]
    copies = widen(at, [m - 1], mine[m - 1 :], other[m - 1 :], g_in, g_outer, wide, sems)
    for s in range(m):
        i = at[3] ^ s
        packed[0, i] = pick(first, mine[s][rows:, :], other[s][rows:, :])
        packed[1, i] = pick(first, other[s][rows:, :], mine[s][rows:, :])
    width = g_q.shape[0]
    one = join(packed[0, i] for i in range(m)).astype(f32)
    two = join(packed[1, i] for i in range(m)).astype(f32)
    g_out[...] = one[:width]
    g_q[...] = one[width : 2 * width]
    tail = one[2 * width : 2 * width + 16]
    values = []
    for h in range(width // HEAD_DIM):
        part = slice(h * HEAD_DIM, (h + 1) * HEAD_DIM)
        g_k[part, :] = two[h * LANES : h * LANES + HEAD_DIM]
        g_v[part, :] = two[h * LANES + HEAD_DIM : (h + 1) * LANES]
        values.append(tail[9:10, h * LANES + HEAD_DIM : (h + 1) * LANES])
    b_q, b_v = vectors[7:]
    for i, ref in enumerate(vectors[:7]):
        ref[...] = tail[i]
    b_q[...] = tail[8, :width]
    b_v[...] = jnp.concatenate(values, axis=1)[0]
    for copy in copies:
        copy.wait()


def rows_kernel(at, *refs):
    out = refs[-1]
    rows = [v[i * BLOCK : (i + 1) * BLOCK, :] for v in refs[:-1] for i in range(v.shape[0] // BLOCK)]
    for i, value in enumerate(rows):
        out[row_at(at, i)] = value


def solution(mesh):
    n_dp = mesh.shape["dp"]
    n_blk = mesh.shape["blk"]
    n = mesh.shape["tensor"]
    half_blk = n_blk // 2
    m = n_dp * half_blk

    def swap(v, bit):
        return lax.ppermute(v, "tensor", [(i, i ^ bit) for i in range(n)])

    def flip(v, bit):
        return lax.ppermute(v, "blk", [(i, i ^ bit) for i in range(n_blk)])

    def flip_member(v, s):
        perm = []
        for dp in range(n_dp):
            for blk in range(n_blk):
                i = (dp * half_blk + blk // 2) ^ s
                to = (i // half_blk) * n_blk + (i % half_blk) * 2 + blk % 2
                perm.append((dp * n_blk + blk, to))
        return lax.ppermute(v, ("dp", "blk"), perm)

    def share_pieces(keep, recv, member):
        def piece(s):
            mine = lax.dynamic_index_in_dim(keep, member ^ s, 0, keepdims=False)
            theirs = lax.dynamic_index_in_dim(recv, member ^ s, 0, keepdims=False)
            return (mine.astype(f32) + theirs.astype(f32)).astype(bf16)

        return [piece(s) for s in range(m)]

    def add(own, got):
        total = own.astype(f32)
        for part in got:
            total = total + part.astype(f32)
        return total.astype(bf16)

    def body(
        tokens, bucket_ids, seq_lengths, w_query, b_query, w_key, w_value, b_value, w_out, b_out,
        norm1_gain, norm1_bias, w_inner, b_inner, w_outer, b_outer, norm2_gain, norm2_bias,
        cotangent,
    ):
        row_count, block, width = tokens.shape
        count = row_count * block
        local = w_query.shape[1]
        heads = local // HEAD_DIM
        lanes = heads * LANES
        units = w_inner.shape[1]
        blk = lax.axis_index("blk").astype(i32)
        z = lax.axis_index("tensor").astype(i32)
        core = blk % 2
        member = (lax.axis_index("dp") * half_blk + blk // 2).astype(i32)
        cut_at = (lax.axis_index("dp") % 2) * n_blk + blk
        at = jnp.stack([z, core, blk, member, cut_at]).astype(i32)
        tok = tokens.reshape(count, width)
        cot = cotangent.reshape(count, width)
        row = lambda v: v.reshape(1, -1)
        wq_t, wk_t, wv_t = w_query.T, w_key.T, w_value.T
        fence = lax.optimization_barrier

        part = local // 4
        piece_rows = (width + units) // 8
        kv, piece, out_piece = pl.pallas_call(
            front_kernel,
            out_shape=(
                near((count, lanes), bf16), near((piece_rows + part, width), bf16),
                near((part, width), bf16),
            ),
            in_specs=[SMEM] + [HBM] * 6 + [VMEM],
            out_specs=(VMEM,) * 3,
            scratch_shapes=[
                pltpu.VMEM((count, width), bf16), pltpu.VMEM((local, width), bf16),
                pltpu.VMEM((local, width), bf16), pltpu.SemaphoreType.DMA((6,)),
            ],
            compiler_params=pltpu.CompilerParams(vmem_limit_bytes=16 * MIB),
            name="front",
        )(at, *[pltpu.with_memory_space_constraint(v, pltpu.HBM) for v in (tok, wk_t, wv_t, w_inner, w_outer, w_out)], row(b_value))
        kv, piece, out_piece, b_far = fence((kv, piece, out_piece, b_inner))
        kv_far = flip(kv, 2)
        kv_core = flip(kv, 1)
        pieces = [swap(piece, 1)] + [swap(out_piece, s) for s in range(2, n)]
        b_inner_far = swap(b_far, 1)
        kv_far, b_inner_far, *pieces = fence((kv_far, b_inner_far, *pieces))
        kv_both = flip(kv_far, 1)
        own_piece = jnp.concatenate(pieces, axis=0)
        ffn_piece = pieces[0][:piece_rows]

        def across(v, dp_bit, blk_bit):
            there = lambda i: ((i // n_blk) ^ dp_bit) * n_blk + ((i % n_blk) ^ blk_bit)
            return lax.ppermute(v, ("dp", "blk"), [(i, there(i)) for i in range(n_dp * n_blk)])

        arrived = {4: across(ffn_piece, 1, 0), 6: across(ffn_piece, 1, 2)}
        arrived |= {0: own_piece, 2: across(own_piece, 0, 2)}

        q = call(q_kernel, near((count, lanes), bf16), "query_rows", (tok, wq_t, row(b_query)), us=0.5)
        kvs = [kv, kv_core, kv_far, kv_both]

        prob_rows = 2 * heads * BLOCK
        hp_other, hp_mine, probs_other, probs_mine, hp_late = pl.pallas_call(
            functools.partial(attend_kernel, n_blk, (2, 3, 0, 1)),
            out_shape=(near((2 * PACKED, LANES), bf16),) * 2
            + (pltpu.HBM((prob_rows, n_blk * BLOCK), bf16),) * 2
            + (pltpu.HBM((4 * PACKED, LANES), bf16),),
            in_specs=[SMEM] * 3 + [VMEM] * (1 + n_blk),
            out_specs=(VMEM,) * 2 + (HBM,) * 3,
            scratch_shapes=[
                pltpu.VMEM((2 * prob_rows, n_blk * BLOCK), bf16), pltpu.SemaphoreType.DMA((6,)),
            ],
            compiler_params=pltpu.CompilerParams(vmem_limit_bytes=16 * MIB),
            cost_estimate=pl.CostEstimate(
                flops=int(ATTEND_US * FLOPS_US), bytes_accessed=1, transcendentals=0
            ),
            name="attend",
        )(at, bucket_ids, seq_lengths, q, *kvs)
        hps = {0: hp_mine, 1: swap(hp_other, 1), 2: swap(hp_mine, 2), 3: swap(hp_other, 3)}
        held = [arrived[2], arrived[4], arrived[6]]
        hps[1], hps[2], hps[3], *held = fence((hps[1], hps[2], hps[3], *held))
        arrived[2], arrived[4], arrived[6] = held
        arrived |= {j + 1: flip(v, 1) for j, v in arrived.items()}
        w_out_all, w_inner_far, w_outer_far = call(
            functools.partial(weights_kernel, n),
            (near((n * local, width), bf16), near(w_inner.shape, bf16), near(w_outer.shape, bf16)),
            "far_weights",
            (at, w_out, *[arrived[j] for j in range(8)]),
            us=2.2,
            scalars=1,
        )

        chunk = lambda rows, dt: near((rows, width), dt)
        gains1 = (row(norm1_gain), row(norm1_bias))

        def ffn(i, heads_in):
            return call(
                functools.partial(ffn_kernel, n, i),
                (
                    chunk(BLOCK, bf16), chunk(BLOCK, f32), near((BLOCK, LANES), f32),
                    chunk(BLOCK, bf16), near((BLOCK, units), bf16), near((BLOCK, units), bf16),
                    near((2 * BLOCK, units), bf16),
                )
                + ((near((n * PACKED, LANES), bf16),) if i == 0 else ()),
                "ffn",
                (
                    at, tok, w_out_all, row(b_out), *gains1, w_inner, w_inner_far, row(b_inner),
                    row(b_inner_far), w_outer, w_outer_far, *heads_in,
                ),
                us=2.4,
                scalars=1,
                scratch=[pltpu.VMEM((n, BLOCK, width), f32)],
            )

        *row0, second_heads = ffn(0, [hps[s] for s in range(n)])
        parts, n1s, s1s, lows, acts, acts_far, slopes = map(list, zip(row0, ffn(1, [second_heads])))
        theirs = [swap(v, 2) for v in parts]

        def ffn_back(i):
            return call(
                functools.partial(ffn_back_kernel, i),
                (
                    chunk(BLOCK, bf16), chunk(BLOCK, bf16), near((BLOCK, units), bf16),
                    near((BLOCK, units), bf16), chunk(BLOCK, bf16), chunk(BLOCK, f32), chunk(8, f32),
                ),
                "ffn_back",
                (
                    at, cot, n1s[i], slopes[i], parts[i], theirs[i], *gains1, row(b_outer),
                    row(norm2_gain), row(norm2_bias), w_inner, w_inner_far, w_outer, w_outer_far,
                ),
                us=2.7,
                scalars=1,
            )

        outs, dffns, dinners, dinners_far, parts2, dres2, sums2 = map(list, zip(*[ffn_back(i) for i in range(2)]))
        theirs2 = [swap(v, 2) for v in parts2]
        keep1, send1 = call(
            functools.partial(ffn_grad_kernel, m),
            (near((m, 2, width // m, width), bf16),) * 2,
            "ffn_grads",
            (at, *lows, *acts, *acts_far, *dffns, *dinners, *dinners_far),
            us=FILL_US,
            vmem=24,
            scalars=1,
        )
        recv1 = flip(send1, 1)
        pieces1 = share_pieces(keep1, recv1, member)

        def norm_back(i):
            return call(
                functools.partial(norm_back_kernel, n),
                (
                    chunk(BLOCK, f32), chunk(BLOCK + 16, bf16), near((PACKED, LANES), bf16),
                    near((PACKED, LANES), bf16),
                ),
                "norm_back",
                (at, parts2[i], theirs2[i], dres2[i], n1s[i], s1s[i], gains1[0], w_out_all, sums2[i]),
                us=1.2,
                scalars=1,
            )

        dres1, shares, dheads, dheads_far = map(list, zip(*[norm_back(i) for i in range(2)]))
        dheads += [swap(v, 1) for v in dheads_far]
        shares += [swap(v, 1) for v in shares]
        outs += [swap(v, 1) for v in outs]

        def attend_back(ids, probs, *packed):
            return call(
                functools.partial(attend_back_kernel, n_blk, ids),
                (
                    near((2 * BLOCK, local), bf16), near((half_blk, 2, lanes, BLOCK), bf16),
                    near((half_blk, 2, lanes, BLOCK), bf16),
                ),
                "attend_back",
                (at, *packed, q, probs, *kvs),
                scalars=1,
                us=BACK_US,
            )

        own = attend_back((0, 1), probs_mine, dheads[0], dheads[1])
        after, dheads[2], dheads[3], pieces1 = fence((own[1], dheads[2], dheads[3], pieces1))
        own = (own[0], after, own[2])
        other = attend_back((2, 3), probs_other, dheads[2], dheads[3])

        def exchange(third):
            _, send, keep = third
            recv = flip(send, 1)
            return recv, (keep[1].astype(f32) + recv[1].astype(f32)).astype(bf16)

        def input_part(third, recv, far, us):
            dq, _, keep = third
            return call(
                input_kernel,
                (chunk(2 * BLOCK, bf16), near((lanes, 2 * BLOCK), bf16), chunk(8, f32)),
                "input_part",
                (dq, keep, recv, far, wq_t, wk_t, wv_t),
                us=us,
            )

        recv_own, sum_own = exchange(own)
        recv_other, sum_other = exchange(other)
        far_own, far_other = flip(sum_own, 2), flip(sum_other, 2)
        far_own, far_other, pieces1 = fence((far_own, far_other, pieces1))
        part, *late = input_part(other, recv_other, far_other, 1.0)
        part, pieces1 = fence((part, pieces1))
        from_near, *ends = fence((swap(part, 1), *shares[2:]))
        shares[2:] = ends
        got1 = [flip_member(v, s) for s, v in enumerate(pieces1[1:], 1)]
        part_own, dkv_own, sums_own = input_part(own, recv_own, far_own, INPUT_US)
        pair = (part_own.astype(f32) + from_near.astype(f32)).astype(bf16)

        rows2 = 2 * local + 16
        rows2 += -rows2 % (16 * m)
        hp_late, _ = fence((hp_late, pair))
        keep2, send2 = call(
            functools.partial(attend_grad_kernel, m),
            (chunk(rows2, bf16), chunk(rows2, bf16)),
            "attend_grads",
            (
                at, tok, hp_late, *shares, own[0], other[0], dkv_own, late[0], sums_own,
                late[1],
            ),
            us=GRADS_US,
            scalars=1,
            scratch=[pltpu.VMEM((n, 8, width), f32)],
        )
        by_member = lambda v: v.reshape(m, rows2 // m, width)
        pieces2 = share_pieces(by_member(keep2), by_member(flip(send2, 1)), member)
        got2 = [flip_member(v, s) for s, v in enumerate(pieces2[1:], 1)]
        got1, _, _ = fence((got1, keep2, pair))
        total1 = fence(add(pieces1[0], got1))
        near1 = swap(total1[1], 1)
        crossed, *ends = fence((swap(pair, 2), *outs[2:]))
        outs[2:] = ends
        near1, got2 = fence((near1, got2))
        d_tok = pair.astype(f32) + crossed.astype(f32) + jnp.concatenate(dres1, axis=0)
        d_tok = d_tok.astype(bf16)
        share = call(
            share_kernel,
            chunk(width // m + rows2 // m, bf16),
            "grad_share",
            (total1, near1, pieces2[0], *got2),
            us=0.5,
        )
        shares_in = [flip_member(share, k) for k in range(1, m)]
        shares_in[0], d_far = fence((shares_in[0], swap(d_tok, 1)))
        d_toks = [d_tok, d_far]
        assemble = lambda parts, name: call(
            rows_kernel,
            shape((row_count, block, width), bf16),
            name,
            (at, *parts),
            us=1.5,
            scalars=1,
        )
        output = assemble(outs, "output_rows")
        d_tokens = assemble(d_toks, "input_grad_rows")
        mine = [share] + shares_in
        held, _, _ = fence((shares_in[0], output, d_tokens))
        others = [flip(v, 1) for v in [share, held] + shares_in[1:]]
        vector = shape((width,), f32)
        short = shape((local,), f32)
        wide = shape((local, width), f32)
        squares = (pltpu.HBM((width, units), f32), pltpu.HBM((units, width), f32))
        rows1 = width // m

        def grads_out(kernel, outs, arrays, before, members, scratch, us, name):
            return pl.pallas_call(
                kernel,
                out_shape=squares + outs,
                in_specs=[SMEM] + [VMEM] * len(arrays) + [HBM] * len(before),
                out_specs=(HBM,) * 2 + (VMEM,) * len(outs),
                scratch_shapes=scratch
                + [pltpu.VMEM((2, members, rows1, width), f32), pltpu.SemaphoreType.DMA((2 * members,))],
                input_output_aliases={1 + len(arrays) + k: k for k in range(len(before))},
                compiler_params=pltpu.CompilerParams(vmem_limit_bytes=24 * MIB),
                cost_estimate=pl.CostEstimate(
                    flops=int(us * FLOPS_US), bytes_accessed=1, transcendentals=0
                ),
                name=name,
            )(at, *arrays, *before)

        early = grads_out(
            functools.partial(early_kernel, m), (), (*mine[:-1], *others[:-1]), (), m - 1, [], 2.0,
            "early_grads",
        )
        (
            g_w_inner, g_w_outer, g_w_out, g_q, g_k, g_v, g_gain1, g_bias1, g_b_out, g_gain2, g_bias2,
            g_b_outer, g_b_inner, g_b_query, g_b_value,
        ) = grads_out(
            functools.partial(final_kernel, m), (wide,) * 4 + (vector,) * 7 + (short,) * 2,
            (*mine, *others), tuple(early), 1, [pltpu.VMEM((2, m, rows2 // m, width), bf16)], 2.0,
            "grads_out",
        )
        return (
            output, d_tokens, g_q.T, g_b_query, g_k.T, g_v.T, g_b_value, g_w_out, g_b_out, g_gain1,
            g_bias1, g_w_inner, g_b_inner, g_w_outer, g_b_outer, g_gain2, g_bias2,
        )

    spread, cols, vec, rows_ = P("dp", "blk", None), P(None, "tensor"), P("tensor"), P("tensor", None)
    return jax.shard_map(
        body,
        mesh=mesh,
        in_specs=(
            spread, P("dp"), P("dp", None), cols, vec, cols, cols, vec, rows_, P(), P(), P(),
            cols, vec, rows_, P(), P(), P(), spread,
        ),
        out_specs=(
            spread, spread, cols, vec, cols, cols, vec, rows_, P(), P(), P(), cols, vec, rows_,
            P(), P(), P(),
        ),
        check_vma=False,
    )
```

```python
import functools

import jax
import jax.numpy as jnp
from jax import lax
from jax.experimental import pallas as pl
from jax.experimental.pallas import tpu as pltpu
from jax.sharding import PartitionSpec as P

HEAD_DIM = 64
BLOCK = 128
LANES = 128
SCALE = HEAD_DIM**-0.5
EPS = 1e-12
f32 = jnp.float32
bf16 = jnp.bfloat16
i32 = jnp.int32
MIB = 1 << 20
FLOPS_US = 1e9
ATTEND_US = 50.0
BACK_US = 50.0
FILL_US = 50.0
INPUT_US = 10.0
GRADS_US = 4.0
PACKED = BLOCK + HEAD_DIM


def nn(a, b):
    return lax.dot_general(a, b, (((1,), (0,)), ((), ())), preferred_element_type=f32)


def nt(a, b):
    return lax.dot_general(a, b, (((1,), (1,)), ((), ())), preferred_element_type=f32)


def tn(a, b):
    return lax.dot_general(a, b, (((0,), (0,)), ((), ())), preferred_element_type=f32)


def mean(v):
    return jnp.mean(v, axis=-1, keepdims=True)


def col_sum(v):
    return jnp.sum(v, axis=0, keepdims=True)


def row_at(at, i):
    half = at[0] % 2
    return 2 * half + i if i < 2 else 2 * (1 - half) + (i - 2)


def rows8(*rows):
    width = rows[0].shape[1]
    pad = jnp.zeros((8 - len(rows), width), f32)
    return jnp.concatenate(rows + (pad,), axis=0)


def shape(dims, dtype):
    return jax.ShapeDtypeStruct(dims, dtype)


def near(dims, dtype):
    return pltpu.VMEM(dims, dtype)


SMEM = pl.BlockSpec(memory_space=pltpu.SMEM)
VMEM = pl.BlockSpec(memory_space=pltpu.VMEM)
HBM = pl.BlockSpec(memory_space=pltpu.HBM)


def call(kernel, outs, name, args, scalars=0, us=1.0, vmem=16, scratch=()):
    return pl.pallas_call(
        kernel,
        out_shape=outs,
        in_specs=[SMEM] * scalars + [VMEM] * (len(args) - scalars),
        out_specs=jax.tree.map(lambda _: VMEM, outs),
        scratch_shapes=list(scratch),
        compiler_params=pltpu.CompilerParams(vmem_limit_bytes=vmem * MIB),
        cost_estimate=pl.CostEstimate(flops=int(us * FLOPS_US), bytes_accessed=1, transcendentals=0),
        name=name,
    )(*args)


def chunk_of(ref, c, rows):
    return ref[pl.ds(pl.multiple_of(c * rows, rows), rows), :]


def both_rows(wk_t, wv_t):
    rows = []
    for h in range(wk_t.shape[0] // HEAD_DIM):
        part = slice(h * HEAD_DIM, (h + 1) * HEAD_DIM)
        rows += [wk_t[part, :], wv_t[part, :]]
    return jnp.concatenate(rows, axis=0)


def front_kernel(at, tok, wk_t, wv_t, w_in, w_outer, w_out, bv, kv, piece, out_piece, tok_v, wk_v, wv_v, sems):
    tail = out_piece.shape[0]
    half = (piece.shape[0] - tail) // 2

    def part(ref, index, size):
        return ref.at[pl.ds(pl.multiple_of(index * size, 16), size), :]

    moves = [
        (tok, tok_v),
        (wk_t, wk_v),
        (wv_t, wv_v),
        (part(w_in, at[4], half), piece.at[pl.ds(0, half), :]),
        (part(w_outer, at[4], half), piece.at[pl.ds(half, half), :]),
        (part(w_out, at[2], tail), out_piece),
    ]
    copies = [pltpu.make_async_copy(a, b, sems.at[i]) for i, (a, b) in enumerate(moves)]
    for copy in copies:
        copy.start()
    for copy in copies[:3]:
        copy.wait()
    bias = []
    for h in range(wk_v.shape[0] // HEAD_DIM):
        bias += [jnp.zeros((1, HEAD_DIM), f32), bv[:, h * HEAD_DIM : (h + 1) * HEAD_DIM]]
    kv[...] = (nt(tok_v[...], both_rows(wk_v, wv_v)) + jnp.concatenate(bias, axis=1)).astype(bf16)
    for copy in copies[3:]:
        copy.wait()
    piece[2 * half :, :] = out_piece[...]


def q_kernel(tok, wq_t, bq, q):
    heads = wq_t.shape[0] // HEAD_DIM
    full = (nt(tok[...], wq_t[...]) + bq[...]).astype(bf16) * jnp.asarray(SCALE, bf16)
    zero = jnp.zeros((full.shape[0], HEAD_DIM), bf16)
    cols = []
    for h in range(heads):
        cols += [full[:, h * HEAD_DIM : (h + 1) * HEAD_DIM], zero]
    q[...] = jnp.concatenate(cols, axis=1)


def weights_kernel(n, at, w_out, *refs):
    pieces, (w_out_all, w_in_far, w_outer_far) = refs[:8], refs[8:]
    z = at[0]
    local = w_out.shape[0]
    part = local // 4
    rows = w_in_far.shape[0] // 8

    def put(ref, base, value):
        size = value.shape[0]
        ref[pl.ds(pl.multiple_of(base, 16), size), :] = value

    put(w_out_all, z * local, w_out[...])
    for j, piece in enumerate(pieces):
        put(w_in_far, (at[4] ^ j) * rows, piece[:rows, :])
        put(w_outer_far, (at[4] ^ j) * rows, piece[rows : 2 * rows, :])
        for s in range(1, n if j < 4 else 0):
            base = 2 * rows + (s - 1) * part
            put(w_out_all, (z ^ s) * local + (at[2] ^ j) * part, piece[base : base + part, :])


def attend_kernel(n_blk, ids, at, bucket, lens, q, *refs):
    kvs = refs[:n_blk]
    hp_first, hp_second, probs_first, probs_second, hp_late, held, sems = refs[n_blk:]
    copies = []
    heads = q.shape[1] // LANES
    b = at[2]
    q_at = lax.broadcasted_iota(i32, (BLOCK, 1), 0)
    k_at = lax.broadcasted_iota(i32, (1, BLOCK), 1)
    for order, row in enumerate(ids):
        hp, probs = ((hp_first, probs_first), (hp_second, probs_second))[order // 2]
        i = order % 2
        r = row_at(at, row)
        bk = bucket[r]
        size = BLOCK << bk
        slot = b >> bk
        limit = lens[r, slot]
        q_in = jnp.where(q_at + (b * BLOCK - slot * size) < limit, 1, 0)
        k_in = []
        for j in range(n_blk):
            kb = b ^ j
            k_slot = kb >> bk
            inside = jnp.where(k_at + (kb * BLOCK - k_slot * size) < limit, 1, 0)
            k_in.append(jnp.where(k_slot == slot, inside, 2))
        allowed = q_in == jnp.concatenate(k_in, axis=1)
        here = pl.ds(pl.multiple_of(r * BLOCK, BLOCK), BLOCK)
        outs = []
        for h in range(heads):
            lanes = slice(h * LANES, (h + 1) * LANES)
            kvh = jnp.concatenate([kv[here, lanes] for kv in kvs], axis=0)
            scores = jnp.where(allowed, nt(q[here, lanes], kvh), -1e30)
            weights = jnp.exp(scores - jnp.max(scores, axis=-1, keepdims=True))
            total = jnp.sum(weights, axis=-1, keepdims=True)
            p = (weights / total).astype(bf16)
            held[(order * heads + h) * BLOCK : (order * heads + h + 1) * BLOCK, :] = p
            outs.append(nn(p, kvh)[:, HEAD_DIM:].astype(bf16))
        base = i * PACKED
        hp[base : base + BLOCK, :] = jnp.concatenate(outs[:2], axis=1)
        hp[base + BLOCK : base + PACKED, :] = jnp.concatenate(
            [outs[2][:HEAD_DIM], outs[2][HEAD_DIM:]], axis=1
        )
        size = heads * BLOCK
        copies.append(
            pltpu.make_async_copy(
                held.at[pl.ds(order * size, size), :], probs.at[pl.ds(i * size, size), :], sems.at[order]
            )
        )
        copies[-1].start()
    for i, hp in enumerate((hp_first, hp_second)):
        rows = hp.shape[0]
        copies.append(pltpu.make_async_copy(hp, hp_late.at[pl.ds(i * rows, rows), :], sems.at[4 + i]))
        copies[-1].start()
    for copy in copies:
        copy.wait()


def unpack(h):
    odd = jnp.concatenate([h[BLOCK:, :HEAD_DIM], h[BLOCK:, HEAD_DIM:]], axis=0)
    return jnp.concatenate([h[:BLOCK, :], odd], axis=1)


def pack(v):
    odd = jnp.concatenate([v[:HEAD_DIM, LANES:], v[HEAD_DIM:, LANES:]], axis=1)
    return jnp.concatenate([v[:, :LANES], odd], axis=0)


def gelu_and_slope(inner):
    cdf = 0.5 * (1.0 + lax.erf(inner * (0.5**0.5)))
    slope = cdf + inner * (0.3989422804014327 * jnp.exp(-0.5 * inner * inner))
    return (inner * cdf).astype(bf16), slope.astype(bf16)


def ffn_kernel(
    n, i, at, tok, w_out, b_out, g1, b1, w_in, w_in_far, b_in, b_in_far, w_outer, w_outer_far, *refs
):
    hps = refs[:n] if len(refs) > n + 7 + 1 else [refs[0].at[pl.ds(s * PACKED, PACKED), :] for s in range(n)]
    refs = refs if len(refs) > n + 7 + 1 else refs[:1] * n + refs[1:]
    part, n1_out, s1_out, low_out, act_out, act_far_out, slopes, *rest, held = refs[n:]
    z = at[0]
    local = w_out.shape[0] // n
    for s in range(n):
        j = z ^ s
        held[j] = nn(unpack(hps[s][:PACKED, :]), chunk_of(w_out, j, local))
        if rest:
            rest[0][s * PACKED : (s + 1) * PACKED, :] = hps[s][PACKED:, :]
    attn = held[0]
    for j in range(1, n):
        attn = attn + held[j]
    resid = chunk_of(tok, row_at(at, i), BLOCK).astype(f32) + (attn + b_out[...])
    center = resid - mean(resid)
    s1 = lax.rsqrt(mean(center * center) + EPS)
    n1 = center * s1
    low = (n1 * g1[...] + b1[...]).astype(bf16)
    act, slope = gelu_and_slope(nn(low, w_in[...]) + b_in[...])
    act_far, slope_far = gelu_and_slope(nn(low, w_in_far[...]) + b_in_far[...])
    part[...] = (nn(act, w_outer[...]) + nn(act_far, w_outer_far[...])).astype(bf16)
    n1_out[...] = n1
    s1_out[...] = jnp.broadcast_to(s1, s1_out.shape)
    low_out[...] = low
    act_out[...] = act
    act_far_out[...] = act_far
    slopes[:BLOCK, :] = slope
    slopes[BLOCK:, :] = slope_far


def ffn_back_kernel(
    i, at, cot, n1, slopes, mine, theirs, g1, b1, b_outer, g2, b2, w_in, w_in_far, w_outer,
    w_outer_far, out, dffn_out, dinner_out, dinner_far_out, part, dres2_out, sums
):
    hidden = n1[...] * g1[...] + b1[...]
    ffn = mine[...].astype(f32) + theirs[...].astype(f32)
    resid = hidden + (ffn + b_outer[...])
    center = resid - mean(resid)
    s2 = lax.rsqrt(mean(center * center) + EPS)
    n2 = center * s2
    ct = chunk_of(cot, row_at(at, i), BLOCK).astype(f32)
    dn = ct * g2[...]
    dres2 = s2 * (dn - mean(dn) - n2 * mean(dn * n2))
    dffn = dres2.astype(bf16)
    dinner = (nt(dffn, w_outer[...]) * slopes[:BLOCK, :].astype(f32)).astype(bf16)
    dinner_far = (nt(dffn, w_outer_far[...]) * slopes[BLOCK:, :].astype(f32)).astype(bf16)
    part[...] = (nt(dinner, w_in[...]) + nt(dinner_far, w_in_far[...])).astype(bf16)
    dres2_out[...] = dres2
    dinner_out[...] = dinner
    out[...] = (n2 * g2[...] + b2[...]).astype(bf16)
    dffn_out[...] = dffn
    dinner_far_out[...] = dinner_far
    sums[...] = rows8(
        col_sum(ct * n2), col_sum(ct), col_sum(dffn.astype(f32)),
        col_sum(dinner.astype(f32)), col_sum(dinner_far.astype(f32)),
    )


def norm_back_kernel(n, at, mine, theirs, dres2, n1, s1, g1, w_out, sums2, dres1_out, share, dh, dh_far):
    dhidden = (mine[...].astype(f32) + theirs[...].astype(f32)) + dres2[...]
    norm = n1[...]
    dn = dhidden * g1[...]
    dres1 = s1[:, :1] * (dn - mean(dn) - norm * mean(dn * norm))
    dattn = dres1.astype(bf16)
    dres1_out[...] = dres1
    share[:BLOCK, :] = dattn
    sums = jnp.concatenate(
        [col_sum(dhidden * norm), col_sum(dhidden), col_sum(dattn.astype(f32)), sums2[:5, :]], axis=0
    )
    share[BLOCK:, :] = jnp.concatenate([sums, jnp.zeros_like(sums)], axis=0).astype(bf16)
    local = w_out.shape[0] // n
    dh[...] = pack(nt(dattn, chunk_of(w_out, at[0], local)).astype(bf16))
    dh_far[...] = pack(nt(dattn, chunk_of(w_out, at[0] ^ 1, local)).astype(bf16))


def attend_back_kernel(n_blk, ids, at, first, second, q, probs, *refs):
    kvs = refs[:n_blk]
    dq_out, send, keep = refs[n_blk:]
    heads = q.shape[1] // LANES
    zero = jnp.zeros((BLOCK, HEAD_DIM), bf16)
    for i, packed in enumerate((first, second)):
        c = row_at(at, ids[i])
        here = pl.ds(pl.multiple_of(c * BLOCK, BLOCK), BLOCK)
        flat = unpack(packed[...])
        dqs = []
        for h in range(heads):
            lanes = slice(h * LANES, (h + 1) * LANES)
            dhead = jnp.concatenate([zero, flat[:, h * HEAD_DIM : (h + 1) * HEAD_DIM]], axis=1)
            kvh = jnp.concatenate([kv[here, lanes] for kv in kvs], axis=0)
            at_p = (i * heads + h) * BLOCK
            p = probs[at_p : at_p + BLOCK, :]
            pf = p.astype(f32)
            dp = nt(dhead, kvh)
            delta = jnp.sum(pf * dp, axis=-1, keepdims=True)
            ds = (pf * (dp - delta)).astype(bf16)
            dqs.append((nn(ds, kvh) * SCALE)[:, :HEAD_DIM].astype(bf16))
            left = jnp.concatenate([q[here, lanes], dhead], axis=0)
            dkv = tn(left, jnp.concatenate([ds, p], axis=0)).astype(bf16)
            for j in range(n_blk):
                target = keep if j % 2 == 0 else send
                target[j // 2, i, lanes, :] = dkv[:, j * BLOCK : (j + 1) * BLOCK]
        dq_out[i * BLOCK : (i + 1) * BLOCK, :] = jnp.concatenate(dqs, axis=1)


def input_kernel(dq, keep, recv, far, wq_t, wk_t, wv_t, part, dkv_t, sums):
    total = keep[0].astype(f32) + recv[0].astype(f32) + far[...].astype(f32)
    lows = [total[i].astype(bf16) for i in range(2)]
    low = jnp.concatenate([v.T for v in lows], axis=0)
    grad = nn(dq[...], wq_t[...]) + nn(low, both_rows(wk_t, wv_t))
    part[...] = grad.astype(bf16)
    dkv_t[...] = jnp.concatenate(lows, axis=1)
    width = sums.shape[1]
    one = col_sum(dq[...].astype(f32))
    two = col_sum(low.astype(f32))
    sums[...] = rows8(
        jnp.concatenate([one, jnp.zeros((1, width - one.shape[1]), f32)], axis=1),
        jnp.concatenate([two, jnp.zeros((1, width - two.shape[1]), f32)], axis=1),
    )


def pick(first, one, other):
    return jnp.where(first, one, other)


def join(values, axis=0):
    return jnp.concatenate(list(values), axis=axis)


def ordered_sum(at, parts, held):
    for i, part in enumerate(parts):
        held[row_at(at, i)] = part.astype(f32)
    total = held[0]
    for r in range(1, len(parts)):
        total = total + held[r]
    return total


def ffn_grad_kernel(m, at, *refs):
    low, act, act_far, dffn, dinner, dinner_far = (refs[2 * i : 2 * i + 2] for i in range(6))
    keep, send = refs[12:]
    first = at[1] == 0
    both = lambda pair: join(x[...] for x in pair)
    lows, dffns = both(low), both(dffn)
    rows = lows.shape[1] // m
    for q, (acts, dinners) in enumerate(((both(act), both(dinner)), (both(act_far), both(dinner_far)))):
        for target, one in ((keep, first), (send, jnp.logical_not(first))):
            main = tn(pick(one, lows, acts), pick(one, dinners, dffns)).astype(bf16)
            for i in range(m):
                target[i, q] = main[i * rows : (i + 1) * rows]


def attend_grad_kernel(m, at, tok, hp_late, *refs):
    shares, (dq, dkv_t, sums) = refs[:4], (refs[4 + 2 * i : 6 + 2 * i] for i in range(3))
    keep, send, held = refs[10:]
    first = at[1] == 0
    toks = join(chunk_of(tok, row_at(at, i), BLOCK) for i in range(4))
    heads = join(unpack(hp_late[i * PACKED : (i + 1) * PACKED, :]) for i in (2, 3, 0, 1))
    g_out = tn(heads, join(x[:BLOCK, :] for x in shares))
    g_q = tn(join(x[...] for x in dq), toks)
    g_kv = nn(join((x[...] for x in dkv_t), axis=1), toks)
    one = join([g_out, g_q]).astype(bf16)
    two = g_kv.astype(bf16)
    half = two.shape[0]
    tails = [x[BLOCK : BLOCK + 16, :].astype(f32) for x in shares]
    norm = ordered_sum(at, [x[:8] for x in tails], held)
    total = sums[0][...] + sums[1][...]
    inner = tails[0][6:7] + tails[1][6:7] + tails[2][7:8] + tails[3][7:8]
    norm = join([norm[:6], inner, jnp.zeros_like(inner)])
    rest = keep.shape[0] - half
    tail = join([norm, total, jnp.zeros((rest - 16, total.shape[1]), f32)]).astype(bf16)
    keep[:half, :] = pick(first, one, two)
    keep[half:, :] = tail
    send[:half, :] = pick(first, two, one)
    send[half:, :] = tail


def share_kernel(total1, near1, *refs):
    parts, share = refs[:-1], refs[-1]
    rows = near1.shape[0]
    share[:rows, :] = (total1[0].astype(f32) + near1[...].astype(f32)).astype(bf16)
    total = parts[0][...].astype(f32)
    for part in parts[1:]:
        total = total + part[...].astype(f32)
    share[rows:, :] = total.astype(bf16)


def widen(at, members, mine, other, g_in, g_outer, wide, sems):
    first = at[1] == 0
    rows = wide.shape[2]
    copies = []
    for c, s in enumerate(members):
        here = pl.ds(pl.multiple_of((at[3] ^ s) * rows, rows), rows)
        a, b = mine[c][:rows, :], other[c][:rows, :]
        wide[0, c] = pick(first, a, b).astype(f32)
        wide[1, c] = pick(first, b, a).astype(f32)
        for k, ref in enumerate((g_in, g_outer)):
            copies.append(pltpu.make_async_copy(wide.at[k, c], ref.at[here, :], sems.at[2 * c + k]))
            copies[-1].start()
    return copies


def early_kernel(m, at, *refs):
    count = m - 1
    for copy in widen(at, range(count), refs[:count], refs[count : 2 * count], *refs[2 * count :]):
        copy.wait()


def final_kernel(m, at, *refs):
    mine, other = refs[:m], refs[m : 2 * m]
    g_in, g_outer, g_out, g_q, g_k, g_v, *vectors, packed, wide, sems = refs[2 * m + 2 :]
    first = at[1] == 0
    rows = wide.shape[2]
    copies = widen(at, [m - 1], mine[m - 1 :], other[m - 1 :], g_in, g_outer, wide, sems)
    for s in range(m):
        i = at[3] ^ s
        packed[0, i] = pick(first, mine[s][rows:, :], other[s][rows:, :])
        packed[1, i] = pick(first, other[s][rows:, :], mine[s][rows:, :])
    width = g_q.shape[0]
    one = join(packed[0, i] for i in range(m)).astype(f32)
    two = join(packed[1, i] for i in range(m)).astype(f32)
    g_out[...] = one[:width]
    g_q[...] = one[width : 2 * width]
    tail = one[2 * width : 2 * width + 16]
    values = []
    for h in range(width // HEAD_DIM):
        part = slice(h * HEAD_DIM, (h + 1) * HEAD_DIM)
        g_k[part, :] = two[h * LANES : h * LANES + HEAD_DIM]
        g_v[part, :] = two[h * LANES + HEAD_DIM : (h + 1) * LANES]
        values.append(tail[9:10, h * LANES + HEAD_DIM : (h + 1) * LANES])
    b_q, b_v = vectors[7:]
    for i, ref in enumerate(vectors[:7]):
        ref[...] = tail[i]
    b_q[...] = tail[8, :width]
    b_v[...] = jnp.concatenate(values, axis=1)[0]
    for copy in copies:
        copy.wait()


def rows_kernel(at, *refs):
    out = refs[-1]
    rows = [v[i * BLOCK : (i + 1) * BLOCK, :] for v in refs[:-1] for i in range(v.shape[0] // BLOCK)]
    for i, value in enumerate(rows):
        out[row_at(at, i)] = value


def solution(mesh):
    n_dp = mesh.shape["dp"]
    n_blk = mesh.shape["blk"]
    n = mesh.shape["tensor"]
    half_blk = n_blk // 2
    m = n_dp * half_blk

    def swap(v, bit):
        return lax.ppermute(v, "tensor", [(i, i ^ bit) for i in range(n)])

    def flip(v, bit):
        return lax.ppermute(v, "blk", [(i, i ^ bit) for i in range(n_blk)])

    def flip_member(v, s):
        perm = []
        for dp in range(n_dp):
            for blk in range(n_blk):
                i = (dp * half_blk + blk // 2) ^ s
                to = (i // half_blk) * n_blk + (i % half_blk) * 2 + blk % 2
                perm.append((dp * n_blk + blk, to))
        return lax.ppermute(v, ("dp", "blk"), perm)

    def share_pieces(keep, recv, member):
        def piece(s):
            mine = lax.dynamic_index_in_dim(keep, member ^ s, 0, keepdims=False)
            theirs = lax.dynamic_index_in_dim(recv, member ^ s, 0, keepdims=False)
            return (mine.astype(f32) + theirs.astype(f32)).astype(bf16)

        return [piece(s) for s in range(m)]

    def add(own, got):
        total = own.astype(f32)
        for part in got:
            total = total + part.astype(f32)
        return total.astype(bf16)

    def body(
        tokens, bucket_ids, seq_lengths, w_query, b_query, w_key, w_value, b_value, w_out, b_out,
        norm1_gain, norm1_bias, w_inner, b_inner, w_outer, b_outer, norm2_gain, norm2_bias,
        cotangent,
    ):
        row_count, block, width = tokens.shape
        count = row_count * block
        local = w_query.shape[1]
        heads = local // HEAD_DIM
        lanes = heads * LANES
        units = w_inner.shape[1]
        blk = lax.axis_index("blk").astype(i32)
        z = lax.axis_index("tensor").astype(i32)
        core = blk % 2
        member = (lax.axis_index("dp") * half_blk + blk // 2).astype(i32)
        cut_at = (lax.axis_index("dp") % 2) * n_blk + blk
        at = jnp.stack([z, core, blk, member, cut_at]).astype(i32)
        tok = tokens.reshape(count, width)
        cot = cotangent.reshape(count, width)
        row = lambda v: v.reshape(1, -1)
        wq_t, wk_t, wv_t = w_query.T, w_key.T, w_value.T
        fence = lax.optimization_barrier

        part = local // 4
        piece_rows = (width + units) // 8
        kv, piece, out_piece = pl.pallas_call(
            front_kernel,
            out_shape=(
                near((count, lanes), bf16), near((piece_rows + part, width), bf16),
                near((part, width), bf16),
            ),
            in_specs=[SMEM] + [HBM] * 6 + [VMEM],
            out_specs=(VMEM,) * 3,
            scratch_shapes=[
                pltpu.VMEM((count, width), bf16), pltpu.VMEM((local, width), bf16),
                pltpu.VMEM((local, width), bf16), pltpu.SemaphoreType.DMA((6,)),
            ],
            compiler_params=pltpu.CompilerParams(vmem_limit_bytes=16 * MIB),
            name="front",
        )(at, *[pltpu.with_memory_space_constraint(v, pltpu.HBM) for v in (tok, wk_t, wv_t, w_inner, w_outer, w_out)], row(b_value))
        kv, piece, out_piece, b_far = fence((kv, piece, out_piece, b_inner))
        kv_far = flip(kv, 2)
        kv_core = flip(kv, 1)
        pieces = [swap(piece, 1)] + [swap(out_piece, s) for s in range(2, n)]
        b_inner_far = swap(b_far, 1)
        kv_far, b_inner_far, *pieces = fence((kv_far, b_inner_far, *pieces))
        kv_both = flip(kv_far, 1)
        own_piece = jnp.concatenate(pieces, axis=0)
        ffn_piece = pieces[0][:piece_rows]

        def across(v, dp_bit, blk_bit):
            there = lambda i: ((i // n_blk) ^ dp_bit) * n_blk + ((i % n_blk) ^ blk_bit)
            return lax.ppermute(v, ("dp", "blk"), [(i, there(i)) for i in range(n_dp * n_blk)])

        arrived = {4: across(ffn_piece, 1, 0), 6: across(ffn_piece, 1, 2)}
        arrived |= {0: own_piece, 2: across(own_piece, 0, 2)}

        q = call(q_kernel, near((count, lanes), bf16), "query_rows", (tok, wq_t, row(b_query)), us=0.5)
        kvs = [kv, kv_core, kv_far, kv_both]

        prob_rows = 2 * heads * BLOCK
        hp_other, hp_mine, probs_other, probs_mine, hp_late = pl.pallas_call(
            functools.partial(attend_kernel, n_blk, (2, 3, 0, 1)),
            out_shape=(near((2 * PACKED, LANES), bf16),) * 2
            + (pltpu.HBM((prob_rows, n_blk * BLOCK), bf16),) * 2
            + (pltpu.HBM((4 * PACKED, LANES), bf16),),
            in_specs=[SMEM] * 3 + [VMEM] * (1 + n_blk),
            out_specs=(VMEM,) * 2 + (HBM,) * 3,
            scratch_shapes=[
                pltpu.VMEM((2 * prob_rows, n_blk * BLOCK), bf16), pltpu.SemaphoreType.DMA((6,)),
            ],
            compiler_params=pltpu.CompilerParams(vmem_limit_bytes=16 * MIB),
            cost_estimate=pl.CostEstimate(
                flops=int(ATTEND_US * FLOPS_US), bytes_accessed=1, transcendentals=0
            ),
            name="attend",
        )(at, bucket_ids, seq_lengths, q, *kvs)
        hps = {0: hp_mine, 1: swap(hp_other, 1), 2: swap(hp_mine, 2), 3: swap(hp_other, 3)}
        held = [arrived[2], arrived[4], arrived[6]]
        hps[1], hps[2], hps[3], *held = fence((hps[1], hps[2], hps[3], *held))
        arrived[2], arrived[4], arrived[6] = held
        arrived |= {j + 1: flip(v, 1) for j, v in arrived.items()}
        w_out_all, w_inner_far, w_outer_far = call(
            functools.partial(weights_kernel, n),
            (near((n * local, width), bf16), near(w_inner.shape, bf16), near(w_outer.shape, bf16)),
            "far_weights",
            (at, w_out, *[arrived[j] for j in range(8)]),
            us=2.2,
            scalars=1,
        )

        chunk = lambda rows, dt: near((rows, width), dt)
        gains1 = (row(norm1_gain), row(norm1_bias))

        def ffn(i, heads_in):
            return call(
                functools.partial(ffn_kernel, n, i),
                (
                    chunk(BLOCK, bf16), chunk(BLOCK, f32), near((BLOCK, LANES), f32),
                    chunk(BLOCK, bf16), near((BLOCK, units), bf16), near((BLOCK, units), bf16),
                    near((2 * BLOCK, units), bf16),
                )
                + ((near((n * PACKED, LANES), bf16),) if i == 0 else ()),
                "ffn",
                (
                    at, tok, w_out_all, row(b_out), *gains1, w_inner, w_inner_far, row(b_inner),
                    row(b_inner_far), w_outer, w_outer_far, *heads_in,
                ),
                us=2.4,
                scalars=1,
                scratch=[pltpu.VMEM((n, BLOCK, width), f32)],
            )

        *row0, second_heads = ffn(0, [hps[s] for s in range(n)])
        parts, n1s, s1s, lows, acts, acts_far, slopes = map(list, zip(row0, ffn(1, [second_heads])))
        theirs = [swap(v, 2) for v in parts]

        def ffn_back(i):
            return call(
                functools.partial(ffn_back_kernel, i),
                (
                    chunk(BLOCK, bf16), chunk(BLOCK, bf16), near((BLOCK, units), bf16),
                    near((BLOCK, units), bf16), chunk(BLOCK, bf16), chunk(BLOCK, f32), chunk(8, f32),
                ),
                "ffn_back",
                (
                    at, cot, n1s[i], slopes[i], parts[i], theirs[i], *gains1, row(b_outer),
                    row(norm2_gain), row(norm2_bias), w_inner, w_inner_far, w_outer, w_outer_far,
                ),
                us=2.7,
                scalars=1,
            )

        outs, dffns, dinners, dinners_far, parts2, dres2, sums2 = map(list, zip(*[ffn_back(i) for i in range(2)]))
        theirs2 = [swap(v, 2) for v in parts2]
        keep1, send1 = call(
            functools.partial(ffn_grad_kernel, m),
            (near((m, 2, width // m, width), bf16),) * 2,
            "ffn_grads",
            (at, *lows, *acts, *acts_far, *dffns, *dinners, *dinners_far),
            us=FILL_US,
            vmem=24,
            scalars=1,
        )
        recv1 = flip(send1, 1)
        pieces1 = share_pieces(keep1, recv1, member)

        def norm_back(i):
            return call(
                functools.partial(norm_back_kernel, n),
                (
                    chunk(BLOCK, f32), chunk(BLOCK + 16, bf16), near((PACKED, LANES), bf16),
                    near((PACKED, LANES), bf16),
                ),
                "norm_back",
                (at, parts2[i], theirs2[i], dres2[i], n1s[i], s1s[i], gains1[0], w_out_all, sums2[i]),
                us=1.2,
                scalars=1,
            )

        dres1, shares, dheads, dheads_far = map(list, zip(*[norm_back(i) for i in range(2)]))
        dheads += [swap(v, 1) for v in dheads_far]
        shares += [swap(v, 1) for v in shares]
        outs += [swap(v, 1) for v in outs]

        def attend_back(ids, probs, *packed):
            return call(
                functools.partial(attend_back_kernel, n_blk, ids),
                (
                    near((2 * BLOCK, local), bf16), near((half_blk, 2, lanes, BLOCK), bf16),
                    near((half_blk, 2, lanes, BLOCK), bf16),
                ),
                "attend_back",
                (at, *packed, q, probs, *kvs),
                scalars=1,
                us=BACK_US,
            )

        own = attend_back((0, 1), probs_mine, dheads[0], dheads[1])
        after, dheads[2], dheads[3], pieces1 = fence((own[1], dheads[2], dheads[3], pieces1))
        own = (own[0], after, own[2])
        other = attend_back((2, 3), probs_other, dheads[2], dheads[3])

        def exchange(third):
            _, send, keep = third
            recv = flip(send, 1)
            return recv, (keep[1].astype(f32) + recv[1].astype(f32)).astype(bf16)

        def input_part(third, recv, far, us):
            dq, _, keep = third
            return call(
                input_kernel,
                (chunk(2 * BLOCK, bf16), near((lanes, 2 * BLOCK), bf16), chunk(8, f32)),
                "input_part",
                (dq, keep, recv, far, wq_t, wk_t, wv_t),
                us=us,
            )

        recv_own, sum_own = exchange(own)
        recv_other, sum_other = exchange(other)
        far_own, far_other = flip(sum_own, 2), flip(sum_other, 2)
        far_own, far_other, pieces1 = fence((far_own, far_other, pieces1))
        part, *late = input_part(other, recv_other, far_other, 1.0)
        part, pieces1 = fence((part, pieces1))
        from_near, *ends = fence((swap(part, 1), *shares[2:]))
        shares[2:] = ends
        got1 = [flip_member(v, s) for s, v in enumerate(pieces1[1:], 1)]
        part_own, dkv_own, sums_own = input_part(own, recv_own, far_own, INPUT_US)
        pair = (part_own.astype(f32) + from_near.astype(f32)).astype(bf16)

        rows2 = 2 * local + 16
        rows2 += -rows2 % (16 * m)
        hp_late, _ = fence((hp_late, pair))
        keep2, send2 = call(
            functools.partial(attend_grad_kernel, m),
            (chunk(rows2, bf16), chunk(rows2, bf16)),
            "attend_grads",
            (
                at, tok, hp_late, *shares, own[0], other[0], dkv_own, late[0], sums_own,
                late[1],
            ),
            us=GRADS_US,
            scalars=1,
            scratch=[pltpu.VMEM((n, 8, width), f32)],
        )
        by_member = lambda v: v.reshape(m, rows2 // m, width)
        pieces2 = share_pieces(by_member(keep2), by_member(flip(send2, 1)), member)
        got2 = [flip_member(v, s) for s, v in enumerate(pieces2[1:], 1)]
        got1, _, _ = fence((got1, keep2, pair))
        total1 = fence(add(pieces1[0], got1))
        near1 = swap(total1[1], 1)
        crossed, *ends = fence((swap(pair, 2), *outs[2:]))
        outs[2:] = ends
        near1, got2 = fence((near1, got2))
        d_tok = pair.astype(f32) + crossed.astype(f32) + jnp.concatenate(dres1, axis=0)
        d_tok = d_tok.astype(bf16)
        share = call(
            share_kernel,
            chunk(width // m + rows2 // m, bf16),
            "grad_share",
            (total1, near1, pieces2[0], *got2),
            us=0.5,
        )
        shares_in = [flip_member(share, k) for k in range(1, m)]
        shares_in[0], d_far = fence((shares_in[0], swap(d_tok, 1)))
        d_toks = [d_tok, d_far]
        assemble = lambda parts, name: call(
            rows_kernel,
            shape((row_count, block, width), bf16),
            name,
            (at, *parts),
            us=1.5,
            scalars=1,
        )
        output = assemble(outs, "output_rows")
        d_tokens = assemble(d_toks, "input_grad_rows")
        mine = [share] + shares_in
        held, _, _ = fence((shares_in[0], output, d_tokens))
        others = [flip(v, 1) for v in [share, held] + shares_in[1:]]
        vector = shape((width,), f32)
        short = shape((local,), f32)
        wide = shape((local, width), f32)
        squares = (pltpu.HBM((width, units), f32), pltpu.HBM((units, width), f32))
        rows1 = width // m

        def grads_out(kernel, outs, arrays, before, members, scratch, us, name):
            return pl.pallas_call(
                kernel,
                out_shape=squares + outs,
                in_specs=[SMEM] + [VMEM] * len(arrays) + [HBM] * len(before),
                out_specs=(HBM,) * 2 + (VMEM,) * len(outs),
                scratch_shapes=scratch
                + [pltpu.VMEM((2, members, rows1, width), f32), pltpu.SemaphoreType.DMA((2 * members,))],
                input_output_aliases={1 + len(arrays) + k: k for k in range(len(before))},
                compiler_params=pltpu.CompilerParams(vmem_limit_bytes=24 * MIB),
                cost_estimate=pl.CostEstimate(
                    flops=int(us * FLOPS_US), bytes_accessed=1, transcendentals=0
                ),
                name=name,
            )(at, *arrays, *before)

        early = grads_out(
            functools.partial(early_kernel, m), (), (*mine[:-1], *others[:-1]), (), m - 1, [], 2.0,
            "early_grads",
        )
        (
            g_w_inner, g_w_outer, g_w_out, g_q, g_k, g_v, g_gain1, g_bias1, g_b_out, g_gain2, g_bias2,
            g_b_outer, g_b_inner, g_b_query, g_b_value,
        ) = grads_out(
            functools.partial(final_kernel, m), (wide,) * 4 + (vector,) * 7 + (short,) * 2,
            (*mine, *others), tuple(early), 1, [pltpu.VMEM((2, m, rows2 // m, width), bf16)], 2.0,
            "grads_out",
        )
        return (
            output, d_tokens, g_q.T, g_b_query, g_k.T, g_v.T, g_b_value, g_w_out, g_b_out, g_gain1,
            g_bias1, g_w_inner, g_b_inner, g_w_outer, g_b_outer, g_gain2, g_bias2,
        )

    spread, cols, vec, rows_ = P("dp", "blk", None), P(None, "tensor"), P("tensor"), P("tensor", None)
    return jax.shard_map(
        body,
        mesh=mesh,
        in_specs=(
            spread, P("dp"), P("dp", None), cols, vec, cols, cols, vec, rows_, P(), P(), P(),
            cols, vec, rows_, P(), P(), P(), spread,
        ),
        out_specs=(
            spread, spread, cols, vec, cols, cols, vec, rows_, P(), P(), P(), cols, vec, rows_,
            P(), P(), P(),
        ),
        check_vma=False,
    )
```
